32 devices in a mesh: ax: 4 (over y, core), az: 4 (over z), rad: 2 (over x).
Axes of the slice: x: 2, y: 2, z: 4, core: 2. Of those that a mesh axis runs over, the one named last changes fastest.
Arguments:
- density: float32 [32, 64, 256], P('ax', 'az', 'rad'), may hold values from 0.855 to 1.21
- velocity: float32 [3, 32, 64, 256], P(None, 'ax', 'az', 'rad'), may hold values from -2.9 to 2.9
- pressure: float32 [32, 64, 256], P('ax', 'az', 'rad'), may hold values from 0.51 to 1.84
- panel_cell: int32 [1024], P(('ax', 'az', 'rad')), may hold values from -1 to 16383, as said below
- obs_weight: bfloat16 [8192, 1024], P(('ax', 'az', 'rad')), may hold values from -1 to 1
- bin_offset: int32 [32, 32], P(('ax', 'az', 'rad')), may hold values from 0 to 125
Outputs:
- state: float32 [5, 32, 64, 256], P(None, 'ax', 'az', 'rad')
- signal: float32 [8192, 128], P(('ax', 'az', 'rad'))
The draws below stay inside these ranges and needn't reach their ends.
Inputs may be any that keep to these rules, and one draw needn't show every extreme that they name: `panel_cell`: live slots of one device come first, then -1; some device has all 32 slots live.
All inputs are finite; a program needn't handle non-finite values.
Results may differ from the reference program's by a relative error of at most 0.0029.
Values may be sent and summed in bfloat16 or wider, within the bound.
No kernel may reach another device: no remote copies, remote signals or barrier semaphores. Data moves between devices by JAX's collectives and lax.ppermute only.
A program may use at most 64 MiB of HBM per device.

```python
import jax
import jax.numpy as jnp
from jax import lax

CA = 8
CZ = 16
CR = 128
PSLOT = 32
OBS_DEV = 256
NB = 128
NA = 32
NZ = 64
NR = 256
PANELS = 1024
OBSERVERS = 8192
N_AZ = 4
N_RAD = 2
DEVICES = 32


def spread_blocks(level):
    wide = jnp.repeat(level, CA, axis=level.ndim - 3)
    wide = jnp.repeat(wide, CZ, axis=level.ndim - 2)
    return jnp.repeat(wide, CR, axis=level.ndim - 1)


def block_shape():
    return (NA // CA, NZ // CZ, NR // CR)


def draw_density(key, part):
    key = jax.random.fold_in(key, 3)
    key_level, key_cell = jax.random.split(key)
    level = jax.random.uniform(key_level, block_shape(), jnp.float32, 0.95, 1.1)
    factor = jax.random.uniform(key_cell, (NA, NZ, NR), jnp.float32, 0.9, 1.1)
    return (spread_blocks(level) * factor).astype(jnp.float32)


def draw_velocity(key, part):
    key = jax.random.fold_in(key, 5)
    key_level, key_cell = jax.random.split(key)
    lshape = (3,) + block_shape()
    level = jnp.clip(jax.random.normal(key_level, lshape, jnp.float32), -2.0, 2.0)
    noise = jnp.clip(0.3 * jax.random.normal(key_cell, (3, NA, NZ, NR), jnp.float32), -0.9, 0.9)
    return (spread_blocks(level) + noise).astype(jnp.float32)


def draw_pressure(key, part):
    key = jax.random.fold_in(key, 9)
    key_level, key_cell = jax.random.split(key)
    level = jnp.exp(jax.random.uniform(key_level, block_shape(), jnp.float32, jnp.log(0.6), jnp.log(1.6)))
    factor = jax.random.uniform(key_cell, (NA, NZ, NR), jnp.float32, 0.85, 1.15)
    return (spread_blocks(level) * factor).astype(jnp.float32)


def draw_panel_cell(key, part):
    key = jax.random.fold_in(key, 7)
    key_count, key_full, key_cell = jax.random.split(key, 3)
    ndev = PANELS // PSLOT
    counts = jax.random.randint(key_count, (ndev,), 0, PSLOT + 1)
    full = jax.random.randint(key_full, (), 0, ndev)
    counts = jnp.where(jnp.arange(ndev) == full, PSLOT, counts)
    cells = jax.random.randint(key_cell, (ndev, PSLOT), 0, CA * CZ * CR)
    live = jnp.arange(PSLOT)[None, :] < counts[:, None]
    return jnp.where(live, cells, -1).reshape(-1).astype(jnp.int32)


def set_ends(values, key, low, high):
    place = [jax.random.randint(jax.random.fold_in(key, axis), (), 0, length) for axis, length in enumerate(values.shape)]
    widest = values.shape.index(max(values.shape))
    next_to = place[:widest] + [(place[widest] + 1) % values.shape[widest]] + place[widest + 1:]
    return values.at[tuple(place)].set(low).at[tuple(next_to)].set(high)


def shard_levels(own_key, shape, cuts, low, largest):
    gain, own = 1.0, jax.random.fold_in(own_key, 6)
    for dim, parts in cuts:
        heights = jnp.exp(jax.random.uniform(jax.random.fold_in(own, dim), (parts,), jnp.float32, low / len(cuts), largest / len(cuts)))
        gain = gain * jnp.repeat(heights, shape[dim] // parts).reshape([-1 if axis == dim else 1 for axis in range(len(shape))])
    return gain


def gaussian(rng, shape, spread, bound, shards=(), held_as=jnp.bfloat16):
    values = jax.random.normal(rng, shape, jnp.float32) * spread
    if len(shards) > 0:
        values = shard_levels(rng, shape, shards, -0.22, 0.18) * values
    return jnp.clip(values, min=-bound, max=bound).astype(held_as)


def setup_inputs(seed: int = 0) -> dict:
    key_list = jax.random.split(jax.random.key(seed), 7)
    return {
        "density": draw_density(jax.random.fold_in(key_list[6], 71), 0),
        "velocity": draw_velocity(jax.random.fold_in(key_list[6], 71), 0),
        "pressure": draw_pressure(jax.random.fold_in(key_list[6], 71), 0),
        "panel_cell": draw_panel_cell(jax.random.fold_in(key_list[6], 71), 0),
        "obs_weight": gaussian(key_list[4], (OBSERVERS, PANELS), PSLOT ** -0.5, 1.0, ((0, 32),)),
        "bin_offset": set_ends(jax.random.randint(key_list[5], (DEVICES, DEVICES), 0, NB - 2), jax.random.fold_in(key_list[5], 1), 0, (NB - 2) - 1).astype(jnp.int32),
    }


GAMMA_M = 0.4
LAMBDA = 0.1
P_REF = 1.0


def primitives(state):
    rho = state[0]
    vel = state[1:4] / rho
    pres = GAMMA_M * (state[4] - 0.5 * rho * jnp.sum(vel * vel, axis=0))
    return jnp.concatenate([rho[None], vel, pres[None]], 0)


def flux(prim, direc):
    rho = prim[0]
    vel = prim[1:4]
    pres = prim[4]
    normal = vel[direc]
    energy = pres / GAMMA_M + 0.5 * rho * jnp.sum(vel * vel, axis=0)
    moment = rho[None] * normal[None] * vel
    moment = moment.at[direc].add(pres)
    return jnp.concatenate([(rho * normal)[None], moment, ((energy + pres) * normal)[None]], 0)


def deriv(padded, axis, count):
    def piece(low):
        return lax.slice_in_dim(padded, low, low + count, axis=axis)
    return (piece(0) - 8.0 * piece(1) + 8.0 * piece(3) - piece(4)) / 12.0


def tendency(state):
    prim = primitives(state)
    total = jnp.zeros_like(state)
    for direc, mode in ((0, "constant"), (1, "wrap"), (2, "constant")):
        axis = direc + 1
        widths = [(0, 0)] * 4
        widths[axis] = (2, 2)
        padded = jnp.pad(flux(prim, direc), widths, mode=mode)
        total = total + deriv(padded, axis, state.shape[axis])
    return -LAMBDA * total, prim


def sample(state, prim, panel_cell):
    npan = panel_cell.shape[0]
    dev = jnp.arange(npan, dtype=jnp.int32) // PSLOT
    i_ax = dev // (N_AZ * N_RAD)
    i_az = (dev // N_RAD) % N_AZ
    i_rad = dev % N_RAD
    cell = jnp.maximum(panel_cell, 0)
    g_ax = i_ax * CA + cell // (CZ * CR)
    g_az = i_az * CZ + (cell // CR) % CZ
    g_rad = i_rad * CR + cell % CR
    value = prim[4] - P_REF + state[1]
    picked = value[g_ax, g_az, g_rad]
    return jnp.where(panel_cell >= 0, picked, 0.0).astype(jnp.bfloat16)


def reference(density, velocity, pressure, panel_cell, obs_weight, bin_offset):
    momentum = density[None] * velocity
    energy = pressure / GAMMA_M + 0.5 * density * jnp.sum(velocity * velocity, axis=0)
    first = jnp.concatenate([density[None], momentum, energy[None]], 0)
    change, prim = tendency(first)
    samples = [sample(first, prim, panel_cell)]
    second = first + change
    change, prim = tendency(second)
    samples.append(sample(second, prim, panel_cell))
    third = 0.75 * first + 0.25 * (second + change)
    change, prim = tendency(third)
    samples.append(sample(third, prim, panel_cell))
    final = first / 3.0 + (2.0 / 3.0) * (third + change)
    ndev = bin_offset.shape[0]
    q_all = jnp.stack(samples, 0).astype(jnp.float32).reshape(3, ndev, PSLOT)
    blocks = obs_weight.reshape(ndev, OBS_DEV, ndev, PSLOT)
    times = jnp.arange(NB, dtype=jnp.int32)
    sections = jnp.arange(3, dtype=jnp.int32)

    def one_owner(item):
        weights, offs = item
        grouped = jnp.einsum("obp,sbp->sob", weights.astype(jnp.float32), q_all, precision=lax.Precision.HIGHEST)
        table = (times[None, None, :] == offs[None, :, None] + sections[:, None, None]).astype(jnp.float32)
        return jnp.einsum("sob,sbt->ot", grouped, table, precision=lax.Precision.HIGHEST)

    signal = lax.map(one_owner, (blocks, bin_offset)).reshape(ndev * OBS_DEV, NB)
    return final, signal
```

```python
import jax
import jax.numpy as jnp
from jax import lax
from jax.sharding import PartitionSpec as P

NB = 128
GAMMA_M = 0.4
LAMBDA = 0.1
P_REF = 1.0


def shift_pairs(count, periodic):
    pairs = [(i, i + 1) for i in range(count - 1)]
    if periodic:
        pairs.append((count - 1, 0))
    return pairs


def with_halo(block, axis, dim, width, periodic):
    count = lax.axis_size(axis)
    forward = shift_pairs(count, periodic)
    backward = [(target, source) for source, target in forward]
    last = lax.slice_in_dim(block, block.shape[dim] - width, None, axis=dim)
    first = lax.slice_in_dim(block, 0, width, axis=dim)
    low = lax.ppermute(last, axis, forward)
    high = lax.ppermute(first, axis, backward)
    return jnp.concatenate([low, block, high], axis=dim)


def with_swap(block, axis, dim, width):
    index = lax.axis_index(axis)
    last = lax.slice_in_dim(block, block.shape[dim] - width, None, axis=dim)
    first = lax.slice_in_dim(block, 0, width, axis=dim)
    edge = jnp.where(index == 0, last, first)
    moved = jnp.moveaxis(edge, dim, 0).reshape(-1, block.shape[1] * block.shape[2])
    got = lax.ppermute(moved, axis, [(0, 1), (1, 0)])
    got = jnp.moveaxis(got.reshape((width,) + edge.shape[:3]), 0, dim)
    zero = jnp.zeros_like(got)
    low = jnp.where(index == 1, got, zero)
    high = jnp.where(index == 0, got, zero)
    return jnp.concatenate([low, block, high], axis=dim)


def primitives(state):
    rho = state[0]
    vel = state[1:4] / rho
    pres = GAMMA_M * (state[4] - 0.5 * rho * jnp.sum(vel * vel, axis=0))
    return jnp.concatenate([rho[None], vel, pres[None]], 0)


def flux(prim, direc):
    rho = prim[0]
    vel = prim[1:4]
    pres = prim[4]
    normal = vel[direc]
    energy = pres / GAMMA_M + 0.5 * rho * jnp.sum(vel * vel, axis=0)
    moment = rho[None] * normal[None] * vel
    moment = moment.at[direc].add(pres)
    return jnp.concatenate([(rho * normal)[None], moment, ((energy + pres) * normal)[None]], 0)


def deriv(padded, axis, count):
    def piece(low):
        return lax.slice_in_dim(padded, low, low + count, axis=axis)

    return (piece(0) - 8.0 * piece(1) + 8.0 * piece(3) - piece(4)) / 12.0


def tendency(state):
    prim = primitives(state)
    pad_ax = with_halo(flux(prim, 0), "ax", 1, 2, False)
    pad_az = with_halo(flux(prim, 1), "az", 2, 2, True)
    if lax.axis_size("rad") == 2:
        pad_rad = with_swap(flux(prim, 2), "rad", 3, 2)
    else:
        pad_rad = with_halo(flux(prim, 2), "rad", 3, 2, False)
    total = deriv(pad_ax, 1, state.shape[1])
    total = total + deriv(pad_az, 2, state.shape[2])
    total = total + deriv(pad_rad, 3, state.shape[3])
    return (-LAMBDA * total, prim)


def sample(state, prim, panel_cell):
    value = (prim[4] - P_REF + state[1]).reshape(-1)
    picked = value[jnp.maximum(panel_cell, 0)]
    return jnp.where(panel_cell >= 0, picked, 0.0)


def local(density, velocity, pressure, panel_cell, obs_weight, bin_offset):
    slots = panel_cell.shape[0]
    offsets = bin_offset[0]
    ndev = offsets.shape[0]
    times = jnp.arange(NB, dtype=jnp.int32)

    momentum = density[None] * velocity
    energy = pressure / GAMMA_M + 0.5 * density * jnp.sum(velocity * velocity, axis=0)
    first = jnp.concatenate([density[None], momentum, energy[None]], 0)
    change, prim = tendency(first)
    samples = [sample(first, prim, panel_cell)]
    second = first + change
    change, prim = tendency(second)
    samples.append(sample(second, prim, panel_cell))
    third = 0.75 * first + 0.25 * (second + change)
    change, prim = tendency(third)
    samples.append(sample(third, prim, panel_cell))

    row = jnp.concatenate(samples + [jnp.zeros((128 - 3 * slots,), jnp.float32)])
    row = jnp.broadcast_to(row[None, None], (ndev, 1, 128))
    rows = lax.all_to_all(row, ("ax", "az", "rad"), 0, 0, tiled=True)
    rows = rows[:, 0, : 3 * slots].reshape(ndev, 3, slots).astype(jnp.bfloat16)

    final = first / 3.0 + 2.0 / 3.0 * (third + change)

    bins = offsets[:, None, None] + jnp.arange(3, dtype=jnp.int32)[None, :, None]
    hit = times[None, None, :] == bins
    spread = jnp.zeros((ndev, slots, NB), jnp.bfloat16)
    for section in range(3):
        spread = spread + jnp.where(hit[:, section][:, None, :], rows[:, section, :, None], 0)
    signal = jnp.dot(
        obs_weight, spread.reshape(ndev * slots, NB), preferred_element_type=jnp.float32
    )
    return (final, signal)


def solution(mesh):
    in_specs = (
        P("ax", "az", "rad"),
        P(None, "ax", "az", "rad"),
        P("ax", "az", "rad"),
        P(("ax", "az", "rad")),
        P(("ax", "az", "rad"), None),
        P(("ax", "az", "rad"), None),
    )
    out_specs = (P(None, "ax", "az", "rad"), P(("ax", "az", "rad"), None))
    return jax.shard_map(local, mesh=mesh, in_specs=in_specs, out_specs=out_specs, check_vma=False)
```

```python
import functools

import jax
import jax.numpy as jnp
from jax import lax
from jax.experimental import pallas as pl
from jax.experimental.pallas import tpu as pltpu
from jax.sharding import PartitionSpec as P

NB = 128
GAMMA_M = 0.4
LAMBDA = 0.1
P_REF = 1.0
REACH = 6
MID = 4
STRIP = 8
C1 = -LAMBDA * 8.0 / 12.0
C2 = LAMBDA / 12.0
HIGHEST = lax.Precision.HIGHEST
VMEM = pltpu.MemorySpace.VMEM
SMEM = pltpu.MemorySpace.SMEM


def params():
    return pltpu.CompilerParams(vmem_limit_bytes=56 * 1024 * 1024)


def call(kernel, outs, in_spaces, scratch=()):
    return pl.pallas_call(
        kernel,
        out_shape=outs,
        in_specs=[pl.BlockSpec(memory_space=s) for s in in_spaces],
        out_specs=jax.tree.map(lambda _: pl.BlockSpec(memory_space=VMEM), outs),
        scratch_shapes=list(scratch),
        compiler_params=params(),
    )


def f32(*shape):
    return jax.ShapeDtypeStruct(shape, jnp.float32)


def field(f, den, vel, pre):
    return den if f == 0 else (pre if f == 4 else vel.at[f - 1])


def pack_ax(den, vel, pre, low_out, high_out):
    ca = den.shape[0]
    for f in range(5):
        home = field(f, den, vel, pre)
        low_out[f] = home[0:REACH]
        high_out[f] = home[ca - REACH : ca]


def pack_az(den, vel, pre, lo, hi, low_out, high_out):
    ca, cz, _ = den.shape
    for f in range(5):
        home = field(f, den, vel, pre)
        for out, rows in ((low_out, slice(0, STRIP)), (high_out, slice(cz - STRIP, cz))):
            out[f, 0:MID] = lo[f, REACH - MID : REACH, rows]
            out[f, MID : MID + ca] = home[:, rows]
            out[f, MID + ca : ca + 2 * MID] = hi[f, 0:MID, rows]


def one_hot_lanes(start, lanes):
    row = lax.broadcasted_iota(jnp.int32, (8, lanes), 0)
    lane = lax.broadcasted_iota(jnp.int32, (8, lanes), 1)
    return jnp.where((row < REACH) & (lane == row + start), 1.0, 0.0)


def pack_rad(ends, den, vel, pre, lo, hi, azlo, azhi, *outs):
    ca, cz, cr = den.shape
    rad = lax.axis_index("rad")
    planes = ca + 2 * MID
    rows = cz + 2 * STRIP
    for f in range(5):
        home = field(f, den, vel, pre)
        mid = jnp.concatenate([lo[f, REACH - MID : REACH], home[...], hi[f, 0:MID]], axis=0)
        whole = jnp.concatenate([azlo[f], mid, azhi[f]], axis=1).reshape(planes * rows, cr)
        for end, out in zip(ends, outs):
            start = {"low": 0, "high": cr - REACH, "either": jnp.where(rad == 0, cr - REACH, 0)}[end]
            out[f] = lax.dot_general(
                one_hot_lanes(start, cr),
                whole,
                (((1,), (1,)), ((), ())),
                precision=HIGHEST,
                preferred_element_type=jnp.float32,
            )


def fluxes(rho, mom, vel, pres, energy, want):
    total = energy + pres
    out = {}
    for d in want:
        parts = [mom[d]]
        for j in range(3):
            parts.append(mom[d] * vel[j] + pres if j == d else mom[d] * vel[j])
        parts.append(total * vel[d])
        out[d] = parts
    return out


def diff(value, axis):
    n = value.shape[axis]
    near = pltpu.roll(value, n - 1, axis) - pltpu.roll(value, 1, axis)
    far = pltpu.roll(value, n - 2, axis) - pltpu.roll(value, 2, axis)
    return C1 * near + C2 * far


def stages(counts, den, vel, pre, lo, hi, azlo, azhi, rlo, rhi, cells, cell_col, state, q_out, prim, first, second, third, fax, part, value, picked):
    n_ax, n_rad = counts
    ca, cz, cr = den.shape
    slots = cells.shape[0]
    rows = cz + 2 * STRIP
    wide = 2 * cr
    planes = ca + 2 * REACH
    inner = (slice(STRIP, STRIP + cz), slice(0, cr))
    full = (slice(0, rows), slice(0, wide))
    ax = lax.axis_index("ax")
    rad = lax.axis_index("rad")

    lane = lax.broadcasted_iota(jnp.int32, (rows, wide), 1)
    lane_ok = (
        (lane < cr)
        | ((lane < cr + REACH) & (rad < n_rad - 1))
        | ((lane >= wide - REACH) & (rad > 0))
    )
    lane_base = jnp.where(lane_ok, 0.0, 1.0)[:, cr:wide]

    place_high = one_hot_lanes(0, cr)
    place_low = one_hot_lanes(cr - REACH, cr)
    place_high = jnp.where(rad < n_rad - 1, place_high, 0.0)
    place_low = jnp.where(rad > 0, place_low, 0.0)
    inside = slice(REACH - MID, REACH + ca + MID)
    for f in range(5):
        home = field(f, den, vel, pre)
        prim[f, 0:REACH, STRIP : STRIP + cz, 0:cr] = lo[f]
        prim[f, REACH : REACH + ca, STRIP : STRIP + cz, 0:cr] = home[...]
        prim[f, REACH + ca : planes, STRIP : STRIP + cz, 0:cr] = hi[f]
        prim[f, inside, 0:STRIP, 0:cr] = azlo[f]
        prim[f, inside, STRIP + cz : rows, 0:cr] = azhi[f]
        side = 0.0
        for got, place in ((rhi, place_high), (rlo, place_low)):
            side = side + lax.dot_general(
                got[f],
                place,
                (((0,), (0,)), ((), ())),
                precision=HIGHEST,
                preferred_element_type=jnp.float32,
            )
        side = side.reshape(ca + 2 * MID, rows, cr)
        if f == 0:
            side = side + lane_base[None]
        prim[f, inside, :, cr:wide] = side

    def load(ref, j):
        return [ref[f, j] for f in range(5)]

    def work(stage, j, with_sides):
        if stage == 0:
            rho, u, v, w, pres = load(prim, j)
            vels = [u, v, w]
            mom = [rho * x for x in vels]
            energy = pres * (1.0 / GAMMA_M) + 0.5 * (mom[0] * u + mom[1] * v + mom[2] * w)
            if with_sides:
                for f, x in enumerate([rho] + mom + [energy]):
                    first[f, j] = x
        else:
            rho, m0, m1, m2, energy = load(second if stage == 1 else third, j)
            mom = [m0, m1, m2]
            inv = 1.0 / rho
            vels = [m * inv for m in mom]
            pres = GAMMA_M * (energy - 0.5 * (m0 * vels[0] + m1 * vels[1] + m2 * vels[2]))
        got = fluxes(rho, mom, vels, pres, energy, (0, 1, 2) if with_sides else (0,))
        if with_sides:
            value[stage, j] = (pres - P_REF + mom[0])[inner]
            region = inner if stage == 2 else full
            for f in range(5):
                fax[f, j] = got[0][f]
                part[(f, j) + region] = (diff(got[1][f], 0) + diff(got[2][f], 1))[region]
        else:
            for f in range(5):
                fax[(f, j) + inner] = got[0][f][inner]

    def update(stage, j, region):
        beyond = ((j < REACH) & (ax == 0)) | ((j >= REACH + ca) & (ax == n_ax - 1))
        ok = lane_ok[region] & jnp.logical_not(beyond)
        for f in range(5):
            near = fax[(f, j + 1) + region] - fax[(f, j - 1) + region]
            far = fax[(f, j + 2) + region] - fax[(f, j - 2) + region]
            change = C1 * near + C2 * far + part[(f, j) + region]
            base = 1.0 if f == 0 else 0.0
            u0 = first[(f, j) + region]
            if stage == 0:
                second[(f, j) + region] = jnp.where(ok, u0 + change, base)
            elif stage == 1:
                mixed = 0.75 * u0 + 0.25 * (second[(f, j) + region] + change)
                third[(f, j) + region] = jnp.where(ok, mixed, base)
            else:
                mixed = u0 * (1.0 / 3.0) + (2.0 / 3.0) * (third[(f, j) + region] + change)
                state[f, j - REACH] = mixed

    def loop(low, high, body):
        @pl.loop(low, high)
        def _(j):
            body(j)

    start, stop = REACH, REACH + ca
    for stage in range(3):
        reach = 4 - 2 * stage
        for a, b in ((start - reach - 2, start - reach), (stop + reach, stop + reach + 2)):
            loop(a, b, lambda j: work(stage, j, False))
        loop(start - reach, stop + reach, lambda j: work(stage, j, True))
        if reach > 0:
            for a, b in ((start - reach, start - reach + 2), (stop + reach - 2, stop + reach)):
                loop(a, b, lambda j: update(stage, j, inner))
        inset = max(reach - 2, 0)
        region = full if reach > 0 else inner
        loop(start - inset, stop + inset, lambda j: update(stage, j, region))

    picked[...] = jnp.zeros_like(picked)
    col = cell_col[...]
    want = jnp.where(col >= 0, col % cr, -1)
    hit = lax.broadcasted_iota(jnp.int32, (slots, cr), 1) == want
    for p in range(slots):
        cell = jnp.maximum(cells[p], 0)
        plane = cell // (cz * cr) + REACH
        row = (cell // cr) % cz
        for s in range(3):
            picked[s * slots + p, :] = value[s, plane, row, :]
    for s in range(3):
        rowset = pl.ds(s * slots, slots)
        picked[rowset, :] = jnp.where(hit, picked[rowset, :], 0.0)
    ones = jnp.ones((8, cr), jnp.bfloat16)
    q = lax.dot_general(
        ones,
        picked[...].astype(jnp.bfloat16),
        (((1,), (1,)), ((), ())),
        preferred_element_type=jnp.float32,
    )
    q_out[...] = jnp.broadcast_to(q[0:1][None], q_out.shape)


def signals(slots, rows, offsets, weight, out):
    ndev = rows.shape[0]
    group = 32
    cols = group * slots
    lanes = rows.shape[2]
    col = lax.broadcasted_iota(jnp.int32, (1, cols), 1)
    owner = lax.broadcasted_iota(jnp.int32, (group, cols), 0) == col // slots
    lane = lax.broadcasted_iota(jnp.int32, (lanes, cols), 0)
    time = lax.broadcasted_iota(jnp.int32, (NB, cols), 0).astype(jnp.float32)
    total = jnp.zeros(out.shape, jnp.float32)
    for g in range(ndev // group):
        q = rows[g * group : (g + 1) * group, 0, :].astype(jnp.bfloat16)
        off = offsets[0:1, g * group : (g + 1) * group].astype(jnp.float32)
        off = jnp.broadcast_to(off, (8, group)).astype(jnp.bfloat16)
        bins = jnp.dot(off, owner.astype(jnp.bfloat16), preferred_element_type=jnp.float32)[0:1]
        table = jnp.zeros((NB, cols), jnp.float32)
        for s in range(3):
            pick = jnp.where(lane == s * slots + col % slots, 1.0, 0.0).astype(jnp.bfloat16)
            spread = jnp.dot(q, pick, preferred_element_type=jnp.float32)
            line = jnp.sum(jnp.where(owner, spread, 0.0), axis=0, keepdims=True)
            table = jnp.where(time == bins + s, line, table)
        total = total + lax.dot_general(
            weight[:, g * cols : (g + 1) * cols],
            table.astype(jnp.bfloat16),
            (((1,), (1,)), ((), ())),
            preferred_element_type=jnp.float32,
        )
    out[...] = total


def neighbour_pairs(count, periodic):
    pairs = [(i, i + 1) for i in range(count - 1)]
    if periodic:
        pairs.append((count - 1, 0))
    return pairs


def exchange(low_edge, high_edge, axis, periodic):
    forward = neighbour_pairs(lax.axis_size(axis), periodic)
    backward = [(target, source) for source, target in forward]
    return lax.ppermute(high_edge, axis, forward), lax.ppermute(low_edge, axis, backward)


def local(density, velocity, pressure, panel_cell, obs_weight, bin_offset):
    ca, cz, cr = density.shape
    slots = panel_cell.shape[0]
    ndev = bin_offset.shape[1]
    n_ax, n_rad = lax.axis_size("ax"), lax.axis_size("rad")
    home = (density, velocity, pressure)

    edge = f32(5, REACH, cz, cr)
    low, high = call(pack_ax, (edge, edge), [VMEM] * 3)(*home)
    lo, hi = exchange(low, high, "ax", False)

    strip = f32(5, ca + 2 * MID, STRIP, cr)
    low, high = call(pack_az, (strip, strip), [VMEM] * 5)(*home, lo, hi)
    azlo, azhi = exchange(low, high, "az", True)

    lanes = f32(5, 8, (ca + 2 * MID) * (cz + 2 * STRIP))
    ends = ("either",) if n_rad == 2 else ("low", "high")
    sides = call(functools.partial(pack_rad, ends), tuple(lanes for _ in ends), [VMEM] * 7)(
        *home, lo, hi, azlo, azhi
    )
    if n_rad == 2:
        rlo = rhi = lax.ppermute(sides[0], "rad", [(0, 1), (1, 0)])
    else:
        rlo, rhi = exchange(sides[0], sides[1], "rad", False)

    grid = (5, ca + 2 * REACH, cz + 2 * STRIP, 2 * cr)
    scratch = [pltpu.VMEM(grid, jnp.float32) for _ in range(6)]
    scratch += [pltpu.VMEM((3, ca + 2 * REACH, cz, cr), jnp.float32)]
    scratch += [pltpu.VMEM((128, cr), jnp.float32)]
    state, q = call(
        functools.partial(stages, (n_ax, n_rad)),
        (f32(5, ca, cz, cr), f32(ndev, 1, 128)),
        [VMEM] * 9 + [SMEM, VMEM],
        scratch,
    )(*home, lo, hi, azlo, azhi, rlo, rhi, panel_cell, panel_cell[:, None])

    rows = lax.all_to_all(q, ("ax", "az", "rad"), 0, 0, tiled=True)
    signal = call(functools.partial(signals, slots), f32(obs_weight.shape[0], NB), [VMEM] * 3)(
        rows, bin_offset, obs_weight
    )
    return (state, signal)


def solution(mesh):
    in_specs = (
        P("ax", "az", "rad"),
        P(None, "ax", "az", "rad"),
        P("ax", "az", "rad"),
        P(("ax", "az", "rad")),
        P(("ax", "az", "rad"), None),
        P(("ax", "az", "rad"), None),
    )
    out_specs = (P(None, "ax", "az", "rad"), P(("ax", "az", "rad"), None))
    return jax.shard_map(local, mesh=mesh, in_specs=in_specs, out_specs=out_specs, check_vma=False)
```

```python
import functools

import jax
import jax.numpy as jnp
from jax import lax
from jax.experimental import pallas as pl
from jax.experimental.pallas import tpu as pltpu
from jax.sharding import PartitionSpec as P

NB = 128
GAMMA_M = 0.4
LAMBDA = 0.1
P_REF = 1.0
REACH = 6
MID = 4
SCALE = -LAMBDA / 12.0
ROWS = 32
OFF = 8
VMEM = pltpu.MemorySpace.VMEM
SMEM = pltpu.MemorySpace.SMEM
F32 = jnp.float32
BF16 = jnp.bfloat16


def call(kernel, outs, in_spaces, scratch=(), mib=8, cost=None):
    return pl.pallas_call(
        kernel,
        out_shape=outs,
        in_specs=[pl.BlockSpec(memory_space=s) for s in in_spaces],
        out_specs=jax.tree.map(lambda _: pl.BlockSpec(memory_space=VMEM), outs),
        scratch_shapes=list(scratch),
        compiler_params=pltpu.CompilerParams(vmem_limit_bytes=mib * 1024 * 1024),
        cost_estimate=cost,
    )


def struct(shape, dtype=F32):
    return jax.ShapeDtypeStruct(shape, dtype)


def kept(row):
    return 8 * (row % 4) + row // 4


def home_ref(f, den, vel, pre):
    if f == 0:
        return den, 0
    if f == 4:
        return pre, 0
    return vel, (f - 1) * den.shape[0]


def is_even(axis):
    return lax.axis_index(axis) % 2 == 0


def pack_ax(ca, cz, den, vel, pre, first_out, second_out):
    even = is_even("ax")
    size = REACH * cz
    for f in range(5):
        ref, at = home_ref(f, den, vel, pre)
        low = ref[at : at + size, :]
        high = ref[at + ca * cz - size : at + ca * cz, :]
        rows = slice(f * size, (f + 1) * size)
        first_out[rows, :] = jnp.where(even, high, low).astype(BF16)
        second_out[rows, :] = jnp.where(even, low, high).astype(BF16)


def ax_sides(n_ax, got1, got2, rows):
    ax = lax.axis_index("ax")
    a, b = got1[rows, :].astype(F32), got2[rows, :].astype(F32)
    even = is_even("ax")
    lo = jnp.where(ax == 0, 0.0, jnp.where(even, b, a))
    hi = jnp.where(ax == n_ax - 1, 0.0, jnp.where(even, a, b))
    return lo, hi


def pack_az(n_ax, ca, cz, den, vel, pre, got1, got2, first_out, second_out, near):
    even = is_even("az")
    half = MID * cz
    for f in range(5):
        base = f * REACH * cz
        lo, hi = ax_sides(n_ax, got1, got2, slice(base, base + REACH * cz))
        near[f, 0:half, :] = lo[REACH * cz - half :]
        near[f, half : 2 * half, :] = hi[0:half]
    low, high = [], []
    for f in range(5):
        ref, at = home_ref(f, den, vel, pre)
        for d in range(REACH):
            low.append(ref[pl.ds(at + d, ca, stride=cz), :])
            high.append(ref[pl.ds(at + cz - 1 - d, ca, stride=cz), :])
        for d in range(MID):
            low.append(near[f, pl.ds(d, 2 * MID, stride=cz), :])
            high.append(near[f, pl.ds(cz - 1 - d, 2 * MID, stride=cz), :])
    low, high = jnp.concatenate(low, axis=0), jnp.concatenate(high, axis=0)
    first_out[...] = jnp.where(even, high, low).astype(BF16)
    second_out[...] = jnp.where(even, low, high).astype(BF16)


def one_hot_lanes(start, height, lanes, row0=0):
    row = lax.broadcasted_iota(jnp.int32, (height, lanes), 0) - row0
    lane = lax.broadcasted_iota(jnp.int32, (height, lanes), 1)
    return jnp.where((row >= 0) & (row < REACH) & (lane == row + start), 1.0, 0.0).astype(BF16)


def assemble(n_ax, ends, ca, cz, den, vel, pre, ax1, ax2, az1, az2, block, *rest):
    outs, (sides, strips) = rest[: len(ends)], rest[len(ends) :]
    cr = den.shape[1]
    planes = ca + 2 * REACH
    size = REACH * cz
    quarter = cz // 4
    first = OFF // 4

    def put(f, plane, ref, at):
        for l in range(4):
            row = (f * planes + plane) * ROWS + 8 * l + first
            block[pl.ds(row, quarter), :] = ref[pl.ds(at + l, quarter, stride=4), :]

    for f in range(5):
        ref, at = home_ref(f, den, vel, pre)
        for k in range(ca):
            put(f, REACH + k, ref, at + k * cz)
        lo, hi = ax_sides(n_ax, ax1, ax2, slice(f * size, (f + 1) * size))
        sides[f, 0:size, :] = lo
        sides[f, size : 2 * size, :] = hi
    for f in range(5):
        for k in range(REACH):
            put(f, k, sides.at[f], k * cz)
            put(f, REACH + ca + k, sides.at[f], size + k * cz)

    even = is_even("az")
    a, b = az1[...].astype(F32), az2[...].astype(F32)
    strips[0] = jnp.where(even, b, a)
    strips[1] = jnp.where(even, a, b)
    for f in range(5):
        base = f * (REACH * ca + MID * 2 * MID)
        for d in range(REACH):
            for side, row in ((0, OFF - 1 - d), (1, OFF + cz + d)):
                at = kept(row) + f * planes * ROWS
                block[pl.ds(at + REACH * ROWS, ca, stride=ROWS), :] = strips[side, pl.ds(base + d * ca, ca), :]
                if d < MID:
                    start = base + REACH * ca + d * 2 * MID
                    block[pl.ds(at + (REACH - MID) * ROWS, MID, stride=ROWS), :] = strips[side, pl.ds(start, MID), :]
                    block[pl.ds(at + (REACH + ca) * ROWS, MID, stride=ROWS), :] = strips[side, pl.ds(start + MID, MID), :]

    rad = lax.axis_index("rad")
    for end, out in zip(ends, outs):
        start = {"low": 0, "high": cr - REACH, "either": jnp.where(rad == 0, cr - REACH, 0)}[end]
        hot = one_hot_lanes(start, 8, cr)
        packed = []
        for f in range(5):
            row = (f * planes + REACH - MID) * ROWS
            cells = block[pl.ds(row, (ca + 2 * MID) * ROWS), :].astype(BF16)
            packed.append(
                lax.dot_general(hot, cells, (((1,), (1,)), ((), ())), preferred_element_type=F32)
            )
        packed.append(jnp.zeros_like(packed[0]))
        out[...] = jnp.concatenate(packed, axis=0).astype(BF16)


def az_terms(flux):
    out = []
    for group in (0, 4):
        v = [flux[8 * (group + l) : 8 * (group + l + 1)] for l in range(4)]
        v = [pltpu.roll(v[2], 1, 0), pltpu.roll(v[3], 1, 0)] + v + [pltpu.roll(v[0], 7, 0), pltpu.roll(v[1], 7, 0)]
        for l in range(4):
            out.append(8.0 * (v[l + 3] - v[l + 1]) - (v[l + 4] - v[l]))
    return jnp.concatenate(out, axis=0)


def band(wide):
    k = lax.broadcasted_iota(jnp.int32, (wide, wide), 0)
    n = lax.broadcasted_iota(jnp.int32, (wide, wide), 1)
    gap = (k - n + wide) % wide
    out = jnp.where(gap == 1, 8.0, 0.0) + jnp.where(gap == wide - 1, -8.0, 0.0)
    out = out + jnp.where(gap == 2, -1.0, 0.0) + jnp.where(gap == wide - 2, 1.0, 0.0)
    return out.astype(BF16)


def split_state(u):
    rho, m0, m1, m2, energy = u
    inv = 1.0 / rho
    vel = [m0 * inv, m1 * inv, m2 * inv]
    pres = GAMMA_M * (energy - 0.5 * (m0 * vel[0] + m1 * vel[1] + m2 * vel[2]))
    return [m0, m1, m2], vel, pres, energy


def flux(d, mom, vel, pres, energy):
    parts = [mom[d]]
    for j in range(3):
        parts.append(mom[d] * vel[j] + pres if j == d else mom[d] * vel[j])
    parts.append((energy + pres) * vel[d])
    return parts


def ax_only(u, fax, j):
    got = flux(0, *u)
    for f in range(5):
        fax[f, j, 0:ROWS] = got[f]


def both_sides(us, js, fax, part, banded):
    rows = []
    for u, j in zip(us, js):
        got = flux(0, *u)
        for f in range(5):
            fax[f, j] = got[f]
        got = flux(2, *u)
        for f in range(5):
            rows.append(jnp.concatenate([got[f][0:ROWS], got[f][ROWS:]], axis=1))
    rows = jnp.concatenate(rows, axis=0)
    coarse = rows.astype(BF16)
    fine = (rows - coarse.astype(F32)).astype(BF16)
    matrix = banded[...]
    out = jnp.dot(coarse, matrix, preferred_element_type=F32)
    out = out + jnp.dot(fine, matrix, preferred_element_type=F32)
    half = out.shape[1] // 2
    for i, (u, j) in enumerate(zip(us, js)):
        got = flux(1, *u)
        for f in range(5):
            at = (i * 5 + f) * ROWS
            mine = out[at : at + ROWS]
            radial = jnp.concatenate([mine[:, 0:half], mine[:, half:]], axis=0)
            part[f, j] = az_terms(got[f]) + radial


def change(fa, part, f, j, size):
    near = fa(j + 1)[0:size] - fa(j - 1)[0:size]
    far = fa(j + 2)[0:size] - fa(j - 2)[0:size]
    return SCALE * (8.0 * near - far + part[f, j, 0:size])


def window(fax, f):
    held = {}

    def get(j):
        if j not in held:
            held[j] = fax[f, j]
        return held[j]

    return get


def stages(n_ax, n_rad, ca, cz, block, rlo, rhi, cells, q_out, u2_out, u0_out, ghost, first, second, fax, part, banded, value, picked):
    cr = block.shape[-1]
    slots = cells.shape[0]
    low, high = REACH, REACH + ca
    ax = lax.axis_index("ax")
    rad = lax.axis_index("rad")
    banded[...] = band(2 * cr)

    lane = lax.broadcasted_iota(jnp.int32, (ROWS, cr), 1)
    kept_row = lax.broadcasted_iota(jnp.int32, (ROWS, cr), 0)
    row = 4 * (kept_row % 8) + kept_row // 8
    steps_rad = jnp.where(
        (lane < REACH) & (rad < n_rad - 1),
        1 + lane // 2,
        jnp.where((lane >= cr - REACH) & (rad > 0), 1 + (cr - 1 - lane) // 2, 99),
    )
    beyond_row = jnp.maximum(OFF - row, row - (OFF + cz - 1))
    steps = steps_rad + jnp.where(beyond_row > 0, (beyond_row + 1) // 2, 0)
    base0 = jnp.where(steps_rad < 99, 0.0, 1.0)

    count = ca + 2 * MID
    got_hi, got_lo = rhi[...], rlo[...]
    for f in range(5):
        side = 0.0
        for got, start, there in ((got_hi, 0, rad < n_rad - 1), (got_lo, cr - REACH, rad > 0)):
            place = one_hot_lanes(start, got.shape[0], cr, row0=8 * f)
            place = jnp.where(there, place, jnp.zeros_like(place))
            side = side + lax.dot_general(
                got, place, (((0,), (0,)), ((), ())), preferred_element_type=F32
            )
        side = side.reshape(count, ROWS, cr)
        ghost[f] = side + base0[None] if f == 0 else side

    def start_state(j, both):
        u = []
        for f in range(5):
            x = block[f, j]
            u.append(jnp.concatenate([x, ghost[f, j - (REACH - MID)]], axis=0) if both else x)
        rho, vel, pres = u[0], u[1:4], u[4]
        mom = [rho * x for x in vel]
        energy = pres * (1.0 / GAMMA_M) + 0.5 * (mom[0] * vel[0] + mom[1] * vel[1] + mom[2] * vel[2])
        return rho, (mom, vel, pres, energy)

    def note(s, j, u):
        value[s, j] = (u[2] - P_REF + u[0][0])[0:ROWS]

    for j in (low - 6, low - 5, high + 4, high + 5):
        ax_only(start_state(j, False)[1], fax, j)

    @pl.loop(0, (ca + 8) // 2)
    def _(i):
        js = [low - 4 + 2 * i, low - 3 + 2 * i]
        us = []
        for j in js:
            rho, u = start_state(j, True)
            for f, x in enumerate([rho] + u[0] + [u[3]]):
                first[f, j] = x
            note(0, j, u)
            us.append(u)
        both_sides(us, js, fax, part, banded)

    def update(f, j, fa, stage):
        a = max(low - j, j - (high - 1), 0)
        a = (a + 1) // 2
        lim = 2 - stage
        base = jnp.where(f == 0, 1.0, 0.0)
        size = ROWS if a == lim else 2 * ROWS
        new = change(fa, part, f, j, size)
        u0 = first[f, j, 0:size]
        if stage == 0:
            new = u0 + new
        else:
            new = 0.75 * u0 + 0.25 * (second[f, j, 0:size] + new)
        beyond = (ax == 0) if j < low else (ax == n_ax - 1)
        home = new[0:ROWS]
        if a > 0:
            home = jnp.where(beyond, base, home)
        if size == ROWS:
            return home, None
        ok = steps <= lim - a
        if a > 0:
            ok = ok & jnp.logical_not(beyond)
        return home, jnp.where(ok, new[ROWS:], base)

    @pl.loop(0, 5)
    def _(f):
        fa = window(fax, f)
        for j in range(low - 4, high + 4):
            home, side = update(f, j, fa, 0)
            second[f, j, 0:ROWS] = home
            if side is not None:
                second[f, j, ROWS:] = side

    for j in (low - 4, low - 3, high + 2, high + 3):
        ax_only(split_state([second[f, j, 0:ROWS] for f in range(5)]), fax, j)

    @pl.loop(0, (ca + 4) // 2)
    def _(i):
        js = [low - 2 + 2 * i, low - 1 + 2 * i]
        us = []
        for j in js:
            u = split_state([second[f, j] for f in range(5)])
            note(1, j, u)
            us.append(u)
        both_sides(us, js, fax, part, banded)

    @pl.loop(0, 5)
    def _(f):
        fa = window(fax, f)
        for j in range(low - 2, high + 2):
            home, side = update(f, j, fa, 1)
            u2_out[f, j - (low - 2), 0:ROWS] = home
            if side is not None:
                u2_out[f, j - (low - 2), ROWS:] = side
        for j in range(low, high):
            u0_out[f, j - low] = first[f, j, 0:ROWS]

    @pl.loop(0, ca)
    def _(i):
        u = split_state([u2_out[f, i + 2, 0:ROWS] for f in range(5)])
        note(2, low + i, u)

    picked[...] = jnp.zeros_like(picked)
    lanes = lax.broadcasted_iota(jnp.int32, (1, cr), 1)
    for p in range(slots):
        cell = cells[p]
        at = jnp.maximum(cell, 0)
        column = jnp.where(cell >= 0, lax.rem(at, cr), -1)
        at = lax.div(at, cr)
        plane = low + lax.div(at, cz)
        r = lax.rem(at, cz) + OFF
        r = 8 * lax.rem(r, 4) + lax.div(r, 4)
        hit = lanes == column
        for s in range(3):
            picked[pl.ds(s * slots + p, 1), :] = jnp.where(hit, value[s, plane, pl.ds(r, 1), :], 0.0)
    q = lax.dot_general(
        jnp.ones((8, cr), BF16),
        picked[...].astype(BF16),
        (((1,), (1,)), ((), ())),
        preferred_element_type=F32,
    )
    q_out[...] = jnp.broadcast_to(q[0:1][None], q_out.shape)


def last_stage(ca, cz, u2, u0, state, fax, part, banded):
    cr = u2.shape[-1]
    banded[...] = band(2 * cr)
    for j in (0, 1, ca + 2, ca + 3):
        ax_only(split_state([u2[f, j, 0:ROWS] for f in range(5)]), fax, j)

    @pl.loop(0, ca // 2)
    def _(i):
        js = [2 + 2 * i, 3 + 2 * i]
        us = [split_state([u2[f, j] for f in range(5)]) for j in js]
        both_sides(us, js, fax, part, banded)

    first, quarter = OFF // 4, cz // 4

    @pl.loop(0, 5)
    def _(f):
        fa = window(fax, f)
        for k in range(ca):
            j = k + 2
            new = u2[f, j, 0:ROWS] + change(fa, part, f, j, ROWS)
            new = u0[f, k] * (1.0 / 3.0) + (2.0 / 3.0) * new
            for l in range(4):
                state[f, k, pl.ds(l, quarter, stride=4), :] = new[8 * l + first : 8 * l + first + quarter]


def signals(slots, rows, offsets, weight, out):
    ndev = rows.shape[0]
    group = 32
    cols = group * slots
    lanes = rows.shape[2]
    col = lax.broadcasted_iota(jnp.int32, (1, cols), 1)
    owner = lax.broadcasted_iota(jnp.int32, (group, cols), 0) == col // slots
    lane = lax.broadcasted_iota(jnp.int32, (lanes, cols), 0)
    time = lax.broadcasted_iota(jnp.int32, (NB, cols), 0).astype(F32)
    total = jnp.zeros(out.shape, F32)
    for g in range(ndev // group):
        q = rows[g * group : (g + 1) * group, 0, :].astype(BF16)
        off = offsets[0:1, g * group : (g + 1) * group].astype(F32)
        off = jnp.broadcast_to(off, (8, group)).astype(BF16)
        bins = jnp.dot(off, owner.astype(BF16), preferred_element_type=F32)[0:1]
        table = jnp.zeros((NB, cols), F32)
        for s in range(3):
            pick = jnp.where(lane == s * slots + col % slots, 1.0, 0.0).astype(BF16)
            spread = jnp.dot(q, pick, preferred_element_type=F32)
            line = jnp.sum(jnp.where(owner, spread, 0.0), axis=0, keepdims=True)
            table = jnp.where(time == bins + s, line, table)
        total = total + lax.dot_general(
            weight[:, g * cols : (g + 1) * cols],
            table.astype(BF16),
            (((1,), (1,)), ((), ())),
            preferred_element_type=F32,
        )
    out[...] = total


def swap_pairs(count, periodic):
    one = [(i, i ^ 1) for i in range(count)]
    two = []
    for i in range(count):
        j = i - 1 if i % 2 == 0 else i + 1
        two.append((i, j % count if periodic or 0 <= j < count else i))
    return one, two


def swap(first, second, axis, periodic):
    one, two = swap_pairs(lax.axis_size(axis), periodic)
    return lax.ppermute(first, axis, one), lax.ppermute(second, axis, two)


def local(density, velocity, pressure, panel_cell, obs_weight, bin_offset):
    ca, cz, cr = density.shape
    slots = panel_cell.shape[0]
    ndev = bin_offset.shape[1]
    n_ax, n_rad = lax.axis_size("ax"), lax.axis_size("rad")
    home = (density.reshape(ca * cz, cr), velocity.reshape(3 * ca * cz, cr), pressure.reshape(ca * cz, cr))
    planes = ca + 2 * REACH
    part = functools.partial

    edge = struct((5 * REACH * cz, cr), BF16)
    ax1, ax2 = call(part(pack_ax, ca, cz), (edge, edge), [VMEM] * 3)(*home)
    ax1, ax2 = swap(ax1, ax2, "ax", False)

    strip = struct((5 * (REACH * ca + MID * 2 * MID), cr), BF16)
    near = pltpu.VMEM((5, 2 * MID * cz, cr), F32)
    az1, az2 = call(part(pack_az, n_ax, ca, cz), (strip, strip), [VMEM] * 5, [near])(*home, ax1, ax2)
    az1, az2 = swap(az1, az2, "az", True)

    side = struct((48, (ca + 2 * MID) * ROWS), BF16)
    ends = ("either",) if n_rad == 2 else ("low", "high")
    got = call(
        part(assemble, n_ax, ends, ca, cz),
        (struct((5 * planes * ROWS, cr)),) + tuple(side for _ in ends),
        [VMEM] * 7,
        [pltpu.VMEM((5, 2 * REACH * cz, cr), F32), pltpu.VMEM((2,) + strip.shape, F32)],
        mib=12,
    )(*home, ax1, ax2, az1, az2)
    block = got[0].reshape(5, planes, ROWS, cr)
    if n_rad == 2:
        rlo = rhi = lax.ppermute(got[1], "rad", [(0, 1), (1, 0)])
    else:
        up = [(i, i + 1) for i in range(n_rad - 1)]
        rlo = lax.ppermute(got[2], "rad", up)
        rhi = lax.ppermute(got[1], "rad", [(j, i) for i, j in up])

    grid = (5, planes, 2 * ROWS, cr)
    banded = pltpu.VMEM((2 * cr, 2 * cr), BF16)
    q, u2, u0 = call(
        part(stages, n_ax, n_rad, ca, cz),
        (struct((ndev, 1, 128)), struct((5, ca + 4, 2 * ROWS, cr)), struct((5, ca, ROWS, cr))),
        [VMEM] * 3 + [SMEM],
        [pltpu.VMEM((5, ca + 2 * MID, ROWS, cr), F32)]
        + [pltpu.VMEM(grid, F32) for _ in range(4)]
        + [banded, pltpu.VMEM((3, planes, ROWS, cr), F32), pltpu.VMEM((128, cr), F32)],
        mib=28,
    )(block, rlo, rhi, panel_cell)

    rows = lax.all_to_all(q, ("ax", "az", "rad"), 0, 0, tiled=True)

    grid = (5, ca + 4, 2 * ROWS, cr)
    state = call(
        part(last_stage, ca, cz),
        struct((5, ca, cz, cr)),
        [VMEM] * 2,
        [pltpu.VMEM(grid, F32), pltpu.VMEM(grid, F32), banded],
        mib=12,
        cost=pl.CostEstimate(flops=400_000_000, bytes_accessed=8_000_000, transcendentals=0),
    )(u2, u0)
    signal = call(part(signals, slots), struct((obs_weight.shape[0], NB)), [VMEM] * 3, mib=24)(
        rows, bin_offset, obs_weight
    )
    return (state, signal)


def solution(mesh):
    in_specs = (
        P("ax", "az", "rad"),
        P(None, "ax", "az", "rad"),
        P("ax", "az", "rad"),
        P(("ax", "az", "rad")),
        P(("ax", "az", "rad"), None),
        P(("ax", "az", "rad"), None),
    )
    out_specs = (P(None, "ax", "az", "rad"), P(("ax", "az", "rad"), None))
    return jax.shard_map(local, mesh=mesh, in_specs=in_specs, out_specs=out_specs, check_vma=False)
```

```python
import functools

import jax
import jax.numpy as jnp
from jax import lax
from jax.experimental import pallas as pl
from jax.experimental.pallas import tpu as pltpu
from jax.sharding import PartitionSpec as P

NB = 128
GAMMA_M = 0.4
LAMBDA = 0.1
P_REF = 1.0
REACH = 6
MID = 4
SCALE = -LAMBDA / 12.0
ROWS = 32
OFF = 8
HBM = pltpu.MemorySpace.HBM
VMEM = pltpu.MemorySpace.VMEM
SMEM = pltpu.MemorySpace.SMEM
F32 = jnp.float32
BF16 = jnp.bfloat16


def call(kernel, outs, in_spaces, scratch=(), mib=8, cost=None, alias={}):
    return pl.pallas_call(
        kernel,
        out_shape=outs,
        in_specs=[pl.BlockSpec(memory_space=s) for s in in_spaces],
        out_specs=jax.tree.map(lambda _: pl.BlockSpec(memory_space=VMEM), outs),
        scratch_shapes=list(scratch),
        compiler_params=pltpu.CompilerParams(vmem_limit_bytes=mib * 1024 * 1024),
        cost_estimate=cost,
        input_output_aliases=alias,
    )


def struct(shape, dtype=F32):
    return jax.ShapeDtypeStruct(shape, dtype)


def kept(row):
    return 8 * (row % 4) + row // 4


def is_even(axis):
    return lax.axis_index(axis) % 2 == 0


def load_and_pack(ca, cz, den, vel, pre, home, ax1, ax2, az1, az2, sems):
    size = ca * cz
    copies = [
        pltpu.make_async_copy(den, home.at[pl.ds(0, size)], sems.at[0]),
        pltpu.make_async_copy(vel, home.at[pl.ds(size, 3 * size)], sems.at[1]),
        pltpu.make_async_copy(pre, home.at[pl.ds(4 * size, size)], sems.at[2]),
    ]
    for copy in copies:
        copy.start()
    for copy in copies:
        copy.wait()
    even = is_even("ax")
    edge = REACH * cz
    for f in range(5):
        at = f * size
        low = home[at : at + edge, :]
        high = home[at + size - edge : at + size, :]
        rows = slice(f * edge, (f + 1) * edge)
        ax1[rows, :] = jnp.where(even, high, low).astype(BF16)
        ax2[rows, :] = jnp.where(even, low, high).astype(BF16)
    even = is_even("az")
    low, high = [], []
    for f in range(5):
        for d in range(REACH):
            low.append(home[pl.ds(f * size + d, ca, stride=cz), :])
            high.append(home[pl.ds(f * size + cz - 1 - d, ca, stride=cz), :])
    low, high = jnp.concatenate(low, axis=0), jnp.concatenate(high, axis=0)
    az1[...] = jnp.where(even, high, low).astype(BF16)
    az2[...] = jnp.where(even, low, high).astype(BF16)


def ax_sides(n_ax, got1, got2, rows):
    ax = lax.axis_index("ax")
    a, b = got1[rows, :].astype(F32), got2[rows, :].astype(F32)
    even = is_even("ax")
    lo = jnp.where(ax == 0, 0.0, jnp.where(even, b, a))
    hi = jnp.where(ax == n_ax - 1, 0.0, jnp.where(even, a, b))
    return lo, hi


def pack_corners(n_ax, cz, got1, got2, first_out, second_out, near):
    even = is_even("az")
    half = MID * cz
    size = REACH * cz
    for f in range(5):
        lo, hi = ax_sides(n_ax, got1, got2, slice(f * size, (f + 1) * size))
        near[f, 0:half, :] = lo[size - half :]
        near[f, half : 2 * half, :] = hi[0:half]
    low, high = [], []
    for f in range(5):
        for d in range(MID):
            low.append(near[f, pl.ds(d, 2 * MID, stride=cz), :])
            high.append(near[f, pl.ds(cz - 1 - d, 2 * MID, stride=cz), :])
    low, high = jnp.concatenate(low, axis=0), jnp.concatenate(high, axis=0)
    first_out[...] = jnp.where(even, high, low).astype(BF16)
    second_out[...] = jnp.where(even, low, high).astype(BF16)


def spread_rows(planes, cz, f, plane, ref, at, block):
    quarter = cz // 4
    for l in range(4):
        row = (f * planes + plane) * ROWS + 8 * l + OFF // 4
        block[pl.ds(row, quarter), :] = ref[pl.ds(at + l, quarter, stride=4), :]


def prepare(ca, cz, home, block, banded):
    for f in range(5):
        for k in range(ca):
            spread_rows(ca + 2 * REACH, cz, f, REACH + k, home, (f * ca + k) * cz, block)
    banded[...] = band(2 * home.shape[1])


def one_hot_lanes(start, height, lanes, row0=0):
    row = lax.broadcasted_iota(jnp.int32, (height, lanes), 0) - row0
    lane = lax.broadcasted_iota(jnp.int32, (height, lanes), 1)
    return jnp.where((row >= 0) & (row < REACH) & (lane == row + start), 1.0, 0.0).astype(BF16)


def assemble(n_ax, ends, ca, cz, block_in, ax1, ax2, az1, az2, corner1, corner2, block, *rest):
    outs, (sides, strips, corners) = rest[: len(ends)], rest[len(ends) :]
    cr = ax1.shape[1]
    planes = ca + 2 * REACH
    size = REACH * cz
    for f in range(5):
        lo, hi = ax_sides(n_ax, ax1, ax2, slice(f * size, (f + 1) * size))
        sides[f, 0:size, :] = lo
        sides[f, size : 2 * size, :] = hi
    for f in range(5):
        for k in range(REACH):
            spread_rows(planes, cz, f, k, sides.at[f], k * cz, block)
            spread_rows(planes, cz, f, REACH + ca + k, sides.at[f], size + k * cz, block)

    even = is_even("az")
    for one, two, into in ((az1, az2, strips), (corner1, corner2, corners)):
        a, b = one[...].astype(F32), two[...].astype(F32)
        into[0] = jnp.where(even, b, a)
        into[1] = jnp.where(even, a, b)
    for f in range(5):
        for d in range(REACH):
            for side, row in ((0, OFF - 1 - d), (1, OFF + cz + d)):
                at = kept(row) + f * planes * ROWS
                got = strips[side, pl.ds((f * REACH + d) * ca, ca), :]
                block[pl.ds(at + REACH * ROWS, ca, stride=ROWS), :] = got
                if d < MID:
                    start = (f * MID + d) * 2 * MID
                    got = corners[side, pl.ds(start, MID), :]
                    block[pl.ds(at + (REACH - MID) * ROWS, MID, stride=ROWS), :] = got
                    got = corners[side, pl.ds(start + MID, MID), :]
                    block[pl.ds(at + (REACH + ca) * ROWS, MID, stride=ROWS), :] = got

    rad = lax.axis_index("rad")
    for end, out in zip(ends, outs):
        start = {"low": 0, "high": cr - REACH, "either": jnp.where(rad == 0, cr - REACH, 0)}[end]
        hot = one_hot_lanes(start, 8, cr)
        packed = []
        for f in range(5):
            row = (f * planes + REACH - MID) * ROWS
            cells = block[pl.ds(row, (ca + 2 * MID) * ROWS), :].astype(BF16)
            packed.append(
                lax.dot_general(hot, cells, (((1,), (1,)), ((), ())), preferred_element_type=F32)
            )
        packed.append(jnp.zeros_like(packed[0]))
        out[...] = jnp.concatenate(packed, axis=0).astype(BF16)


def az_terms(flux):
    out = []
    for group in (0, 4):
        v = [flux[8 * (group + l) : 8 * (group + l + 1)] for l in range(4)]
        v = [pltpu.roll(v[2], 1, 0), pltpu.roll(v[3], 1, 0)] + v + [pltpu.roll(v[0], 7, 0), pltpu.roll(v[1], 7, 0)]
        for l in range(4):
            out.append(8.0 * (v[l + 3] - v[l + 1]) - (v[l + 4] - v[l]))
    return jnp.concatenate(out, axis=0)


def band(wide):
    k = lax.broadcasted_iota(jnp.int32, (wide, wide), 0)
    n = lax.broadcasted_iota(jnp.int32, (wide, wide), 1)
    gap = (k - n + wide) % wide
    out = jnp.where(gap == 1, 8.0, 0.0) + jnp.where(gap == wide - 1, -8.0, 0.0)
    out = out + jnp.where(gap == 2, -1.0, 0.0) + jnp.where(gap == wide - 2, 1.0, 0.0)
    return out.astype(BF16)


def split_state(u):
    rho, m0, m1, m2, energy = u
    inv = 1.0 / rho
    vel = [m0 * inv, m1 * inv, m2 * inv]
    pres = GAMMA_M * (energy - 0.5 * (m0 * vel[0] + m1 * vel[1] + m2 * vel[2]))
    return [m0, m1, m2], vel, pres, energy


def flux(d, mom, vel, pres, energy):
    parts = [mom[d]]
    for j in range(3):
        parts.append(mom[d] * vel[j] + pres if j == d else mom[d] * vel[j])
    parts.append((energy + pres) * vel[d])
    return parts


def ax_only(u, fax, j):
    got = flux(0, *u)
    for f in range(5):
        fax[f, j, 0:ROWS] = got[f]


def both_sides(us, js, fax, part, banded):
    rows = []
    for u, j in zip(us, js):
        got = flux(0, *u)
        for f in range(5):
            fax[f, j] = got[f]
        got = flux(2, *u)
        for f in range(5):
            rows.append(jnp.concatenate([got[f][0:ROWS], got[f][ROWS:]], axis=1))
    rows = jnp.concatenate(rows, axis=0)
    coarse = rows.astype(BF16)
    fine = (rows - coarse.astype(F32)).astype(BF16)
    matrix = banded[...]
    out = jnp.dot(coarse, matrix, preferred_element_type=F32)
    out = out + jnp.dot(fine, matrix, preferred_element_type=F32)
    half = out.shape[1] // 2
    for i, (u, j) in enumerate(zip(us, js)):
        got = flux(1, *u)
        for f in range(5):
            at = (i * 5 + f) * ROWS
            mine = out[at : at + ROWS]
            radial = jnp.concatenate([mine[:, 0:half], mine[:, half:]], axis=0)
            part[f, j] = az_terms(got[f]) + radial


def change(fa, part, f, j, size):
    near = fa(j + 1)[0:size] - fa(j - 1)[0:size]
    far = fa(j + 2)[0:size] - fa(j - 2)[0:size]
    return SCALE * (8.0 * near - far + part[f, j, 0:size])


def window(fax, f):
    held = {}

    def get(j):
        if j not in held:
            held[j] = fax[f, j]
        return held[j]

    return get


def stages(n_ax, n_rad, ca, cz, slots, block, banded, cells_far, *refs):
    sides, refs = refs[: len(refs) - 12], refs[len(refs) - 12 :]
    q_out, u2_out, u0_out, ghost, first, second, fax, part, value, picked, cells, cells_sem = refs
    fetch = pltpu.make_async_copy(cells_far, cells, cells_sem)
    fetch.start()
    cr = block.shape[-1]
    low, high = REACH, REACH + ca
    ax = lax.axis_index("ax")
    rad = lax.axis_index("rad")

    lane = lax.broadcasted_iota(jnp.int32, (ROWS, cr), 1)
    kept_row = lax.broadcasted_iota(jnp.int32, (ROWS, cr), 0)
    row = 4 * (kept_row % 8) + kept_row // 8
    steps_rad = jnp.where(
        (lane < REACH) & (rad < n_rad - 1),
        1 + lane // 2,
        jnp.where((lane >= cr - REACH) & (rad > 0), 1 + (cr - 1 - lane) // 2, 99),
    )
    beyond_row = jnp.maximum(OFF - row, row - (OFF + cz - 1))
    steps = steps_rad + jnp.where(beyond_row > 0, (beyond_row + 1) // 2, 0)
    base0 = jnp.where(steps_rad < 99, 0.0, 1.0)

    count = ca + 2 * MID
    places = ((0, rad < n_rad - 1), (cr - REACH, rad > 0))
    messages = [x[...] for x in sides]
    for f in range(5):
        hots = []
        for start, there in places:
            place = one_hot_lanes(start, messages[0].shape[0], cr, row0=8 * f)
            hots.append(jnp.where(there, place, jnp.zeros_like(place)))
        if len(messages) == 1:
            hots = [hots[0] + hots[1]]
        side = 0.0
        for got, hot in zip(messages, hots):
            side = side + lax.dot_general(
                got, hot, (((0,), (0,)), ((), ())), preferred_element_type=F32
            )
        side = side.reshape(count, ROWS, cr)
        ghost[f] = side + base0[None] if f == 0 else side

    def start_state(j, both):
        u = []
        for f in range(5):
            x = block[f, j]
            u.append(jnp.concatenate([x, ghost[f, j - (REACH - MID)]], axis=0) if both else x)
        rho, vel, pres = u[0], u[1:4], u[4]
        mom = [rho * x for x in vel]
        energy = pres * (1.0 / GAMMA_M) + 0.5 * (mom[0] * vel[0] + mom[1] * vel[1] + mom[2] * vel[2])
        return rho, (mom, vel, pres, energy)

    def note(s, j, u):
        value[s, j] = (u[2] - P_REF + u[0][0])[0:ROWS]

    for j in (low - 6, low - 5, high + 4, high + 5):
        ax_only(start_state(j, False)[1], fax, j)

    @pl.loop(0, (ca + 8) // 2)
    def _(i):
        js = [low - 4 + 2 * i, low - 3 + 2 * i]
        us = []
        for j in js:
            rho, u = start_state(j, True)
            for f, x in enumerate([rho] + u[0] + [u[3]]):
                first[f, j] = x
            note(0, j, u)
            us.append(u)
        both_sides(us, js, fax, part, banded)

    def update(f, j, fa, stage):
        a = max(low - j, j - (high - 1), 0)
        a = (a + 1) // 2
        lim = 2 - stage
        base = jnp.where(f == 0, 1.0, 0.0)
        size = ROWS if a == lim else 2 * ROWS
        new = change(fa, part, f, j, size)
        u0 = first[f, j, 0:size]
        if stage == 0:
            new = u0 + new
        else:
            new = 0.75 * u0 + 0.25 * (second[f, j, 0:size] + new)
        beyond = (ax == 0) if j < low else (ax == n_ax - 1)
        home = new[0:ROWS]
        if a > 0:
            home = jnp.where(beyond, base, home)
        if size == ROWS:
            return home, None
        ok = steps <= lim - a
        if a > 0:
            ok = ok & jnp.logical_not(beyond)
        return home, jnp.where(ok, new[ROWS:], base)

    @pl.loop(0, 5)
    def _(f):
        fa = window(fax, f)
        for j in range(low - 4, high + 4):
            home, side = update(f, j, fa, 0)
            second[f, j, 0:ROWS] = home
            if side is not None:
                second[f, j, ROWS:] = side

    for j in (low - 4, low - 3, high + 2, high + 3):
        ax_only(split_state([second[f, j, 0:ROWS] for f in range(5)]), fax, j)

    @pl.loop(0, (ca + 4) // 2)
    def _(i):
        js = [low - 2 + 2 * i, low - 1 + 2 * i]
        us = []
        for j in js:
            u = split_state([second[f, j] for f in range(5)])
            note(1, j, u)
            us.append(u)
        both_sides(us, js, fax, part, banded)

    @pl.loop(0, 5)
    def _(f):
        fa = window(fax, f)
        for j in range(low - 2, high + 2):
            home, side = update(f, j, fa, 1)
            u2_out[f, j - (low - 2), 0:ROWS] = home
            if side is not None:
                u2_out[f, j - (low - 2), ROWS:] = side
        for j in range(low, high):
            u0_out[f, j - low] = first[f, j, 0:ROWS]

    @pl.loop(0, ca)
    def _(i):
        u = split_state([u2_out[f, i + 2, 0:ROWS] for f in range(5)])
        note(2, low + i, u)

    fetch.wait()
    picked[...] = jnp.zeros_like(picked)
    lanes = lax.broadcasted_iota(jnp.int32, (1, cr), 1)
    for p in range(slots):
        cell = cells[p]
        at = jnp.maximum(cell, 0)
        column = jnp.where(cell >= 0, lax.rem(at, cr), -1)
        at = lax.div(at, cr)
        plane = low + lax.div(at, cz)
        r = lax.rem(at, cz) + OFF
        r = 8 * lax.rem(r, 4) + lax.div(r, 4)
        hit = lanes == column
        for s in range(3):
            picked[pl.ds(s * slots + p, 1), :] = jnp.where(hit, value[s, plane, pl.ds(r, 1), :], 0.0)
    q = lax.dot_general(
        jnp.ones((8, cr), BF16),
        picked[...].astype(BF16),
        (((1,), (1,)), ((), ())),
        preferred_element_type=F32,
    )
    q_out[...] = jnp.broadcast_to(q[0:1][None], q_out.shape)


def last_stage(ca, cz, u2, u0, banded, state, fax, part):
    for j in (0, 1, ca + 2, ca + 3):
        ax_only(split_state([u2[f, j, 0:ROWS] for f in range(5)]), fax, j)

    @pl.loop(0, ca // 2)
    def _(i):
        js = [2 + 2 * i, 3 + 2 * i]
        us = [split_state([u2[f, j] for f in range(5)]) for j in js]
        both_sides(us, js, fax, part, banded)

    first, quarter = OFF // 4, cz // 4

    @pl.loop(0, 5)
    def _(f):
        fa = window(fax, f)
        for k in range(ca):
            j = k + 2
            new = u2[f, j, 0:ROWS] + change(fa, part, f, j, ROWS)
            new = u0[f, k] * (1.0 / 3.0) + (2.0 / 3.0) * new
            for l in range(4):
                state[f, k, pl.ds(l, quarter, stride=4), :] = new[8 * l + first : 8 * l + first + quarter]


def repeat_rows(rows, out):
    out[...] = jnp.broadcast_to(rows[...].reshape(1, rows.shape[0], rows.shape[2]), out.shape)


def signals(slots, n_az, n_rad, rows, offsets, weight, out):
    ndev = rows.shape[0]
    group = 32
    cols = group * slots
    lanes = rows.shape[1]
    col = lax.broadcasted_iota(jnp.int32, (1, cols), 1)
    place = lax.broadcasted_iota(jnp.int32, (group, cols), 0)
    pair = n_az * n_rad
    device = place - place % pair + (place % n_az) * n_rad + (place % pair) // n_az
    owner = device == col // slots
    holder = place == col // slots
    lane = lax.broadcasted_iota(jnp.int32, (lanes, cols), 0)
    time = lax.broadcasted_iota(jnp.int32, (NB, cols), 0).astype(F32)
    total = jnp.zeros(out.shape, F32)
    for g in range(ndev // group):
        q = rows[g * group : (g + 1) * group, :].astype(BF16)
        off = offsets[0:1, g * group : (g + 1) * group].astype(F32)
        off = jnp.broadcast_to(off, (8, group)).astype(BF16)
        bins = jnp.dot(off, holder.astype(BF16), preferred_element_type=F32)[0:1]
        table = jnp.zeros((NB, cols), F32)
        for s in range(3):
            pick = jnp.where(lane == s * slots + col % slots, 1.0, 0.0).astype(BF16)
            spread = jnp.dot(q, pick, preferred_element_type=F32)
            line = jnp.sum(jnp.where(owner, spread, 0.0), axis=0, keepdims=True)
            table = jnp.where(time == bins + s, line, table)
        total = total + lax.dot_general(
            weight[:, g * cols : (g + 1) * cols],
            table.astype(BF16),
            (((1,), (1,)), ((), ())),
            preferred_element_type=F32,
        )
    out[...] = total


def swap_pairs(count, periodic):
    one = [(i, i ^ 1) for i in range(count)]
    two = []
    for i in range(count):
        j = i - 1 if i % 2 == 0 else i + 1
        two.append((i, j % count if periodic or 0 <= j < count else i))
    return one, two


def swap(first, second, axis, periodic):
    one, two = swap_pairs(lax.axis_size(axis), periodic)
    return lax.ppermute(first, axis, one), lax.ppermute(second, axis, two)


def local(density, velocity, pressure, panel_cell, obs_weight, bin_offset):
    ca, cz, cr = density.shape
    slots = panel_cell.shape[0]
    ndev = bin_offset.shape[1]
    n_ax, n_rad = lax.axis_size("ax"), lax.axis_size("rad")
    n_az = lax.axis_size("az")
    planes = ca + 2 * REACH
    part = functools.partial
    given = (density.reshape(ca * cz, cr), velocity.reshape(3 * ca * cz, cr), pressure.reshape(ca * cz, cr))

    edge = struct((5 * REACH * cz, cr), BF16)
    strip = struct((5 * REACH * ca, cr), BF16)
    home, ax1, ax2, az1, az2 = call(
        part(load_and_pack, ca, cz),
        (struct((5 * ca * cz, cr)), edge, edge, strip, strip),
        [HBM] * 3,
        [pltpu.SemaphoreType.DMA((3,))],
    )(*given)
    ax1, ax2 = swap(ax1, ax2, "ax", False)
    az1, az2 = swap(az1, az2, "az", True)
    grid = struct((5 * planes * ROWS, cr))
    block, banded = call(
        part(prepare, ca, cz), (grid, struct((2 * cr, 2 * cr), BF16)), [VMEM], mib=8
    )(home)

    corner = struct((5 * MID * 2 * MID, cr), BF16)
    near = pltpu.VMEM((5, 2 * MID * cz, cr), F32)
    corner1, corner2 = call(part(pack_corners, n_ax, cz), (corner, corner), [VMEM] * 2, [near])(ax1, ax2)
    corner1, corner2 = swap(corner1, corner2, "az", True)

    side = struct((48, (ca + 2 * MID) * ROWS), BF16)
    ends = ("either",) if n_rad == 2 else ("low", "high")
    got = call(
        part(assemble, n_ax, ends, ca, cz),
        (grid,) + tuple(side for _ in ends),
        [VMEM] * 7,
        [
            pltpu.VMEM((5, 2 * REACH * cz, cr), F32),
            pltpu.VMEM((2,) + strip.shape, F32),
            pltpu.VMEM((2,) + corner.shape, F32),
        ],
        mib=12,
        alias={0: 0},
    )(block, ax1, ax2, az1, az2, corner1, corner2)
    block = got[0].reshape(5, planes, ROWS, cr)
    if n_rad == 2:
        sides = (lax.ppermute(got[1], "rad", [(0, 1), (1, 0)]),)
    else:
        up = [(i, i + 1) for i in range(n_rad - 1)]
        sides = (lax.ppermute(got[1], "rad", [(j, i) for i, j in up]), lax.ppermute(got[2], "rad", up))

    grid = (5, planes, 2 * ROWS, cr)
    q, u2, u0 = call(
        part(stages, n_ax, n_rad, ca, cz, slots),
        (struct((n_az, 1, 128)), struct((5, ca + 4, 2 * ROWS, cr)), struct((5, ca, ROWS, cr))),
        [VMEM, VMEM, HBM] + [VMEM] * len(sides),
        [pltpu.VMEM((5, ca + 2 * MID, ROWS, cr), F32)]
        + [pltpu.VMEM(grid, F32) for _ in range(4)]
        + [pltpu.VMEM((3, planes, ROWS, cr), F32), pltpu.VMEM((128, cr), F32)]
        + [pltpu.SMEM((slots,), jnp.int32), pltpu.SemaphoreType.DMA],
        mib=28,
    )(block, banded, panel_cell, *sides)

    rows = lax.all_to_all(q, "az", 0, 0, tiled=True)
    rows = call(repeat_rows, struct((n_ax * n_rad, n_az, 128)), [VMEM], mib=2)(rows)
    rows = lax.all_to_all(rows, ("ax", "rad"), 0, 0, tiled=True).reshape(ndev, 128)

    grid = (5, ca + 4, 2 * ROWS, cr)
    state = call(
        part(last_stage, ca, cz),
        struct((5, ca, cz, cr)),
        [VMEM] * 3,
        [pltpu.VMEM(grid, F32), pltpu.VMEM(grid, F32)],
        mib=12,
        cost=pl.CostEstimate(flops=400_000_000, bytes_accessed=8_000_000, transcendentals=0),
    )(u2, u0, banded)
    signal = call(
        part(signals, slots, n_az, n_rad), struct((obs_weight.shape[0], NB)), [VMEM] * 3, mib=24
    )(rows, bin_offset, obs_weight)
    return (state, signal)


def solution(mesh):
    in_specs = (
        P("ax", "az", "rad"),
        P(None, "ax", "az", "rad"),
        P("ax", "az", "rad"),
        P(("ax", "az", "rad")),
        P(("ax", "az", "rad"), None),
        P(("ax", "az", "rad"), None),
    )
    out_specs = (P(None, "ax", "az", "rad"), P(("ax", "az", "rad"), None))
    return jax.shard_map(local, mesh=mesh, in_specs=in_specs, out_specs=out_specs, check_vma=False)
```

```python
import functools

import jax
import jax.numpy as jnp
from jax import lax
from jax.experimental import pallas as pl
from jax.experimental.pallas import tpu as pltpu
from jax.sharding import PartitionSpec as P

NB = 128
GAMMA_M = 0.4
LAMBDA = 0.1
P_REF = 1.0
REACH = 6
MID = 4
SCALE = -LAMBDA / 12.0
ROWS = 32
OFF = 8
HBM = pltpu.MemorySpace.HBM
VMEM = pltpu.MemorySpace.VMEM
SMEM = pltpu.MemorySpace.SMEM
F32 = jnp.float32
BF16 = jnp.bfloat16


def call(kernel, outs, in_spaces, scratch=(), mib=8, cost=None, alias={}):
    return pl.pallas_call(
        kernel,
        out_shape=outs,
        in_specs=[pl.BlockSpec(memory_space=s) for s in in_spaces],
        out_specs=jax.tree.map(lambda _: pl.BlockSpec(memory_space=VMEM), outs),
        scratch_shapes=list(scratch),
        compiler_params=pltpu.CompilerParams(vmem_limit_bytes=mib * 1024 * 1024),
        cost_estimate=cost,
        input_output_aliases=alias,
    )


def far(x):
    return pltpu.with_memory_space_constraint(x, HBM)


def struct(shape, dtype=F32):
    return jax.ShapeDtypeStruct(shape, dtype)


def kept(row):
    return 8 * (row % 4) + row // 4


def is_even(axis):
    return lax.axis_index(axis) % 2 == 0


def load_and_pack(ca, cz, den, vel, pre, home, ax1, ax2, az1, az2, sems):
    size = ca * cz
    copies = [
        pltpu.make_async_copy(den, home.at[pl.ds(0, size)], sems.at[0]),
        pltpu.make_async_copy(vel, home.at[pl.ds(size, 3 * size)], sems.at[1]),
        pltpu.make_async_copy(pre, home.at[pl.ds(4 * size, size)], sems.at[2]),
    ]
    for copy in copies:
        copy.start()
    for copy in copies:
        copy.wait()
    even = is_even("ax")
    edge = REACH * cz
    for f in range(5):
        at = f * size
        low = home[at : at + edge, :]
        high = home[at + size - edge : at + size, :]
        rows = slice(f * edge, (f + 1) * edge)
        ax1[rows, :] = jnp.where(even, high, low).astype(BF16)
        ax2[rows, :] = jnp.where(even, low, high).astype(BF16)
    even = is_even("az")
    low, high = [], []
    for f in range(5):
        for d in range(REACH):
            low.append(home[pl.ds(f * size + d, ca, stride=cz), :])
            high.append(home[pl.ds(f * size + cz - 1 - d, ca, stride=cz), :])
    low, high = jnp.concatenate(low, axis=0), jnp.concatenate(high, axis=0)
    az1[...] = jnp.where(even, high, low).astype(BF16)
    az2[...] = jnp.where(even, low, high).astype(BF16)


def ax_sides(n_ax, got1, got2, rows):
    ax = lax.axis_index("ax")
    a, b = got1[rows, :].astype(F32), got2[rows, :].astype(F32)
    even = is_even("ax")
    lo = jnp.where(ax == 0, 0.0, jnp.where(even, b, a))
    hi = jnp.where(ax == n_ax - 1, 0.0, jnp.where(even, a, b))
    return lo, hi


def pack_corners(n_ax, cz, got1, got2, first_out, second_out, near):
    even = is_even("az")
    half = MID * cz
    size = REACH * cz
    for f in range(5):
        lo, hi = ax_sides(n_ax, got1, got2, slice(f * size, (f + 1) * size))
        near[f, 0:half, :] = lo[size - half :]
        near[f, half : 2 * half, :] = hi[0:half]
    low, high = [], []
    for f in range(5):
        for d in range(MID):
            low.append(near[f, pl.ds(d, 2 * MID, stride=cz), :])
            high.append(near[f, pl.ds(cz - 1 - d, 2 * MID, stride=cz), :])
    low, high = jnp.concatenate(low, axis=0), jnp.concatenate(high, axis=0)
    first_out[...] = jnp.where(even, high, low).astype(BF16)
    second_out[...] = jnp.where(even, low, high).astype(BF16)


def spread_rows(planes, cz, f, plane, ref, at, block):
    quarter = cz // 4
    for l in range(4):
        row = (f * planes + plane) * ROWS + 8 * l + OFF // 4
        block[pl.ds(row, quarter), :] = ref[pl.ds(at + l, quarter, stride=4), :]


def prepare(ca, cz, home, block, banded):
    for f in range(5):
        for k in range(ca):
            spread_rows(ca + 2 * REACH, cz, f, REACH + k, home, (f * ca + k) * cz, block)
    banded[...] = band(2 * home.shape[1])


def one_hot_lanes(start, height, lanes, row0=0):
    row = lax.broadcasted_iota(jnp.int32, (height, lanes), 0) - row0
    lane = lax.broadcasted_iota(jnp.int32, (height, lanes), 1)
    return jnp.where((row >= 0) & (row < REACH) & (lane == row + start), 1.0, 0.0).astype(BF16)


def assemble(n_ax, ends, ca, cz, block_in, ax1, ax2, az1, az2, corner1, corner2, block, *rest):
    outs, (sides, strips, corners) = rest[: len(ends)], rest[len(ends) :]
    cr = ax1.shape[1]
    planes = ca + 2 * REACH
    size = REACH * cz
    for f in range(5):
        lo, hi = ax_sides(n_ax, ax1, ax2, slice(f * size, (f + 1) * size))
        sides[f, 0:size, :] = lo
        sides[f, size : 2 * size, :] = hi
    for f in range(5):
        for k in range(REACH):
            spread_rows(planes, cz, f, k, sides.at[f], k * cz, block)
            spread_rows(planes, cz, f, REACH + ca + k, sides.at[f], size + k * cz, block)

    even = is_even("az")
    for one, two, into in ((az1, az2, strips), (corner1, corner2, corners)):
        a, b = one[...].astype(F32), two[...].astype(F32)
        into[0] = jnp.where(even, b, a)
        into[1] = jnp.where(even, a, b)
    for f in range(5):
        for d in range(REACH):
            for side, row in ((0, OFF - 1 - d), (1, OFF + cz + d)):
                at = kept(row) + f * planes * ROWS
                got = strips[side, pl.ds((f * REACH + d) * ca, ca), :]
                block[pl.ds(at + REACH * ROWS, ca, stride=ROWS), :] = got
                if d < MID:
                    start = (f * MID + d) * 2 * MID
                    got = corners[side, pl.ds(start, MID), :]
                    block[pl.ds(at + (REACH - MID) * ROWS, MID, stride=ROWS), :] = got
                    got = corners[side, pl.ds(start + MID, MID), :]
                    block[pl.ds(at + (REACH + ca) * ROWS, MID, stride=ROWS), :] = got

    rad = lax.axis_index("rad")
    for end, out in zip(ends, outs):
        start = {"low": 0, "high": cr - REACH, "either": jnp.where(rad == 0, cr - REACH, 0)}[end]
        hot = one_hot_lanes(start, 8, cr)
        packed = []
        for f in range(5):
            row = (f * planes + REACH - MID) * ROWS
            cells = block[pl.ds(row, (ca + 2 * MID) * ROWS), :].astype(BF16)
            packed.append(
                lax.dot_general(hot, cells, (((1,), (1,)), ((), ())), preferred_element_type=F32)
            )
        packed.append(jnp.zeros_like(packed[0]))
        out[...] = jnp.concatenate(packed, axis=0).astype(BF16)


def az_terms(flux):
    out = []
    for group in (0, 4):
        v = [flux[8 * (group + l) : 8 * (group + l + 1)] for l in range(4)]
        v = [pltpu.roll(v[2], 1, 0), pltpu.roll(v[3], 1, 0)] + v + [pltpu.roll(v[0], 7, 0), pltpu.roll(v[1], 7, 0)]
        for l in range(4):
            out.append(8.0 * (v[l + 3] - v[l + 1]) - (v[l + 4] - v[l]))
    return jnp.concatenate(out, axis=0)


def band(wide):
    k = lax.broadcasted_iota(jnp.int32, (wide, wide), 0)
    n = lax.broadcasted_iota(jnp.int32, (wide, wide), 1)
    gap = (k - n + wide) % wide
    out = jnp.where(gap == 1, 8.0, 0.0) + jnp.where(gap == wide - 1, -8.0, 0.0)
    out = out + jnp.where(gap == 2, -1.0, 0.0) + jnp.where(gap == wide - 2, 1.0, 0.0)
    return out.astype(BF16)


def split_state(u):
    rho, m0, m1, m2, energy = u
    inv = 1.0 / rho
    vel = [m0 * inv, m1 * inv, m2 * inv]
    pres = GAMMA_M * (energy - 0.5 * (m0 * vel[0] + m1 * vel[1] + m2 * vel[2]))
    return [m0, m1, m2], vel, pres, energy


def flux(d, mom, vel, pres, energy):
    parts = [mom[d]]
    for j in range(3):
        parts.append(mom[d] * vel[j] + pres if j == d else mom[d] * vel[j])
    parts.append((energy + pres) * vel[d])
    return parts


def ax_only(u, fax, j):
    got = flux(0, *u)
    for f in range(5):
        fax[f, j, 0:ROWS] = got[f]


def both_sides(us, js, fax, part, banded):
    rows = []
    for u, j in zip(us, js):
        got = flux(0, *u)
        for f in range(5):
            fax[f, j] = got[f]
        got = flux(2, *u)
        for f in range(5):
            rows.append(jnp.concatenate([got[f][0:ROWS], got[f][ROWS:]], axis=1))
    rows = jnp.concatenate(rows, axis=0)
    coarse = rows.astype(BF16)
    fine = (rows - coarse.astype(F32)).astype(BF16)
    matrix = banded[...]
    out = jnp.dot(coarse, matrix, preferred_element_type=F32)
    out = out + jnp.dot(fine, matrix, preferred_element_type=F32)
    half = out.shape[1] // 2
    for i, (u, j) in enumerate(zip(us, js)):
        got = flux(1, *u)
        for f in range(5):
            at = (i * 5 + f) * ROWS
            mine = out[at : at + ROWS]
            radial = jnp.concatenate([mine[:, 0:half], mine[:, half:]], axis=0)
            part[f, j] = az_terms(got[f]) + radial


def change(fa, part, f, j, size):
    near = fa(j + 1)[0:size] - fa(j - 1)[0:size]
    far = fa(j + 2)[0:size] - fa(j - 2)[0:size]
    return SCALE * (8.0 * near - far + part[f, j, 0:size])


def window(fax, f):
    held = {}

    def get(j):
        if j not in held:
            held[j] = fax[f, j]
        return held[j]

    return get


def stages(n_ax, n_rad, ca, cz, slots, block, banded, cells_far, *refs):
    sides, refs = refs[: len(refs) - 12], refs[len(refs) - 12 :]
    q_out, u2_out, u0_out, ghost, first, second, fax, part, value, picked, cells, cells_sem = refs
    fetch = pltpu.make_async_copy(cells_far, cells, cells_sem)
    fetch.start()
    cr = block.shape[-1]
    low, high = REACH, REACH + ca
    ax = lax.axis_index("ax")
    rad = lax.axis_index("rad")

    lane = lax.broadcasted_iota(jnp.int32, (ROWS, cr), 1)
    kept_row = lax.broadcasted_iota(jnp.int32, (ROWS, cr), 0)
    row = 4 * (kept_row % 8) + kept_row // 8
    steps_rad = jnp.where(
        (lane < REACH) & (rad < n_rad - 1),
        1 + lane // 2,
        jnp.where((lane >= cr - REACH) & (rad > 0), 1 + (cr - 1 - lane) // 2, 99),
    )
    beyond_row = jnp.maximum(OFF - row, row - (OFF + cz - 1))
    steps = steps_rad + jnp.where(beyond_row > 0, (beyond_row + 1) // 2, 0)
    base0 = jnp.where(steps_rad < 99, 0.0, 1.0)

    count = ca + 2 * MID
    places = ((0, rad < n_rad - 1), (cr - REACH, rad > 0))
    messages = [x[...] for x in sides]
    for f in range(5):
        hots = []
        for start, there in places:
            place = one_hot_lanes(start, messages[0].shape[0], cr, row0=8 * f)
            hots.append(jnp.where(there, place, jnp.zeros_like(place)))
        if len(messages) == 1:
            hots = [hots[0] + hots[1]]
        side = 0.0
        for got, hot in zip(messages, hots):
            side = side + lax.dot_general(
                got, hot, (((0,), (0,)), ((), ())), preferred_element_type=F32
            )
        side = side.reshape(count, ROWS, cr)
        ghost[f] = side + base0[None] if f == 0 else side

    def start_state(j, both):
        u = []
        for f in range(5):
            x = block[f, j]
            u.append(jnp.concatenate([x, ghost[f, j - (REACH - MID)]], axis=0) if both else x)
        rho, vel, pres = u[0], u[1:4], u[4]
        mom = [rho * x for x in vel]
        energy = pres * (1.0 / GAMMA_M) + 0.5 * (mom[0] * vel[0] + mom[1] * vel[1] + mom[2] * vel[2])
        return rho, (mom, vel, pres, energy)

    def note(s, j, u):
        value[s, j] = (u[2] - P_REF + u[0][0])[0:ROWS]

    for j in (low - 6, low - 5, high + 4, high + 5):
        ax_only(start_state(j, False)[1], fax, j)

    @pl.loop(0, (ca + 8) // 2)
    def _(i):
        js = [low - 4 + 2 * i, low - 3 + 2 * i]
        us = []
        for j in js:
            rho, u = start_state(j, True)
            for f, x in enumerate([rho] + u[0] + [u[3]]):
                first[f, j] = x
            note(0, j, u)
            us.append(u)
        both_sides(us, js, fax, part, banded)

    def update(f, j, fa, stage):
        a = max(low - j, j - (high - 1), 0)
        a = (a + 1) // 2
        lim = 2 - stage
        base = jnp.where(f == 0, 1.0, 0.0)
        size = ROWS if a == lim else 2 * ROWS
        new = change(fa, part, f, j, size)
        u0 = first[f, j, 0:size]
        if stage == 0:
            new = u0 + new
        else:
            new = 0.75 * u0 + 0.25 * (second[f, j, 0:size] + new)
        beyond = (ax == 0) if j < low else (ax == n_ax - 1)
        home = new[0:ROWS]
        if a > 0:
            home = jnp.where(beyond, base, home)
        if size == ROWS:
            return home, None
        ok = steps <= lim - a
        if a > 0:
            ok = ok & jnp.logical_not(beyond)
        return home, jnp.where(ok, new[ROWS:], base)

    @pl.loop(0, 5)
    def _(f):
        fa = window(fax, f)
        for j in range(low - 4, high + 4):
            home, side = update(f, j, fa, 0)
            second[f, j, 0:ROWS] = home
            if side is not None:
                second[f, j, ROWS:] = side

    for j in (low - 4, low - 3, high + 2, high + 3):
        ax_only(split_state([second[f, j, 0:ROWS] for f in range(5)]), fax, j)

    @pl.loop(0, (ca + 4) // 2)
    def _(i):
        js = [low - 2 + 2 * i, low - 1 + 2 * i]
        us = []
        for j in js:
            u = split_state([second[f, j] for f in range(5)])
            note(1, j, u)
            us.append(u)
        both_sides(us, js, fax, part, banded)

    @pl.loop(0, 5)
    def _(f):
        fa = window(fax, f)
        for j in range(low - 2, high + 2):
            home, side = update(f, j, fa, 1)
            u2_out[f, j - (low - 2), 0:ROWS] = home
            if side is not None:
                u2_out[f, j - (low - 2), ROWS:] = side
        for j in range(low, high):
            u0_out[f, j - low] = first[f, j, 0:ROWS]

    @pl.loop(0, ca)
    def _(i):
        u = split_state([u2_out[f, i + 2, 0:ROWS] for f in range(5)])
        note(2, low + i, u)

    fetch.wait()
    picked[...] = jnp.zeros_like(picked)
    lanes = lax.broadcasted_iota(jnp.int32, (1, cr), 1)
    for p in range(slots):
        cell = cells[p]
        at = jnp.maximum(cell, 0)
        column = jnp.where(cell >= 0, lax.rem(at, cr), -1)
        at = lax.div(at, cr)
        plane = low + lax.div(at, cz)
        r = lax.rem(at, cz) + OFF
        r = 8 * lax.rem(r, 4) + lax.div(r, 4)
        hit = lanes == column
        for s in range(3):
            picked[pl.ds(s * slots + p, 1), :] = jnp.where(hit, value[s, plane, pl.ds(r, 1), :], 0.0)
    q = lax.dot_general(
        jnp.ones((8, cr), BF16),
        picked[...].astype(BF16),
        (((1,), (1,)), ((), ())),
        preferred_element_type=F32,
    )
    q_out[...] = jnp.broadcast_to(q[0:1][None], q_out.shape)


def last_stage(ca, cz, u2, u0, banded, state, fax, part):
    for j in (0, 1, ca + 2, ca + 3):
        ax_only(split_state([u2[f, j, 0:ROWS] for f in range(5)]), fax, j)

    @pl.loop(0, ca // 2)
    def _(i):
        js = [2 + 2 * i, 3 + 2 * i]
        us = [split_state([u2[f, j] for f in range(5)]) for j in js]
        both_sides(us, js, fax, part, banded)

    first, quarter = OFF // 4, cz // 4

    @pl.loop(0, 5)
    def _(f):
        fa = window(fax, f)
        for k in range(ca):
            j = k + 2
            new = u2[f, j, 0:ROWS] + change(fa, part, f, j, ROWS)
            new = u0[f, k] * (1.0 / 3.0) + (2.0 / 3.0) * new
            for l in range(4):
                state[f, k, pl.ds(l, quarter, stride=4), :] = new[8 * l + first : 8 * l + first + quarter]


def signals(slots, rows, offsets, weight, out):
    ndev = rows.shape[0]
    group = 32
    cols = group * slots
    lanes = rows.shape[1]
    col = lax.broadcasted_iota(jnp.int32, (1, cols), 1)
    owner = lax.broadcasted_iota(jnp.int32, (group, cols), 0) == col // slots
    lane = lax.broadcasted_iota(jnp.int32, (lanes, cols), 0)
    time = lax.broadcasted_iota(jnp.int32, (NB, cols), 0).astype(F32)
    total = jnp.zeros(out.shape, F32)
    for g in range(ndev // group):
        q = rows[g * group : (g + 1) * group, :].astype(BF16)
        off = offsets[0:1, g * group : (g + 1) * group].astype(F32)
        off = jnp.broadcast_to(off, (8, group)).astype(BF16)
        bins = jnp.dot(off, owner.astype(BF16), preferred_element_type=F32)[0:1]
        table = jnp.zeros((NB, cols), F32)
        for s in range(3):
            pick = jnp.where(lane == s * slots + col % slots, 1.0, 0.0).astype(BF16)
            spread = jnp.dot(q, pick, preferred_element_type=F32)
            line = jnp.sum(jnp.where(owner, spread, 0.0), axis=0, keepdims=True)
            table = jnp.where(time == bins + s, line, table)
        total = total + lax.dot_general(
            weight[:, g * cols : (g + 1) * cols],
            table.astype(BF16),
            (((1,), (1,)), ((), ())),
            preferred_element_type=F32,
        )
    out[...] = total


def swap_pairs(count, periodic):
    one = [(i, i ^ 1) for i in range(count)]
    two = []
    for i in range(count):
        j = i - 1 if i % 2 == 0 else i + 1
        two.append((i, j % count if periodic or 0 <= j < count else i))
    return one, two


def swap(first, second, axis, periodic):
    one, two = swap_pairs(lax.axis_size(axis), periodic)
    return lax.ppermute(first, axis, one), lax.ppermute(second, axis, two)


def local(density, velocity, pressure, panel_cell, obs_weight, bin_offset):
    ca, cz, cr = density.shape
    slots = panel_cell.shape[0]
    ndev = bin_offset.shape[1]
    n_ax, n_rad = lax.axis_size("ax"), lax.axis_size("rad")
    planes = ca + 2 * REACH
    part = functools.partial
    given = (density.reshape(ca * cz, cr), velocity.reshape(3 * ca * cz, cr), pressure.reshape(ca * cz, cr))

    edge = struct((5 * REACH * cz, cr), BF16)
    strip = struct((5 * REACH * ca, cr), BF16)
    home, ax1, ax2, az1, az2 = call(
        part(load_and_pack, ca, cz),
        (struct((5 * ca * cz, cr)), edge, edge, strip, strip),
        [HBM] * 3,
        [pltpu.SemaphoreType.DMA((3,))],
    )(*[far(x) for x in given])
    ax1, ax2 = swap(ax1, ax2, "ax", False)
    az1, az2 = swap(az1, az2, "az", True)
    grid = struct((5 * planes * ROWS, cr))
    block, banded = call(
        part(prepare, ca, cz), (grid, struct((2 * cr, 2 * cr), BF16)), [VMEM], mib=8
    )(home)

    corner = struct((5 * MID * 2 * MID, cr), BF16)
    near = pltpu.VMEM((5, 2 * MID * cz, cr), F32)
    corner1, corner2 = call(part(pack_corners, n_ax, cz), (corner, corner), [VMEM] * 2, [near])(ax1, ax2)
    corner1, corner2 = swap(corner1, corner2, "az", True)

    side = struct((48, (ca + 2 * MID) * ROWS), BF16)
    ends = ("either",) if n_rad == 2 else ("low", "high")
    got = call(
        part(assemble, n_ax, ends, ca, cz),
        (grid,) + tuple(side for _ in ends),
        [VMEM] * 7,
        [
            pltpu.VMEM((5, 2 * REACH * cz, cr), F32),
            pltpu.VMEM((2,) + strip.shape, F32),
            pltpu.VMEM((2,) + corner.shape, F32),
        ],
        mib=12,
        alias={0: 0},
    )(block, ax1, ax2, az1, az2, corner1, corner2)
    block = got[0].reshape(5, planes, ROWS, cr)
    if n_rad == 2:
        sides = (lax.ppermute(got[1], "rad", [(0, 1), (1, 0)]),)
    else:
        up = [(i, i + 1) for i in range(n_rad - 1)]
        sides = (lax.ppermute(got[1], "rad", [(j, i) for i, j in up]), lax.ppermute(got[2], "rad", up))

    grid = (5, planes, 2 * ROWS, cr)
    q, u2, u0 = call(
        part(stages, n_ax, n_rad, ca, cz, slots),
        (struct((1, 1, 128)), struct((5, ca + 4, 2 * ROWS, cr)), struct((5, ca, ROWS, cr))),
        [VMEM, VMEM, HBM] + [VMEM] * len(sides),
        [pltpu.VMEM((5, ca + 2 * MID, ROWS, cr), F32)]
        + [pltpu.VMEM(grid, F32) for _ in range(4)]
        + [pltpu.VMEM((3, planes, ROWS, cr), F32), pltpu.VMEM((128, cr), F32)]
        + [pltpu.SMEM((slots,), jnp.int32), pltpu.SemaphoreType.DMA],
        mib=28,
    )(block, banded, far(panel_cell), *sides)

    rows = lax.all_gather(q, ("ax", "az", "rad"), axis=0, tiled=True).reshape(ndev, 128)

    grid = (5, ca + 4, 2 * ROWS, cr)
    state = call(
        part(last_stage, ca, cz),
        struct((5, ca, cz, cr)),
        [VMEM] * 3,
        [pltpu.VMEM(grid, F32), pltpu.VMEM(grid, F32)],
        mib=12,
        cost=pl.CostEstimate(flops=400_000_000, bytes_accessed=8_000_000, transcendentals=0),
    )(u2, u0, banded)
    signal = call(
        part(signals, slots), struct((obs_weight.shape[0], NB)), [VMEM] * 3, mib=24
    )(rows, bin_offset, obs_weight)
    return (state, signal)


def solution(mesh):
    in_specs = (
        P("ax", "az", "rad"),
        P(None, "ax", "az", "rad"),
        P("ax", "az", "rad"),
        P(("ax", "az", "rad")),
        P(("ax", "az", "rad"), None),
        P(("ax", "az", "rad"), None),
    )
    out_specs = (P(None, "ax", "az", "rad"), P(("ax", "az", "rad"), None))
    return jax.shard_map(local, mesh=mesh, in_specs=in_specs, out_specs=out_specs, check_vma=False)
```

```python
import functools

import jax
import jax.numpy as jnp
from jax import lax
from jax.experimental import pallas as pl
from jax.experimental.pallas import tpu as pltpu
from jax.sharding import PartitionSpec as P

NB = 128
GAMMA_M = 0.4
LAMBDA = 0.1
P_REF = 1.0
REACH = 6
MID = 4
SCALE = -LAMBDA / 12.0
ROWS = 32
OFF = 8
HBM = pltpu.MemorySpace.HBM
VMEM = pltpu.MemorySpace.VMEM
SMEM = pltpu.MemorySpace.SMEM
F32 = jnp.float32
BF16 = jnp.bfloat16


def call(kernel, outs, in_spaces, scratch=(), mib=8, cost=None, alias={}):
    return pl.pallas_call(
        kernel,
        out_shape=outs,
        in_specs=[pl.BlockSpec(memory_space=s) for s in in_spaces],
        out_specs=jax.tree.map(lambda _: pl.BlockSpec(memory_space=VMEM), outs),
        scratch_shapes=list(scratch),
        compiler_params=pltpu.CompilerParams(vmem_limit_bytes=mib * 1024 * 1024),
        cost_estimate=cost,
        input_output_aliases=alias,
    )


def far(x):
    return pltpu.with_memory_space_constraint(x, HBM)


def struct(shape, dtype=F32):
    return jax.ShapeDtypeStruct(shape, dtype)


def kept(row):
    return 8 * (row % 4) + row // 4


def is_even(axis):
    return lax.axis_index(axis) % 2 == 0


def load_and_pack(ca, cz, den, vel, pre, home, ax1, ax2, az1, az2, sems):
    size = ca * cz
    copies = [
        pltpu.make_async_copy(den, home.at[pl.ds(0, size)], sems.at[0]),
        pltpu.make_async_copy(vel, home.at[pl.ds(size, 3 * size)], sems.at[1]),
        pltpu.make_async_copy(pre, home.at[pl.ds(4 * size, size)], sems.at[2]),
    ]
    for copy in copies:
        copy.start()
    for copy in copies:
        copy.wait()
    even = is_even("ax")
    edge = REACH * cz
    for f in range(5):
        at = f * size
        low = home[at : at + edge, :]
        high = home[at + size - edge : at + size, :]
        rows = slice(f * edge, (f + 1) * edge)
        ax1[rows, :] = jnp.where(even, high, low).astype(BF16)
        ax2[rows, :] = jnp.where(even, low, high).astype(BF16)
    even = is_even("az")
    low, high = [], []
    for f in range(5):
        for d in range(REACH):
            low.append(home[pl.ds(f * size + d, ca, stride=cz), :])
            high.append(home[pl.ds(f * size + cz - 1 - d, ca, stride=cz), :])
    low, high = jnp.concatenate(low, axis=0), jnp.concatenate(high, axis=0)
    az1[...] = jnp.where(even, high, low).astype(BF16)
    az2[...] = jnp.where(even, low, high).astype(BF16)


def ax_sides(n_ax, got1, got2, rows):
    ax = lax.axis_index("ax")
    a, b = got1[rows, :].astype(F32), got2[rows, :].astype(F32)
    even = is_even("ax")
    lo = jnp.where(ax == 0, 0.0, jnp.where(even, b, a))
    hi = jnp.where(ax == n_ax - 1, 0.0, jnp.where(even, a, b))
    return lo, hi


def pack_corners(n_ax, cz, got1, got2, first_out, second_out, near):
    even = is_even("az")
    half = MID * cz
    size = REACH * cz
    for f in range(5):
        lo, hi = ax_sides(n_ax, got1, got2, slice(f * size, (f + 1) * size))
        near[f, 0:half, :] = lo[size - half :]
        near[f, half : 2 * half, :] = hi[0:half]
    low, high = [], []
    for f in range(5):
        for d in range(MID):
            low.append(near[f, pl.ds(d, 2 * MID, stride=cz), :])
            high.append(near[f, pl.ds(cz - 1 - d, 2 * MID, stride=cz), :])
    low, high = jnp.concatenate(low, axis=0), jnp.concatenate(high, axis=0)
    first_out[...] = jnp.where(even, high, low).astype(BF16)
    second_out[...] = jnp.where(even, low, high).astype(BF16)


def spread_rows(planes, cz, f, plane, ref, at, block):
    quarter = cz // 4
    for l in range(4):
        row = (f * planes + plane) * ROWS + 8 * l + OFF // 4
        block[pl.ds(row, quarter), :] = ref[pl.ds(at + l, quarter, stride=4), :]


def prepare(ca, cz, home, block, banded):
    for f in range(5):
        for k in range(ca):
            spread_rows(ca + 2 * REACH, cz, f, REACH + k, home, (f * ca + k) * cz, block)
    banded[...] = band(2 * home.shape[1])


def one_hot_lanes(start, height, lanes, row0=0):
    row = lax.broadcasted_iota(jnp.int32, (height, lanes), 0) - row0
    lane = lax.broadcasted_iota(jnp.int32, (height, lanes), 1)
    return jnp.where((row >= 0) & (row < REACH) & (lane == row + start), 1.0, 0.0).astype(BF16)


def assemble(n_ax, ends, ca, cz, block_in, ax1, ax2, az1, az2, corner1, corner2, block, *rest):
    outs, (sides, strips, corners) = rest[: len(ends)], rest[len(ends) :]
    cr = ax1.shape[1]
    planes = ca + 2 * REACH
    size = REACH * cz
    for f in range(5):
        lo, hi = ax_sides(n_ax, ax1, ax2, slice(f * size, (f + 1) * size))
        sides[f, 0:size, :] = lo
        sides[f, size : 2 * size, :] = hi
    for f in range(5):
        for k in range(REACH):
            spread_rows(planes, cz, f, k, sides.at[f], k * cz, block)
            spread_rows(planes, cz, f, REACH + ca + k, sides.at[f], size + k * cz, block)

    even = is_even("az")
    for one, two, into in ((az1, az2, strips), (corner1, corner2, corners)):
        a, b = one[...].astype(F32), two[...].astype(F32)
        into[0] = jnp.where(even, b, a)
        into[1] = jnp.where(even, a, b)
    for f in range(5):
        for d in range(REACH):
            for side, row in ((0, OFF - 1 - d), (1, OFF + cz + d)):
                at = kept(row) + f * planes * ROWS
                got = strips[side, pl.ds((f * REACH + d) * ca, ca), :]
                block[pl.ds(at + REACH * ROWS, ca, stride=ROWS), :] = got
                if d < MID:
                    start = (f * MID + d) * 2 * MID
                    got = corners[side, pl.ds(start, MID), :]
                    block[pl.ds(at + (REACH - MID) * ROWS, MID, stride=ROWS), :] = got
                    got = corners[side, pl.ds(start + MID, MID), :]
                    block[pl.ds(at + (REACH + ca) * ROWS, MID, stride=ROWS), :] = got

    rad = lax.axis_index("rad")
    for end, out in zip(ends, outs):
        start = {"low": 0, "high": cr - REACH, "either": jnp.where(rad == 0, cr - REACH, 0)}[end]
        hot = one_hot_lanes(start, 8, cr)
        packed = []
        for f in range(5):
            row = (f * planes + REACH - MID) * ROWS
            cells = block[pl.ds(row, (ca + 2 * MID) * ROWS), :].astype(BF16)
            packed.append(
                lax.dot_general(hot, cells, (((1,), (1,)), ((), ())), preferred_element_type=F32)
            )
        packed.append(jnp.zeros_like(packed[0]))
        out[...] = jnp.concatenate(packed, axis=0).astype(BF16)


def az_terms(flux):
    out = []
    for group in (0, 4):
        v = [flux[8 * (group + l) : 8 * (group + l + 1)] for l in range(4)]
        v = [pltpu.roll(v[2], 1, 0), pltpu.roll(v[3], 1, 0)] + v + [pltpu.roll(v[0], 7, 0), pltpu.roll(v[1], 7, 0)]
        for l in range(4):
            out.append(8.0 * (v[l + 3] - v[l + 1]) - (v[l + 4] - v[l]))
    return jnp.concatenate(out, axis=0)


def band(wide):
    k = lax.broadcasted_iota(jnp.int32, (wide, wide), 0)
    n = lax.broadcasted_iota(jnp.int32, (wide, wide), 1)
    gap = (k - n + wide) % wide
    out = jnp.where(gap == 1, 8.0, 0.0) + jnp.where(gap == wide - 1, -8.0, 0.0)
    out = out + jnp.where(gap == 2, -1.0, 0.0) + jnp.where(gap == wide - 2, 1.0, 0.0)
    return out.astype(BF16)


def split_state(u):
    rho, m0, m1, m2, energy = u
    inv = 1.0 / rho
    vel = [m0 * inv, m1 * inv, m2 * inv]
    pres = GAMMA_M * (energy - 0.5 * (m0 * vel[0] + m1 * vel[1] + m2 * vel[2]))
    return [m0, m1, m2], vel, pres, energy


def flux(d, mom, vel, pres, energy):
    parts = [mom[d]]
    for j in range(3):
        parts.append(mom[d] * vel[j] + pres if j == d else mom[d] * vel[j])
    parts.append((energy + pres) * vel[d])
    return parts


def ax_only(u, fax, j):
    got = flux(0, *u)
    for f in range(5):
        fax[f, j, 0:ROWS] = got[f]


def both_sides(us, js, fax, part, banded):
    rows = []
    for u, j in zip(us, js):
        got = flux(0, *u)
        for f in range(5):
            fax[f, j] = got[f]
        got = flux(2, *u)
        for f in range(5):
            rows.append(jnp.concatenate([got[f][0:ROWS], got[f][ROWS:]], axis=1))
    rows = jnp.concatenate(rows, axis=0)
    coarse = rows.astype(BF16)
    fine = (rows - coarse.astype(F32)).astype(BF16)
    matrix = banded[...]
    out = jnp.dot(coarse, matrix, preferred_element_type=F32)
    out = out + jnp.dot(fine, matrix, preferred_element_type=F32)
    half = out.shape[1] // 2
    for i, (u, j) in enumerate(zip(us, js)):
        got = flux(1, *u)
        for f in range(5):
            at = (i * 5 + f) * ROWS
            mine = out[at : at + ROWS]
            radial = jnp.concatenate([mine[:, 0:half], mine[:, half:]], axis=0)
            part[f, j] = az_terms(got[f]) + radial


def change(fa, part, f, j, size):
    near = fa(j + 1)[0:size] - fa(j - 1)[0:size]
    far = fa(j + 2)[0:size] - fa(j - 2)[0:size]
    return SCALE * (8.0 * near - far + part[f, j, 0:size])


def window(fax, f):
    held = {}

    def get(j):
        if j not in held:
            held[j] = fax[f, j]
        return held[j]

    return get


def stages(n_ax, n_rad, ca, cz, slots, block, banded, cells_far, *refs):
    sides, refs = refs[: len(refs) - 12], refs[len(refs) - 12 :]
    q_out, u2_out, u0_out, ghost, first, second, fax, part, value, picked, cells, cells_sem = refs
    fetch = pltpu.make_async_copy(cells_far, cells, cells_sem)
    fetch.start()
    cr = block.shape[-1]
    low, high = REACH, REACH + ca
    ax = lax.axis_index("ax")
    rad = lax.axis_index("rad")

    lane = lax.broadcasted_iota(jnp.int32, (ROWS, cr), 1)
    kept_row = lax.broadcasted_iota(jnp.int32, (ROWS, cr), 0)
    row = 4 * (kept_row % 8) + kept_row // 8
    steps_rad = jnp.where(
        (lane < REACH) & (rad < n_rad - 1),
        1 + lane // 2,
        jnp.where((lane >= cr - REACH) & (rad > 0), 1 + (cr - 1 - lane) // 2, 99),
    )
    beyond_row = jnp.maximum(OFF - row, row - (OFF + cz - 1))
    steps = steps_rad + jnp.where(beyond_row > 0, (beyond_row + 1) // 2, 0)
    base0 = jnp.where(steps_rad < 99, 0.0, 1.0)

    count = ca + 2 * MID
    places = ((0, rad < n_rad - 1), (cr - REACH, rad > 0))
    messages = [x[...] for x in sides]
    for f in range(5):
        hots = []
        for start, there in places:
            place = one_hot_lanes(start, messages[0].shape[0], cr, row0=8 * f)
            hots.append(jnp.where(there, place, jnp.zeros_like(place)))
        if len(messages) == 1:
            hots = [hots[0] + hots[1]]
        side = 0.0
        for got, hot in zip(messages, hots):
            side = side + lax.dot_general(
                got, hot, (((0,), (0,)), ((), ())), preferred_element_type=F32
            )
        side = side.reshape(count, ROWS, cr)
        ghost[f] = side + base0[None] if f == 0 else side

    def start_state(j, both):
        u = []
        for f in range(5):
            x = block[f, j]
            u.append(jnp.concatenate([x, ghost[f, j - (REACH - MID)]], axis=0) if both else x)
        rho, vel, pres = u[0], u[1:4], u[4]
        mom = [rho * x for x in vel]
        energy = pres * (1.0 / GAMMA_M) + 0.5 * (mom[0] * vel[0] + mom[1] * vel[1] + mom[2] * vel[2])
        return rho, (mom, vel, pres, energy)

    def note(s, j, u):
        value[s, j] = (u[2] - P_REF + u[0][0])[0:ROWS]

    for j in (low - 6, low - 5, high + 4, high + 5):
        ax_only(start_state(j, False)[1], fax, j)

    @pl.loop(0, (ca + 8) // 2)
    def _(i):
        js = [low - 4 + 2 * i, low - 3 + 2 * i]
        us = []
        for j in js:
            rho, u = start_state(j, True)
            for f, x in enumerate([rho] + u[0] + [u[3]]):
                first[f, j] = x
            note(0, j, u)
            us.append(u)
        both_sides(us, js, fax, part, banded)

    def update(f, j, fa, stage):
        a = max(low - j, j - (high - 1), 0)
        a = (a + 1) // 2
        lim = 2 - stage
        base = jnp.where(f == 0, 1.0, 0.0)
        size = ROWS if a == lim else 2 * ROWS
        new = change(fa, part, f, j, size)
        u0 = first[f, j, 0:size]
        if stage == 0:
            new = u0 + new
        else:
            new = 0.75 * u0 + 0.25 * (second[f, j, 0:size] + new)
        beyond = (ax == 0) if j < low else (ax == n_ax - 1)
        home = new[0:ROWS]
        if a > 0:
            home = jnp.where(beyond, base, home)
        if size == ROWS:
            return home, None
        ok = steps <= lim - a
        if a > 0:
            ok = ok & jnp.logical_not(beyond)
        return home, jnp.where(ok, new[ROWS:], base)

    @pl.loop(0, 5)
    def _(f):
        fa = window(fax, f)
        for j in range(low - 4, high + 4):
            home, side = update(f, j, fa, 0)
            second[f, j, 0:ROWS] = home
            if side is not None:
                second[f, j, ROWS:] = side

    for j in (low - 4, low - 3, high + 2, high + 3):
        ax_only(split_state([second[f, j, 0:ROWS] for f in range(5)]), fax, j)

    @pl.loop(0, (ca + 4) // 2)
    def _(i):
        js = [low - 2 + 2 * i, low - 1 + 2 * i]
        us = []
        for j in js:
            u = split_state([second[f, j] for f in range(5)])
            note(1, j, u)
            us.append(u)
        both_sides(us, js, fax, part, banded)

    @pl.loop(0, 5)
    def _(f):
        fa = window(fax, f)
        for j in range(low - 2, high + 2):
            home, side = update(f, j, fa, 1)
            u2_out[f, j - (low - 2), 0:ROWS] = home
            if side is not None:
                u2_out[f, j - (low - 2), ROWS:] = side
        for j in range(low, high):
            u0_out[f, j - low] = first[f, j, 0:ROWS]

    @pl.loop(0, ca)
    def _(i):
        u = split_state([u2_out[f, i + 2, 0:ROWS] for f in range(5)])
        note(2, low + i, u)

    fetch.wait()
    picked[...] = jnp.zeros_like(picked)
    lanes = lax.broadcasted_iota(jnp.int32, (1, cr), 1)
    for p in range(slots):
        cell = cells[p]
        at = jnp.maximum(cell, 0)
        column = jnp.where(cell >= 0, lax.rem(at, cr), -1)
        at = lax.div(at, cr)
        plane = low + lax.div(at, cz)
        r = lax.rem(at, cz) + OFF
        r = 8 * lax.rem(r, 4) + lax.div(r, 4)
        hit = lanes == column
        for s in range(3):
            picked[pl.ds(s * slots + p, 1), :] = jnp.where(hit, value[s, plane, pl.ds(r, 1), :], 0.0)
    q = lax.dot_general(
        jnp.ones((8, cr), BF16),
        picked[...].astype(BF16),
        (((1,), (1,)), ((), ())),
        preferred_element_type=F32,
    )
    q_out[...] = jnp.broadcast_to(q[0:1][None], q_out.shape)


def last_stage(ca, cz, u2, u0, banded, state, fax, part):
    for j in (0, 1, ca + 2, ca + 3):
        ax_only(split_state([u2[f, j, 0:ROWS] for f in range(5)]), fax, j)

    @pl.loop(0, ca // 2)
    def _(i):
        js = [2 + 2 * i, 3 + 2 * i]
        us = [split_state([u2[f, j] for f in range(5)]) for j in js]
        both_sides(us, js, fax, part, banded)

    first, quarter = OFF // 4, cz // 4

    @pl.loop(0, 5)
    def _(f):
        fa = window(fax, f)
        for k in range(ca):
            j = k + 2
            new = u2[f, j, 0:ROWS] + change(fa, part, f, j, ROWS)
            new = u0[f, k] * (1.0 / 3.0) + (2.0 / 3.0) * new
            for l in range(4):
                state[f, k, pl.ds(l, quarter, stride=4), :] = new[8 * l + first : 8 * l + first + quarter]


def signals(slots, rows, offsets, weight, out):
    ndev = rows.shape[0]
    group = 32
    cols = group * slots
    lanes = rows.shape[1]
    col = lax.broadcasted_iota(jnp.int32, (1, cols), 1)
    owner = lax.broadcasted_iota(jnp.int32, (group, cols), 0) == col // slots
    lane = lax.broadcasted_iota(jnp.int32, (lanes, cols), 0)
    time = lax.broadcasted_iota(jnp.int32, (NB, cols), 0).astype(F32)
    total = jnp.zeros(out.shape, F32)
    for g in range(ndev // group):
        q = rows[g * group : (g + 1) * group, :].astype(BF16)
        off = offsets[0:1, g * group : (g + 1) * group].astype(F32)
        off = jnp.broadcast_to(off, (8, group)).astype(BF16)
        bins = jnp.dot(off, owner.astype(BF16), preferred_element_type=F32)[0:1]
        table = jnp.zeros((NB, cols), F32)
        for s in range(3):
            pick = jnp.where(lane == s * slots + col % slots, 1.0, 0.0).astype(BF16)
            spread = jnp.dot(q, pick, preferred_element_type=F32)
            line = jnp.sum(jnp.where(owner, spread, 0.0), axis=0, keepdims=True)
            table = jnp.where(time == bins + s, line, table)
        total = total + lax.dot_general(
            weight[:, g * cols : (g + 1) * cols],
            table.astype(BF16),
            (((1,), (1,)), ((), ())),
            preferred_element_type=F32,
        )
    out[...] = total


def swap_pairs(count, periodic):
    one = [(i, i ^ 1) for i in range(count)]
    two = []
    for i in range(count):
        j = i - 1 if i % 2 == 0 else i + 1
        two.append((i, j % count if periodic or 0 <= j < count else i))
    return one, two


def swap(first, second, axis, periodic):
    one, two = swap_pairs(lax.axis_size(axis), periodic)
    return lax.ppermute(first, axis, one), lax.ppermute(second, axis, two)


def local(density, velocity, pressure, panel_cell, obs_weight, bin_offset):
    ca, cz, cr = density.shape
    slots = panel_cell.shape[0]
    ndev = bin_offset.shape[1]
    n_ax, n_rad = lax.axis_size("ax"), lax.axis_size("rad")
    planes = ca + 2 * REACH
    part = functools.partial
    given = (density.reshape(ca * cz, cr), velocity.reshape(3 * ca * cz, cr), pressure.reshape(ca * cz, cr))

    edge = struct((5 * REACH * cz, cr), BF16)
    strip = struct((5 * REACH * ca, cr), BF16)
    home, ax1, ax2, az1, az2 = call(
        part(load_and_pack, ca, cz),
        (struct((5 * ca * cz, cr)), edge, edge, strip, strip),
        [HBM] * 3,
        [pltpu.SemaphoreType.DMA((3,))],
    )(*[far(x) for x in given])
    ax1, ax2 = swap(ax1, ax2, "ax", False)
    az1, az2 = swap(az1, az2, "az", True)
    grid = struct((5 * planes * ROWS, cr))
    block, banded = call(
        part(prepare, ca, cz), (grid, struct((2 * cr, 2 * cr), BF16)), [VMEM], mib=8
    )(home)

    corner = struct((5 * MID * 2 * MID, cr), BF16)
    near = pltpu.VMEM((5, 2 * MID * cz, cr), F32)
    corner1, corner2 = call(part(pack_corners, n_ax, cz), (corner, corner), [VMEM] * 2, [near])(ax1, ax2)
    corner1, corner2 = swap(corner1, corner2, "az", True)

    side = struct((48, (ca + 2 * MID) * ROWS), BF16)
    ends = ("either",) if n_rad == 2 else ("low", "high")
    got = call(
        part(assemble, n_ax, ends, ca, cz),
        (grid,) + tuple(side for _ in ends),
        [VMEM] * 7,
        [
            pltpu.VMEM((5, 2 * REACH * cz, cr), F32),
            pltpu.VMEM((2,) + strip.shape, F32),
            pltpu.VMEM((2,) + corner.shape, F32),
        ],
        mib=12,
        alias={0: 0},
    )(block, ax1, ax2, az1, az2, corner1, corner2)
    block = got[0].reshape(5, planes, ROWS, cr)
    if n_rad == 2:
        sides = (lax.ppermute(got[1], "rad", [(0, 1), (1, 0)]),)
    else:
        up = [(i, i + 1) for i in range(n_rad - 1)]
        sides = (lax.ppermute(got[1], "rad", [(j, i) for i, j in up]), lax.ppermute(got[2], "rad", up))

    grid = (5, planes, 2 * ROWS, cr)
    q, u2, u0 = call(
        part(stages, n_ax, n_rad, ca, cz, slots),
        (struct((ndev, 1, 128)), struct((5, ca + 4, 2 * ROWS, cr)), struct((5, ca, ROWS, cr))),
        [VMEM, VMEM, HBM] + [VMEM] * len(sides),
        [pltpu.VMEM((5, ca + 2 * MID, ROWS, cr), F32)]
        + [pltpu.VMEM(grid, F32) for _ in range(4)]
        + [pltpu.VMEM((3, planes, ROWS, cr), F32), pltpu.VMEM((128, cr), F32)]
        + [pltpu.SMEM((slots,), jnp.int32), pltpu.SemaphoreType.DMA],
        mib=28,
    )(block, banded, far(panel_cell), *sides)

    rows = lax.all_to_all(q, ("ax", "az", "rad"), 0, 0, tiled=True).reshape(ndev, 128)

    grid = (5, ca + 4, 2 * ROWS, cr)
    state = call(
        part(last_stage, ca, cz),
        struct((5, ca, cz, cr)),
        [VMEM] * 3,
        [pltpu.VMEM(grid, F32), pltpu.VMEM(grid, F32)],
        mib=12,
        cost=pl.CostEstimate(flops=400_000_000, bytes_accessed=8_000_000, transcendentals=0),
    )(u2, u0, banded)
    signal = call(
        part(signals, slots), struct((obs_weight.shape[0], NB)), [VMEM] * 3, mib=24
    )(rows, bin_offset, obs_weight)
    return (state, signal)


def solution(mesh):
    in_specs = (
        P("ax", "az", "rad"),
        P(None, "ax", "az", "rad"),
        P("ax", "az", "rad"),
        P(("ax", "az", "rad")),
        P(("ax", "az", "rad"), None),
        P(("ax", "az", "rad"), None),
    )
    out_specs = (P(None, "ax", "az", "rad"), P(("ax", "az", "rad"), None))
    return jax.shard_map(local, mesh=mesh, in_specs=in_specs, out_specs=out_specs, check_vma=False)
```

```python
import functools

import jax
import jax.numpy as jnp
from jax import lax
from jax.experimental import pallas as pl
from jax.experimental.pallas import tpu as pltpu
from jax.sharding import PartitionSpec as P

NB = 128
GAMMA_M = 0.4
LAMBDA = 0.1
P_REF = 1.0
REACH = 6
MID = 4
SCALE = -LAMBDA / 12.0
ROWS = 32
OFF = 8
SPAN = 32
TALL = ROWS + 8
SLOT = 8
HBM = pltpu.MemorySpace.HBM
VMEM = pltpu.MemorySpace.VMEM
SMEM = pltpu.MemorySpace.SMEM
F32 = jnp.float32
BF16 = jnp.bfloat16


def call(kernel, outs, in_spaces, scratch=(), mib=8, cost=None, alias={}):
    return pl.pallas_call(
        kernel,
        out_shape=outs,
        in_specs=[pl.BlockSpec(memory_space=s) for s in in_spaces],
        out_specs=jax.tree.map(lambda _: pl.BlockSpec(memory_space=VMEM), outs),
        scratch_shapes=list(scratch),
        compiler_params=pltpu.CompilerParams(vmem_limit_bytes=mib * 1024 * 1024),
        cost_estimate=cost,
        input_output_aliases=alias,
    )


def far(x):
    return pltpu.with_memory_space_constraint(x, HBM)


def struct(shape, dtype=F32):
    return jax.ShapeDtypeStruct(shape, dtype)


def kept(row):
    return 8 * (row % 4) + row // 4


def is_even(axis):
    return lax.axis_index(axis) % 2 == 0


def load_and_pack(ca, cz, den, vel, pre, home, ax1, ax2, az1, az2, sems):
    size = ca * cz
    copies = [
        pltpu.make_async_copy(den, home.at[pl.ds(0, size)], sems.at[0]),
        pltpu.make_async_copy(vel, home.at[pl.ds(size, 3 * size)], sems.at[1]),
        pltpu.make_async_copy(pre, home.at[pl.ds(4 * size, size)], sems.at[2]),
    ]
    for copy in copies:
        copy.start()
    for copy in copies:
        copy.wait()
    even = is_even("ax")
    edge = REACH * cz
    for f in range(5):
        at = f * size
        low = home[at : at + edge, :]
        high = home[at + size - edge : at + size, :]
        rows = slice(f * edge, (f + 1) * edge)
        ax1[rows, :] = jnp.where(even, high, low).astype(BF16)
        ax2[rows, :] = jnp.where(even, low, high).astype(BF16)
    even = is_even("az")
    low, high = [], []
    for f in range(5):
        for d in range(REACH):
            low.append(home[pl.ds(f * size + d, ca, stride=cz), :])
            high.append(home[pl.ds(f * size + cz - 1 - d, ca, stride=cz), :])
    low, high = jnp.concatenate(low, axis=0), jnp.concatenate(high, axis=0)
    az1[...] = jnp.where(even, high, low).astype(BF16)
    az2[...] = jnp.where(even, low, high).astype(BF16)


def ax_sides(n_ax, got1, got2, rows):
    ax = lax.axis_index("ax")
    a, b = got1[rows, :].astype(F32), got2[rows, :].astype(F32)
    even = is_even("ax")
    lo = jnp.where(ax == 0, 0.0, jnp.where(even, b, a))
    hi = jnp.where(ax == n_ax - 1, 0.0, jnp.where(even, a, b))
    return lo, hi


def pack_corners(n_ax, cz, got1, got2, first_out, second_out, near):
    even = is_even("az")
    half = MID * cz
    size = REACH * cz
    for f in range(5):
        lo, hi = ax_sides(n_ax, got1, got2, slice(f * size, (f + 1) * size))
        near[f, 0:half, :] = lo[size - half :]
        near[f, half : 2 * half, :] = hi[0:half]
    low, high = [], []
    for f in range(5):
        for d in range(MID):
            low.append(near[f, pl.ds(d, 2 * MID, stride=cz), :])
            high.append(near[f, pl.ds(cz - 1 - d, 2 * MID, stride=cz), :])
    low, high = jnp.concatenate(low, axis=0), jnp.concatenate(high, axis=0)
    first_out[...] = jnp.where(even, high, low).astype(BF16)
    second_out[...] = jnp.where(even, low, high).astype(BF16)


def spread_rows(planes, cz, f, plane, ref, at, block):
    quarter = cz // 4
    for l in range(4):
        row = (f * planes + plane) * ROWS + 8 * l + OFF // 4
        block[pl.ds(row, quarter), :] = ref[pl.ds(at + l, quarter, stride=4), :]


def prepare(ends, ca, cz, n_rad, home, block, banded, *tables):
    cr = home.shape[1]
    rad = lax.axis_index("rad")
    for f in range(5):
        for k in range(ca):
            spread_rows(ca + 2 * REACH, cz, f, REACH + k, home, (f * ca + k) * cz, block)
    banded[...] = band(cr)
    edges, places = tables[: len(ends)], tables[len(ends) :]
    tiles = cr // SLOT
    there = {"high": jnp.where(rad < n_rad - 1, 1.0, 0.0), "low": jnp.where(rad > 0, 1.0, 0.0)}
    high = place_matrix(0, tiles, cr) * there["high"]
    low = place_matrix(SPAN - REACH, tiles, cr) * there["low"]
    for end, edge, place in zip(ends, edges, places):
        start = {"low": 0, "high": cr - REACH, "either": jnp.where(rad == 0, cr - REACH, 0)}[end]
        edge[...] = edge_matrix(start, tiles, cr)
        place[...] = {"low": high, "high": low, "either": high + low}[end].astype(BF16)


def edge_matrix(start, tiles, cr):
    k = lax.broadcasted_iota(jnp.int32, (tiles * cr, tiles * SLOT), 0)
    n = lax.broadcasted_iota(jnp.int32, (tiles * cr, tiles * SLOT), 1)
    hit = (k // cr == n // SLOT) & (n % SLOT < REACH) & (k % cr == n % SLOT + start)
    return jnp.where(hit, 1.0, 0.0).astype(BF16)


def place_matrix(start, tiles, cr):
    k = lax.broadcasted_iota(jnp.int32, (tiles * SLOT, tiles * cr // 4), 0)
    n = lax.broadcasted_iota(jnp.int32, (tiles * SLOT, tiles * cr // 4), 1)
    hit = (k // SLOT == n // SPAN) & (k % SLOT < REACH) & (n % SPAN == k % SLOT + start)
    return jnp.where(hit, 1.0, 0.0)


def assemble(n_ax, count, ca, cz, block_in, ax1, ax2, az1, az2, corner1, corner2, *rest):
    edges, block, outs, (sides, strips, corners) = rest[:count], rest[count], rest[count + 1 : -3], rest[-3:]
    cr = ax1.shape[1]
    planes = ca + 2 * REACH
    size = REACH * cz
    for f in range(5):
        lo, hi = ax_sides(n_ax, ax1, ax2, slice(f * size, (f + 1) * size))
        sides[f, 0:size, :] = lo
        sides[f, size : 2 * size, :] = hi
    for f in range(5):
        for k in range(REACH):
            spread_rows(planes, cz, f, k, sides.at[f], k * cz, block)
            spread_rows(planes, cz, f, REACH + ca + k, sides.at[f], size + k * cz, block)

    even = is_even("az")
    for one, two, into in ((az1, az2, strips), (corner1, corner2, corners)):
        a, b = one[...].astype(F32), two[...].astype(F32)
        into[0] = jnp.where(even, b, a)
        into[1] = jnp.where(even, a, b)
    for f in range(5):
        for d in range(REACH):
            for side, row in ((0, OFF - 1 - d), (1, OFF + cz + d)):
                at = kept(row) + f * planes * ROWS
                got = strips[side, pl.ds((f * REACH + d) * ca, ca), :]
                block[pl.ds(at + REACH * ROWS, ca, stride=ROWS), :] = got
                if d < MID:
                    start = (f * MID + d) * 2 * MID
                    got = corners[side, pl.ds(start, MID), :]
                    block[pl.ds(at + (REACH - MID) * ROWS, MID, stride=ROWS), :] = got
                    got = corners[side, pl.ds(start + MID, MID), :]
                    block[pl.ds(at + (REACH + ca) * ROWS, MID, stride=ROWS), :] = got

    tiles = cr // SLOT
    step = tiles * 8
    rows = []
    for f in range(5):
        for k in range((ca + 2 * MID) * ROWS // step):
            at = (f * planes + REACH - MID) * ROWS + k * step
            rows.append(jnp.concatenate([block[at + 8 * t : at + 8 * t + 8, :] for t in range(tiles)], axis=1))
    rows = jnp.concatenate(rows, axis=0).astype(BF16)
    for edge, out in zip(edges, outs):
        out[...] = jnp.dot(rows, edge[...], preferred_element_type=F32).astype(BF16)


def az_terms(flux):
    v = [flux[8 * l : 8 * l + 8] for l in range(4)]
    v = [pltpu.roll(v[2], 1, 0), pltpu.roll(v[3], 1, 0)] + v + [pltpu.roll(v[0], 7, 0), pltpu.roll(v[1], 7, 0)]
    out = [8.0 * (v[l + 3] - v[l + 1]) - (v[l + 4] - v[l]) for l in range(4)]
    side = flux[ROWS:]
    lanes = side.shape[1]
    span = lax.broadcasted_iota(jnp.int32, side.shape, 1) // SPAN
    up, down = pltpu.roll(side, 7, 0), pltpu.roll(side, 1, 0)
    up1 = pltpu.roll(jnp.where(span == 0, up, side), lanes - SPAN, 1)
    up2 = pltpu.roll(jnp.where(span < 2, up, side), lanes - 2 * SPAN, 1)
    down1 = pltpu.roll(jnp.where(span == 3, down, side), SPAN, 1)
    down2 = pltpu.roll(jnp.where(span >= 2, down, side), 2 * SPAN, 1)
    out.append(8.0 * (up1 - down1) - (up2 - down2))
    return jnp.concatenate(out, axis=0)


def band(cr):
    def place(axis, none):
        i = lax.broadcasted_iota(jnp.int32, (2 * cr, 2 * cr), axis)
        j = i % SPAN
        beyond = jnp.where(j < REACH, cr + j, jnp.where(j >= SPAN - REACH, j - SPAN, none))
        return jnp.where(i < cr, i, beyond), jnp.where(i < cr, -1, i // SPAN)

    k, k_span = place(0, 4 * cr)
    n, n_span = place(1, -4 * cr)
    gap = k - n
    out = jnp.where(gap == 1, 8.0, 0.0) + jnp.where(gap == -1, -8.0, 0.0)
    out = out + jnp.where(gap == 2, -1.0, 0.0) + jnp.where(gap == -2, 1.0, 0.0)
    apart = (k_span >= 0) & (n_span >= 0) & (k_span != n_span)
    return jnp.where(apart, 0.0, out).astype(BF16)


def split_state(u):
    rho, m0, m1, m2, energy = u
    inv = 1.0 / rho
    vel = [m0 * inv, m1 * inv, m2 * inv]
    pres = GAMMA_M * (energy - 0.5 * (m0 * vel[0] + m1 * vel[1] + m2 * vel[2]))
    return [m0, m1, m2], vel, pres, energy


def flux(d, mom, vel, pres, energy):
    parts = [mom[d]]
    for j in range(3):
        parts.append(mom[d] * vel[j] + pres if j == d else mom[d] * vel[j])
    parts.append((energy + pres) * vel[d])
    return parts


def ax_only(u, fax, j):
    got = flux(0, *u)
    for f in range(5):
        fax[f, j, 0:ROWS] = got[f]


def both_sides(us, js, fax, part, banded):
    rows = []
    shape = (ROWS, banded.shape[0] // 2)
    span = lax.broadcasted_iota(jnp.int32, shape, 1) // SPAN
    mine = span == lax.broadcasted_iota(jnp.int32, shape, 0) // 8
    for u, j in zip(us, js):
        got = flux(0, *u)
        for f in range(5):
            fax[f, j] = got[f]
        got = flux(2, *u)
        for f in range(5):
            side = jnp.where(mine, jnp.concatenate([got[f][ROWS:]] * 4, axis=0), 0.0)
            rows.append(jnp.concatenate([got[f][0:ROWS], side], axis=1))
    rows = jnp.concatenate(rows, axis=0)
    coarse = rows.astype(BF16)
    fine = (rows - coarse.astype(F32)).astype(BF16)
    matrix = banded[...]
    out = jnp.dot(coarse, matrix, preferred_element_type=F32)
    out = out + jnp.dot(fine, matrix, preferred_element_type=F32)
    half = out.shape[1] // 2
    for i, (u, j) in enumerate(zip(us, js)):
        got = flux(1, *u)
        for f in range(5):
            at = (i * 5 + f) * ROWS
            side = out[at : at + 8, half:]
            for l in range(1, 4):
                side = jnp.where(span[0:8] == l, out[at + 8 * l : at + 8 * l + 8, half:], side)
            radial = jnp.concatenate([out[at : at + ROWS, 0:half], side], axis=0)
            part[f, j] = az_terms(got[f]) + radial


def change(fa, part, f, j, size):
    near = fa(j + 1)[0:size] - fa(j - 1)[0:size]
    far = fa(j + 2)[0:size] - fa(j - 2)[0:size]
    return SCALE * (8.0 * near - far + part[f, j, 0:size])


def window(fax, f):
    held = {}

    def get(j):
        if j not in held:
            held[j] = fax[f, j]
        return held[j]

    return get


def stages(n_ax, n_rad, ca, cz, slots, block, banded, cells_far, *refs):
    sides, refs = refs[: len(refs) - 12], refs[len(refs) - 12 :]
    sides, places = sides[: len(sides) // 2], sides[len(sides) // 2 :]
    q_out, u2_out, u0_out, ghost, first, second, fax, part, value, picked, cells, cells_sem = refs
    fetch = pltpu.make_async_copy(cells_far, cells, cells_sem)
    fetch.start()
    cr = block.shape[-1]
    low, high = REACH, REACH + ca
    ax = lax.axis_index("ax")
    rad = lax.axis_index("rad")

    lane = lax.broadcasted_iota(jnp.int32, (8, cr), 1)
    row = 4 * lax.broadcasted_iota(jnp.int32, (8, cr), 0) + lane // SPAN
    j = lane % SPAN
    steps_rad = jnp.where(
        (j < REACH) & (rad < n_rad - 1),
        1 + j // 2,
        jnp.where((j >= SPAN - REACH) & (rad > 0), 1 + (SPAN - 1 - j) // 2, 99),
    )
    beyond_row = jnp.maximum(OFF - row, row - (OFF + cz - 1))
    steps = steps_rad + jnp.where(beyond_row > 0, (beyond_row + 1) // 2, 0)
    base0 = jnp.where(steps_rad < 99, 0.0, 1.0)

    side = 0.0
    for got, place in zip(sides, places):
        side = side + jnp.dot(got[...], place[...], preferred_element_type=F32)
    group = side.shape[1] // cr
    count = (ca + 2 * MID) // group
    for f in range(5):
        for k in range(count):
            for i in range(group):
                at = (f * count + k) * 8
                tile = side[at : at + 8, i * cr : (i + 1) * cr]
                ghost[f, k * group + i] = tile + base0 if f == 0 else tile

    def start_state(j, both):
        u = []
        for f in range(5):
            x = block[f, j]
            u.append(jnp.concatenate([x, ghost[f, j - (REACH - MID)]], axis=0) if both else x)
        rho, vel, pres = u[0], u[1:4], u[4]
        mom = [rho * x for x in vel]
        energy = pres * (1.0 / GAMMA_M) + 0.5 * (mom[0] * vel[0] + mom[1] * vel[1] + mom[2] * vel[2])
        return rho, (mom, vel, pres, energy)

    def note(s, j, u):
        value[s, j] = (u[2] - P_REF + u[0][0])[0:ROWS]

    for j in (low - 6, low - 5, high + 4, high + 5):
        ax_only(start_state(j, False)[1], fax, j)

    @pl.loop(0, (ca + 8) // 2)
    def _(i):
        js = [low - 4 + 2 * i, low - 3 + 2 * i]
        us = []
        for j in js:
            rho, u = start_state(j, True)
            for f, x in enumerate([rho] + u[0] + [u[3]]):
                first[f, j] = x
            note(0, j, u)
            us.append(u)
        both_sides(us, js, fax, part, banded)

    def update(f, j, fa, stage):
        a = max(low - j, j - (high - 1), 0)
        a = (a + 1) // 2
        lim = 2 - stage
        base = jnp.where(f == 0, 1.0, 0.0)
        size = ROWS if a == lim else TALL
        new = change(fa, part, f, j, size)
        u0 = first[f, j, 0:size]
        if stage == 0:
            new = u0 + new
        else:
            new = 0.75 * u0 + 0.25 * (second[f, j, 0:size] + new)
        beyond = (ax == 0) if j < low else (ax == n_ax - 1)
        home = new[0:ROWS]
        if a > 0:
            home = jnp.where(beyond, base, home)
        if size == ROWS:
            return home, None
        ok = steps <= lim - a
        if a > 0:
            ok = ok & jnp.logical_not(beyond)
        return home, jnp.where(ok, new[ROWS:], base)

    @pl.loop(0, 5)
    def _(f):
        fa = window(fax, f)
        for j in range(low - 4, high + 4):
            home, side = update(f, j, fa, 0)
            second[f, j, 0:ROWS] = home
            if side is not None:
                second[f, j, ROWS:] = side

    for j in (low - 4, low - 3, high + 2, high + 3):
        ax_only(split_state([second[f, j, 0:ROWS] for f in range(5)]), fax, j)

    @pl.loop(0, (ca + 4) // 2)
    def _(i):
        js = [low - 2 + 2 * i, low - 1 + 2 * i]
        us = []
        for j in js:
            u = split_state([second[f, j] for f in range(5)])
            note(1, j, u)
            us.append(u)
        both_sides(us, js, fax, part, banded)

    @pl.loop(0, 5)
    def _(f):
        fa = window(fax, f)
        for j in range(low - 2, high + 2):
            home, side = update(f, j, fa, 1)
            u2_out[f, j - (low - 2), 0:ROWS] = home
            if side is not None:
                u2_out[f, j - (low - 2), ROWS:] = side
        for j in range(low, high):
            u0_out[f, j - low] = first[f, j, 0:ROWS]

    @pl.loop(0, ca)
    def _(i):
        u = split_state([u2_out[f, i + 2, 0:ROWS] for f in range(5)])
        note(2, low + i, u)

    fetch.wait()
    picked[...] = jnp.zeros_like(picked)
    lanes = lax.broadcasted_iota(jnp.int32, (1, cr), 1)
    for p in range(slots):
        cell = cells[p]
        at = jnp.maximum(cell, 0)
        column = jnp.where(cell >= 0, lax.rem(at, cr), -1)
        at = lax.div(at, cr)
        plane = low + lax.div(at, cz)
        r = lax.rem(at, cz) + OFF
        r = 8 * lax.rem(r, 4) + lax.div(r, 4)
        hit = lanes == column
        for s in range(3):
            picked[pl.ds(s * slots + p, 1), :] = jnp.where(hit, value[s, plane, pl.ds(r, 1), :], 0.0)
    q = lax.dot_general(
        jnp.ones((8, cr), BF16),
        picked[...].astype(BF16),
        (((1,), (1,)), ((), ())),
        preferred_element_type=F32,
    )
    q_out[...] = jnp.broadcast_to(q[0:1][None], q_out.shape)


def last_stage(ca, cz, u2, u0, banded, state, fax, part):
    for j in (0, 1, ca + 2, ca + 3):
        ax_only(split_state([u2[f, j, 0:ROWS] for f in range(5)]), fax, j)

    @pl.loop(0, ca // 2)
    def _(i):
        js = [2 + 2 * i, 3 + 2 * i]
        us = [split_state([u2[f, j] for f in range(5)]) for j in js]
        both_sides(us, js, fax, part, banded)

    first, quarter = OFF // 4, cz // 4

    @pl.loop(0, 5)
    def _(f):
        fa = window(fax, f)
        for k in range(ca):
            j = k + 2
            new = u2[f, j, 0:ROWS] + change(fa, part, f, j, ROWS)
            new = u0[f, k] * (1.0 / 3.0) + (2.0 / 3.0) * new
            for l in range(4):
                state[f, k, pl.ds(l, quarter, stride=4), :] = new[8 * l + first : 8 * l + first + quarter]


def signals(slots, rows, offsets, weight, out):
    ndev = rows.shape[0]
    group = 32
    cols = group * slots
    lanes = rows.shape[1]
    col = lax.broadcasted_iota(jnp.int32, (1, cols), 1)
    owner = lax.broadcasted_iota(jnp.int32, (group, cols), 0) == col // slots
    lane = lax.broadcasted_iota(jnp.int32, (lanes, cols), 0)
    time = lax.broadcasted_iota(jnp.int32, (NB, cols), 0).astype(F32)
    total = jnp.zeros(out.shape, F32)
    for g in range(ndev // group):
        q = rows[g * group : (g + 1) * group, :].astype(BF16)
        off = offsets[0:1, g * group : (g + 1) * group].astype(F32)
        off = jnp.broadcast_to(off, (8, group)).astype(BF16)
        bins = jnp.dot(off, owner.astype(BF16), preferred_element_type=F32)[0:1]
        table = jnp.zeros((NB, cols), F32)
        for s in range(3):
            pick = jnp.where(lane == s * slots + col % slots, 1.0, 0.0).astype(BF16)
            spread = jnp.dot(q, pick, preferred_element_type=F32)
            line = jnp.sum(jnp.where(owner, spread, 0.0), axis=0, keepdims=True)
            table = jnp.where(time == bins + s, line, table)
        total = total + lax.dot_general(
            weight[:, g * cols : (g + 1) * cols],
            table.astype(BF16),
            (((1,), (1,)), ((), ())),
            preferred_element_type=F32,
        )
    out[...] = total


def swap_pairs(count, periodic):
    one = [(i, i ^ 1) for i in range(count)]
    two = []
    for i in range(count):
        j = i - 1 if i % 2 == 0 else i + 1
        two.append((i, j % count if periodic or 0 <= j < count else i))
    return one, two


def swap(first, second, axis, periodic):
    one, two = swap_pairs(lax.axis_size(axis), periodic)
    return lax.ppermute(first, axis, one), lax.ppermute(second, axis, two)


def local(density, velocity, pressure, panel_cell, obs_weight, bin_offset):
    ca, cz, cr = density.shape
    slots = panel_cell.shape[0]
    ndev = bin_offset.shape[1]
    n_ax, n_rad = lax.axis_size("ax"), lax.axis_size("rad")
    planes = ca + 2 * REACH
    part = functools.partial
    given = (density.reshape(ca * cz, cr), velocity.reshape(3 * ca * cz, cr), pressure.reshape(ca * cz, cr))

    edge = struct((5 * REACH * cz, cr), BF16)
    strip = struct((5 * REACH * ca, cr), BF16)
    home, ax1, ax2, az1, az2 = call(
        part(load_and_pack, ca, cz),
        (struct((5 * ca * cz, cr)), edge, edge, strip, strip),
        [HBM] * 3,
        [pltpu.SemaphoreType.DMA((3,))],
    )(*[far(x) for x in given])
    ax1, ax2 = swap(ax1, ax2, "ax", False)
    az1, az2 = swap(az1, az2, "az", True)
    grid = struct((5 * planes * ROWS, cr))
    ends = ("either",) if n_rad == 2 else ("low", "high")
    tiles = cr // SLOT
    table = [struct((tiles * cr, cr), BF16)] * len(ends) + [struct((cr, tiles * cr // 4), BF16)] * len(ends)
    block, banded, *tables = call(
        part(prepare, ends, ca, cz, n_rad),
        (grid, struct((2 * cr, 2 * cr), BF16), *table),
        [VMEM],
    )(home)
    edges, places = tables[: len(ends)], tables[len(ends) :]

    corner = struct((5 * MID * 2 * MID, cr), BF16)
    near = pltpu.VMEM((5, 2 * MID * cz, cr), F32)
    corner1, corner2 = call(part(pack_corners, n_ax, cz), (corner, corner), [VMEM] * 2, [near])(ax1, ax2)
    corner1, corner2 = swap(corner1, corner2, "az", True)

    side = struct((5 * (ca + 2 * MID) * ROWS // tiles, cr), BF16)
    got = call(
        part(assemble, n_ax, len(ends), ca, cz),
        (grid,) + tuple(side for _ in ends),
        [VMEM] * (7 + len(ends)),
        [
            pltpu.VMEM((5, 2 * REACH * cz, cr), F32),
            pltpu.VMEM((2,) + strip.shape, F32),
            pltpu.VMEM((2,) + corner.shape, F32),
        ],
        mib=12,
        alias={0: 0},
    )(block, ax1, ax2, az1, az2, corner1, corner2, *edges)
    block = got[0].reshape(5, planes, ROWS, cr)
    if n_rad == 2:
        sides = (lax.ppermute(got[1], "rad", [(0, 1), (1, 0)]),)
    else:
        up = [(i, i + 1) for i in range(n_rad - 1)]
        sides = (lax.ppermute(got[1], "rad", [(j, i) for i, j in up]), lax.ppermute(got[2], "rad", up))

    grid = (5, planes, TALL, cr)
    q, u2, u0 = call(
        part(stages, n_ax, n_rad, ca, cz, slots),
        (struct((ndev, 1, 128)), struct((5, ca + 4, TALL, cr)), struct((5, ca, ROWS, cr))),
        [VMEM, VMEM, HBM] + [VMEM] * (2 * len(sides)),
        [pltpu.VMEM((5, ca + 2 * MID, 8, cr), F32)]
        + [pltpu.VMEM(grid, F32) for _ in range(4)]
        + [pltpu.VMEM((3, planes, ROWS, cr), F32), pltpu.VMEM((128, cr), F32)]
        + [pltpu.SMEM((slots,), jnp.int32), pltpu.SemaphoreType.DMA],
        mib=28,
    )(block, banded, far(panel_cell), *sides, *places)

    rows = lax.all_to_all(q, ("ax", "az", "rad"), 0, 0, tiled=True).reshape(ndev, 128)

    grid = (5, ca + 4, TALL, cr)
    state = call(
        part(last_stage, ca, cz),
        struct((5, ca, cz, cr)),
        [VMEM] * 3,
        [pltpu.VMEM(grid, F32), pltpu.VMEM(grid, F32)],
        mib=12,
        cost=pl.CostEstimate(flops=400_000_000, bytes_accessed=8_000_000, transcendentals=0),
    )(u2, u0, banded)
    signal = call(
        part(signals, slots), struct((obs_weight.shape[0], NB)), [VMEM] * 3, mib=24
    )(rows, bin_offset, obs_weight)
    return (state, signal)


def solution(mesh):
    in_specs = (
        P("ax", "az", "rad"),
        P(None, "ax", "az", "rad"),
        P("ax", "az", "rad"),
        P(("ax", "az", "rad")),
        P(("ax", "az", "rad"), None),
        P(("ax", "az", "rad"), None),
    )
    out_specs = (P(None, "ax", "az", "rad"), P(("ax", "az", "rad"), None))
    return jax.shard_map(local, mesh=mesh, in_specs=in_specs, out_specs=out_specs, check_vma=False)
```

```python
import functools

import jax
import jax.numpy as jnp
from jax import lax
from jax.experimental import pallas as pl
from jax.experimental.pallas import tpu as pltpu
from jax.sharding import Mesh, PartitionSpec as P

NB = 128
GAMMA_M = 0.4
LAMBDA = 0.1
P_REF = 1.0
REACH = 6
MID = 4
SCALE = -LAMBDA / 12.0
ROWS = 32
OFF = 8
SPAN = 32
TALL = ROWS + 8
STEP = 4
SLOT = 8
HBM = pltpu.MemorySpace.HBM
VMEM = pltpu.MemorySpace.VMEM
SMEM = pltpu.MemorySpace.SMEM
F32 = jnp.float32
BF16 = jnp.bfloat16


def call(kernel, outs, in_spaces, scratch=(), mib=8, cost=None, alias={}):
    return pl.pallas_call(
        kernel,
        out_shape=outs,
        in_specs=[pl.BlockSpec(memory_space=s) for s in in_spaces],
        out_specs=jax.tree.map(lambda _: pl.BlockSpec(memory_space=VMEM), outs),
        scratch_shapes=list(scratch),
        compiler_params=pltpu.CompilerParams(vmem_limit_bytes=mib * 1024 * 1024),
        cost_estimate=cost,
        input_output_aliases=alias,
    )


def far(x):
    return pltpu.with_memory_space_constraint(x, HBM)


def struct(shape, dtype=F32):
    return jax.ShapeDtypeStruct(shape, dtype)


def kept(row):
    return 8 * (row % 4) + row // 4


def ax_index():
    return lax.axis_index("y") * lax.axis_size("core") + lax.axis_index("core")


def is_even(axis):
    return lax.axis_index("core" if axis == "ax" else axis) % 2 == 0


def load_and_pack(ca, cz, den, vel, pre, home, ax1, ax2, az1, az2, sems):
    size = ca * cz
    copies = [
        pltpu.make_async_copy(den, home.at[pl.ds(0, size)], sems.at[0]),
        pltpu.make_async_copy(vel, home.at[pl.ds(size, 3 * size)], sems.at[1]),
        pltpu.make_async_copy(pre, home.at[pl.ds(4 * size, size)], sems.at[2]),
    ]
    for copy in copies:
        copy.start()
    for copy in copies:
        copy.wait()
    even = is_even("ax")
    edge = REACH * cz
    for f in range(5):
        at = f * size
        low = home[at : at + edge, :]
        high = home[at + size - edge : at + size, :]
        rows = slice(f * edge, (f + 1) * edge)
        ax1[rows, :] = jnp.where(even, high, low).astype(BF16)
        ax2[rows, :] = jnp.where(even, low, high).astype(BF16)
    even = is_even("az")
    low, high = [], []
    for f in range(5):
        for d in range(REACH):
            low.append(home[pl.ds(f * size + d, ca, stride=cz), :])
            high.append(home[pl.ds(f * size + cz - 1 - d, ca, stride=cz), :])
    low, high = jnp.concatenate(low, axis=0), jnp.concatenate(high, axis=0)
    az1[...] = jnp.where(even, high, low).astype(BF16)
    az2[...] = jnp.where(even, low, high).astype(BF16)


def ax_sides(n_ax, got1, got2, rows):
    ax = ax_index()
    a, b = got1[rows, :].astype(F32), got2[rows, :].astype(F32)
    even = is_even("ax")
    lo = jnp.where(ax == 0, 0.0, jnp.where(even, b, a))
    hi = jnp.where(ax == n_ax - 1, 0.0, jnp.where(even, a, b))
    return lo, hi


def pack_corners(n_ax, cz, got1, got2, first_out, second_out, near):
    even = is_even("az")
    half = MID * cz
    size = REACH * cz
    for f in range(5):
        lo, hi = ax_sides(n_ax, got1, got2, slice(f * size, (f + 1) * size))
        near[f, 0:half, :] = lo[size - half :]
        near[f, half : 2 * half, :] = hi[0:half]
    low, high = [], []
    for f in range(5):
        for d in range(MID):
            low.append(near[f, pl.ds(d, 2 * MID, stride=cz), :])
            high.append(near[f, pl.ds(cz - 1 - d, 2 * MID, stride=cz), :])
    low, high = jnp.concatenate(low, axis=0), jnp.concatenate(high, axis=0)
    first_out[...] = jnp.where(even, high, low).astype(BF16)
    second_out[...] = jnp.where(even, low, high).astype(BF16)


def spread_rows(planes, cz, f, plane, ref, at, block):
    quarter = cz // 4
    for l in range(4):
        row = (f * planes + plane) * ROWS + 8 * l + OFF // 4
        block[pl.ds(row, quarter), :] = ref[pl.ds(at + l, quarter, stride=4), :]


def prepare(ends, ca, cz, n_rad, home, block, banded, *tables):
    cr = home.shape[1]
    rad = lax.axis_index("rad")
    for f in range(5):
        for k in range(ca):
            spread_rows(ca + 2 * REACH, cz, f, REACH + k, home, (f * ca + k) * cz, block)
    banded[...] = band(cr)
    edges, places = tables[: len(ends)], tables[len(ends) :]
    tiles = cr // SLOT
    there = {"high": jnp.where(rad < n_rad - 1, 1.0, 0.0), "low": jnp.where(rad > 0, 1.0, 0.0)}
    high = place_matrix(0, tiles, cr) * there["high"]
    low = place_matrix(SPAN - REACH, tiles, cr) * there["low"]
    for end, edge, place in zip(ends, edges, places):
        start = {"low": 0, "high": cr - REACH, "either": jnp.where(rad == 0, cr - REACH, 0)}[end]
        edge[...] = edge_matrix(start, tiles, cr)
        place[...] = {"low": high, "high": low, "either": high + low}[end].astype(BF16)


def edge_matrix(start, tiles, cr):
    k = lax.broadcasted_iota(jnp.int32, (tiles * cr, tiles * SLOT), 0)
    n = lax.broadcasted_iota(jnp.int32, (tiles * cr, tiles * SLOT), 1)
    hit = (k // cr == n // SLOT) & (n % SLOT < REACH) & (k % cr == n % SLOT + start)
    return jnp.where(hit, 1.0, 0.0).astype(BF16)


def place_matrix(start, tiles, cr):
    k = lax.broadcasted_iota(jnp.int32, (tiles * SLOT, tiles * cr // 4), 0)
    n = lax.broadcasted_iota(jnp.int32, (tiles * SLOT, tiles * cr // 4), 1)
    hit = (k // SLOT == n // SPAN) & (k % SLOT < REACH) & (n % SPAN == k % SLOT + start)
    return jnp.where(hit, 1.0, 0.0)


def assemble(n_ax, count, ca, cz, block_in, ax1, ax2, az1, az2, corner1, corner2, *rest):
    edges, block, outs, (sides, strips, corners) = rest[:count], rest[count], rest[count + 1 : -3], rest[-3:]
    cr = ax1.shape[1]
    planes = ca + 2 * REACH
    size = REACH * cz
    for f in range(5):
        lo, hi = ax_sides(n_ax, ax1, ax2, slice(f * size, (f + 1) * size))
        sides[f, 0:size, :] = lo
        sides[f, size : 2 * size, :] = hi
    for f in range(5):
        for k in range(REACH):
            spread_rows(planes, cz, f, k, sides.at[f], k * cz, block)
            spread_rows(planes, cz, f, REACH + ca + k, sides.at[f], size + k * cz, block)

    even = is_even("az")
    for one, two, into in ((az1, az2, strips), (corner1, corner2, corners)):
        a, b = one[...].astype(F32), two[...].astype(F32)
        into[0] = jnp.where(even, b, a)
        into[1] = jnp.where(even, a, b)
    for f in range(5):
        for d in range(REACH):
            for side, row in ((0, OFF - 1 - d), (1, OFF + cz + d)):
                at = kept(row) + f * planes * ROWS
                got = strips[side, pl.ds((f * REACH + d) * ca, ca), :]
                block[pl.ds(at + REACH * ROWS, ca, stride=ROWS), :] = got
                if d < MID:
                    start = (f * MID + d) * 2 * MID
                    got = corners[side, pl.ds(start, MID), :]
                    block[pl.ds(at + (REACH - MID) * ROWS, MID, stride=ROWS), :] = got
                    got = corners[side, pl.ds(start + MID, MID), :]
                    block[pl.ds(at + (REACH + ca) * ROWS, MID, stride=ROWS), :] = got

    tiles = cr // SLOT
    step = tiles * 8
    rows = []
    for f in range(5):
        for k in range((ca + 2 * MID) * ROWS // step):
            at = (f * planes + REACH - MID) * ROWS + k * step
            rows.append(jnp.concatenate([block[at + 8 * t : at + 8 * t + 8, :] for t in range(tiles)], axis=1))
    rows = jnp.concatenate(rows, axis=0).astype(BF16)
    for edge, out in zip(edges, outs):
        out[...] = jnp.dot(rows, edge[...], preferred_element_type=F32).astype(BF16)


def az_terms(flux):
    v = [flux[8 * l : 8 * l + 8] for l in range(4)]
    v = [pltpu.roll(v[2], 1, 0), pltpu.roll(v[3], 1, 0)] + v + [pltpu.roll(v[0], 7, 0), pltpu.roll(v[1], 7, 0)]
    out = [8.0 * (v[l + 3] - v[l + 1]) - (v[l + 4] - v[l]) for l in range(4)]
    side = flux[ROWS:]
    lanes = side.shape[1]
    span = lax.broadcasted_iota(jnp.int32, side.shape, 1) // SPAN
    up, down = pltpu.roll(side, 7, 0), pltpu.roll(side, 1, 0)
    up1 = pltpu.roll(jnp.where(span == 0, up, side), lanes - SPAN, 1)
    up2 = pltpu.roll(jnp.where(span < 2, up, side), lanes - 2 * SPAN, 1)
    down1 = pltpu.roll(jnp.where(span == 3, down, side), SPAN, 1)
    down2 = pltpu.roll(jnp.where(span >= 2, down, side), 2 * SPAN, 1)
    out.append(8.0 * (up1 - down1) - (up2 - down2))
    return jnp.concatenate(out, axis=0)


def band(cr):
    def place(axis, none):
        i = lax.broadcasted_iota(jnp.int32, (2 * cr, 2 * cr), axis)
        j = i % SPAN
        beyond = jnp.where(j < REACH, cr + j, jnp.where(j >= SPAN - REACH, j - SPAN, none))
        return jnp.where(i < cr, i, beyond), jnp.where(i < cr, -1, i // SPAN)

    k, k_span = place(0, 4 * cr)
    n, n_span = place(1, -4 * cr)
    gap = k - n
    out = jnp.where(gap == 1, 8.0, 0.0) + jnp.where(gap == -1, -8.0, 0.0)
    out = out + jnp.where(gap == 2, -1.0, 0.0) + jnp.where(gap == -2, 1.0, 0.0)
    apart = (k_span >= 0) & (n_span >= 0) & (k_span != n_span)
    return jnp.where(apart, 0.0, out).astype(BF16)


def split_state(u):
    rho, m0, m1, m2, energy = u
    inv = 1.0 / rho
    vel = [m0 * inv, m1 * inv, m2 * inv]
    pres = GAMMA_M * (energy - 0.5 * (m0 * vel[0] + m1 * vel[1] + m2 * vel[2]))
    return [m0, m1, m2], vel, pres, energy


def flux(d, mom, vel, pres, energy):
    parts = [mom[d]]
    for j in range(3):
        parts.append(mom[d] * vel[j] + pres if j == d else mom[d] * vel[j])
    parts.append((energy + pres) * vel[d])
    return parts


def ax_only(u, fax, j):
    got = flux(0, *u)
    for f in range(5):
        fax[f, j, 0:ROWS] = got[f]


def both_sides(us, js, fax, part, banded):
    rows = []
    shape = (ROWS, banded.shape[0] // 2)
    span = lax.broadcasted_iota(jnp.int32, shape, 1) // SPAN
    mine = span == lax.broadcasted_iota(jnp.int32, shape, 0) // 8
    for u, j in zip(us, js):
        got = flux(0, *u)
        for f in range(5):
            fax[f, j] = got[f]
        got = flux(2, *u)
        for f in range(5):
            side = jnp.where(mine, jnp.concatenate([got[f][ROWS:]] * 4, axis=0), 0.0)
            rows.append(jnp.concatenate([got[f][0:ROWS], side], axis=1))
    rows = jnp.concatenate(rows, axis=0)
    coarse = rows.astype(BF16)
    fine = (rows - coarse.astype(F32)).astype(BF16)
    matrix = banded[...]
    out = jnp.dot(coarse, matrix, preferred_element_type=F32)
    out = out + jnp.dot(fine, matrix, preferred_element_type=F32)
    half = out.shape[1] // 2
    for i, (u, j) in enumerate(zip(us, js)):
        got = flux(1, *u)
        for f in range(5):
            at = (i * 5 + f) * ROWS
            side = out[at : at + 8, half:]
            for l in range(1, 4):
                side = jnp.where(span[0:8] == l, out[at + 8 * l : at + 8 * l + 8, half:], side)
            radial = jnp.concatenate([out[at : at + ROWS, 0:half], side], axis=0)
            part[f, j] = az_terms(got[f]) + radial


def change(fa, part, f, j, size):
    near = fa(j + 1)[0:size] - fa(j - 1)[0:size]
    far = fa(j + 2)[0:size] - fa(j - 2)[0:size]
    return SCALE * (8.0 * near - far + part[f, j, 0:size])


def window(fax, f):
    held = {}

    def get(j):
        if j not in held:
            held[j] = fax[f, j]
        return held[j]

    return get


def stages(n_ax, n_rad, ca, cz, slots, block, banded, cells_far, *refs):
    sides, refs = refs[: len(refs) - 12], refs[len(refs) - 12 :]
    sides, places = sides[: len(sides) // 2], sides[len(sides) // 2 :]
    q_out, u2_out, u0_out, ghost, first, second, fax, part, value, picked, cells, cells_sem = refs
    fetch = pltpu.make_async_copy(cells_far, cells, cells_sem)
    fetch.start()
    cr = block.shape[-1]
    low, high = REACH, REACH + ca
    ax = ax_index()
    rad = lax.axis_index("rad")

    lane = lax.broadcasted_iota(jnp.int32, (8, cr), 1)
    row = 4 * lax.broadcasted_iota(jnp.int32, (8, cr), 0) + lane // SPAN
    j = lane % SPAN
    steps_rad = jnp.where(
        (j < REACH) & (rad < n_rad - 1),
        1 + j // 2,
        jnp.where((j >= SPAN - REACH) & (rad > 0), 1 + (SPAN - 1 - j) // 2, 99),
    )
    beyond_row = jnp.maximum(OFF - row, row - (OFF + cz - 1))
    steps = steps_rad + jnp.where(beyond_row > 0, (beyond_row + 1) // 2, 0)
    base0 = jnp.where(steps_rad < 99, 0.0, 1.0)

    side = 0.0
    for got, place in zip(sides, places):
        side = side + jnp.dot(got[...], place[...], preferred_element_type=F32)
    group = side.shape[1] // cr
    count = (ca + 2 * MID) // group
    for f in range(5):
        for k in range(count):
            for i in range(group):
                at = (f * count + k) * 8
                tile = side[at : at + 8, i * cr : (i + 1) * cr]
                ghost[f, k * group + i] = tile + base0 if f == 0 else tile

    def start_state(j, both):
        u = []
        for f in range(5):
            x = block[f, j]
            u.append(jnp.concatenate([x, ghost[f, j - (REACH - MID)]], axis=0) if both else x)
        rho, vel, pres = u[0], u[1:4], u[4]
        mom = [rho * x for x in vel]
        energy = pres * (1.0 / GAMMA_M) + 0.5 * (mom[0] * vel[0] + mom[1] * vel[1] + mom[2] * vel[2])
        return rho, (mom, vel, pres, energy)

    def note(s, j, u):
        value[s, j] = (u[2] - P_REF + u[0][0])[0:ROWS]

    for j in (low - 6, low - 5, high + 4, high + 5):
        ax_only(start_state(j, False)[1], fax, j)

    @pl.loop(0, (ca + 8) // STEP)
    def _(i):
        js = [low - 4 + STEP * i + k for k in range(STEP)]
        us = []
        for j in js:
            rho, u = start_state(j, True)
            for f, x in enumerate([rho] + u[0] + [u[3]]):
                first[f, j] = x
            note(0, j, u)
            us.append(u)
        both_sides(us, js, fax, part, banded)

    def update(f, j, fa, stage):
        a = max(low - j, j - (high - 1), 0)
        a = (a + 1) // 2
        lim = 2 - stage
        base = jnp.where(f == 0, 1.0, 0.0)
        size = ROWS if a == lim else TALL
        new = change(fa, part, f, j, size)
        u0 = first[f, j, 0:size]
        if stage == 0:
            new = u0 + new
        else:
            new = 0.75 * u0 + 0.25 * (second[f, j, 0:size] + new)
        beyond = (ax == 0) if j < low else (ax == n_ax - 1)
        home = new[0:ROWS]
        if a > 0:
            home = jnp.where(beyond, base, home)
        if size == ROWS:
            return home, None
        ok = steps <= lim - a
        if a > 0:
            ok = ok & jnp.logical_not(beyond)
        return home, jnp.where(ok, new[ROWS:], base)

    @pl.loop(0, 5)
    def _(f):
        fa = window(fax, f)
        for j in range(low - 4, high + 4):
            home, side = update(f, j, fa, 0)
            second[f, j, 0:ROWS] = home
            if side is not None:
                second[f, j, ROWS:] = side

    for j in (low - 4, low - 3, high + 2, high + 3):
        ax_only(split_state([second[f, j, 0:ROWS] for f in range(5)]), fax, j)

    @pl.loop(0, (ca + 4) // STEP)
    def _(i):
        js = [low - 2 + STEP * i + k for k in range(STEP)]
        us = []
        for j in js:
            u = split_state([second[f, j] for f in range(5)])
            note(1, j, u)
            us.append(u)
        both_sides(us, js, fax, part, banded)

    @pl.loop(0, 5)
    def _(f):
        fa = window(fax, f)
        for j in range(low - 2, high + 2):
            home, side = update(f, j, fa, 1)
            u2_out[f, j - (low - 2), 0:ROWS] = home
            if side is not None:
                u2_out[f, j - (low - 2), ROWS:] = side
        for j in range(low, high):
            u0_out[f, j - low] = first[f, j, 0:ROWS]

    @pl.loop(0, ca)
    def _(i):
        u = split_state([u2_out[f, i + 2, 0:ROWS] for f in range(5)])
        note(2, low + i, u)

    fetch.wait()
    picked[...] = jnp.zeros_like(picked)
    lanes = lax.broadcasted_iota(jnp.int32, (1, cr), 1)
    for p in range(slots):
        cell = cells[p]
        at = jnp.maximum(cell, 0)
        column = jnp.where(cell >= 0, lax.rem(at, cr), -1)
        at = lax.div(at, cr)
        plane = low + lax.div(at, cz)
        r = lax.rem(at, cz) + OFF
        r = 8 * lax.rem(r, 4) + lax.div(r, 4)
        hit = lanes == column
        for s in range(3):
            picked[pl.ds(s * slots + p, 1), :] = jnp.where(hit, value[s, plane, pl.ds(r, 1), :], 0.0)
    q = lax.dot_general(
        jnp.ones((8, cr), BF16),
        picked[...].astype(BF16),
        (((1,), (1,)), ((), ())),
        preferred_element_type=F32,
    )
    q_out[...] = jnp.broadcast_to(q[0:1][None], q_out.shape)


def last_stage(ca, cz, u2, u0, banded, after, state, fax, part):
    del after
    for j in (0, 1, ca + 2, ca + 3):
        ax_only(split_state([u2[f, j, 0:ROWS] for f in range(5)]), fax, j)

    @pl.loop(0, ca // STEP)
    def _(i):
        js = [2 + STEP * i + k for k in range(STEP)]
        us = [split_state([u2[f, j] for f in range(5)]) for j in js]
        both_sides(us, js, fax, part, banded)

    first, quarter = OFF // 4, cz // 4

    @pl.loop(0, 5)
    def _(f):
        fa = window(fax, f)
        for k in range(ca):
            j = k + 2
            new = u2[f, j, 0:ROWS] + change(fa, part, f, j, ROWS)
            new = u0[f, k] * (1.0 / 3.0) + (2.0 / 3.0) * new
            for l in range(4):
                state[f, k, pl.ds(l, quarter, stride=4), :] = new[8 * l + first : 8 * l + first + quarter]


def pair_rows(mine, other, out):
    first = is_even("ax")
    a, b = mine[0], other[0]
    rows = jnp.concatenate([jnp.where(first, a, b), jnp.where(first, b, a)], axis=0)
    out[...] = jnp.broadcast_to(rows[None], out.shape)


def signals(slots, cores, pair, rows, offsets, weight, out):
    ndev = rows.shape[0]
    group = max(32, cores * pair)
    cols = group * slots
    lanes = rows.shape[1]
    col = lax.broadcasted_iota(jnp.int32, (1, cols), 1)
    place = lax.broadcasted_iota(jnp.int32, (group, cols), 0)
    inner = place % (cores * pair)
    device = place - inner + (inner % cores) * pair + inner // cores
    owner = device == col // slots
    holder = place == col // slots
    lane = lax.broadcasted_iota(jnp.int32, (lanes, cols), 0)
    time = lax.broadcasted_iota(jnp.int32, (NB, cols), 0).astype(F32)
    total = jnp.zeros(out.shape, F32)
    for g in range(ndev // group):
        q = rows[g * group : (g + 1) * group, :].astype(BF16)
        off = offsets[0:1, g * group : (g + 1) * group].astype(F32)
        off = jnp.broadcast_to(off, (8, group)).astype(BF16)
        bins = jnp.dot(off, holder.astype(BF16), preferred_element_type=F32)[0:1]
        table = jnp.zeros((NB, cols), F32)
        for s in range(3):
            pick = jnp.where(lane == s * slots + col % slots, 1.0, 0.0).astype(BF16)
            spread = jnp.dot(q, pick, preferred_element_type=F32)
            line = jnp.sum(jnp.where(owner, spread, 0.0), axis=0, keepdims=True)
            table = jnp.where(time == bins + s, line, table)
        total = total + lax.dot_general(
            weight[:, g * cols : (g + 1) * cols],
            table.astype(BF16),
            (((1,), (1,)), ((), ())),
            preferred_element_type=F32,
        )
    out[...] = total


def swap_pairs(count, periodic):
    one = [(i, i ^ 1) for i in range(count)]
    two = []
    for i in range(count):
        j = i - 1 if i % 2 == 0 else i + 1
        two.append((i, j % count if periodic or 0 <= j < count else i))
    return one, two


def swap(first, second, axis, periodic):
    count = 1
    for name in (axis,) if isinstance(axis, str) else axis:
        count = count * lax.axis_size(name)
    one, two = swap_pairs(count, periodic)
    return lax.ppermute(first, axis, one), lax.ppermute(second, axis, two)


def local(density, velocity, pressure, panel_cell, obs_weight, bin_offset):
    ca, cz, cr = density.shape
    slots = panel_cell.shape[0]
    ndev = bin_offset.shape[1]
    n_ax, n_rad = lax.axis_size("y") * lax.axis_size("core"), lax.axis_size("rad")
    planes = ca + 2 * REACH
    part = functools.partial
    given = (density.reshape(ca * cz, cr), velocity.reshape(3 * ca * cz, cr), pressure.reshape(ca * cz, cr))

    edge = struct((5 * REACH * cz, cr), BF16)
    strip = struct((5 * REACH * ca, cr), BF16)
    home, ax1, ax2, az1, az2 = call(
        part(load_and_pack, ca, cz),
        (struct((5 * ca * cz, cr)), edge, edge, strip, strip),
        [HBM] * 3,
        [pltpu.SemaphoreType.DMA((3,))],
    )(*[far(x) for x in given])
    ax1, ax2 = swap(ax1, ax2, ("y", "core"), False)
    az1, az2 = swap(az1, az2, "az", True)
    grid = struct((5 * planes * ROWS, cr))
    ends = ("either",) if n_rad == 2 else ("low", "high")
    tiles = cr // SLOT
    table = [struct((tiles * cr, cr), BF16)] * len(ends) + [struct((cr, tiles * cr // 4), BF16)] * len(ends)
    block, banded, *tables = call(
        part(prepare, ends, ca, cz, n_rad),
        (grid, struct((2 * cr, 2 * cr), BF16), *table),
        [VMEM],
    )(home)
    edges, places = tables[: len(ends)], tables[len(ends) :]

    corner = struct((5 * MID * 2 * MID, cr), BF16)
    near = pltpu.VMEM((5, 2 * MID * cz, cr), F32)
    corner1, corner2 = call(part(pack_corners, n_ax, cz), (corner, corner), [VMEM] * 2, [near])(ax1, ax2)
    corner1, corner2 = swap(corner1, corner2, "az", True)

    side = struct((5 * (ca + 2 * MID) * ROWS // tiles, cr), BF16)
    got = call(
        part(assemble, n_ax, len(ends), ca, cz),
        (grid,) + tuple(side for _ in ends),
        [VMEM] * (7 + len(ends)),
        [
            pltpu.VMEM((5, 2 * REACH * cz, cr), F32),
            pltpu.VMEM((2,) + strip.shape, F32),
            pltpu.VMEM((2,) + corner.shape, F32),
        ],
        mib=12,
        alias={0: 0},
    )(block, ax1, ax2, az1, az2, corner1, corner2, *edges)
    block = got[0].reshape(5, planes, ROWS, cr)
    if n_rad == 2:
        sides = (lax.ppermute(got[1], "rad", [(0, 1), (1, 0)]),)
    else:
        up = [(i, i + 1) for i in range(n_rad - 1)]
        sides = (lax.ppermute(got[1], "rad", [(j, i) for i, j in up]), lax.ppermute(got[2], "rad", up))

    grid = (5, planes, TALL, cr)
    q, u2, u0 = call(
        part(stages, n_ax, n_rad, ca, cz, slots),
        (struct((1, 1, 128)), struct((5, ca + 4, TALL, cr)), struct((5, ca, ROWS, cr))),
        [VMEM, VMEM, HBM] + [VMEM] * (2 * len(sides)),
        [pltpu.VMEM((5, ca + 2 * MID, 8, cr), F32)]
        + [pltpu.VMEM(grid, F32) for _ in range(4)]
        + [pltpu.VMEM((3, planes, ROWS, cr), F32), pltpu.VMEM((128, cr), F32)]
        + [pltpu.SMEM((slots,), jnp.int32), pltpu.SemaphoreType.DMA],
        mib=28,
    )(block, banded, far(panel_cell), *sides, *places)

    cores, n_az = lax.axis_size("core"), lax.axis_size("az")
    other = lax.ppermute(q, "core", [(0, 1), (1, 0)])
    rows = call(pair_rows, struct((ndev // cores, cores, 128)), [VMEM] * 2, mib=2)(q, other)
    sent = rows
    rows = lax.all_to_all(rows, ("y", "az", "rad"), 0, 0, tiled=True).reshape(ndev, 128)

    grid = (5, ca + 4, TALL, cr)
    state = call(
        part(last_stage, ca, cz),
        struct((5, ca, cz, cr)),
        [VMEM] * 3 + [pl.ANY],
        [pltpu.VMEM(grid, F32), pltpu.VMEM(grid, F32)],
        mib=12,
        cost=pl.CostEstimate(flops=400_000_000, bytes_accessed=8_000_000, transcendentals=0),
    )(u2, u0, banded, sent)
    signal = call(
        part(signals, slots, cores, n_az * n_rad), struct((obs_weight.shape[0], NB)), [VMEM] * 3, mib=24
    )(rows, bin_offset, obs_weight)
    return (state, signal)


def solution(mesh):
    n_ax, n_az, n_rad = (mesh.shape[name] for name in ("ax", "az", "rad"))
    split = Mesh(mesh.devices.reshape(n_ax // 2, 2, n_az, n_rad), ("y", "core", "az", "rad"))
    ax = ("y", "core")
    every = ax + ("az", "rad")
    in_specs = (
        P(ax, "az", "rad"),
        P(None, ax, "az", "rad"),
        P(ax, "az", "rad"),
        P(every),
        P(every, None),
        P(every, None),
    )
    out_specs = (P(None, ax, "az", "rad"), P(every, None))
    return jax.shard_map(local, mesh=split, in_specs=in_specs, out_specs=out_specs, check_vma=False)
```

```python
import functools

import jax
import jax.numpy as jnp
from jax import lax
from jax.experimental import pallas as pl
from jax.experimental.pallas import tpu as pltpu
from jax.sharding import Mesh, PartitionSpec as P

NB = 128
GAMMA_M = 0.4
LAMBDA = 0.1
P_REF = 1.0
REACH = 6
MID = 4
SCALE = -LAMBDA / 12.0
ROWS = 32
OFF = 8
SPAN = 32
TALL = ROWS + 8
STEP = 4
SLOT = 8
HBM = pltpu.MemorySpace.HBM
VMEM = pltpu.MemorySpace.VMEM
SMEM = pltpu.MemorySpace.SMEM
F32 = jnp.float32
BF16 = jnp.bfloat16


def call(kernel, outs, in_spaces, scratch=(), mib=8, cost=None, alias={}):
    return pl.pallas_call(
        kernel,
        out_shape=outs,
        in_specs=[pl.BlockSpec(memory_space=s) for s in in_spaces],
        out_specs=jax.tree.map(lambda _: pl.BlockSpec(memory_space=VMEM), outs),
        scratch_shapes=list(scratch),
        compiler_params=pltpu.CompilerParams(vmem_limit_bytes=mib * 1024 * 1024),
        cost_estimate=cost,
        input_output_aliases=alias,
    )


def far(x):
    return pltpu.with_memory_space_constraint(x, HBM)


def struct(shape, dtype=F32):
    return jax.ShapeDtypeStruct(shape, dtype)


def kept(row):
    return 8 * (row % 4) + row // 4


def ax_index():
    return lax.axis_index("y") * lax.axis_size("core") + lax.axis_index("core")


def first_is_up(axis):
    return lax.axis_index("core" if axis == "ax" else axis) % 2 == 1


def load_and_pack(ca, cz, den, vel, pre, home, ax1, ax2, az1, az2, sems):
    size = ca * cz
    copies = [
        pltpu.make_async_copy(den, home.at[pl.ds(0, size)], sems.at[0]),
        pltpu.make_async_copy(vel, home.at[pl.ds(size, 3 * size)], sems.at[1]),
        pltpu.make_async_copy(pre, home.at[pl.ds(4 * size, size)], sems.at[2]),
    ]
    for copy in copies:
        copy.start()
    for copy in copies:
        copy.wait()
    up = first_is_up("ax")
    edge = REACH * cz
    for f in range(5):
        at = f * size
        low = home[at : at + edge, :]
        high = home[at + size - edge : at + size, :]
        rows = slice(f * edge, (f + 1) * edge)
        ax1[rows, :] = jnp.where(up, high, low).astype(BF16)
        ax2[rows, :] = jnp.where(up, low, high).astype(BF16)
    up = first_is_up("az")
    low, high = [], []
    for f in range(5):
        for d in range(REACH):
            low.append(home[pl.ds(f * size + d, ca, stride=cz), :])
            high.append(home[pl.ds(f * size + cz - 1 - d, ca, stride=cz), :])
    low, high = jnp.concatenate(low, axis=0), jnp.concatenate(high, axis=0)
    az1[...] = jnp.where(up, high, low).astype(BF16)
    az2[...] = jnp.where(up, low, high).astype(BF16)


def ax_sides(n_ax, got1, got2, rows):
    ax = ax_index()
    a, b = got1[rows, :].astype(F32), got2[rows, :].astype(F32)
    up = first_is_up("ax")
    lo = jnp.where(ax == 0, 0.0, jnp.where(up, b, a))
    hi = jnp.where(ax == n_ax - 1, 0.0, jnp.where(up, a, b))
    return lo, hi


def pack_corners(n_ax, cz, got1, got2, first_out, second_out, near):
    up = first_is_up("az")
    half = MID * cz
    size = REACH * cz
    for f in range(5):
        lo, hi = ax_sides(n_ax, got1, got2, slice(f * size, (f + 1) * size))
        near[f, 0:half, :] = lo[size - half :]
        near[f, half : 2 * half, :] = hi[0:half]
    low, high = [], []
    for f in range(5):
        for d in range(MID):
            low.append(near[f, pl.ds(d, 2 * MID, stride=cz), :])
            high.append(near[f, pl.ds(cz - 1 - d, 2 * MID, stride=cz), :])
    low, high = jnp.concatenate(low, axis=0), jnp.concatenate(high, axis=0)
    first_out[...] = jnp.where(up, high, low).astype(BF16)
    second_out[...] = jnp.where(up, low, high).astype(BF16)


def spread_rows(planes, cz, f, plane, ref, at, block):
    quarter = cz // 4
    for l in range(4):
        row = (f * planes + plane) * ROWS + 8 * l + OFF // 4
        block[pl.ds(row, quarter), :] = ref[pl.ds(at + l, quarter, stride=4), :]


def prepare(ends, ca, cz, n_rad, home, block, banded, *tables):
    cr = home.shape[1]
    rad = lax.axis_index("rad")
    for f in range(5):
        for k in range(ca):
            spread_rows(ca + 2 * REACH, cz, f, REACH + k, home, (f * ca + k) * cz, block)
    banded[...] = band(cr)
    edges, places = tables[: len(ends)], tables[len(ends) :]
    tiles = cr // SLOT
    there = {"high": jnp.where(rad < n_rad - 1, 1.0, 0.0), "low": jnp.where(rad > 0, 1.0, 0.0)}
    high = place_matrix(0, tiles, cr) * there["high"]
    low = place_matrix(SPAN - REACH, tiles, cr) * there["low"]
    for end, edge, place in zip(ends, edges, places):
        start = {"low": 0, "high": cr - REACH, "either": jnp.where(rad == 0, cr - REACH, 0)}[end]
        edge[...] = edge_matrix(start, tiles, cr)
        place[...] = {"low": high, "high": low, "either": high + low}[end].astype(BF16)


def edge_matrix(start, tiles, cr):
    k = lax.broadcasted_iota(jnp.int32, (tiles * cr, tiles * SLOT), 0)
    n = lax.broadcasted_iota(jnp.int32, (tiles * cr, tiles * SLOT), 1)
    hit = (k // cr == n // SLOT) & (n % SLOT < REACH) & (k % cr == n % SLOT + start)
    return jnp.where(hit, 1.0, 0.0).astype(BF16)


def place_matrix(start, tiles, cr):
    k = lax.broadcasted_iota(jnp.int32, (tiles * SLOT, tiles * cr // 4), 0)
    n = lax.broadcasted_iota(jnp.int32, (tiles * SLOT, tiles * cr // 4), 1)
    hit = (k // SLOT == n // SPAN) & (k % SLOT < REACH) & (n % SPAN == k % SLOT + start)
    return jnp.where(hit, 1.0, 0.0)


def assemble(n_ax, count, ca, cz, block_in, ax1, ax2, az1, az2, corner1, corner2, *rest):
    edges, block, outs, (sides, strips, corners) = rest[:count], rest[count], rest[count + 1 : -3], rest[-3:]
    cr = ax1.shape[1]
    planes = ca + 2 * REACH
    size = REACH * cz
    for f in range(5):
        lo, hi = ax_sides(n_ax, ax1, ax2, slice(f * size, (f + 1) * size))
        sides[f, 0:size, :] = lo
        sides[f, size : 2 * size, :] = hi
    for f in range(5):
        for k in range(REACH):
            spread_rows(planes, cz, f, k, sides.at[f], k * cz, block)
            spread_rows(planes, cz, f, REACH + ca + k, sides.at[f], size + k * cz, block)

    up = first_is_up("az")
    for one, two, into in ((az1, az2, strips), (corner1, corner2, corners)):
        a, b = one[...].astype(F32), two[...].astype(F32)
        into[0] = jnp.where(up, b, a)
        into[1] = jnp.where(up, a, b)
    for f in range(5):
        for d in range(REACH):
            for side, row in ((0, OFF - 1 - d), (1, OFF + cz + d)):
                at = kept(row) + f * planes * ROWS
                got = strips[side, pl.ds((f * REACH + d) * ca, ca), :]
                block[pl.ds(at + REACH * ROWS, ca, stride=ROWS), :] = got
                if d < MID:
                    start = (f * MID + d) * 2 * MID
                    got = corners[side, pl.ds(start, MID), :]
                    block[pl.ds(at + (REACH - MID) * ROWS, MID, stride=ROWS), :] = got
                    got = corners[side, pl.ds(start + MID, MID), :]
                    block[pl.ds(at + (REACH + ca) * ROWS, MID, stride=ROWS), :] = got

    tiles = cr // SLOT
    step = tiles * 8
    rows = []
    for f in range(5):
        for k in range((ca + 2 * MID) * ROWS // step):
            at = (f * planes + REACH - MID) * ROWS + k * step
            rows.append(jnp.concatenate([block[at + 8 * t : at + 8 * t + 8, :] for t in range(tiles)], axis=1))
    rows = jnp.concatenate(rows, axis=0).astype(BF16)
    for edge, out in zip(edges, outs):
        out[...] = jnp.dot(rows, edge[...], preferred_element_type=F32).astype(BF16)


def az_terms(flux):
    v = [flux[8 * l : 8 * l + 8] for l in range(4)]
    v = [pltpu.roll(v[2], 1, 0), pltpu.roll(v[3], 1, 0)] + v + [pltpu.roll(v[0], 7, 0), pltpu.roll(v[1], 7, 0)]
    out = [8.0 * (v[l + 3] - v[l + 1]) - (v[l + 4] - v[l]) for l in range(4)]
    side = flux[ROWS:]
    lanes = side.shape[1]
    span = lax.broadcasted_iota(jnp.int32, side.shape, 1) // SPAN
    up, down = pltpu.roll(side, 7, 0), pltpu.roll(side, 1, 0)
    up1 = pltpu.roll(jnp.where(span == 0, up, side), lanes - SPAN, 1)
    up2 = pltpu.roll(jnp.where(span < 2, up, side), lanes - 2 * SPAN, 1)
    down1 = pltpu.roll(jnp.where(span == 3, down, side), SPAN, 1)
    down2 = pltpu.roll(jnp.where(span >= 2, down, side), 2 * SPAN, 1)
    out.append(8.0 * (up1 - down1) - (up2 - down2))
    return jnp.concatenate(out, axis=0)


def band(cr):
    def place(axis, none):
        i = lax.broadcasted_iota(jnp.int32, (2 * cr, 2 * cr), axis)
        j = i % SPAN
        beyond = jnp.where(j < REACH, cr + j, jnp.where(j >= SPAN - REACH, j - SPAN, none))
        return jnp.where(i < cr, i, beyond), jnp.where(i < cr, -1, i // SPAN)

    k, k_span = place(0, 4 * cr)
    n, n_span = place(1, -4 * cr)
    gap = k - n
    out = jnp.where(gap == 1, 8.0, 0.0) + jnp.where(gap == -1, -8.0, 0.0)
    out = out + jnp.where(gap == 2, -1.0, 0.0) + jnp.where(gap == -2, 1.0, 0.0)
    apart = (k_span >= 0) & (n_span >= 0) & (k_span != n_span)
    return jnp.where(apart, 0.0, out).astype(BF16)


def split_state(u):
    rho, m0, m1, m2, energy = u
    inv = 1.0 / rho
    vel = [m0 * inv, m1 * inv, m2 * inv]
    pres = GAMMA_M * (energy - 0.5 * (m0 * vel[0] + m1 * vel[1] + m2 * vel[2]))
    return [m0, m1, m2], vel, pres, energy


def flux(d, mom, vel, pres, energy):
    parts = [mom[d]]
    for j in range(3):
        parts.append(mom[d] * vel[j] + pres if j == d else mom[d] * vel[j])
    parts.append((energy + pres) * vel[d])
    return parts


def ax_only(u, fax, j):
    got = flux(0, *u)
    for f in range(5):
        fax[f, j, 0:ROWS] = got[f]


def both_sides(us, js, fax, part, banded):
    rows = []
    shape = (ROWS, banded.shape[0] // 2)
    span = lax.broadcasted_iota(jnp.int32, shape, 1) // SPAN
    mine = span == lax.broadcasted_iota(jnp.int32, shape, 0) // 8
    for u, j in zip(us, js):
        got = flux(0, *u)
        for f in range(5):
            fax[f, j] = got[f]
        got = flux(2, *u)
        for f in range(5):
            side = jnp.where(mine, jnp.concatenate([got[f][ROWS:]] * 4, axis=0), 0.0)
            rows.append(jnp.concatenate([got[f][0:ROWS], side], axis=1))
    rows = jnp.concatenate(rows, axis=0)
    coarse = rows.astype(BF16)
    fine = (rows - coarse.astype(F32)).astype(BF16)
    matrix = banded[...]
    out = jnp.dot(coarse, matrix, preferred_element_type=F32)
    out = out + jnp.dot(fine, matrix, preferred_element_type=F32)
    half = out.shape[1] // 2
    for i, (u, j) in enumerate(zip(us, js)):
        got = flux(1, *u)
        for f in range(5):
            at = (i * 5 + f) * ROWS
            side = out[at : at + 8, half:]
            for l in range(1, 4):
                side = jnp.where(span[0:8] == l, out[at + 8 * l : at + 8 * l + 8, half:], side)
            radial = jnp.concatenate([out[at : at + ROWS, 0:half], side], axis=0)
            part[f, j] = az_terms(got[f]) + radial


def change(fa, part, f, j, size):
    near = fa(j + 1)[0:size] - fa(j - 1)[0:size]
    far = fa(j + 2)[0:size] - fa(j - 2)[0:size]
    return SCALE * (8.0 * near - far + part[f, j, 0:size])


def window(fax, f):
    held = {}

    def get(j):
        if j not in held:
            held[j] = fax[f, j]
        return held[j]

    return get


def stages(n_ax, n_rad, ca, cz, slots, block, banded, cells_far, *refs):
    sides, refs = refs[: len(refs) - 12], refs[len(refs) - 12 :]
    sides, places = sides[: len(sides) // 2], sides[len(sides) // 2 :]
    q_out, u2_out, u0_out, ghost, first, second, fax, part, value, picked, cells, cells_sem = refs
    fetch = pltpu.make_async_copy(cells_far, cells, cells_sem)
    fetch.start()
    cr = block.shape[-1]
    low, high = REACH, REACH + ca
    ax = ax_index()
    rad = lax.axis_index("rad")

    lane = lax.broadcasted_iota(jnp.int32, (8, cr), 1)
    row = 4 * lax.broadcasted_iota(jnp.int32, (8, cr), 0) + lane // SPAN
    j = lane % SPAN
    steps_rad = jnp.where(
        (j < REACH) & (rad < n_rad - 1),
        1 + j // 2,
        jnp.where((j >= SPAN - REACH) & (rad > 0), 1 + (SPAN - 1 - j) // 2, 99),
    )
    beyond_row = jnp.maximum(OFF - row, row - (OFF + cz - 1))
    steps = steps_rad + jnp.where(beyond_row > 0, (beyond_row + 1) // 2, 0)
    base0 = jnp.where(steps_rad < 99, 0.0, 1.0)

    side = 0.0
    for got, place in zip(sides, places):
        side = side + jnp.dot(got[...], place[...], preferred_element_type=F32)
    group = side.shape[1] // cr
    count = (ca + 2 * MID) // group
    for f in range(5):
        for k in range(count):
            for i in range(group):
                at = (f * count + k) * 8
                tile = side[at : at + 8, i * cr : (i + 1) * cr]
                ghost[f, k * group + i] = tile + base0 if f == 0 else tile

    def start_state(j, both):
        u = []
        for f in range(5):
            x = block[f, j]
            u.append(jnp.concatenate([x, ghost[f, j - (REACH - MID)]], axis=0) if both else x)
        rho, vel, pres = u[0], u[1:4], u[4]
        mom = [rho * x for x in vel]
        energy = pres * (1.0 / GAMMA_M) + 0.5 * (mom[0] * vel[0] + mom[1] * vel[1] + mom[2] * vel[2])
        return rho, (mom, vel, pres, energy)

    def note(s, j, u):
        value[s, j] = (u[2] - P_REF + u[0][0])[0:ROWS]

    for j in (low - 6, low - 5, high + 4, high + 5):
        ax_only(start_state(j, False)[1], fax, j)

    @pl.loop(0, (ca + 8) // STEP)
    def _(i):
        js = [low - 4 + STEP * i + k for k in range(STEP)]
        us = []
        for j in js:
            rho, u = start_state(j, True)
            for f, x in enumerate([rho] + u[0] + [u[3]]):
                first[f, j] = x
            note(0, j, u)
            us.append(u)
        both_sides(us, js, fax, part, banded)

    def update(f, j, fa, stage):
        a = max(low - j, j - (high - 1), 0)
        a = (a + 1) // 2
        lim = 2 - stage
        base = jnp.where(f == 0, 1.0, 0.0)
        size = ROWS if a == lim else TALL
        new = change(fa, part, f, j, size)
        u0 = first[f, j, 0:size]
        if stage == 0:
            new = u0 + new
        else:
            new = 0.75 * u0 + 0.25 * (second[f, j, 0:size] + new)
        beyond = (ax == 0) if j < low else (ax == n_ax - 1)
        home = new[0:ROWS]
        if a > 0:
            home = jnp.where(beyond, base, home)
        if size == ROWS:
            return home, None
        ok = steps <= lim - a
        if a > 0:
            ok = ok & jnp.logical_not(beyond)
        return home, jnp.where(ok, new[ROWS:], base)

    @pl.loop(0, 5)
    def _(f):
        fa = window(fax, f)
        for j in range(low - 4, high + 4):
            home, side = update(f, j, fa, 0)
            second[f, j, 0:ROWS] = home
            if side is not None:
                second[f, j, ROWS:] = side

    for j in (low - 4, low - 3, high + 2, high + 3):
        ax_only(split_state([second[f, j, 0:ROWS] for f in range(5)]), fax, j)

    @pl.loop(0, (ca + 4) // STEP)
    def _(i):
        js = [low - 2 + STEP * i + k for k in range(STEP)]
        us = []
        for j in js:
            u = split_state([second[f, j] for f in range(5)])
            note(1, j, u)
            us.append(u)
        both_sides(us, js, fax, part, banded)

    @pl.loop(0, 5)
    def _(f):
        fa = window(fax, f)
        for j in range(low - 2, high + 2):
            home, side = update(f, j, fa, 1)
            u2_out[f, j - (low - 2), 0:ROWS] = home
            if side is not None:
                u2_out[f, j - (low - 2), ROWS:] = side
        for j in range(low, high):
            u0_out[f, j - low] = first[f, j, 0:ROWS]

    @pl.loop(0, ca)
    def _(i):
        u = split_state([u2_out[f, i + 2, 0:ROWS] for f in range(5)])
        note(2, low + i, u)

    fetch.wait()
    picked[...] = jnp.zeros_like(picked)
    lanes = lax.broadcasted_iota(jnp.int32, (1, cr), 1)
    for p in range(slots):
        cell = cells[p]
        at = jnp.maximum(cell, 0)
        column = jnp.where(cell >= 0, lax.rem(at, cr), -1)
        at = lax.div(at, cr)
        plane = low + lax.div(at, cz)
        r = lax.rem(at, cz) + OFF
        r = 8 * lax.rem(r, 4) + lax.div(r, 4)
        hit = lanes == column
        for s in range(3):
            picked[pl.ds(s * slots + p, 1), :] = jnp.where(hit, value[s, plane, pl.ds(r, 1), :], 0.0)
    q = lax.dot_general(
        jnp.ones((8, cr), BF16),
        picked[...].astype(BF16),
        (((1,), (1,)), ((), ())),
        preferred_element_type=F32,
    )
    q_out[...] = jnp.broadcast_to(q[0:1][None], q_out.shape)


def last_stage(ca, cz, u2, u0, banded, state, fax, part):
    for j in (0, 1, ca + 2, ca + 3):
        ax_only(split_state([u2[f, j, 0:ROWS] for f in range(5)]), fax, j)

    @pl.loop(0, ca // STEP)
    def _(i):
        js = [2 + STEP * i + k for k in range(STEP)]
        us = [split_state([u2[f, j] for f in range(5)]) for j in js]
        both_sides(us, js, fax, part, banded)

    first, quarter = OFF // 4, cz // 4

    @pl.loop(0, 5)
    def _(f):
        fa = window(fax, f)
        for k in range(ca):
            j = k + 2
            new = u2[f, j, 0:ROWS] + change(fa, part, f, j, ROWS)
            new = u0[f, k] * (1.0 / 3.0) + (2.0 / 3.0) * new
            for l in range(4):
                state[f, k, pl.ds(l, quarter, stride=4), :] = new[8 * l + first : 8 * l + first + quarter]


def signals(slots, rows, offsets, weight, out):
    ndev = rows.shape[0]
    group = 32
    cols = group * slots
    lanes = rows.shape[1]
    col = lax.broadcasted_iota(jnp.int32, (1, cols), 1)
    owner = lax.broadcasted_iota(jnp.int32, (group, cols), 0) == col // slots
    lane = lax.broadcasted_iota(jnp.int32, (lanes, cols), 0)
    time = lax.broadcasted_iota(jnp.int32, (NB, cols), 0).astype(F32)
    total = jnp.zeros(out.shape, F32)
    for g in range(ndev // group):
        q = rows[g * group : (g + 1) * group, :].astype(BF16)
        off = offsets[0:1, g * group : (g + 1) * group].astype(F32)
        off = jnp.broadcast_to(off, (8, group)).astype(BF16)
        bins = jnp.dot(off, owner.astype(BF16), preferred_element_type=F32)[0:1]
        table = jnp.zeros((NB, cols), F32)
        for s in range(3):
            pick = jnp.where(lane == s * slots + col % slots, 1.0, 0.0).astype(BF16)
            spread = jnp.dot(q, pick, preferred_element_type=F32)
            line = jnp.sum(jnp.where(owner, spread, 0.0), axis=0, keepdims=True)
            table = jnp.where(time == bins + s, line, table)
        total = total + lax.dot_general(
            weight[:, g * cols : (g + 1) * cols],
            table.astype(BF16),
            (((1,), (1,)), ((), ())),
            preferred_element_type=F32,
        )
    out[...] = total


def swap_pairs(count, periodic):
    one = []
    for i in range(count):
        j = i - 1 if i % 2 == 0 else i + 1
        one.append((i, j % count if periodic or 0 <= j < count else i))
    return one, [(i, i ^ 1) for i in range(count)]


def swap(first, second, axis, periodic):
    count = 1
    for name in (axis,) if isinstance(axis, str) else axis:
        count = count * lax.axis_size(name)
    one, two = swap_pairs(count, periodic)
    return lax.ppermute(first, axis, one), lax.ppermute(second, axis, two)


def local(density, velocity, pressure, panel_cell, obs_weight, bin_offset):
    ca, cz, cr = density.shape
    slots = panel_cell.shape[0]
    ndev = bin_offset.shape[1]
    n_ax, n_rad = lax.axis_size("y") * lax.axis_size("core"), lax.axis_size("rad")
    planes = ca + 2 * REACH
    part = functools.partial
    given = (density.reshape(ca * cz, cr), velocity.reshape(3 * ca * cz, cr), pressure.reshape(ca * cz, cr))

    edge = struct((5 * REACH * cz, cr), BF16)
    strip = struct((5 * REACH * ca, cr), BF16)
    home, ax1, ax2, az1, az2 = call(
        part(load_and_pack, ca, cz),
        (struct((5 * ca * cz, cr)), edge, edge, strip, strip),
        [HBM] * 3,
        [pltpu.SemaphoreType.DMA((3,))],
    )(*[far(x) for x in given])
    ax1, ax2 = swap(ax1, ax2, ("y", "core"), False)
    az1, az2 = swap(az1, az2, "az", True)
    grid = struct((5 * planes * ROWS, cr))
    ends = ("either",) if n_rad == 2 else ("low", "high")
    tiles = cr // SLOT
    table = [struct((tiles * cr, cr), BF16)] * len(ends) + [struct((cr, tiles * cr // 4), BF16)] * len(ends)
    block, banded, *tables = call(
        part(prepare, ends, ca, cz, n_rad),
        (grid, struct((2 * cr, 2 * cr), BF16), *table),
        [VMEM],
    )(home)
    edges, places = tables[: len(ends)], tables[len(ends) :]

    corner = struct((5 * MID * 2 * MID, cr), BF16)
    near = pltpu.VMEM((5, 2 * MID * cz, cr), F32)
    corner1, corner2 = call(part(pack_corners, n_ax, cz), (corner, corner), [VMEM] * 2, [near])(ax1, ax2)
    corner1, corner2 = swap(corner1, corner2, "az", True)

    side = struct((5 * (ca + 2 * MID) * ROWS // tiles, cr), BF16)
    got = call(
        part(assemble, n_ax, len(ends), ca, cz),
        (grid,) + tuple(side for _ in ends),
        [VMEM] * (7 + len(ends)),
        [
            pltpu.VMEM((5, 2 * REACH * cz, cr), F32),
            pltpu.VMEM((2,) + strip.shape, F32),
            pltpu.VMEM((2,) + corner.shape, F32),
        ],
        mib=12,
        alias={0: 0},
    )(block, ax1, ax2, az1, az2, corner1, corner2, *edges)
    block = got[0].reshape(5, planes, ROWS, cr)
    if n_rad == 2:
        sides = (lax.ppermute(got[1], "rad", [(0, 1), (1, 0)]),)
    else:
        up = [(i, i + 1) for i in range(n_rad - 1)]
        sides = (lax.ppermute(got[1], "rad", [(j, i) for i, j in up]), lax.ppermute(got[2], "rad", up))

    grid = (5, planes, TALL, cr)
    q, u2, u0 = call(
        part(stages, n_ax, n_rad, ca, cz, slots),
        (struct((ndev, 1, 128)), struct((5, ca + 4, TALL, cr)), struct((5, ca, ROWS, cr))),
        [VMEM, VMEM, HBM] + [VMEM] * (2 * len(sides)),
        [pltpu.VMEM((5, ca + 2 * MID, 8, cr), F32)]
        + [pltpu.VMEM(grid, F32) for _ in range(4)]
        + [pltpu.VMEM((3, planes, ROWS, cr), F32), pltpu.VMEM((128, cr), F32)]
        + [pltpu.SMEM((slots,), jnp.int32), pltpu.SemaphoreType.DMA],
        mib=28,
    )(block, banded, far(panel_cell), *sides, *places)

    rows = lax.all_to_all(q, ("y", "core", "az", "rad"), 0, 0, tiled=True).reshape(ndev, 128)

    grid = (5, ca + 4, TALL, cr)
    state = call(
        part(last_stage, ca, cz),
        struct((5, ca, cz, cr)),
        [VMEM] * 3,
        [pltpu.VMEM(grid, F32), pltpu.VMEM(grid, F32)],
        mib=12,
        cost=pl.CostEstimate(flops=400_000_000, bytes_accessed=8_000_000, transcendentals=0),
    )(u2, u0, banded)
    signal = call(
        part(signals, slots), struct((obs_weight.shape[0], NB)), [VMEM] * 3, mib=24
    )(rows, bin_offset, obs_weight)
    return (state, signal)


def solution(mesh):
    n_ax, n_az, n_rad = (mesh.shape[name] for name in ("ax", "az", "rad"))
    split = Mesh(mesh.devices.reshape(n_ax // 2, 2, n_az, n_rad), ("y", "core", "az", "rad"))
    ax = ("y", "core")
    every = ax + ("az", "rad")
    in_specs = (
        P(ax, "az", "rad"),
        P(None, ax, "az", "rad"),
        P(ax, "az", "rad"),
        P(every),
        P(every, None),
        P(every, None),
    )
    out_specs = (P(None, ax, "az", "rad"), P(every, None))
    return jax.shard_map(local, mesh=split, in_specs=in_specs, out_specs=out_specs, check_vma=False)
```

```python
import functools

import jax
import jax.numpy as jnp
from jax import lax
from jax.experimental import pallas as pl
from jax.experimental.pallas import tpu as pltpu
from jax.sharding import Mesh, PartitionSpec as P

NB = 128
GAMMA_M = 0.4
LAMBDA = 0.1
P_REF = 1.0
REACH = 4
MID = 2
SCALE = -LAMBDA / 12.0
ROWS = 32
OFF = 8
SPAN = 32
TALL = ROWS + 8
STEP = 4
SLOT = 8
HBM = pltpu.MemorySpace.HBM
VMEM = pltpu.MemorySpace.VMEM
SMEM = pltpu.MemorySpace.SMEM
F32 = jnp.float32
BF16 = jnp.bfloat16


def call(kernel, outs, in_spaces, scratch=(), mib=8, cost=None, alias={}):
    return pl.pallas_call(
        kernel,
        out_shape=outs,
        in_specs=[pl.BlockSpec(memory_space=s) for s in in_spaces],
        out_specs=jax.tree.map(lambda _: pl.BlockSpec(memory_space=VMEM), outs),
        scratch_shapes=list(scratch),
        compiler_params=pltpu.CompilerParams(vmem_limit_bytes=mib * 1024 * 1024),
        cost_estimate=cost,
        input_output_aliases=alias,
    )


def far(x):
    return pltpu.with_memory_space_constraint(x, HBM)


def struct(shape, dtype=F32):
    return jax.ShapeDtypeStruct(shape, dtype)


def kept(row):
    return 8 * (row % 4) + row // 4


def ax_index():
    return lax.axis_index("y") * lax.axis_size("core") + lax.axis_index("core")


def first_is_up(axis):
    return lax.axis_index("core" if axis == "ax" else axis) % 2 == 0


def load_and_pack(ca, cz, den, vel, pre, home, ax1, ax2, az1, az2, sems):
    size = ca * cz
    copies = [
        pltpu.make_async_copy(den, home.at[pl.ds(0, size)], sems.at[0]),
        pltpu.make_async_copy(vel, home.at[pl.ds(size, 3 * size)], sems.at[1]),
        pltpu.make_async_copy(pre, home.at[pl.ds(4 * size, size)], sems.at[2]),
    ]
    for copy in copies:
        copy.start()
    for copy in copies:
        copy.wait()
    up = first_is_up("ax")
    edge = REACH * cz
    for f in range(5):
        at = f * size
        low = home[at : at + edge, :]
        high = home[at + size - edge : at + size, :]
        rows = slice(f * edge, (f + 1) * edge)
        ax1[rows, :] = jnp.where(up, high, low).astype(BF16)
        ax2[rows, :] = jnp.where(up, low, high).astype(BF16)
    up = first_is_up("az")
    low, high = [], []
    for f in range(5):
        for d in range(REACH):
            low.append(home[pl.ds(f * size + d, ca, stride=cz), :])
            high.append(home[pl.ds(f * size + cz - 1 - d, ca, stride=cz), :])
    low, high = jnp.concatenate(low, axis=0), jnp.concatenate(high, axis=0)
    az1[...] = jnp.where(up, high, low).astype(BF16)
    az2[...] = jnp.where(up, low, high).astype(BF16)


def ax_sides(n_ax, got1, got2, rows):
    ax = ax_index()
    a, b = got1[rows, :].astype(F32), got2[rows, :].astype(F32)
    up = first_is_up("ax")
    lo = jnp.where(ax == 0, 0.0, jnp.where(up, b, a))
    hi = jnp.where(ax == n_ax - 1, 0.0, jnp.where(up, a, b))
    return lo, hi


def pack_corners(n_ax, cz, got1, got2, first_out, second_out, near, strips):
    up = first_is_up("az")
    half = MID * cz
    size = REACH * cz
    for f in range(5):
        lo, hi = ax_sides(n_ax, got1, got2, slice(f * size, (f + 1) * size))
        near[f, 0:half, :] = lo[size - half :]
        near[f, half : 2 * half, :] = hi[0:half]
    strips[...] = jnp.zeros_like(strips)
    for f in range(5):
        for d in range(MID):
            at = (f * MID + d) * 2 * MID
            strips[0, at : at + 2 * MID, :] = near[f, pl.ds(d, 2 * MID, stride=cz), :]
            strips[1, at : at + 2 * MID, :] = near[f, pl.ds(cz - 1 - d, 2 * MID, stride=cz), :]
    low, high = strips[0], strips[1]
    first_out[...] = jnp.where(up, high, low).astype(BF16)
    second_out[...] = jnp.where(up, low, high).astype(BF16)


def spread_rows(planes, cz, f, plane, ref, at, block):
    quarter = cz // 4
    for l in range(4):
        row = (f * planes + plane) * ROWS + 8 * l + OFF // 4
        block[pl.ds(row, quarter), :] = ref[pl.ds(at + l, quarter, stride=4), :]


def prepare(ends, ca, cz, n_rad, home, block, banded, *tables):
    cr = home.shape[1]
    rad = lax.axis_index("rad")
    block[...] = jnp.zeros_like(block)
    for f in range(5):
        for k in range(ca):
            spread_rows(ca + 2 * REACH, cz, f, REACH + k, home, (f * ca + k) * cz, block)
    banded[...] = band(cr)
    edges, places = tables[: len(ends)], tables[len(ends) :]
    tiles = cr // SLOT
    there = {"high": jnp.where(rad < n_rad - 1, 1.0, 0.0), "low": jnp.where(rad > 0, 1.0, 0.0)}
    high = place_matrix(0, tiles, cr) * there["high"]
    low = place_matrix(SPAN - REACH, tiles, cr) * there["low"]
    for end, edge, place in zip(ends, edges, places):
        start = {"low": 0, "high": cr - REACH, "either": jnp.where(rad == 0, cr - REACH, 0)}[end]
        edge[...] = edge_matrix(start, tiles, cr)
        place[...] = {"low": high, "high": low, "either": high + low}[end].astype(BF16)


def edge_matrix(start, tiles, cr):
    k = lax.broadcasted_iota(jnp.int32, (tiles * cr, tiles * SLOT), 0)
    n = lax.broadcasted_iota(jnp.int32, (tiles * cr, tiles * SLOT), 1)
    hit = (k // cr == n // SLOT) & (n % SLOT < REACH) & (k % cr == n % SLOT + start)
    return jnp.where(hit, 1.0, 0.0).astype(BF16)


def place_matrix(start, tiles, cr):
    k = lax.broadcasted_iota(jnp.int32, (tiles * SLOT, tiles * cr // 4), 0)
    n = lax.broadcasted_iota(jnp.int32, (tiles * SLOT, tiles * cr // 4), 1)
    hit = (k // SLOT == n // SPAN) & (k % SLOT < REACH) & (n % SPAN == k % SLOT + start)
    return jnp.where(hit, 1.0, 0.0)


def assemble(n_ax, count, ca, cz, block_in, ax1, ax2, az1, az2, corner1, corner2, *rest):
    edges, block, outs, (sides, strips, corners) = rest[:count], rest[count], rest[count + 1 : -3], rest[-3:]
    cr = ax1.shape[1]
    planes = ca + 2 * REACH
    size = REACH * cz
    for f in range(5):
        lo, hi = ax_sides(n_ax, ax1, ax2, slice(f * size, (f + 1) * size))
        sides[f, 0:size, :] = lo
        sides[f, size : 2 * size, :] = hi
    for f in range(5):
        for k in range(REACH):
            spread_rows(planes, cz, f, k, sides.at[f], k * cz, block)
            spread_rows(planes, cz, f, REACH + ca + k, sides.at[f], size + k * cz, block)

    up = first_is_up("az")
    for one, two, into in ((az1, az2, strips), (corner1, corner2, corners)):
        a, b = one[...].astype(F32), two[...].astype(F32)
        into[0] = jnp.where(up, b, a)
        into[1] = jnp.where(up, a, b)
    for f in range(5):
        for d in range(REACH):
            for side, row in ((0, OFF - 1 - d), (1, OFF + cz + d)):
                at = kept(row) + f * planes * ROWS
                got = strips[side, pl.ds((f * REACH + d) * ca, ca), :]
                block[pl.ds(at + REACH * ROWS, ca, stride=ROWS), :] = got
                if d < MID:
                    start = (f * MID + d) * 2 * MID
                    got = corners[side, pl.ds(start, MID), :]
                    block[pl.ds(at + (REACH - MID) * ROWS, MID, stride=ROWS), :] = got
                    got = corners[side, pl.ds(start + MID, MID), :]
                    block[pl.ds(at + (REACH + ca) * ROWS, MID, stride=ROWS), :] = got

    starts = [(f * planes + REACH - MID) * ROWS for f in range(5)]
    send_edges(block, starts, (ca + 2 * MID) * ROWS, edges, outs)


def send_edges(ref, starts, count, edges, outs):
    tiles = ref.shape[1] // SLOT
    step = tiles * 8
    rows = []
    for start in starts:
        for at in range(start, start + count, step):
            rows.append(jnp.concatenate([ref[at + 8 * t : at + 8 * t + 8, :] for t in range(tiles)], axis=1))
    rows += [jnp.zeros_like(rows[0])] * (outs[0].shape[0] // 8 - len(rows))
    rows = jnp.concatenate(rows, axis=0).astype(BF16)
    for edge, out in zip(edges, outs):
        out[...] = jnp.dot(rows, edge[...], preferred_element_type=F32).astype(BF16)


def az_terms(flux):
    v = [flux[8 * l : 8 * l + 8] for l in range(4)]
    v = [pltpu.roll(v[2], 1, 0), pltpu.roll(v[3], 1, 0)] + v + [pltpu.roll(v[0], 7, 0), pltpu.roll(v[1], 7, 0)]
    out = [8.0 * (v[l + 3] - v[l + 1]) - (v[l + 4] - v[l]) for l in range(4)]
    if flux.shape[0] == ROWS:
        return jnp.concatenate(out, axis=0)
    side = flux[ROWS:]
    lanes = side.shape[1]
    span = lax.broadcasted_iota(jnp.int32, side.shape, 1) // SPAN
    up, down = pltpu.roll(side, 7, 0), pltpu.roll(side, 1, 0)
    up1 = pltpu.roll(jnp.where(span == 0, up, side), lanes - SPAN, 1)
    up2 = pltpu.roll(jnp.where(span < 2, up, side), lanes - 2 * SPAN, 1)
    down1 = pltpu.roll(jnp.where(span == 3, down, side), SPAN, 1)
    down2 = pltpu.roll(jnp.where(span >= 2, down, side), 2 * SPAN, 1)
    out.append(8.0 * (up1 - down1) - (up2 - down2))
    return jnp.concatenate(out, axis=0)


def band(cr):
    def place(axis, none):
        i = lax.broadcasted_iota(jnp.int32, (2 * cr, 2 * cr), axis)
        j = i % SPAN
        beyond = jnp.where(j < REACH, cr + j, jnp.where(j >= SPAN - REACH, j - SPAN, none))
        return jnp.where(i < cr, i, beyond), jnp.where(i < cr, -1, i // SPAN)

    k, k_span = place(0, 4 * cr)
    n, n_span = place(1, -4 * cr)
    gap = k - n
    out = jnp.where(gap == 1, 8.0, 0.0) + jnp.where(gap == -1, -8.0, 0.0)
    out = out + jnp.where(gap == 2, -1.0, 0.0) + jnp.where(gap == -2, 1.0, 0.0)
    apart = (k_span >= 0) & (n_span >= 0) & (k_span != n_span)
    return jnp.where(apart, 0.0, out).astype(BF16)


def split_state(u):
    rho, m0, m1, m2, energy = u
    inv = 1.0 / rho
    vel = [m0 * inv, m1 * inv, m2 * inv]
    pres = GAMMA_M * (energy - 0.5 * (m0 * vel[0] + m1 * vel[1] + m2 * vel[2]))
    return [m0, m1, m2], vel, pres, energy


def flux(d, mom, vel, pres, energy):
    parts = [mom[d]]
    for j in range(3):
        parts.append(mom[d] * vel[j] + pres if j == d else mom[d] * vel[j])
    parts.append((energy + pres) * vel[d])
    return parts


def ax_only(u, fax, j):
    got = flux(0, *u)
    for f in range(5):
        fax[f, j, 0:ROWS] = got[f]


def radial_terms(homes, sides, banded):
    shape = homes[0].shape
    span = lax.broadcasted_iota(jnp.int32, shape, 1) // SPAN
    mine = span == lax.broadcasted_iota(jnp.int32, shape, 0) // 8
    rows = []
    for home, side in zip(homes, sides):
        side = jnp.where(mine, jnp.concatenate([side] * 4, axis=0), 0.0)
        rows.append(jnp.concatenate([home, side], axis=1))
    rows = jnp.concatenate(rows, axis=0)
    coarse = rows.astype(BF16)
    fine = (rows - coarse.astype(F32)).astype(BF16)
    matrix = banded[...]
    out = jnp.dot(coarse, matrix, preferred_element_type=F32)
    out = out + jnp.dot(fine, matrix, preferred_element_type=F32)
    got = []
    for i in range(len(homes)):
        at, half = i * ROWS, shape[1]
        side = out[at : at + 8, half:]
        for l in range(1, 4):
            side = jnp.where(span[0:8] == l, out[at + 8 * l : at + 8 * l + 8, half:], side)
        got.append((out[at : at + ROWS, 0:half], side))
    return got


def both_sides(us, js, fax, part, banded, height=TALL):
    homes, sides = [], []
    for u, j in zip(us, js):
        got = flux(0, *u)
        for f in range(5):
            fax[f, j, 0:height] = got[f][0:height]
        for x in flux(2, *u):
            homes.append(x[0:ROWS])
            sides.append(x[ROWS:])
    radial = radial_terms(homes, sides, banded)
    for i, (u, j) in enumerate(zip(us, js)):
        got = flux(1, *u)
        for f in range(5):
            home, side = radial[i * 5 + f]
            if height > ROWS:
                home = jnp.concatenate([home, side], axis=0)
            part[f, j, 0:height] = az_terms(got[f][0:height]) + home


def change(fa, part, f, j, size):
    near = fa(j + 1)[0:size] - fa(j - 1)[0:size]
    far = fa(j + 2)[0:size] - fa(j - 2)[0:size]
    return SCALE * (8.0 * near - far + part[f, j, 0:size])


def window(fax, f):
    held = {}

    def get(j):
        if j not in held:
            held[j] = fax[f, j]
        return held[j]

    return get


def stages(n_ax, n_rad, ca, cz, slots, block, banded, cells_far, *refs):
    sides, refs = refs[: len(refs) - 12], refs[len(refs) - 12 :]
    sides, places = sides[: len(sides) // 2], sides[len(sides) // 2 :]
    q_out, u2_out, u0_out, ghost, first, second, fax, part, value, picked, cells, cells_sem = refs
    fetch = pltpu.make_async_copy(cells_far, cells, cells_sem)
    fetch.start()
    cr = block.shape[-1]
    low, high = REACH, REACH + ca
    ax = ax_index()
    rad = lax.axis_index("rad")

    lane = lax.broadcasted_iota(jnp.int32, (8, cr), 1)
    row = 4 * lax.broadcasted_iota(jnp.int32, (8, cr), 0) + lane // SPAN
    j = lane % SPAN
    steps_rad = jnp.where(
        (j < REACH) & (rad < n_rad - 1),
        1 + j // 2,
        jnp.where((j >= SPAN - REACH) & (rad > 0), 1 + (SPAN - 1 - j) // 2, 99),
    )
    beyond_row = jnp.maximum(OFF - row, row - (OFF + cz - 1))
    steps = steps_rad + jnp.where(beyond_row > 0, (beyond_row + 1) // 2, 0)
    base0 = jnp.where(steps_rad < 99, 0.0, 1.0)

    side = 0.0
    for got, place in zip(sides, places):
        side = side + jnp.dot(got[...], place[...], preferred_element_type=F32)
    group = side.shape[1] // cr
    count = (ca + 2 * MID) // group
    for f in range(5):
        for k in range(count):
            for i in range(group):
                at = (f * count + k) * 8
                tile = side[at : at + 8, i * cr : (i + 1) * cr]
                ghost[f, k * group + i] = tile + base0 if f == 0 else tile

    def start_state(j, both):
        u = []
        for f in range(5):
            x = block[f, j]
            u.append(jnp.concatenate([x, ghost[f, j - (REACH - MID)]], axis=0) if both else x)
        rho, vel, pres = u[0], u[1:4], u[4]
        mom = [rho * x for x in vel]
        energy = pres * (1.0 / GAMMA_M) + 0.5 * (mom[0] * vel[0] + mom[1] * vel[1] + mom[2] * vel[2])
        return rho, (mom, vel, pres, energy)

    def note(s, j, u):
        value[s, j] = (u[2] - P_REF + u[0][0])[0:ROWS]

    for j in (low - 4, low - 3, high + 2, high + 3):
        ax_only(start_state(j, False)[1], fax, j)

    @pl.loop(0, (ca + 4) // STEP)
    def _(i):
        js = [low - 2 + STEP * i + k for k in range(STEP)]
        us = []
        for j in js:
            rho, u = start_state(j, True)
            for f, x in enumerate([rho] + u[0] + [u[3]]):
                first[f, j] = x
            note(0, j, u)
            us.append(u)
        both_sides(us, js, fax, part, banded)

    def update(f, j, fa, stage):
        a = max(low - j, j - (high - 1), 0)
        a = (a + 1) // 2
        lim = 1 - stage
        base = jnp.where(f == 0, 1.0, 0.0)
        size = ROWS if a == lim else TALL
        new = change(fa, part, f, j, size)
        u0 = first[f, j, 0:size]
        if stage == 0:
            new = u0 + new
        else:
            new = 0.75 * u0 + 0.25 * (second[f, j, 0:size] + new)
        beyond = (ax == 0) if j < low else (ax == n_ax - 1)
        home = new[0:ROWS]
        if a > 0:
            home = jnp.where(beyond, base, home)
        if size == ROWS:
            return home, None
        ok = steps <= lim - a
        if a > 0:
            ok = ok & jnp.logical_not(beyond)
        return home, jnp.where(ok, new[ROWS:], base)

    @pl.loop(0, 5)
    def _(f):
        fa = window(fax, f)
        for j in range(low - 2, high + 2):
            home, side = update(f, j, fa, 0)
            second[f, j, 0:ROWS] = home
            if side is not None:
                second[f, j, ROWS:] = side

    for j in (low - 2, low - 1, high, high + 1):
        ax_only(split_state([second[f, j, 0:ROWS] for f in range(5)]), fax, j)

    @pl.loop(0, ca // STEP)
    def _(i):
        js = [low + STEP * i + k for k in range(STEP)]
        us = []
        for j in js:
            u = split_state([second[f, j] for f in range(5)])
            note(1, j, u)
            us.append(u)
        both_sides(us, js, fax, part, banded, ROWS)

    @pl.loop(0, 5)
    def _(f):
        fa = window(fax, f)
        for j in range(low, high):
            u2_out[f, j - low] = update(f, j, fa, 1)[0]
            u0_out[f, j - low] = first[f, j, 0:ROWS]

    @pl.loop(0, ca)
    def _(i):
        note(2, low + i, split_state([u2_out[f, i] for f in range(5)]))

    fetch.wait()
    picked[...] = jnp.zeros_like(picked)
    lanes = lax.broadcasted_iota(jnp.int32, (1, cr), 1)
    for p in range(slots):
        cell = cells[p]
        at = jnp.maximum(cell, 0)
        column = jnp.where(cell >= 0, lax.rem(at, cr), -1)
        at = lax.div(at, cr)
        plane = low + lax.div(at, cz)
        r = lax.rem(at, cz) + OFF
        r = 8 * lax.rem(r, 4) + lax.div(r, 4)
        hit = lanes == column
        for s in range(3):
            picked[pl.ds(s * slots + p, 1), :] = jnp.where(hit, value[s, plane, pl.ds(r, 1), :], 0.0)
    q = lax.dot_general(
        jnp.ones((8, cr), BF16),
        picked[...].astype(BF16),
        (((1,), (1,)), ((), ())),
        preferred_element_type=F32,
    )
    q_out[...] = jnp.broadcast_to(q[0:1][None], q_out.shape)


def edge_fluxes(count, ca, cz, u2, *refs):
    edges, (ax1, ax2, az1, az2), rads = refs[:count], refs[count : count + 4], refs[count + 4 : 2 * count + 4]
    fax, faz, frad, strips = refs[2 * count + 4 :]
    cr = u2.shape[-1]
    first, quarter = OFF // 4, cz // 4

    @pl.loop(0, ca)
    def _(k):
        u = split_state([u2[f, k] for f in range(5)])
        for d, ref in ((0, fax), (1, faz), (2, frad)):
            for f, x in enumerate(flux(d, *u)):
                ref[pl.ds(pl.multiple_of((f * ca + k) * ROWS, ROWS), ROWS), :] = x

    for f in range(5):
        for d in range(MID):
            for side, k in ((0, d), (1, ca - MID + d)):
                for l in range(4):
                    row = (f * ca + k) * ROWS + 8 * l + first
                    at = ((f * MID + d) * 4 + l) * quarter
                    strips[side, at : at + quarter, :] = fax[row : row + quarter, :]
    up = first_is_up("ax")
    ax1[...] = jnp.where(up, strips[1], strips[0]).astype(BF16)
    ax2[...] = jnp.where(up, strips[0], strips[1]).astype(BF16)
    low, high = [], []
    for f in range(5):
        for d in range(MID):
            low.append(faz[pl.ds(f * ca * ROWS + kept(OFF + d), ca, stride=ROWS), :])
            high.append(faz[pl.ds(f * ca * ROWS + kept(OFF + cz - 1 - d), ca, stride=ROWS), :])
    low, high = jnp.concatenate(low, axis=0), jnp.concatenate(high, axis=0)
    up = first_is_up("az")
    az1[...] = jnp.where(up, high, low).astype(BF16)
    az2[...] = jnp.where(up, low, high).astype(BF16)
    send_edges(frad, [f * ca * ROWS for f in range(5)], ca * ROWS, edges, rads)


def last_stage(n_ax, count, ca, cz, faz_in, u2, u0, fax, frad, banded, ax1, ax2, az1, az2, *refs):
    rads, places = refs[:count], refs[count : 2 * count]
    faz, state, part, beyond, strips, sides = refs[2 * count :]
    cr = u2.shape[-1]
    first, quarter = OFF // 4, cz // 4

    lo, hi = ax_sides(n_ax, ax1, ax2, slice(0, ax1.shape[0]))
    strips[0, 0 : lo.shape[0], :] = lo
    strips[1, 0 : hi.shape[0], :] = hi
    for f in range(5):
        for d in range(MID):
            for side in range(2):
                for l in range(4):
                    at = ((f * MID + d) * 4 + l) * quarter
                    row = 8 * l + first
                    beyond[f, side * MID + d, row : row + quarter] = strips[side, at : at + quarter, :]
    up = first_is_up("az")
    a, b = az1[...].astype(F32), az2[...].astype(F32)
    strips[0, 0 : a.shape[0], :] = jnp.where(up, b, a)
    strips[1, 0 : a.shape[0], :] = jnp.where(up, a, b)
    for f in range(5):
        for d in range(MID):
            for side, row in ((0, OFF - 1 - d), (1, OFF + cz + d)):
                got = strips[side, pl.ds((f * MID + d) * ca, ca), :]
                faz[pl.ds(f * ca * ROWS + kept(row), ca, stride=ROWS), :] = got
    packed = 0.0
    for got, place in zip(rads, places):
        packed = packed + jnp.dot(got[...], place[...], preferred_element_type=F32)
    group = packed.shape[1] // cr
    for f in range(5):
        for k in range(ca):
            at = (f * (ca // group) + k // group) * 8
            sides[f, k] = packed[at : at + 8, k % group * cr : (k % group + 1) * cr]

    @pl.loop(0, ca // STEP)
    def _(i):
        ks = [STEP * i + k for k in range(STEP)]

        def plane(ref, f, k):
            return ref[pl.ds(pl.multiple_of((f * ca + k) * ROWS, ROWS), ROWS), :]

        radial = radial_terms(
            [plane(frad, f, k) for k in ks for f in range(5)],
            [sides[f, k] for k in ks for f in range(5)],
            banded,
        )
        for n, k in enumerate(ks):
            for f in range(5):
                part[f, k] = az_terms(plane(faz, f, k)) + radial[n * 5 + f][0]

    @pl.loop(0, 5)
    def _(f):
        def plane(k):
            if k < 0:
                return beyond[f, MID + k]
            if k >= ca:
                return beyond[f, MID + k - ca]
            return fax[pl.ds(pl.multiple_of((f * ca + k) * ROWS, ROWS), ROWS), :]

        held = {k: plane(k) for k in range(-MID, ca + MID)}
        for k in range(ca):
            new = u2[f, k] + change(held.get, part, f, k, ROWS)
            new = u0[f, k] * (1.0 / 3.0) + (2.0 / 3.0) * new
            for l in range(4):
                state[f, k, pl.ds(l, quarter, stride=4), :] = new[8 * l + first : 8 * l + first + quarter]


def signals(slots, rows, offsets, weight, out):
    ndev = rows.shape[0]
    group = 32
    cols = group * slots
    lanes = rows.shape[1]
    col = lax.broadcasted_iota(jnp.int32, (1, cols), 1)
    owner = lax.broadcasted_iota(jnp.int32, (group, cols), 0) == col // slots
    lane = lax.broadcasted_iota(jnp.int32, (lanes, cols), 0)
    time = lax.broadcasted_iota(jnp.int32, (NB, cols), 0).astype(F32)
    total = jnp.zeros(out.shape, F32)
    for g in range(ndev // group):
        q = rows[g * group : (g + 1) * group, :].astype(BF16)
        off = offsets[0:1, g * group : (g + 1) * group].astype(F32)
        off = jnp.broadcast_to(off, (8, group)).astype(BF16)
        bins = jnp.dot(off, owner.astype(BF16), preferred_element_type=F32)[0:1]
        table = jnp.zeros((NB, cols), F32)
        for s in range(3):
            pick = jnp.where(lane == s * slots + col % slots, 1.0, 0.0).astype(BF16)
            spread = jnp.dot(q, pick, preferred_element_type=F32)
            line = jnp.sum(jnp.where(owner, spread, 0.0), axis=0, keepdims=True)
            table = jnp.where(time == bins + s, line, table)
        total = total + lax.dot_general(
            weight[:, g * cols : (g + 1) * cols],
            table.astype(BF16),
            (((1,), (1,)), ((), ())),
            preferred_element_type=F32,
        )
    out[...] = total


def swap_pairs(count, periodic):
    one = [(i, i ^ 1) for i in range(count)]
    two = []
    for i in range(count):
        j = i - 1 if i % 2 == 0 else i + 1
        two.append((i, j % count if periodic or 0 <= j < count else i))
    return one, two


def swap(first, second, axis, periodic):
    count = 1
    for name in (axis,) if isinstance(axis, str) else axis:
        count = count * lax.axis_size(name)
    one, two = swap_pairs(count, periodic)
    return lax.ppermute(first, axis, one), lax.ppermute(second, axis, two)


def radial_exchange(messages):
    n_rad = lax.axis_size("rad")
    if n_rad == 2:
        return (lax.ppermute(messages[0], "rad", [(0, 1), (1, 0)]),)
    up = [(i, i + 1) for i in range(n_rad - 1)]
    down = [(j, i) for i, j in up]
    return (lax.ppermute(messages[0], "rad", down), lax.ppermute(messages[1], "rad", up))


def local(density, velocity, pressure, panel_cell, obs_weight, bin_offset):
    ca, cz, cr = density.shape
    slots = panel_cell.shape[0]
    ndev = bin_offset.shape[1]
    n_ax, n_rad = lax.axis_size("y") * lax.axis_size("core"), lax.axis_size("rad")
    planes = ca + 2 * REACH
    part = functools.partial
    given = (density.reshape(ca * cz, cr), velocity.reshape(3 * ca * cz, cr), pressure.reshape(ca * cz, cr))

    edge = struct((5 * REACH * cz, cr), BF16)
    strip = struct((5 * REACH * ca, cr), BF16)
    home, ax1, ax2, az1, az2 = call(
        part(load_and_pack, ca, cz),
        (struct((5 * ca * cz, cr)), edge, edge, strip, strip),
        [HBM] * 3,
        [pltpu.SemaphoreType.DMA((3,))],
    )(*[far(x) for x in given])
    ax1, ax2 = swap(ax1, ax2, ("y", "core"), False)
    az1, az2 = swap(az1, az2, "az", True)
    grid = struct((5 * planes * ROWS, cr))
    ends = ("either",) if n_rad == 2 else ("low", "high")
    tiles = cr // SLOT
    table = [struct((tiles * cr, cr), BF16)] * len(ends) + [struct((cr, tiles * cr // 4), BF16)] * len(ends)
    block, banded, *tables = call(
        part(prepare, ends, ca, cz, n_rad),
        (grid, struct((2 * cr, 2 * cr), BF16), *table),
        [VMEM],
    )(home)
    edges, places = tables[: len(ends)], tables[len(ends) :]

    corner = struct((-(-5 * MID * 2 * MID // 16) * 16, cr), BF16)
    near = pltpu.VMEM((5, 2 * MID * cz, cr), F32)
    corner1, corner2 = call(
        part(pack_corners, n_ax, cz),
        (corner, corner),
        [VMEM] * 2,
        [near, pltpu.VMEM((2,) + corner.shape, F32)],
    )(ax1, ax2)
    corner1, corner2 = swap(corner1, corner2, "az", True)

    side = struct((-(-5 * (ca + 2 * MID) * ROWS // tiles // 16) * 16, cr), BF16)
    got = call(
        part(assemble, n_ax, len(ends), ca, cz),
        (grid,) + tuple(side for _ in ends),
        [VMEM] * (7 + len(ends)),
        [
            pltpu.VMEM((5, 2 * REACH * cz, cr), F32),
            pltpu.VMEM((2,) + strip.shape, F32),
            pltpu.VMEM((2,) + corner.shape, F32),
        ],
        mib=12,
        alias={0: 0},
    )(block, ax1, ax2, az1, az2, corner1, corner2, *edges)
    block = got[0].reshape(5, planes, ROWS, cr)
    sides = radial_exchange(got[1:])

    grid = (5, planes, TALL, cr)
    q, u2, u0 = call(
        part(stages, n_ax, n_rad, ca, cz, slots),
        (struct((ndev, 1, 128)), struct((5, ca, ROWS, cr)), struct((5, ca, ROWS, cr))),
        [VMEM, VMEM, HBM] + [VMEM] * (2 * len(sides)),
        [pltpu.VMEM((5, ca + 2 * MID, 8, cr), F32)]
        + [pltpu.VMEM(grid, F32) for _ in range(4)]
        + [pltpu.VMEM((3, planes, ROWS, cr), F32), pltpu.VMEM((128, cr), F32)]
        + [pltpu.SMEM((slots,), jnp.int32), pltpu.SemaphoreType.DMA],
        mib=28,
    )(block, banded, far(panel_cell), *sides, *places)

    rows = lax.all_to_all(q, ("y", "core", "az", "rad"), 0, 0, tiled=True).reshape(ndev, 128)

    edge = struct((5 * MID * cz, cr), BF16)
    strip = struct((5 * MID * ca, cr), BF16)
    side = struct((5 * ca * ROWS // tiles, cr), BF16)
    grid = struct((5 * ca * ROWS, cr))
    strips = pltpu.VMEM((2,) + edge.shape, F32)
    ax1, ax2, az1, az2, *rads, fax, faz, frad = call(
        part(edge_fluxes, len(ends), ca, cz),
        (edge, edge, strip, strip) + tuple(side for _ in ends) + (grid,) * 3,
        [VMEM] * (1 + len(ends)),
        [strips],
        cost=pl.CostEstimate(flops=400_000_000, bytes_accessed=8_000_000, transcendentals=0),
    )(u2, *edges)
    ax1, ax2 = swap(ax1, ax2, ("y", "core"), False)
    az1, az2 = swap(az1, az2, "az", True)
    rads = radial_exchange(rads)
    _, state = call(
        part(last_stage, n_ax, len(ends), ca, cz),
        (grid, struct((5, ca, cz, cr))),
        [VMEM] * (10 + 2 * len(ends)),
        [
            pltpu.VMEM((5, ca, ROWS, cr), F32),
            pltpu.VMEM((5, 2 * MID, ROWS, cr), F32),
            strips,
            pltpu.VMEM((5, ca, 8, cr), F32),
        ],
        mib=12,
        alias={0: 0},
    )(faz, u2, u0, fax, frad, banded, ax1, ax2, az1, az2, *rads, *places)
    signal = call(
        part(signals, slots), struct((obs_weight.shape[0], NB)), [VMEM] * 3, mib=24
    )(rows, bin_offset, obs_weight)
    return (state, signal)


def solution(mesh):
    n_ax, n_az, n_rad = (mesh.shape[name] for name in ("ax", "az", "rad"))
    split = Mesh(mesh.devices.reshape(n_ax // 2, 2, n_az, n_rad), ("y", "core", "az", "rad"))
    ax = ("y", "core")
    every = ax + ("az", "rad")
    in_specs = (
        P(ax, "az", "rad"),
        P(None, ax, "az", "rad"),
        P(ax, "az", "rad"),
        P(every),
        P(every, None),
        P(every, None),
    )
    out_specs = (P(None, ax, "az", "rad"), P(every, None))
    return jax.shard_map(local, mesh=split, in_specs=in_specs, out_specs=out_specs, check_vma=False)
```

```python
import functools

import jax
import jax.numpy as jnp
from jax import lax
from jax.experimental import pallas as pl
from jax.experimental.pallas import tpu as pltpu
from jax.sharding import Mesh, PartitionSpec as P

NB = 128
GAMMA_M = 0.4
LAMBDA = 0.1
P_REF = 1.0
REACH = 6
MID = 4
SCALE = -LAMBDA / 12.0
ROWS = 32
OFF = 8
SPAN = 32
TALL = ROWS + 8
STEP = 4
SLOT = 8
HBM = pltpu.MemorySpace.HBM
VMEM = pltpu.MemorySpace.VMEM
SMEM = pltpu.MemorySpace.SMEM
F32 = jnp.float32
BF16 = jnp.bfloat16


def call(kernel, outs, in_spaces, scratch=(), mib=8, cost=None, alias={}):
    return pl.pallas_call(
        kernel,
        out_shape=outs,
        in_specs=[pl.BlockSpec(memory_space=s) for s in in_spaces],
        out_specs=jax.tree.map(lambda _: pl.BlockSpec(memory_space=VMEM), outs),
        scratch_shapes=list(scratch),
        compiler_params=pltpu.CompilerParams(vmem_limit_bytes=mib * 1024 * 1024),
        cost_estimate=cost,
        input_output_aliases=alias,
    )


def far(x):
    return pltpu.with_memory_space_constraint(x, HBM)


def struct(shape, dtype=F32):
    return jax.ShapeDtypeStruct(shape, dtype)


def kept(row):
    return 8 * (row % 4) + row // 4


def ax_index():
    return lax.axis_index("y") * lax.axis_size("core") + lax.axis_index("core")


def first_is_up(axis):
    return lax.axis_index("core" if axis == "ax" else axis) % 2 == 0


def load_and_pack(ca, cz, den, vel, pre, home, ax1, ax2, az1, az2, sems):
    size = ca * cz
    copies = [
        pltpu.make_async_copy(den, home.at[pl.ds(0, size)], sems.at[0]),
        pltpu.make_async_copy(vel, home.at[pl.ds(size, 3 * size)], sems.at[1]),
        pltpu.make_async_copy(pre, home.at[pl.ds(4 * size, size)], sems.at[2]),
    ]
    for copy in copies:
        copy.start()
    for copy in copies:
        copy.wait()
    up = first_is_up("ax")
    edge = REACH * cz
    for f in range(5):
        at = f * size
        low = home[at : at + edge, :]
        high = home[at + size - edge : at + size, :]
        rows = slice(f * edge, (f + 1) * edge)
        ax1[rows, :] = jnp.where(up, high, low).astype(BF16)
        ax2[rows, :] = jnp.where(up, low, high).astype(BF16)
    up = first_is_up("az")
    low, high = [], []
    for f in range(5):
        for d in range(REACH):
            low.append(home[pl.ds(f * size + d, ca, stride=cz), :])
            high.append(home[pl.ds(f * size + cz - 1 - d, ca, stride=cz), :])
    low, high = jnp.concatenate(low, axis=0), jnp.concatenate(high, axis=0)
    az1[...] = jnp.where(up, high, low).astype(BF16)
    az2[...] = jnp.where(up, low, high).astype(BF16)


def ax_sides(n_ax, got1, got2, rows):
    ax = ax_index()
    a, b = got1[rows, :].astype(F32), got2[rows, :].astype(F32)
    up = first_is_up("ax")
    lo = jnp.where(ax == 0, 0.0, jnp.where(up, b, a))
    hi = jnp.where(ax == n_ax - 1, 0.0, jnp.where(up, a, b))
    return lo, hi


def pack_corners(n_ax, cz, got1, got2, first_out, second_out, near):
    up = first_is_up("az")
    half = MID * cz
    size = REACH * cz
    for f in range(5):
        lo, hi = ax_sides(n_ax, got1, got2, slice(f * size, (f + 1) * size))
        near[f, 0:half, :] = lo[size - half :]
        near[f, half : 2 * half, :] = hi[0:half]
    low, high = [], []
    for f in range(5):
        for d in range(MID):
            low.append(near[f, pl.ds(d, 2 * MID, stride=cz), :])
            high.append(near[f, pl.ds(cz - 1 - d, 2 * MID, stride=cz), :])
    low, high = jnp.concatenate(low, axis=0), jnp.concatenate(high, axis=0)
    first_out[...] = jnp.where(up, high, low).astype(BF16)
    second_out[...] = jnp.where(up, low, high).astype(BF16)


def spread_rows(planes, cz, f, plane, ref, at, block):
    quarter = cz // 4
    for l in range(4):
        row = (f * planes + plane) * ROWS + 8 * l + OFF // 4
        block[pl.ds(row, quarter), :] = ref[pl.ds(at + l, quarter, stride=4), :]


def prepare(ends, ca, cz, n_rad, home, block, banded, *tables):
    cr = home.shape[1]
    rad = lax.axis_index("rad")
    for f in range(5):
        for k in range(ca):
            spread_rows(ca + 2 * REACH, cz, f, REACH + k, home, (f * ca + k) * cz, block)
    banded[...] = band(cr)
    edges, places = tables[: len(ends)], tables[len(ends) :]
    tiles = cr // SLOT
    there = {"high": jnp.where(rad < n_rad - 1, 1.0, 0.0), "low": jnp.where(rad > 0, 1.0, 0.0)}
    high = place_matrix(0, tiles, cr) * there["high"]
    low = place_matrix(SPAN - REACH, tiles, cr) * there["low"]
    for end, edge, place in zip(ends, edges, places):
        start = {"low": 0, "high": cr - REACH, "either": jnp.where(rad == 0, cr - REACH, 0)}[end]
        edge[...] = edge_matrix(start, tiles, cr)
        place[...] = {"low": high, "high": low, "either": high + low}[end].astype(BF16)


def edge_matrix(start, tiles, cr):
    k = lax.broadcasted_iota(jnp.int32, (tiles * cr, tiles * SLOT), 0)
    n = lax.broadcasted_iota(jnp.int32, (tiles * cr, tiles * SLOT), 1)
    hit = (k // cr == n // SLOT) & (n % SLOT < REACH) & (k % cr == n % SLOT + start)
    return jnp.where(hit, 1.0, 0.0).astype(BF16)


def place_matrix(start, tiles, cr):
    k = lax.broadcasted_iota(jnp.int32, (tiles * SLOT, tiles * cr // 4), 0)
    n = lax.broadcasted_iota(jnp.int32, (tiles * SLOT, tiles * cr // 4), 1)
    hit = (k // SLOT == n // SPAN) & (k % SLOT < REACH) & (n % SPAN == k % SLOT + start)
    return jnp.where(hit, 1.0, 0.0)


def add_sides(n_ax, ca, cz, block_in, ax1, ax2, az1, az2, block, sides, strips):
    planes = ca + 2 * REACH
    size = REACH * cz
    for f in range(5):
        lo, hi = ax_sides(n_ax, ax1, ax2, slice(f * size, (f + 1) * size))
        sides[f, 0:size, :] = lo
        sides[f, size : 2 * size, :] = hi
    for f in range(5):
        for k in range(REACH):
            spread_rows(planes, cz, f, k, sides.at[f], k * cz, block)
            spread_rows(planes, cz, f, REACH + ca + k, sides.at[f], size + k * cz, block)
    up = first_is_up("az")
    a, b = az1[...].astype(F32), az2[...].astype(F32)
    strips[0] = jnp.where(up, b, a)
    strips[1] = jnp.where(up, a, b)
    for f in range(5):
        for d in range(REACH):
            for side, row in ((0, OFF - 1 - d), (1, OFF + cz + d)):
                at = kept(row) + (f * planes + REACH) * ROWS
                block[pl.ds(at, ca, stride=ROWS), :] = strips[side, pl.ds((f * REACH + d) * ca, ca), :]


def add_corners(count, ca, cz, block_in, corner1, corner2, *rest):
    edges, block, outs, corners = rest[:count], rest[count], rest[count + 1 : -1], rest[-1]
    cr = corner1.shape[1]
    planes = ca + 2 * REACH
    up = first_is_up("az")
    a, b = corner1[...].astype(F32), corner2[...].astype(F32)
    corners[0] = jnp.where(up, b, a)
    corners[1] = jnp.where(up, a, b)
    for f in range(5):
        for d in range(MID):
            for side, row in ((0, OFF - 1 - d), (1, OFF + cz + d)):
                at = kept(row) + f * planes * ROWS
                start = (f * MID + d) * 2 * MID
                got = corners[side, pl.ds(start, MID), :]
                block[pl.ds(at + (REACH - MID) * ROWS, MID, stride=ROWS), :] = got
                got = corners[side, pl.ds(start + MID, MID), :]
                block[pl.ds(at + (REACH + ca) * ROWS, MID, stride=ROWS), :] = got

    tiles = cr // SLOT
    step = tiles * 8
    rows = []
    for f in range(5):
        for k in range((ca + 2 * MID) * ROWS // step):
            at = (f * planes + REACH - MID) * ROWS + k * step
            rows.append(jnp.concatenate([block[at + 8 * t : at + 8 * t + 8, :] for t in range(tiles)], axis=1))
    rows = jnp.concatenate(rows, axis=0).astype(BF16)
    for edge, out in zip(edges, outs):
        out[...] = jnp.dot(rows, edge[...], preferred_element_type=F32).astype(BF16)


def az_terms(flux):
    v = [flux[8 * l : 8 * l + 8] for l in range(4)]
    v = [pltpu.roll(v[2], 1, 0), pltpu.roll(v[3], 1, 0)] + v + [pltpu.roll(v[0], 7, 0), pltpu.roll(v[1], 7, 0)]
    out = [8.0 * (v[l + 3] - v[l + 1]) - (v[l + 4] - v[l]) for l in range(4)]
    side = flux[ROWS:]
    lanes = side.shape[1]
    span = lax.broadcasted_iota(jnp.int32, side.shape, 1) // SPAN
    up, down = pltpu.roll(side, 7, 0), pltpu.roll(side, 1, 0)
    up1 = pltpu.roll(jnp.where(span == 0, up, side), lanes - SPAN, 1)
    up2 = pltpu.roll(jnp.where(span < 2, up, side), lanes - 2 * SPAN, 1)
    down1 = pltpu.roll(jnp.where(span == 3, down, side), SPAN, 1)
    down2 = pltpu.roll(jnp.where(span >= 2, down, side), 2 * SPAN, 1)
    out.append(8.0 * (up1 - down1) - (up2 - down2))
    return jnp.concatenate(out, axis=0)


def band(cr):
    def place(axis, none):
        i = lax.broadcasted_iota(jnp.int32, (2 * cr, 2 * cr), axis)
        j = i % SPAN
        beyond = jnp.where(j < REACH, cr + j, jnp.where(j >= SPAN - REACH, j - SPAN, none))
        return jnp.where(i < cr, i, beyond), jnp.where(i < cr, -1, i // SPAN)

    k, k_span = place(0, 4 * cr)
    n, n_span = place(1, -4 * cr)
    gap = k - n
    out = jnp.where(gap == 1, 8.0, 0.0) + jnp.where(gap == -1, -8.0, 0.0)
    out = out + jnp.where(gap == 2, -1.0, 0.0) + jnp.where(gap == -2, 1.0, 0.0)
    apart = (k_span >= 0) & (n_span >= 0) & (k_span != n_span)
    return jnp.where(apart, 0.0, out).astype(BF16)


def split_state(u):
    rho, m0, m1, m2, energy = u
    inv = 1.0 / rho
    vel = [m0 * inv, m1 * inv, m2 * inv]
    pres = GAMMA_M * (energy - 0.5 * (m0 * vel[0] + m1 * vel[1] + m2 * vel[2]))
    return [m0, m1, m2], vel, pres, energy


def flux(d, mom, vel, pres, energy):
    parts = [mom[d]]
    for j in range(3):
        parts.append(mom[d] * vel[j] + pres if j == d else mom[d] * vel[j])
    parts.append((energy + pres) * vel[d])
    return parts


def ax_only(u, fax, j):
    got = flux(0, *u)
    for f in range(5):
        fax[f, j, 0:ROWS] = got[f]


def both_sides(us, js, fax, part, banded):
    rows = []
    shape = (ROWS, banded.shape[0] // 2)
    span = lax.broadcasted_iota(jnp.int32, shape, 1) // SPAN
    mine = span == lax.broadcasted_iota(jnp.int32, shape, 0) // 8
    for u, j in zip(us, js):
        got = flux(0, *u)
        for f in range(5):
            fax[f, j] = got[f]
        got = flux(2, *u)
        for f in range(5):
            side = jnp.where(mine, jnp.concatenate([got[f][ROWS:]] * 4, axis=0), 0.0)
            rows.append(jnp.concatenate([got[f][0:ROWS], side], axis=1))
    rows = jnp.concatenate(rows, axis=0)
    coarse = rows.astype(BF16)
    fine = (rows - coarse.astype(F32)).astype(BF16)
    matrix = banded[...]
    out = jnp.dot(coarse, matrix, preferred_element_type=F32)
    out = out + jnp.dot(fine, matrix, preferred_element_type=F32)
    half = out.shape[1] // 2
    for i, (u, j) in enumerate(zip(us, js)):
        got = flux(1, *u)
        for f in range(5):
            at = (i * 5 + f) * ROWS
            side = out[at : at + 8, half:]
            for l in range(1, 4):
                side = jnp.where(span[0:8] == l, out[at + 8 * l : at + 8 * l + 8, half:], side)
            radial = jnp.concatenate([out[at : at + ROWS, 0:half], side], axis=0)
            part[f, j] = az_terms(got[f]) + radial


def change(fa, part, f, j, size):
    near = fa(j + 1)[0:size] - fa(j - 1)[0:size]
    far = fa(j + 2)[0:size] - fa(j - 2)[0:size]
    return SCALE * (8.0 * near - far + part[f, j, 0:size])


def window(fax, f):
    held = {}

    def get(j):
        if j not in held:
            held[j] = fax[f, j]
        return held[j]

    return get


def stages(n_ax, n_rad, ca, cz, slots, block, banded, cells_far, *refs):
    sides, refs = refs[: len(refs) - 12], refs[len(refs) - 12 :]
    sides, places = sides[: len(sides) // 2], sides[len(sides) // 2 :]
    q_out, u2_out, u0_out, ghost, first, second, fax, part, value, picked, cells, cells_sem = refs
    fetch = pltpu.make_async_copy(cells_far, cells, cells_sem)
    fetch.start()
    cr = block.shape[-1]
    low, high = REACH, REACH + ca
    ax = ax_index()
    rad = lax.axis_index("rad")

    lane = lax.broadcasted_iota(jnp.int32, (8, cr), 1)
    row = 4 * lax.broadcasted_iota(jnp.int32, (8, cr), 0) + lane // SPAN
    j = lane % SPAN
    steps_rad = jnp.where(
        (j < REACH) & (rad < n_rad - 1),
        1 + j // 2,
        jnp.where((j >= SPAN - REACH) & (rad > 0), 1 + (SPAN - 1 - j) // 2, 99),
    )
    beyond_row = jnp.maximum(OFF - row, row - (OFF + cz - 1))
    steps = steps_rad + jnp.where(beyond_row > 0, (beyond_row + 1) // 2, 0)
    base0 = jnp.where(steps_rad < 99, 0.0, 1.0)

    side = 0.0
    for got, place in zip(sides, places):
        side = side + jnp.dot(got[...], place[...], preferred_element_type=F32)
    group = side.shape[1] // cr
    count = (ca + 2 * MID) // group
    for f in range(5):
        for k in range(count):
            for i in range(group):
                at = (f * count + k) * 8
                tile = side[at : at + 8, i * cr : (i + 1) * cr]
                ghost[f, k * group + i] = tile + base0 if f == 0 else tile

    def start_state(j, both):
        u = []
        for f in range(5):
            x = block[f, j]
            u.append(jnp.concatenate([x, ghost[f, j - (REACH - MID)]], axis=0) if both else x)
        rho, vel, pres = u[0], u[1:4], u[4]
        mom = [rho * x for x in vel]
        energy = pres * (1.0 / GAMMA_M) + 0.5 * (mom[0] * vel[0] + mom[1] * vel[1] + mom[2] * vel[2])
        return rho, (mom, vel, pres, energy)

    def note(s, j, u):
        value[s, j] = (u[2] - P_REF + u[0][0])[0:ROWS]

    for j in (low - 6, low - 5, high + 4, high + 5):
        ax_only(start_state(j, False)[1], fax, j)

    @pl.loop(0, (ca + 8) // STEP)
    def _(i):
        js = [low - 4 + STEP * i + k for k in range(STEP)]
        us = []
        for j in js:
            rho, u = start_state(j, True)
            for f, x in enumerate([rho] + u[0] + [u[3]]):
                first[f, j] = x
            note(0, j, u)
            us.append(u)
        both_sides(us, js, fax, part, banded)

    def update(f, j, fa, stage):
        a = max(low - j, j - (high - 1), 0)
        a = (a + 1) // 2
        lim = 2 - stage
        base = jnp.where(f == 0, 1.0, 0.0)
        size = ROWS if a == lim else TALL
        new = change(fa, part, f, j, size)
        u0 = first[f, j, 0:size]
        if stage == 0:
            new = u0 + new
        else:
            new = 0.75 * u0 + 0.25 * (second[f, j, 0:size] + new)
        beyond = (ax == 0) if j < low else (ax == n_ax - 1)
        home = new[0:ROWS]
        if a > 0:
            home = jnp.where(beyond, base, home)
        if size == ROWS:
            return home, None
        ok = steps <= lim - a
        if a > 0:
            ok = ok & jnp.logical_not(beyond)
        return home, jnp.where(ok, new[ROWS:], base)

    @pl.loop(0, 5)
    def _(f):
        fa = window(fax, f)
        for j in range(low - 4, high + 4):
            home, side = update(f, j, fa, 0)
            second[f, j, 0:ROWS] = home
            if side is not None:
                second[f, j, ROWS:] = side

    for j in (low - 4, low - 3, high + 2, high + 3):
        ax_only(split_state([second[f, j, 0:ROWS] for f in range(5)]), fax, j)

    @pl.loop(0, (ca + 4) // STEP)
    def _(i):
        js = [low - 2 + STEP * i + k for k in range(STEP)]
        us = []
        for j in js:
            u = split_state([second[f, j] for f in range(5)])
            note(1, j, u)
            us.append(u)
        both_sides(us, js, fax, part, banded)

    @pl.loop(0, 5)
    def _(f):
        fa = window(fax, f)
        for j in range(low - 2, high + 2):
            home, side = update(f, j, fa, 1)
            u2_out[f, j - (low - 2), 0:ROWS] = home
            if side is not None:
                u2_out[f, j - (low - 2), ROWS:] = side
        for j in range(low, high):
            u0_out[f, j - low] = first[f, j, 0:ROWS]

    @pl.loop(0, ca)
    def _(i):
        u = split_state([u2_out[f, i + 2, 0:ROWS] for f in range(5)])
        note(2, low + i, u)

    fetch.wait()
    picked[...] = jnp.zeros_like(picked)
    lanes = lax.broadcasted_iota(jnp.int32, (1, cr), 1)
    for p in range(slots):
        cell = cells[p]
        at = jnp.maximum(cell, 0)
        column = jnp.where(cell >= 0, lax.rem(at, cr), -1)
        at = lax.div(at, cr)
        plane = low + lax.div(at, cz)
        r = lax.rem(at, cz) + OFF
        r = 8 * lax.rem(r, 4) + lax.div(r, 4)
        hit = lanes == column
        for s in range(3):
            picked[pl.ds(s * slots + p, 1), :] = jnp.where(hit, value[s, plane, pl.ds(r, 1), :], 0.0)
    q = lax.dot_general(
        jnp.ones((8, cr), BF16),
        picked[...].astype(BF16),
        (((1,), (1,)), ((), ())),
        preferred_element_type=F32,
    )
    q_out[...] = jnp.broadcast_to(q[0:1][None], q_out.shape)


def last_stage(ca, cz, u2, u0, banded, state, fax, part):
    for j in (0, 1, ca + 2, ca + 3):
        ax_only(split_state([u2[f, j, 0:ROWS] for f in range(5)]), fax, j)

    @pl.loop(0, ca // STEP)
    def _(i):
        js = [2 + STEP * i + k for k in range(STEP)]
        us = [split_state([u2[f, j] for f in range(5)]) for j in js]
        both_sides(us, js, fax, part, banded)

    first, quarter = OFF // 4, cz // 4

    @pl.loop(0, 5)
    def _(f):
        fa = window(fax, f)
        for k in range(ca):
            j = k + 2
            new = u2[f, j, 0:ROWS] + change(fa, part, f, j, ROWS)
            new = u0[f, k] * (1.0 / 3.0) + (2.0 / 3.0) * new
            for l in range(4):
                state[f, k, pl.ds(l, quarter, stride=4), :] = new[8 * l + first : 8 * l + first + quarter]


def signal_tables(slots, offsets, pick, wait):
    group = 32
    cols = group * slots
    col = lax.broadcasted_iota(jnp.int32, (1, cols), 1)
    owner = lax.broadcasted_iota(jnp.int32, (group, cols), 0) == col // slots
    lane = lax.broadcasted_iota(jnp.int32, (pick.shape[0], cols), 0)
    for s in range(3):
        hot = jnp.where(lane == s * slots + col % slots, 1.0, 0.0)
        pick[:, s * cols : (s + 1) * cols] = hot.astype(BF16)
    time = lax.broadcasted_iota(jnp.int32, (NB, cols), 0).astype(F32)
    for g in range(offsets.shape[1] // group):
        off = offsets[0:1, g * group : (g + 1) * group].astype(F32)
        off = jnp.broadcast_to(off, (8, group)).astype(BF16)
        bins = jnp.dot(off, owner.astype(BF16), preferred_element_type=F32)[0:1]
        wait[:, g * cols : (g + 1) * cols] = time - bins


def signals(slots, rows, pick, wait, weight, out):
    group = 32
    cols = group * slots
    col = lax.broadcasted_iota(jnp.int32, (1, cols), 1)
    owner = lax.broadcasted_iota(jnp.int32, (group, cols), 0) == col // slots
    total = jnp.zeros(out.shape, F32)
    for g in range(rows.shape[0] // group):
        q = rows[g * group : (g + 1) * group, :].astype(BF16)
        spread = jnp.dot(q, pick[...], preferred_element_type=F32)
        bins = wait[:, g * cols : (g + 1) * cols]
        table = jnp.zeros((NB, cols), F32)
        for s in range(3):
            line = jnp.where(owner, spread[:, s * cols : (s + 1) * cols], 0.0)
            line = jnp.sum(line, axis=0, keepdims=True)
            table = jnp.where(bins == s, line, table)
        total = total + lax.dot_general(
            weight[:, g * cols : (g + 1) * cols],
            table.astype(BF16),
            (((1,), (1,)), ((), ())),
            preferred_element_type=F32,
        )
    out[...] = total


def swap_pairs(count, periodic):
    one = [(i, i ^ 1) for i in range(count)]
    two = []
    for i in range(count):
        j = i - 1 if i % 2 == 0 else i + 1
        two.append((i, j % count if periodic or 0 <= j < count else i))
    return one, two


def swap(first, second, axis, periodic):
    count = 1
    for name in (axis,) if isinstance(axis, str) else axis:
        count = count * lax.axis_size(name)
    one, two = swap_pairs(count, periodic)
    return lax.ppermute(first, axis, one), lax.ppermute(second, axis, two)


def local(density, velocity, pressure, panel_cell, obs_weight, bin_offset):
    ca, cz, cr = density.shape
    slots = panel_cell.shape[0]
    ndev = bin_offset.shape[1]
    n_ax, n_rad = lax.axis_size("y") * lax.axis_size("core"), lax.axis_size("rad")
    planes = ca + 2 * REACH
    part = functools.partial
    given = (density.reshape(ca * cz, cr), velocity.reshape(3 * ca * cz, cr), pressure.reshape(ca * cz, cr))

    edge = struct((5 * REACH * cz, cr), BF16)
    strip = struct((5 * REACH * ca, cr), BF16)
    home, ax1, ax2, az1, az2 = call(
        part(load_and_pack, ca, cz),
        (struct((5 * ca * cz, cr)), edge, edge, strip, strip),
        [HBM] * 3,
        [pltpu.SemaphoreType.DMA((3,))],
    )(*[far(x) for x in given])
    ax1, ax2 = swap(ax1, ax2, ("y", "core"), False)
    az1, az2 = swap(az1, az2, "az", True)
    grid = struct((5 * planes * ROWS, cr))
    ends = ("either",) if n_rad == 2 else ("low", "high")
    tiles = cr // SLOT
    table = [struct((tiles * cr, cr), BF16)] * len(ends) + [struct((cr, tiles * cr // 4), BF16)] * len(ends)
    block, banded, *tables = call(
        part(prepare, ends, ca, cz, n_rad),
        (grid, struct((2 * cr, 2 * cr), BF16), *table),
        [VMEM],
    )(home)
    edges, places = tables[: len(ends)], tables[len(ends) :]

    pick, wait = call(
        part(signal_tables, slots),
        (struct((128, 3 * 32 * slots), BF16), struct((NB, ndev * slots))),
        [VMEM],
        cost=pl.CostEstimate(flops=100_000_000, bytes_accessed=4_000_000, transcendentals=0),
    )(bin_offset)

    corner = struct((5 * MID * 2 * MID, cr), BF16)
    near = pltpu.VMEM((5, 2 * MID * cz, cr), F32)
    corner1, corner2 = call(part(pack_corners, n_ax, cz), (corner, corner), [VMEM] * 2, [near])(ax1, ax2)
    corner1, corner2 = swap(corner1, corner2, "az", True)

    side = struct((5 * (ca + 2 * MID) * ROWS // tiles, cr), BF16)
    block = call(
        part(add_sides, n_ax, ca, cz),
        grid,
        [VMEM] * 5,
        [pltpu.VMEM((5, 2 * REACH * cz, cr), F32), pltpu.VMEM((2,) + strip.shape, F32)],
        mib=8,
        alias={0: 0},
        cost=pl.CostEstimate(flops=100_000_000, bytes_accessed=4_000_000, transcendentals=0),
    )(block, ax1, ax2, az1, az2)
    got = call(
        part(add_corners, len(ends), ca, cz),
        (grid,) + tuple(side for _ in ends),
        [VMEM] * (3 + len(ends)),
        [pltpu.VMEM((2,) + corner.shape, F32)],
        mib=8,
        alias={0: 0},
    )(block, corner1, corner2, *edges)
    block = got[0].reshape(5, planes, ROWS, cr)
    if n_rad == 2:
        sides = (lax.ppermute(got[1], "rad", [(0, 1), (1, 0)]),)
    else:
        up = [(i, i + 1) for i in range(n_rad - 1)]
        sides = (lax.ppermute(got[1], "rad", [(j, i) for i, j in up]), lax.ppermute(got[2], "rad", up))

    grid = (5, planes, TALL, cr)
    q, u2, u0 = call(
        part(stages, n_ax, n_rad, ca, cz, slots),
        (struct((ndev, 1, 128)), struct((5, ca + 4, TALL, cr)), struct((5, ca, ROWS, cr))),
        [VMEM, VMEM, HBM] + [VMEM] * (2 * len(sides)),
        [pltpu.VMEM((5, ca + 2 * MID, 8, cr), F32)]
        + [pltpu.VMEM(grid, F32) for _ in range(4)]
        + [pltpu.VMEM((3, planes, ROWS, cr), F32), pltpu.VMEM((128, cr), F32)]
        + [pltpu.SMEM((slots,), jnp.int32), pltpu.SemaphoreType.DMA],
        mib=28,
    )(block, banded, far(panel_cell), *sides, *places)

    rows = lax.all_to_all(q, ("y", "core", "az", "rad"), 0, 0, tiled=True).reshape(ndev, 128)

    grid = (5, ca + 4, TALL, cr)
    state = call(
        part(last_stage, ca, cz),
        struct((5, ca, cz, cr)),
        [VMEM] * 3,
        [pltpu.VMEM(grid, F32), pltpu.VMEM(grid, F32)],
        mib=12,
        cost=pl.CostEstimate(flops=400_000_000, bytes_accessed=8_000_000, transcendentals=0),
    )(u2, u0, banded)
    signal = call(part(signals, slots), struct((obs_weight.shape[0], NB)), [VMEM] * 4, mib=24)(
        rows, pick, wait, obs_weight
    )
    return (state, signal)


def solution(mesh):
    n_ax, n_az, n_rad = (mesh.shape[name] for name in ("ax", "az", "rad"))
    split = Mesh(mesh.devices.reshape(n_ax // 2, 2, n_az, n_rad), ("y", "core", "az", "rad"))
    ax = ("y", "core")
    every = ax + ("az", "rad")
    in_specs = (
        P(ax, "az", "rad"),
        P(None, ax, "az", "rad"),
        P(ax, "az", "rad"),
        P(every),
        P(every, None),
        P(every, None),
    )
    out_specs = (P(None, ax, "az", "rad"), P(every, None))
    return jax.shard_map(local, mesh=split, in_specs=in_specs, out_specs=out_specs, check_vma=False)
```

```python
import functools

import jax
import jax.numpy as jnp
from jax import lax
from jax.experimental import pallas as pl
from jax.experimental.pallas import tpu as pltpu
from jax.sharding import Mesh, PartitionSpec as P

NB = 128
GAMMA_M = 0.4
LAMBDA = 0.1
P_REF = 1.0
REACH = 6
MID = 4
SCALE = -LAMBDA / 12.0
ROWS = 32
OFF = 8
SPAN = 32
TALL = ROWS + 8
STEP = 4
SLOT = 8
HBM = pltpu.MemorySpace.HBM
VMEM = pltpu.MemorySpace.VMEM
SMEM = pltpu.MemorySpace.SMEM
F32 = jnp.float32
BF16 = jnp.bfloat16


def call(kernel, outs, in_spaces, scratch=(), mib=8, cost=None, alias={}):
    return pl.pallas_call(
        kernel,
        out_shape=outs,
        in_specs=[pl.BlockSpec(memory_space=s) for s in in_spaces],
        out_specs=jax.tree.map(lambda _: pl.BlockSpec(memory_space=VMEM), outs),
        scratch_shapes=list(scratch),
        compiler_params=pltpu.CompilerParams(vmem_limit_bytes=mib * 1024 * 1024),
        cost_estimate=cost,
        input_output_aliases=alias,
    )


def far(x):
    return pltpu.with_memory_space_constraint(x, HBM)


def struct(shape, dtype=F32):
    return jax.ShapeDtypeStruct(shape, dtype)


def kept(row):
    return 8 * (row % 4) + row // 4


def ax_index():
    return lax.axis_index("y") * lax.axis_size("core") + lax.axis_index("core")


def first_is_up(axis):
    return lax.axis_index("core" if axis == "ax" else axis) % 2 == 0


def load_and_pack(ca, cz, den, vel, pre, home, ax1, ax2, az1, az2, sems):
    size = ca * cz
    copies = [
        pltpu.make_async_copy(den, home.at[pl.ds(0, size)], sems.at[0]),
        pltpu.make_async_copy(vel, home.at[pl.ds(size, 3 * size)], sems.at[1]),
        pltpu.make_async_copy(pre, home.at[pl.ds(4 * size, size)], sems.at[2]),
    ]
    for copy in copies:
        copy.start()
    for copy in copies:
        copy.wait()
    up = first_is_up("ax")
    edge = REACH * cz
    for f in range(5):
        at = f * size
        low = home[at : at + edge, :]
        high = home[at + size - edge : at + size, :]
        rows = slice(f * edge, (f + 1) * edge)
        ax1[rows, :] = jnp.where(up, high, low).astype(BF16)
        ax2[rows, :] = jnp.where(up, low, high).astype(BF16)
    up = first_is_up("az")
    low, high = [], []
    for f in range(5):
        for d in range(REACH):
            low.append(home[pl.ds(f * size + d, ca, stride=cz), :])
            high.append(home[pl.ds(f * size + cz - 1 - d, ca, stride=cz), :])
    low, high = jnp.concatenate(low, axis=0), jnp.concatenate(high, axis=0)
    az1[...] = jnp.where(up, high, low).astype(BF16)
    az2[...] = jnp.where(up, low, high).astype(BF16)


def ax_sides(n_ax, got1, got2, rows):
    ax = ax_index()
    a, b = got1[rows, :].astype(F32), got2[rows, :].astype(F32)
    up = first_is_up("ax")
    lo = jnp.where(ax == 0, 0.0, jnp.where(up, b, a))
    hi = jnp.where(ax == n_ax - 1, 0.0, jnp.where(up, a, b))
    return lo, hi


def pack_corners(n_ax, cz, got1, got2, first_out, second_out, near):
    up = first_is_up("az")
    half = MID * cz
    size = REACH * cz
    for f in range(5):
        lo, hi = ax_sides(n_ax, got1, got2, slice(f * size, (f + 1) * size))
        near[f, 0:half, :] = lo[size - half :]
        near[f, half : 2 * half, :] = hi[0:half]
    low, high = [], []
    for f in range(5):
        for d in range(MID):
            low.append(near[f, pl.ds(d, 2 * MID, stride=cz), :])
            high.append(near[f, pl.ds(cz - 1 - d, 2 * MID, stride=cz), :])
    low, high = jnp.concatenate(low, axis=0), jnp.concatenate(high, axis=0)
    first_out[...] = jnp.where(up, high, low).astype(BF16)
    second_out[...] = jnp.where(up, low, high).astype(BF16)


def spread_rows(planes, cz, f, plane, ref, at, block):
    quarter = cz // 4
    for l in range(4):
        row = (f * planes + plane) * ROWS + 8 * l + OFF // 4
        block[pl.ds(row, quarter), :] = ref[pl.ds(at + l, quarter, stride=4), :]


def prepare(ends, ca, cz, n_rad, home, block, banded, *tables):
    cr = home.shape[1]
    rad = lax.axis_index("rad")
    for f in range(5):
        for k in range(ca):
            spread_rows(ca + 2 * REACH, cz, f, REACH + k, home, (f * ca + k) * cz, block)
    banded[...] = band(cr)
    edges, places = tables[: len(ends)], tables[len(ends) :]
    tiles = cr // SLOT
    there = {"high": jnp.where(rad < n_rad - 1, 1.0, 0.0), "low": jnp.where(rad > 0, 1.0, 0.0)}
    high = place_matrix(0, tiles, cr) * there["high"]
    low = place_matrix(SPAN - REACH, tiles, cr) * there["low"]
    for end, edge, place in zip(ends, edges, places):
        start = {"low": 0, "high": cr - REACH, "either": jnp.where(rad == 0, cr - REACH, 0)}[end]
        edge[...] = edge_matrix(start, tiles, cr)
        place[...] = {"low": high, "high": low, "either": high + low}[end].astype(BF16)


def edge_matrix(start, tiles, cr):
    k = lax.broadcasted_iota(jnp.int32, (tiles * cr, tiles * SLOT), 0)
    n = lax.broadcasted_iota(jnp.int32, (tiles * cr, tiles * SLOT), 1)
    hit = (k // cr == n // SLOT) & (n % SLOT < REACH) & (k % cr == n % SLOT + start)
    return jnp.where(hit, 1.0, 0.0).astype(BF16)


def place_matrix(start, tiles, cr):
    k = lax.broadcasted_iota(jnp.int32, (tiles * SLOT, tiles * cr // 4), 0)
    n = lax.broadcasted_iota(jnp.int32, (tiles * SLOT, tiles * cr // 4), 1)
    hit = (k // SLOT == n // SPAN) & (k % SLOT < REACH) & (n % SPAN == k % SLOT + start)
    return jnp.where(hit, 1.0, 0.0)


def add_sides(n_ax, ca, cz, block_in, ax1, ax2, az1, az2, block, sides, strips):
    planes = ca + 2 * REACH
    size = REACH * cz
    for f in range(5):
        lo, hi = ax_sides(n_ax, ax1, ax2, slice(f * size, (f + 1) * size))
        sides[f, 0:size, :] = lo
        sides[f, size : 2 * size, :] = hi
    for f in range(5):
        for k in range(REACH):
            spread_rows(planes, cz, f, k, sides.at[f], k * cz, block)
            spread_rows(planes, cz, f, REACH + ca + k, sides.at[f], size + k * cz, block)
    up = first_is_up("az")
    a, b = az1[...].astype(F32), az2[...].astype(F32)
    strips[0] = jnp.where(up, b, a)
    strips[1] = jnp.where(up, a, b)
    for f in range(5):
        for d in range(REACH):
            for side, row in ((0, OFF - 1 - d), (1, OFF + cz + d)):
                at = kept(row) + (f * planes + REACH) * ROWS
                block[pl.ds(at, ca, stride=ROWS), :] = strips[side, pl.ds((f * REACH + d) * ca, ca), :]


def add_corners(count, ca, cz, block_in, corner1, corner2, *rest):
    edges, block, outs, corners = rest[:count], rest[count], rest[count + 1 : -1], rest[-1]
    cr = corner1.shape[1]
    planes = ca + 2 * REACH
    up = first_is_up("az")
    a, b = corner1[...].astype(F32), corner2[...].astype(F32)
    corners[0] = jnp.where(up, b, a)
    corners[1] = jnp.where(up, a, b)
    for f in range(5):
        for d in range(MID):
            for side, row in ((0, OFF - 1 - d), (1, OFF + cz + d)):
                at = kept(row) + f * planes * ROWS
                start = (f * MID + d) * 2 * MID
                got = corners[side, pl.ds(start, MID), :]
                block[pl.ds(at + (REACH - MID) * ROWS, MID, stride=ROWS), :] = got
                got = corners[side, pl.ds(start + MID, MID), :]
                block[pl.ds(at + (REACH + ca) * ROWS, MID, stride=ROWS), :] = got

    tiles = cr // SLOT
    step = tiles * 8
    rows = []
    for f in range(5):
        for k in range((ca + 2 * MID) * ROWS // step):
            at = (f * planes + REACH - MID) * ROWS + k * step
            rows.append(jnp.concatenate([block[at + 8 * t : at + 8 * t + 8, :] for t in range(tiles)], axis=1))
    rows = jnp.concatenate(rows, axis=0).astype(BF16)
    for edge, out in zip(edges, outs):
        out[...] = jnp.dot(rows, edge[...], preferred_element_type=F32).astype(BF16)


def az_terms(flux):
    v = [flux[8 * l : 8 * l + 8] for l in range(4)]
    v = [pltpu.roll(v[2], 1, 0), pltpu.roll(v[3], 1, 0)] + v + [pltpu.roll(v[0], 7, 0), pltpu.roll(v[1], 7, 0)]
    out = [8.0 * (v[l + 3] - v[l + 1]) - (v[l + 4] - v[l]) for l in range(4)]
    side = flux[ROWS:]
    lanes = side.shape[1]
    span = lax.broadcasted_iota(jnp.int32, side.shape, 1) // SPAN
    up, down = pltpu.roll(side, 7, 0), pltpu.roll(side, 1, 0)
    up1 = pltpu.roll(jnp.where(span == 0, up, side), lanes - SPAN, 1)
    up2 = pltpu.roll(jnp.where(span < 2, up, side), lanes - 2 * SPAN, 1)
    down1 = pltpu.roll(jnp.where(span == 3, down, side), SPAN, 1)
    down2 = pltpu.roll(jnp.where(span >= 2, down, side), 2 * SPAN, 1)
    out.append(8.0 * (up1 - down1) - (up2 - down2))
    return jnp.concatenate(out, axis=0)


def band(cr):
    def place(axis, none):
        i = lax.broadcasted_iota(jnp.int32, (2 * cr, 2 * cr), axis)
        j = i % SPAN
        beyond = jnp.where(j < REACH, cr + j, jnp.where(j >= SPAN - REACH, j - SPAN, none))
        return jnp.where(i < cr, i, beyond), jnp.where(i < cr, -1, i // SPAN)

    k, k_span = place(0, 4 * cr)
    n, n_span = place(1, -4 * cr)
    gap = k - n
    out = jnp.where(gap == 1, 8.0, 0.0) + jnp.where(gap == -1, -8.0, 0.0)
    out = out + jnp.where(gap == 2, -1.0, 0.0) + jnp.where(gap == -2, 1.0, 0.0)
    apart = (k_span >= 0) & (n_span >= 0) & (k_span != n_span)
    return jnp.where(apart, 0.0, out).astype(BF16)


def split_state(u):
    rho, m0, m1, m2, energy = u
    inv = 1.0 / rho
    vel = [m0 * inv, m1 * inv, m2 * inv]
    pres = GAMMA_M * (energy - 0.5 * (m0 * vel[0] + m1 * vel[1] + m2 * vel[2]))
    return [m0, m1, m2], vel, pres, energy


def flux(d, mom, vel, pres, energy):
    parts = [mom[d]]
    for j in range(3):
        parts.append(mom[d] * vel[j] + pres if j == d else mom[d] * vel[j])
    parts.append((energy + pres) * vel[d])
    return parts


def ax_only(u, fax, j):
    got = flux(0, *u)
    for f in range(5):
        fax[f, j, 0:ROWS] = got[f]


def both_sides(us, js, fax, part, banded):
    rows = []
    shape = (ROWS, banded.shape[0] // 2)
    span = lax.broadcasted_iota(jnp.int32, shape, 1) // SPAN
    mine = span == lax.broadcasted_iota(jnp.int32, shape, 0) // 8
    for u, j in zip(us, js):
        got = flux(0, *u)
        for f in range(5):
            fax[f, j] = got[f]
        got = flux(2, *u)
        for f in range(5):
            side = jnp.where(mine, jnp.concatenate([got[f][ROWS:]] * 4, axis=0), 0.0)
            rows.append(jnp.concatenate([got[f][0:ROWS], side], axis=1))
    rows = jnp.concatenate(rows, axis=0).astype(BF16)
    out = jnp.dot(rows, banded[...], preferred_element_type=F32)
    half = out.shape[1] // 2
    for i, (u, j) in enumerate(zip(us, js)):
        got = flux(1, *u)
        for f in range(5):
            at = (i * 5 + f) * ROWS
            side = out[at : at + 8, half:]
            for l in range(1, 4):
                side = jnp.where(span[0:8] == l, out[at + 8 * l : at + 8 * l + 8, half:], side)
            radial = jnp.concatenate([out[at : at + ROWS, 0:half], side], axis=0)
            part[f, j] = az_terms(got[f]) + radial


def change(fa, part, f, j, size):
    near = fa(j + 1)[0:size] - fa(j - 1)[0:size]
    far = fa(j + 2)[0:size] - fa(j - 2)[0:size]
    return SCALE * (8.0 * near - far + part[f, j, 0:size])


def window(fax, f):
    held = {}

    def get(j):
        if j not in held:
            held[j] = fax[f, j]
        return held[j]

    return get


def stages(n_ax, n_rad, ca, cz, slots, block, banded, cells_far, *refs):
    sides, refs = refs[: len(refs) - 12], refs[len(refs) - 12 :]
    sides, places = sides[: len(sides) // 2], sides[len(sides) // 2 :]
    q_out, u2_out, u0_out, ghost, first, second, fax, part, value, picked, cells, cells_sem = refs
    fetch = pltpu.make_async_copy(cells_far, cells, cells_sem)
    fetch.start()
    cr = block.shape[-1]
    low, high = REACH, REACH + ca
    ax = ax_index()
    rad = lax.axis_index("rad")

    lane = lax.broadcasted_iota(jnp.int32, (8, cr), 1)
    row = 4 * lax.broadcasted_iota(jnp.int32, (8, cr), 0) + lane // SPAN
    j = lane % SPAN
    steps_rad = jnp.where(
        (j < REACH) & (rad < n_rad - 1),
        1 + j // 2,
        jnp.where((j >= SPAN - REACH) & (rad > 0), 1 + (SPAN - 1 - j) // 2, 99),
    )
    beyond_row = jnp.maximum(OFF - row, row - (OFF + cz - 1))
    steps = steps_rad + jnp.where(beyond_row > 0, (beyond_row + 1) // 2, 0)
    base0 = jnp.where(steps_rad < 99, 0.0, 1.0)

    side = 0.0
    for got, place in zip(sides, places):
        side = side + jnp.dot(got[...], place[...], preferred_element_type=F32)
    group = side.shape[1] // cr
    count = (ca + 2 * MID) // group
    for f in range(5):
        for k in range(count):
            for i in range(group):
                at = (f * count + k) * 8
                tile = side[at : at + 8, i * cr : (i + 1) * cr]
                ghost[f, k * group + i] = tile + base0 if f == 0 else tile

    def start_state(j, both):
        u = []
        for f in range(5):
            x = block[f, j]
            u.append(jnp.concatenate([x, ghost[f, j - (REACH - MID)]], axis=0) if both else x)
        rho, vel, pres = u[0], u[1:4], u[4]
        mom = [rho * x for x in vel]
        energy = pres * (1.0 / GAMMA_M) + 0.5 * (mom[0] * vel[0] + mom[1] * vel[1] + mom[2] * vel[2])
        return rho, (mom, vel, pres, energy)

    def note(s, j, u):
        value[s, j] = (u[2] - P_REF + u[0][0])[0:ROWS]

    for j in (low - 6, low - 5, high + 4, high + 5):
        ax_only(start_state(j, False)[1], fax, j)

    @pl.loop(0, (ca + 8) // STEP)
    def _(i):
        js = [low - 4 + STEP * i + k for k in range(STEP)]
        us = []
        for j in js:
            rho, u = start_state(j, True)
            for f, x in enumerate([rho] + u[0] + [u[3]]):
                first[f, j] = x
            note(0, j, u)
            us.append(u)
        both_sides(us, js, fax, part, banded)

    def update(f, j, fa, stage):
        a = max(low - j, j - (high - 1), 0)
        a = (a + 1) // 2
        lim = 2 - stage
        base = jnp.where(f == 0, 1.0, 0.0)
        size = ROWS if a == lim else TALL
        new = change(fa, part, f, j, size)
        u0 = first[f, j, 0:size]
        if stage == 0:
            new = u0 + new
        else:
            new = 0.75 * u0 + 0.25 * (second[f, j, 0:size] + new)
        beyond = (ax == 0) if j < low else (ax == n_ax - 1)
        home = new[0:ROWS]
        if a > 0:
            home = jnp.where(beyond, base, home)
        if size == ROWS:
            return home, None
        ok = steps <= lim - a
        if a > 0:
            ok = ok & jnp.logical_not(beyond)
        return home, jnp.where(ok, new[ROWS:], base)

    @pl.loop(0, 5)
    def _(f):
        fa = window(fax, f)
        for j in range(low - 4, high + 4):
            home, side = update(f, j, fa, 0)
            second[f, j, 0:ROWS] = home
            if side is not None:
                second[f, j, ROWS:] = side

    for j in (low - 4, low - 3, high + 2, high + 3):
        ax_only(split_state([second[f, j, 0:ROWS] for f in range(5)]), fax, j)

    @pl.loop(0, (ca + 4) // STEP)
    def _(i):
        js = [low - 2 + STEP * i + k for k in range(STEP)]
        us = []
        for j in js:
            u = split_state([second[f, j] for f in range(5)])
            note(1, j, u)
            us.append(u)
        both_sides(us, js, fax, part, banded)

    @pl.loop(0, 5)
    def _(f):
        fa = window(fax, f)
        for j in range(low - 2, high + 2):
            home, side = update(f, j, fa, 1)
            u2_out[f, j - (low - 2), 0:ROWS] = home
            if side is not None:
                u2_out[f, j - (low - 2), ROWS:] = side
        for j in range(low, high):
            u0_out[f, j - low] = first[f, j, 0:ROWS]

    @pl.loop(0, ca)
    def _(i):
        u = split_state([u2_out[f, i + 2, 0:ROWS] for f in range(5)])
        note(2, low + i, u)

    fetch.wait()
    picked[...] = jnp.zeros_like(picked)
    lanes = lax.broadcasted_iota(jnp.int32, (1, cr), 1)
    for p in range(slots):
        cell = cells[p]
        at = jnp.maximum(cell, 0)
        column = jnp.where(cell >= 0, lax.rem(at, cr), -1)
        at = lax.div(at, cr)
        plane = low + lax.div(at, cz)
        r = lax.rem(at, cz) + OFF
        r = 8 * lax.rem(r, 4) + lax.div(r, 4)
        hit = lanes == column
        for s in range(3):
            picked[pl.ds(s * slots + p, 1), :] = jnp.where(hit, value[s, plane, pl.ds(r, 1), :], 0.0)
    q = lax.dot_general(
        jnp.ones((8, cr), BF16),
        picked[...].astype(BF16),
        (((1,), (1,)), ((), ())),
        preferred_element_type=F32,
    )
    q_out[...] = jnp.broadcast_to(q[0:1][None], q_out.shape)


def last_stage(ca, cz, u2, u0, banded, state, fax, part):
    for j in (0, 1, ca + 2, ca + 3):
        ax_only(split_state([u2[f, j, 0:ROWS] for f in range(5)]), fax, j)

    @pl.loop(0, ca // STEP)
    def _(i):
        js = [2 + STEP * i + k for k in range(STEP)]
        us = [split_state([u2[f, j] for f in range(5)]) for j in js]
        both_sides(us, js, fax, part, banded)

    first, quarter = OFF // 4, cz // 4

    @pl.loop(0, 5)
    def _(f):
        fa = window(fax, f)
        for k in range(ca):
            j = k + 2
            new = u2[f, j, 0:ROWS] + change(fa, part, f, j, ROWS)
            new = u0[f, k] * (1.0 / 3.0) + (2.0 / 3.0) * new
            for l in range(4):
                state[f, k, pl.ds(l, quarter, stride=4), :] = new[8 * l + first : 8 * l + first + quarter]


def signals(slots, rows, offsets, weight, out):
    ndev = rows.shape[0]
    group = 32
    cols = group * slots
    lanes = rows.shape[1]
    col = lax.broadcasted_iota(jnp.int32, (1, cols), 1)
    owner = lax.broadcasted_iota(jnp.int32, (group, cols), 0) == col // slots
    lane = lax.broadcasted_iota(jnp.int32, (lanes, cols), 0)
    time = lax.broadcasted_iota(jnp.int32, (NB, cols), 0).astype(F32)
    total = jnp.zeros(out.shape, F32)
    for g in range(ndev // group):
        q = rows[g * group : (g + 1) * group, :].astype(BF16)
        off = offsets[0:1, g * group : (g + 1) * group].astype(F32)
        off = jnp.broadcast_to(off, (8, group)).astype(BF16)
        bins = jnp.dot(off, owner.astype(BF16), preferred_element_type=F32)[0:1]
        table = jnp.zeros((NB, cols), F32)
        for s in range(3):
            pick = jnp.where(lane == s * slots + col % slots, 1.0, 0.0).astype(BF16)
            spread = jnp.dot(q, pick, preferred_element_type=F32)
            line = jnp.sum(jnp.where(owner, spread, 0.0), axis=0, keepdims=True)
            table = jnp.where(time == bins + s, line, table)
        total = total + lax.dot_general(
            weight[:, g * cols : (g + 1) * cols],
            table.astype(BF16),
            (((1,), (1,)), ((), ())),
            preferred_element_type=F32,
        )
    out[...] = total


def swap_pairs(count, periodic):
    one = [(i, i ^ 1) for i in range(count)]
    two = []
    for i in range(count):
        j = i - 1 if i % 2 == 0 else i + 1
        two.append((i, j % count if periodic or 0 <= j < count else i))
    return one, two


def swap(first, second, axis, periodic):
    count = 1
    for name in (axis,) if isinstance(axis, str) else axis:
        count = count * lax.axis_size(name)
    one, two = swap_pairs(count, periodic)
    return lax.ppermute(first, axis, one), lax.ppermute(second, axis, two)


def local(density, velocity, pressure, panel_cell, obs_weight, bin_offset):
    ca, cz, cr = density.shape
    slots = panel_cell.shape[0]
    ndev = bin_offset.shape[1]
    n_ax, n_rad = lax.axis_size("y") * lax.axis_size("core"), lax.axis_size("rad")
    planes = ca + 2 * REACH
    part = functools.partial
    given = (density.reshape(ca * cz, cr), velocity.reshape(3 * ca * cz, cr), pressure.reshape(ca * cz, cr))

    edge = struct((5 * REACH * cz, cr), BF16)
    strip = struct((5 * REACH * ca, cr), BF16)
    home, ax1, ax2, az1, az2 = call(
        part(load_and_pack, ca, cz),
        (struct((5 * ca * cz, cr)), edge, edge, strip, strip),
        [HBM] * 3,
        [pltpu.SemaphoreType.DMA((3,))],
    )(*[far(x) for x in given])
    ax1, ax2 = swap(ax1, ax2, ("y", "core"), False)
    az1, az2 = swap(az1, az2, "az", True)
    grid = struct((5 * planes * ROWS, cr))
    ends = ("either",) if n_rad == 2 else ("low", "high")
    tiles = cr // SLOT
    table = [struct((tiles * cr, cr), BF16)] * len(ends) + [struct((cr, tiles * cr // 4), BF16)] * len(ends)
    block, banded, *tables = call(
        part(prepare, ends, ca, cz, n_rad),
        (grid, struct((2 * cr, 2 * cr), BF16), *table),
        [VMEM],
    )(home)
    edges, places = tables[: len(ends)], tables[len(ends) :]

    corner = struct((5 * MID * 2 * MID, cr), BF16)
    near = pltpu.VMEM((5, 2 * MID * cz, cr), F32)
    corner1, corner2 = call(part(pack_corners, n_ax, cz), (corner, corner), [VMEM] * 2, [near])(ax1, ax2)
    corner1, corner2 = swap(corner1, corner2, "az", True)

    side = struct((5 * (ca + 2 * MID) * ROWS // tiles, cr), BF16)
    block = call(
        part(add_sides, n_ax, ca, cz),
        grid,
        [VMEM] * 5,
        [pltpu.VMEM((5, 2 * REACH * cz, cr), F32), pltpu.VMEM((2,) + strip.shape, F32)],
        mib=8,
        alias={0: 0},
        cost=pl.CostEstimate(flops=100_000_000, bytes_accessed=4_000_000, transcendentals=0),
    )(block, ax1, ax2, az1, az2)
    got = call(
        part(add_corners, len(ends), ca, cz),
        (grid,) + tuple(side for _ in ends),
        [VMEM] * (3 + len(ends)),
        [pltpu.VMEM((2,) + corner.shape, F32)],
        mib=8,
        alias={0: 0},
    )(block, corner1, corner2, *edges)
    block = got[0].reshape(5, planes, ROWS, cr)
    if n_rad == 2:
        sides = (lax.ppermute(got[1], "rad", [(0, 1), (1, 0)]),)
    else:
        up = [(i, i + 1) for i in range(n_rad - 1)]
        sides = (lax.ppermute(got[1], "rad", [(j, i) for i, j in up]), lax.ppermute(got[2], "rad", up))

    grid = (5, planes, TALL, cr)
    q, u2, u0 = call(
        part(stages, n_ax, n_rad, ca, cz, slots),
        (struct((ndev, 1, 128)), struct((5, ca + 4, TALL, cr)), struct((5, ca, ROWS, cr))),
        [VMEM, VMEM, HBM] + [VMEM] * (2 * len(sides)),
        [pltpu.VMEM((5, ca + 2 * MID, 8, cr), F32)]
        + [pltpu.VMEM(grid, F32) for _ in range(4)]
        + [pltpu.VMEM((3, planes, ROWS, cr), F32), pltpu.VMEM((128, cr), F32)]
        + [pltpu.SMEM((slots,), jnp.int32), pltpu.SemaphoreType.DMA],
        mib=28,
    )(block, banded, far(panel_cell), *sides, *places)

    rows = lax.all_to_all(q, ("y", "core", "az", "rad"), 0, 0, tiled=True).reshape(ndev, 128)

    grid = (5, ca + 4, TALL, cr)
    state = call(
        part(last_stage, ca, cz),
        struct((5, ca, cz, cr)),
        [VMEM] * 3,
        [pltpu.VMEM(grid, F32), pltpu.VMEM(grid, F32)],
        mib=12,
        cost=pl.CostEstimate(flops=400_000_000, bytes_accessed=8_000_000, transcendentals=0),
    )(u2, u0, banded)
    signal = call(
        part(signals, slots), struct((obs_weight.shape[0], NB)), [VMEM] * 3, mib=24
    )(rows, bin_offset, obs_weight)
    return (state, signal)


def solution(mesh):
    n_ax, n_az, n_rad = (mesh.shape[name] for name in ("ax", "az", "rad"))
    split = Mesh(mesh.devices.reshape(n_ax // 2, 2, n_az, n_rad), ("y", "core", "az", "rad"))
    ax = ("y", "core")
    every = ax + ("az", "rad")
    in_specs = (
        P(ax, "az", "rad"),
        P(None, ax, "az", "rad"),
        P(ax, "az", "rad"),
        P(every),
        P(every, None),
        P(every, None),
    )
    out_specs = (P(None, ax, "az", "rad"), P(every, None))
    return jax.shard_map(local, mesh=split, in_specs=in_specs, out_specs=out_specs, check_vma=False)
```

```python
import functools

import jax
import jax.numpy as jnp
from jax import lax
from jax.experimental import pallas as pl
from jax.experimental.pallas import tpu as pltpu
from jax.sharding import Mesh, PartitionSpec as P

NB = 128
GAMMA_M = 0.4
LAMBDA = 0.1
P_REF = 1.0
REACH = 6
MID = 4
SCALE = -LAMBDA / 12.0
ROWS = 32
OFF = 8
SPAN = 32
TALL = ROWS + 8
STEPS = 2
SLOT = 8
HBM = pltpu.MemorySpace.HBM
VMEM = pltpu.MemorySpace.VMEM
SMEM = pltpu.MemorySpace.SMEM
F32 = jnp.float32
BF16 = jnp.bfloat16


def call(kernel, outs, in_spaces, scratch=(), mib=8, cost=None, alias={}):
    return pl.pallas_call(
        kernel,
        out_shape=outs,
        in_specs=[pl.BlockSpec(memory_space=s) for s in in_spaces],
        out_specs=jax.tree.map(lambda _: pl.BlockSpec(memory_space=VMEM), outs),
        scratch_shapes=list(scratch),
        compiler_params=pltpu.CompilerParams(vmem_limit_bytes=mib * 1024 * 1024),
        cost_estimate=cost,
        input_output_aliases=alias,
    )


def far(x):
    return pltpu.with_memory_space_constraint(x, HBM)


def struct(shape, dtype=F32):
    return jax.ShapeDtypeStruct(shape, dtype)


def kept(row):
    return 8 * (row % 4) + row // 4


def ax_index():
    return lax.axis_index("y") * lax.axis_size("core") + lax.axis_index("core")


def first_is_up(axis):
    return lax.axis_index("core" if axis == "ax" else axis) % 2 == 0


def load_and_pack(ca, cz, den, vel, pre, home, ax1, ax2, az1, az2, sems):
    size = ca * cz
    copies = [
        pltpu.make_async_copy(den, home.at[pl.ds(0, size)], sems.at[0]),
        pltpu.make_async_copy(vel, home.at[pl.ds(size, 3 * size)], sems.at[1]),
        pltpu.make_async_copy(pre, home.at[pl.ds(4 * size, size)], sems.at[2]),
    ]
    for copy in copies:
        copy.start()
    for copy in copies:
        copy.wait()
    up = first_is_up("ax")
    edge = REACH * cz
    for f in range(5):
        at = f * size
        low = home[at : at + edge, :]
        high = home[at + size - edge : at + size, :]
        rows = slice(f * edge, (f + 1) * edge)
        ax1[rows, :] = jnp.where(up, high, low).astype(BF16)
        ax2[rows, :] = jnp.where(up, low, high).astype(BF16)
    up = first_is_up("az")
    low, high = [], []
    for f in range(5):
        for d in range(REACH):
            low.append(home[pl.ds(f * size + d, ca, stride=cz), :])
            high.append(home[pl.ds(f * size + cz - 1 - d, ca, stride=cz), :])
    low, high = jnp.concatenate(low, axis=0), jnp.concatenate(high, axis=0)
    az1[...] = jnp.where(up, high, low).astype(BF16)
    az2[...] = jnp.where(up, low, high).astype(BF16)


def ax_sides(n_ax, got1, got2, rows):
    ax = ax_index()
    a, b = got1[rows, :].astype(F32), got2[rows, :].astype(F32)
    up = first_is_up("ax")
    lo = jnp.where(ax == 0, 0.0, jnp.where(up, b, a))
    hi = jnp.where(ax == n_ax - 1, 0.0, jnp.where(up, a, b))
    return lo, hi


def pack_corners(n_ax, cz, got1, got2, first_out, second_out, near):
    up = first_is_up("az")
    half = MID * cz
    size = REACH * cz
    for f in range(5):
        lo, hi = ax_sides(n_ax, got1, got2, slice(f * size, (f + 1) * size))
        near[f, 0:half, :] = lo[size - half :]
        near[f, half : 2 * half, :] = hi[0:half]
    low, high = [], []
    for f in range(5):
        for d in range(MID):
            low.append(near[f, pl.ds(d, 2 * MID, stride=cz), :])
            high.append(near[f, pl.ds(cz - 1 - d, 2 * MID, stride=cz), :])
    low, high = jnp.concatenate(low, axis=0), jnp.concatenate(high, axis=0)
    first_out[...] = jnp.where(up, high, low).astype(BF16)
    second_out[...] = jnp.where(up, low, high).astype(BF16)


def spread_rows(planes, cz, f, plane, ref, at, block):
    quarter = cz // 4
    for l in range(4):
        row = (f * planes + plane) * ROWS + 8 * l + OFF // 4
        block[pl.ds(row, quarter), :] = ref[pl.ds(at + l, quarter, stride=4), :]


def prepare(ends, ca, cz, n_rad, home, block, banded, *tables):
    cr = home.shape[1]
    rad = lax.axis_index("rad")
    for f in range(5):
        for k in range(ca):
            spread_rows(ca + 2 * REACH, cz, f, REACH + k, home, (f * ca + k) * cz, block)
    banded[...] = band(cr)
    edges, places = tables[: len(ends)], tables[len(ends) :]
    tiles = cr // SLOT
    there = {"high": jnp.where(rad < n_rad - 1, 1.0, 0.0), "low": jnp.where(rad > 0, 1.0, 0.0)}
    high = place_matrix(0, tiles, cr) * there["high"]
    low = place_matrix(SPAN - REACH, tiles, cr) * there["low"]
    for end, edge, place in zip(ends, edges, places):
        start = {"low": 0, "high": cr - REACH, "either": jnp.where(rad == 0, cr - REACH, 0)}[end]
        edge[...] = edge_matrix(start, tiles, cr)
        place[...] = {"low": high, "high": low, "either": high + low}[end].astype(BF16)


def edge_matrix(start, tiles, cr):
    k = lax.broadcasted_iota(jnp.int32, (tiles * cr, tiles * SLOT), 0)
    n = lax.broadcasted_iota(jnp.int32, (tiles * cr, tiles * SLOT), 1)
    hit = (k // cr == n // SLOT) & (n % SLOT < REACH) & (k % cr == n % SLOT + start)
    return jnp.where(hit, 1.0, 0.0).astype(BF16)


def place_matrix(start, tiles, cr):
    k = lax.broadcasted_iota(jnp.int32, (tiles * SLOT, tiles * cr // 4), 0)
    n = lax.broadcasted_iota(jnp.int32, (tiles * SLOT, tiles * cr // 4), 1)
    hit = (k // SLOT == n // SPAN) & (k % SLOT < REACH) & (n % SPAN == k % SLOT + start)
    return jnp.where(hit, 1.0, 0.0)


def add_sides(n_ax, ca, cz, block_in, ax1, ax2, az1, az2, block, sides, strips):
    planes = ca + 2 * REACH
    size = REACH * cz
    for f in range(5):
        lo, hi = ax_sides(n_ax, ax1, ax2, slice(f * size, (f + 1) * size))
        sides[f, 0:size, :] = lo
        sides[f, size : 2 * size, :] = hi
    for f in range(5):
        for k in range(REACH):
            spread_rows(planes, cz, f, k, sides.at[f], k * cz, block)
            spread_rows(planes, cz, f, REACH + ca + k, sides.at[f], size + k * cz, block)
    up = first_is_up("az")
    a, b = az1[...].astype(F32), az2[...].astype(F32)
    strips[0] = jnp.where(up, b, a)
    strips[1] = jnp.where(up, a, b)
    for f in range(5):
        for d in range(REACH):
            for side, row in ((0, OFF - 1 - d), (1, OFF + cz + d)):
                at = kept(row) + (f * planes + REACH) * ROWS
                block[pl.ds(at, ca, stride=ROWS), :] = strips[side, pl.ds((f * REACH + d) * ca, ca), :]


def add_corners(count, ca, cz, block_in, corner1, corner2, *rest):
    edges, block, outs, corners = rest[:count], rest[count], rest[count + 1 : -1], rest[-1]
    cr = corner1.shape[1]
    planes = ca + 2 * REACH
    up = first_is_up("az")
    a, b = corner1[...].astype(F32), corner2[...].astype(F32)
    corners[0] = jnp.where(up, b, a)
    corners[1] = jnp.where(up, a, b)
    for f in range(5):
        for d in range(MID):
            for side, row in ((0, OFF - 1 - d), (1, OFF + cz + d)):
                at = kept(row) + f * planes * ROWS
                start = (f * MID + d) * 2 * MID
                got = corners[side, pl.ds(start, MID), :]
                block[pl.ds(at + (REACH - MID) * ROWS, MID, stride=ROWS), :] = got
                got = corners[side, pl.ds(start + MID, MID), :]
                block[pl.ds(at + (REACH + ca) * ROWS, MID, stride=ROWS), :] = got

    tiles = cr // SLOT
    step = tiles * 8
    rows = []
    for f in range(5):
        for k in range((ca + 2 * MID) * ROWS // step):
            at = (f * planes + REACH - MID) * ROWS + k * step
            rows.append(jnp.concatenate([block[at + 8 * t : at + 8 * t + 8, :] for t in range(tiles)], axis=1))
    rows = jnp.concatenate(rows, axis=0).astype(BF16)
    for edge, out in zip(edges, outs):
        out[...] = jnp.dot(rows, edge[...], preferred_element_type=F32).astype(BF16)


def az_terms(flux):
    v = [flux[8 * l : 8 * l + 8] for l in range(4)]
    v = [pltpu.roll(v[2], 1, 0), pltpu.roll(v[3], 1, 0)] + v + [pltpu.roll(v[0], 7, 0), pltpu.roll(v[1], 7, 0)]
    out = [8.0 * (v[l + 3] - v[l + 1]) - (v[l + 4] - v[l]) for l in range(4)]
    side = flux[ROWS:]
    lanes = side.shape[1]
    span = lax.broadcasted_iota(jnp.int32, side.shape, 1) // SPAN
    up, down = pltpu.roll(side, 7, 0), pltpu.roll(side, 1, 0)
    up1 = pltpu.roll(jnp.where(span == 0, up, side), lanes - SPAN, 1)
    up2 = pltpu.roll(jnp.where(span < 2, up, side), lanes - 2 * SPAN, 1)
    down1 = pltpu.roll(jnp.where(span == 3, down, side), SPAN, 1)
    down2 = pltpu.roll(jnp.where(span >= 2, down, side), 2 * SPAN, 1)
    out.append(8.0 * (up1 - down1) - (up2 - down2))
    return jnp.concatenate(out, axis=0)


def band(cr):
    def place(axis, none):
        i = lax.broadcasted_iota(jnp.int32, (2 * cr, 2 * cr), axis)
        j = i % SPAN
        beyond = jnp.where(j < REACH, cr + j, jnp.where(j >= SPAN - REACH, j - SPAN, none))
        return jnp.where(i < cr, i, beyond), jnp.where(i < cr, -1, i // SPAN)

    k, k_span = place(0, 4 * cr)
    n, n_span = place(1, -4 * cr)
    gap = k - n
    out = jnp.where(gap == 1, 8.0, 0.0) + jnp.where(gap == -1, -8.0, 0.0)
    out = out + jnp.where(gap == 2, -1.0, 0.0) + jnp.where(gap == -2, 1.0, 0.0)
    apart = (k_span >= 0) & (n_span >= 0) & (k_span != n_span)
    return jnp.where(apart, 0.0, out).astype(BF16)


def split_state(u):
    rho, m0, m1, m2, energy = u
    inv = 1.0 / rho
    vel = [m0 * inv, m1 * inv, m2 * inv]
    pres = GAMMA_M * (energy - 0.5 * (m0 * vel[0] + m1 * vel[1] + m2 * vel[2]))
    return [m0, m1, m2], vel, pres, energy


def flux(d, mom, vel, pres, energy):
    parts = [mom[d]]
    for j in range(3):
        parts.append(mom[d] * vel[j] + pres if j == d else mom[d] * vel[j])
    parts.append((energy + pres) * vel[d])
    return parts


def ax_only(u, fax, j):
    got = flux(0, *u)
    for f in range(5):
        fax[f, j, 0:ROWS] = got[f]


def both_sides(us, js, fax, part, banded):
    rows = []
    shape = (ROWS, banded.shape[0] // 2)
    span = lax.broadcasted_iota(jnp.int32, shape, 1) // SPAN
    mine = span == lax.broadcasted_iota(jnp.int32, shape, 0) // 8
    for u, j in zip(us, js):
        got = flux(0, *u)
        for f in range(5):
            fax[f, j] = got[f]
        got = flux(2, *u)
        for f in range(5):
            side = jnp.where(mine, jnp.concatenate([got[f][ROWS:]] * 4, axis=0), 0.0)
            rows.append(jnp.concatenate([got[f][0:ROWS], side], axis=1))
    rows = jnp.concatenate(rows, axis=0).astype(BF16)
    out = jnp.dot(rows, banded[...], preferred_element_type=F32)
    half = out.shape[1] // 2
    for i, (u, j) in enumerate(zip(us, js)):
        got = flux(1, *u)
        for f in range(5):
            at = (i * 5 + f) * ROWS
            side = out[at : at + 8, half:]
            for l in range(1, 4):
                side = jnp.where(span[0:8] == l, out[at + 8 * l : at + 8 * l + 8, half:], side)
            radial = jnp.concatenate([out[at : at + ROWS, 0:half], side], axis=0)
            part[f, j] = az_terms(got[f]) + radial


def change(fa, part, f, j, size):
    near = fa(j + 1)[0:size] - fa(j - 1)[0:size]
    far = fa(j + 2)[0:size] - fa(j - 2)[0:size]
    return SCALE * (8.0 * near - far + part[f, j, 0:size])


def window(fax, f):
    held = {}

    def get(j):
        if j not in held:
            held[j] = fax[f, j]
        return held[j]

    return get


def stages(n_ax, n_rad, ca, cz, slots, block, banded, cells_far, *refs):
    sides, refs = refs[: len(refs) - 12], refs[len(refs) - 12 :]
    sides, places = sides[: len(sides) // 2], sides[len(sides) // 2 :]
    q_out, u2_out, u0_out, ghost, first, second, fax, part, value, picked, cells, cells_sem = refs
    fetch = pltpu.make_async_copy(cells_far, cells, cells_sem)
    fetch.start()
    cr = block.shape[-1]
    low, high = REACH, REACH + ca
    ax = ax_index()
    rad = lax.axis_index("rad")

    lane = lax.broadcasted_iota(jnp.int32, (8, cr), 1)
    row = 4 * lax.broadcasted_iota(jnp.int32, (8, cr), 0) + lane // SPAN
    j = lane % SPAN
    steps_rad = jnp.where(
        (j < REACH) & (rad < n_rad - 1),
        1 + j // 2,
        jnp.where((j >= SPAN - REACH) & (rad > 0), 1 + (SPAN - 1 - j) // 2, 99),
    )
    beyond_row = jnp.maximum(OFF - row, row - (OFF + cz - 1))
    steps = steps_rad + jnp.where(beyond_row > 0, (beyond_row + 1) // 2, 0)
    base0 = jnp.where(steps_rad < 99, 0.0, 1.0)

    side = 0.0
    for got, place in zip(sides, places):
        side = side + jnp.dot(got[...], place[...], preferred_element_type=F32)
    group = side.shape[1] // cr
    count = (ca + 2 * MID) // group
    for f in range(5):
        for k in range(count):
            for i in range(group):
                at = (f * count + k) * 8
                tile = side[at : at + 8, i * cr : (i + 1) * cr]
                ghost[f, k * group + i] = tile + base0 if f == 0 else tile

    def start_state(j, both):
        u = []
        for f in range(5):
            x = block[f, j]
            u.append(jnp.concatenate([x, ghost[f, j - (REACH - MID)]], axis=0) if both else x)
        rho, vel, pres = u[0], u[1:4], u[4]
        mom = [rho * x for x in vel]
        energy = pres * (1.0 / GAMMA_M) + 0.5 * (mom[0] * vel[0] + mom[1] * vel[1] + mom[2] * vel[2])
        return rho, (mom, vel, pres, energy)

    def note(s, j, u):
        value[s, j] = (u[2] - P_REF + u[0][0])[0:ROWS]

    for j in (low - 6, low - 5, high + 4, high + 5):
        ax_only(start_state(j, False)[1], fax, j)

    step = (ca + 2 * MID) // STEPS

    @pl.loop(0, STEPS)
    def _(i):
        js = [low - 4 + step * i + k for k in range(step)]
        us = []
        for j in js:
            rho, u = start_state(j, True)
            for f, x in enumerate([rho] + u[0] + [u[3]]):
                first[f, j] = x
            note(0, j, u)
            us.append(u)
        both_sides(us, js, fax, part, banded)

    def update(f, j, fa, stage):
        a = max(low - j, j - (high - 1), 0)
        a = (a + 1) // 2
        lim = 2 - stage
        base = jnp.where(f == 0, 1.0, 0.0)
        size = ROWS if a == lim else TALL
        new = change(fa, part, f, j, size)
        u0 = first[f, j, 0:size]
        if stage == 0:
            new = u0 + new
        else:
            new = 0.75 * u0 + 0.25 * (second[f, j, 0:size] + new)
        beyond = (ax == 0) if j < low else (ax == n_ax - 1)
        home = new[0:ROWS]
        if a > 0:
            home = jnp.where(beyond, base, home)
        if size == ROWS:
            return home, None
        ok = steps <= lim - a
        if a > 0:
            ok = ok & jnp.logical_not(beyond)
        return home, jnp.where(ok, new[ROWS:], base)

    @pl.loop(0, 5)
    def _(f):
        fa = window(fax, f)
        for j in range(low - 4, high + 4):
            home, side = update(f, j, fa, 0)
            second[f, j, 0:ROWS] = home
            if side is not None:
                second[f, j, ROWS:] = side

    for j in (low - 4, low - 3, high + 2, high + 3):
        ax_only(split_state([second[f, j, 0:ROWS] for f in range(5)]), fax, j)

    step2 = (ca + MID) // STEPS

    @pl.loop(0, STEPS)
    def _(i):
        js = [low - 2 + step2 * i + k for k in range(step2)]
        us = []
        for j in js:
            u = split_state([second[f, j] for f in range(5)])
            note(1, j, u)
            us.append(u)
        both_sides(us, js, fax, part, banded)

    @pl.loop(0, 5)
    def _(f):
        fa = window(fax, f)
        for j in range(low - 2, high + 2):
            home, side = update(f, j, fa, 1)
            u2_out[f, j - (low - 2), 0:ROWS] = home
            if side is not None:
                u2_out[f, j - (low - 2), ROWS:] = side
        for j in range(low, high):
            u0_out[f, j - low] = first[f, j, 0:ROWS]

    @pl.loop(0, ca)
    def _(i):
        u = split_state([u2_out[f, i + 2, 0:ROWS] for f in range(5)])
        note(2, low + i, u)

    fetch.wait()
    picked[...] = jnp.zeros_like(picked)
    lanes = lax.broadcasted_iota(jnp.int32, (1, cr), 1)
    for p in range(slots):
        cell = cells[p]
        at = jnp.maximum(cell, 0)
        column = jnp.where(cell >= 0, lax.rem(at, cr), -1)
        at = lax.div(at, cr)
        plane = low + lax.div(at, cz)
        r = lax.rem(at, cz) + OFF
        r = 8 * lax.rem(r, 4) + lax.div(r, 4)
        hit = lanes == column
        for s in range(3):
            picked[pl.ds(s * slots + p, 1), :] = jnp.where(hit, value[s, plane, pl.ds(r, 1), :], 0.0)
    q = lax.dot_general(
        jnp.ones((8, cr), BF16),
        picked[...].astype(BF16),
        (((1,), (1,)), ((), ())),
        preferred_element_type=F32,
    )
    q_out[...] = jnp.broadcast_to(q[0:1][None], q_out.shape)


def last_stage(ca, cz, u2, u0, banded, state, fax, part):
    for j in (0, 1, ca + 2, ca + 3):
        ax_only(split_state([u2[f, j, 0:ROWS] for f in range(5)]), fax, j)

    step = ca // STEPS

    @pl.loop(0, STEPS)
    def _(i):
        js = [2 + step * i + k for k in range(step)]
        us = [split_state([u2[f, j] for f in range(5)]) for j in js]
        both_sides(us, js, fax, part, banded)

    first, quarter = OFF // 4, cz // 4

    @pl.loop(0, 5)
    def _(f):
        fa = window(fax, f)
        for k in range(ca):
            j = k + 2
            new = u2[f, j, 0:ROWS] + change(fa, part, f, j, ROWS)
            new = u0[f, k] * (1.0 / 3.0) + (2.0 / 3.0) * new
            for l in range(4):
                state[f, k, pl.ds(l, quarter, stride=4), :] = new[8 * l + first : 8 * l + first + quarter]


def signals(slots, rows, offsets, weight, out):
    ndev = rows.shape[0]
    group = 32
    cols = group * slots
    lanes = rows.shape[1]
    col = lax.broadcasted_iota(jnp.int32, (1, cols), 1)
    owner = lax.broadcasted_iota(jnp.int32, (group, cols), 0) == col // slots
    lane = lax.broadcasted_iota(jnp.int32, (lanes, cols), 0)
    time = lax.broadcasted_iota(jnp.int32, (NB, cols), 0).astype(F32)
    total = jnp.zeros(out.shape, F32)
    for g in range(ndev // group):
        q = rows[g * group : (g + 1) * group, :].astype(BF16)
        off = offsets[0:1, g * group : (g + 1) * group].astype(F32)
        off = jnp.broadcast_to(off, (8, group)).astype(BF16)
        bins = jnp.dot(off, owner.astype(BF16), preferred_element_type=F32)[0:1]
        table = jnp.zeros((NB, cols), F32)
        for s in range(3):
            pick = jnp.where(lane == s * slots + col % slots, 1.0, 0.0).astype(BF16)
            spread = jnp.dot(q, pick, preferred_element_type=F32)
            line = jnp.sum(jnp.where(owner, spread, 0.0), axis=0, keepdims=True)
            table = jnp.where(time == bins + s, line, table)
        total = total + lax.dot_general(
            weight[:, g * cols : (g + 1) * cols],
            table.astype(BF16),
            (((1,), (1,)), ((), ())),
            preferred_element_type=F32,
        )
    out[...] = total


def swap_pairs(count, periodic):
    one = [(i, i ^ 1) for i in range(count)]
    two = []
    for i in range(count):
        j = i - 1 if i % 2 == 0 else i + 1
        two.append((i, j % count if periodic or 0 <= j < count else i))
    return one, two


def swap(first, second, axis, periodic):
    count = 1
    for name in (axis,) if isinstance(axis, str) else axis:
        count = count * lax.axis_size(name)
    one, two = swap_pairs(count, periodic)
    return lax.ppermute(first, axis, one), lax.ppermute(second, axis, two)


def local(density, velocity, pressure, panel_cell, obs_weight, bin_offset):
    ca, cz, cr = density.shape
    slots = panel_cell.shape[0]
    ndev = bin_offset.shape[1]
    n_ax, n_rad = lax.axis_size("y") * lax.axis_size("core"), lax.axis_size("rad")
    planes = ca + 2 * REACH
    part = functools.partial
    given = (density.reshape(ca * cz, cr), velocity.reshape(3 * ca * cz, cr), pressure.reshape(ca * cz, cr))

    edge = struct((5 * REACH * cz, cr), BF16)
    strip = struct((5 * REACH * ca, cr), BF16)
    home, ax1, ax2, az1, az2 = call(
        part(load_and_pack, ca, cz),
        (struct((5 * ca * cz, cr)), edge, edge, strip, strip),
        [HBM] * 3,
        [pltpu.SemaphoreType.DMA((3,))],
    )(*[far(x) for x in given])
    ax1, ax2 = swap(ax1, ax2, ("y", "core"), False)
    az1, az2 = swap(az1, az2, "az", True)
    grid = struct((5 * planes * ROWS, cr))
    ends = ("either",) if n_rad == 2 else ("low", "high")
    tiles = cr // SLOT
    table = [struct((tiles * cr, cr), BF16)] * len(ends) + [struct((cr, tiles * cr // 4), BF16)] * len(ends)
    block, banded, *tables = call(
        part(prepare, ends, ca, cz, n_rad),
        (grid, struct((2 * cr, 2 * cr), BF16), *table),
        [VMEM],
    )(home)
    edges, places = tables[: len(ends)], tables[len(ends) :]

    corner = struct((5 * MID * 2 * MID, cr), BF16)
    near = pltpu.VMEM((5, 2 * MID * cz, cr), F32)
    corner1, corner2 = call(part(pack_corners, n_ax, cz), (corner, corner), [VMEM] * 2, [near])(ax1, ax2)
    corner1, corner2 = swap(corner1, corner2, "az", True)

    side = struct((5 * (ca + 2 * MID) * ROWS // tiles, cr), BF16)
    block = call(
        part(add_sides, n_ax, ca, cz),
        grid,
        [VMEM] * 5,
        [pltpu.VMEM((5, 2 * REACH * cz, cr), F32), pltpu.VMEM((2,) + strip.shape, F32)],
        mib=8,
        alias={0: 0},
        cost=pl.CostEstimate(flops=100_000_000, bytes_accessed=4_000_000, transcendentals=0),
    )(block, ax1, ax2, az1, az2)
    got = call(
        part(add_corners, len(ends), ca, cz),
        (grid,) + tuple(side for _ in ends),
        [VMEM] * (3 + len(ends)),
        [pltpu.VMEM((2,) + corner.shape, F32)],
        mib=8,
        alias={0: 0},
    )(block, corner1, corner2, *edges)
    block = got[0].reshape(5, planes, ROWS, cr)
    if n_rad == 2:
        sides = (lax.ppermute(got[1], "rad", [(0, 1), (1, 0)]),)
    else:
        up = [(i, i + 1) for i in range(n_rad - 1)]
        sides = (lax.ppermute(got[1], "rad", [(j, i) for i, j in up]), lax.ppermute(got[2], "rad", up))

    grid = (5, planes, TALL, cr)
    q, u2, u0 = call(
        part(stages, n_ax, n_rad, ca, cz, slots),
        (struct((ndev, 1, 128)), struct((5, ca + 4, TALL, cr)), struct((5, ca, ROWS, cr))),
        [VMEM, VMEM, HBM] + [VMEM] * (2 * len(sides)),
        [pltpu.VMEM((5, ca + 2 * MID, 8, cr), F32)]
        + [pltpu.VMEM(grid, F32) for _ in range(4)]
        + [pltpu.VMEM((3, planes, ROWS, cr), F32), pltpu.VMEM((128, cr), F32)]
        + [pltpu.SMEM((slots,), jnp.int32), pltpu.SemaphoreType.DMA],
        mib=28,
    )(block, banded, far(panel_cell), *sides, *places)

    rows = lax.all_to_all(q, ("y", "core", "az", "rad"), 0, 0, tiled=True).reshape(ndev, 128)

    grid = (5, ca + 4, TALL, cr)
    state = call(
        part(last_stage, ca, cz),
        struct((5, ca, cz, cr)),
        [VMEM] * 3,
        [pltpu.VMEM(grid, F32), pltpu.VMEM(grid, F32)],
        mib=12,
        cost=pl.CostEstimate(flops=400_000_000, bytes_accessed=8_000_000, transcendentals=0),
    )(u2, u0, banded)
    signal = call(
        part(signals, slots), struct((obs_weight.shape[0], NB)), [VMEM] * 3, mib=24
    )(rows, bin_offset, obs_weight)
    return (state, signal)


def solution(mesh):
    n_ax, n_az, n_rad = (mesh.shape[name] for name in ("ax", "az", "rad"))
    split = Mesh(mesh.devices.reshape(n_ax // 2, 2, n_az, n_rad), ("y", "core", "az", "rad"))
    ax = ("y", "core")
    every = ax + ("az", "rad")
    in_specs = (
        P(ax, "az", "rad"),
        P(None, ax, "az", "rad"),
        P(ax, "az", "rad"),
        P(every),
        P(every, None),
        P(every, None),
    )
    out_specs = (P(None, ax, "az", "rad"), P(every, None))
    return jax.shard_map(local, mesh=split, in_specs=in_specs, out_specs=out_specs, check_vma=False)
```

```python
import functools

import jax
import jax.numpy as jnp
from jax import lax
from jax.experimental import pallas as pl
from jax.experimental.pallas import tpu as pltpu
from jax.sharding import Mesh, PartitionSpec as P

NB = 128
GAMMA_M = 0.4
LAMBDA = 0.1
P_REF = 1.0
REACH = 6
MID = 4
SCALE = -LAMBDA / 12.0
ROWS = 32
OFF = 8
SPAN = 32
TALL = ROWS + 8
STEPS = 1
SLOT = 8
HBM = pltpu.MemorySpace.HBM
VMEM = pltpu.MemorySpace.VMEM
SMEM = pltpu.MemorySpace.SMEM
F32 = jnp.float32
BF16 = jnp.bfloat16


def call(kernel, outs, in_spaces, scratch=(), mib=8, cost=None, alias={}):
    return pl.pallas_call(
        kernel,
        out_shape=outs,
        in_specs=[pl.BlockSpec(memory_space=s) for s in in_spaces],
        out_specs=jax.tree.map(lambda _: pl.BlockSpec(memory_space=VMEM), outs),
        scratch_shapes=list(scratch),
        compiler_params=pltpu.CompilerParams(vmem_limit_bytes=mib * 1024 * 1024),
        cost_estimate=cost,
        input_output_aliases=alias,
    )


def far(x):
    return pltpu.with_memory_space_constraint(x, HBM)


def struct(shape, dtype=F32):
    return jax.ShapeDtypeStruct(shape, dtype)


def kept(row):
    return 8 * (row % 4) + row // 4


def ax_index():
    return lax.axis_index("y") * lax.axis_size("core") + lax.axis_index("core")


def first_is_up(axis):
    if axis == "ax":
        return lax.axis_index("core") == 0
    return lax.axis_index("az") % 2 == 1


def load_and_pack(ca, cz, den, vel, pre, home, ax1, ax2, az1, az2, sems):
    size = ca * cz
    copies = [
        pltpu.make_async_copy(den, home.at[pl.ds(0, size)], sems.at[0]),
        pltpu.make_async_copy(vel, home.at[pl.ds(size, 3 * size)], sems.at[1]),
        pltpu.make_async_copy(pre, home.at[pl.ds(4 * size, size)], sems.at[2]),
    ]
    for copy in copies:
        copy.start()
    for copy in copies:
        copy.wait()
    up = first_is_up("ax")
    edge = REACH * cz
    for f in range(5):
        at = f * size
        low = home[at : at + edge, :]
        high = home[at + size - edge : at + size, :]
        rows = slice(f * edge, (f + 1) * edge)
        ax1[rows, :] = jnp.where(up, high, low).astype(BF16)
        ax2[rows, :] = jnp.where(up, low, high).astype(BF16)
    up = first_is_up("az")
    low, high = [], []
    for f in range(5):
        for d in range(REACH):
            low.append(home[pl.ds(f * size + d, ca, stride=cz), :])
            high.append(home[pl.ds(f * size + cz - 1 - d, ca, stride=cz), :])
    low, high = jnp.concatenate(low, axis=0), jnp.concatenate(high, axis=0)
    az1[...] = jnp.where(up, high, low).astype(BF16)
    az2[...] = jnp.where(up, low, high).astype(BF16)


def ax_sides(n_ax, got1, got2, rows):
    ax = ax_index()
    a, b = got1[rows, :].astype(F32), got2[rows, :].astype(F32)
    up = first_is_up("ax")
    lo = jnp.where(ax == 0, 0.0, jnp.where(up, b, a))
    hi = jnp.where(ax == n_ax - 1, 0.0, jnp.where(up, a, b))
    return lo, hi


def pack_corners(n_ax, cz, got1, got2, first_out, second_out, near):
    up = first_is_up("az")
    half = MID * cz
    size = REACH * cz
    for f in range(5):
        lo, hi = ax_sides(n_ax, got1, got2, slice(f * size, (f + 1) * size))
        near[f, 0:half, :] = lo[size - half :]
        near[f, half : 2 * half, :] = hi[0:half]
    low, high = [], []
    for f in range(5):
        for d in range(MID):
            low.append(near[f, pl.ds(d, 2 * MID, stride=cz), :])
            high.append(near[f, pl.ds(cz - 1 - d, 2 * MID, stride=cz), :])
    low, high = jnp.concatenate(low, axis=0), jnp.concatenate(high, axis=0)
    first_out[...] = jnp.where(up, high, low).astype(BF16)
    second_out[...] = jnp.where(up, low, high).astype(BF16)


def spread_rows(planes, cz, f, plane, ref, at, block):
    quarter = cz // 4
    for l in range(4):
        row = (f * planes + plane) * ROWS + 8 * l + OFF // 4
        block[pl.ds(row, quarter), :] = ref[pl.ds(at + l, quarter, stride=4), :]


def prepare(ends, ca, cz, n_rad, home, block, banded, *tables):
    cr = home.shape[1]
    rad = lax.axis_index("rad")
    for f in range(5):
        for k in range(ca):
            spread_rows(ca + 2 * REACH, cz, f, REACH + k, home, (f * ca + k) * cz, block)
    banded[...] = band(cr)
    edges, places = tables[: len(ends)], tables[len(ends) :]
    tiles = cr // SLOT
    there = {"high": jnp.where(rad < n_rad - 1, 1.0, 0.0), "low": jnp.where(rad > 0, 1.0, 0.0)}
    high = place_matrix(0, tiles, cr) * there["high"]
    low = place_matrix(SPAN - REACH, tiles, cr) * there["low"]
    for end, edge, place in zip(ends, edges, places):
        start = {"low": 0, "high": cr - REACH, "either": jnp.where(rad == 0, cr - REACH, 0)}[end]
        edge[...] = edge_matrix(start, tiles, cr)
        place[...] = {"low": high, "high": low, "either": high + low}[end].astype(BF16)


def edge_matrix(start, tiles, cr):
    k = lax.broadcasted_iota(jnp.int32, (tiles * cr, tiles * SLOT), 0)
    n = lax.broadcasted_iota(jnp.int32, (tiles * cr, tiles * SLOT), 1)
    hit = (k // cr == n // SLOT) & (n % SLOT < REACH) & (k % cr == n % SLOT + start)
    return jnp.where(hit, 1.0, 0.0).astype(BF16)


def place_matrix(start, tiles, cr):
    k = lax.broadcasted_iota(jnp.int32, (tiles * SLOT, tiles * cr // 4), 0)
    n = lax.broadcasted_iota(jnp.int32, (tiles * SLOT, tiles * cr // 4), 1)
    hit = (k // SLOT == n // SPAN) & (k % SLOT < REACH) & (n % SPAN == k % SLOT + start)
    return jnp.where(hit, 1.0, 0.0)


def add_sides(n_ax, ca, cz, block_in, ax1, ax2, az1, az2, block, sides, strips):
    planes = ca + 2 * REACH
    size = REACH * cz
    for f in range(5):
        lo, hi = ax_sides(n_ax, ax1, ax2, slice(f * size, (f + 1) * size))
        sides[f, 0:size, :] = lo
        sides[f, size : 2 * size, :] = hi
    for f in range(5):
        for k in range(REACH):
            spread_rows(planes, cz, f, k, sides.at[f], k * cz, block)
            spread_rows(planes, cz, f, REACH + ca + k, sides.at[f], size + k * cz, block)
    up = first_is_up("az")
    a, b = az1[...].astype(F32), az2[...].astype(F32)
    strips[0] = jnp.where(up, b, a)
    strips[1] = jnp.where(up, a, b)
    for f in range(5):
        for d in range(REACH):
            for side, row in ((0, OFF - 1 - d), (1, OFF + cz + d)):
                at = kept(row) + (f * planes + REACH) * ROWS
                block[pl.ds(at, ca, stride=ROWS), :] = strips[side, pl.ds((f * REACH + d) * ca, ca), :]


def add_corners(count, ca, cz, block_in, corner1, corner2, *rest):
    edges, block, outs, corners = rest[:count], rest[count], rest[count + 1 : -1], rest[-1]
    cr = corner1.shape[1]
    planes = ca + 2 * REACH
    up = first_is_up("az")
    a, b = corner1[...].astype(F32), corner2[...].astype(F32)
    corners[0] = jnp.where(up, b, a)
    corners[1] = jnp.where(up, a, b)
    for f in range(5):
        for d in range(MID):
            for side, row in ((0, OFF - 1 - d), (1, OFF + cz + d)):
                at = kept(row) + f * planes * ROWS
                start = (f * MID + d) * 2 * MID
                got = corners[side, pl.ds(start, MID), :]
                block[pl.ds(at + (REACH - MID) * ROWS, MID, stride=ROWS), :] = got
                got = corners[side, pl.ds(start + MID, MID), :]
                block[pl.ds(at + (REACH + ca) * ROWS, MID, stride=ROWS), :] = got

    tiles = cr // SLOT
    step = tiles * 8
    rows = []
    for f in range(5):
        for k in range((ca + 2 * MID) * ROWS // step):
            at = (f * planes + REACH - MID) * ROWS + k * step
            rows.append(jnp.concatenate([block[at + 8 * t : at + 8 * t + 8, :] for t in range(tiles)], axis=1))
    rows = jnp.concatenate(rows, axis=0).astype(BF16)
    for edge, out in zip(edges, outs):
        out[...] = jnp.dot(rows, edge[...], preferred_element_type=F32).astype(BF16)


def az_terms(flux):
    v = [flux[8 * l : 8 * l + 8] for l in range(4)]
    v = [pltpu.roll(v[2], 1, 0), pltpu.roll(v[3], 1, 0)] + v + [pltpu.roll(v[0], 7, 0), pltpu.roll(v[1], 7, 0)]
    out = [8.0 * (v[l + 3] - v[l + 1]) - (v[l + 4] - v[l]) for l in range(4)]
    side = flux[ROWS:]
    lanes = side.shape[1]
    span = lax.broadcasted_iota(jnp.int32, side.shape, 1) // SPAN
    up, down = pltpu.roll(side, 7, 0), pltpu.roll(side, 1, 0)
    up1 = pltpu.roll(jnp.where(span == 0, up, side), lanes - SPAN, 1)
    up2 = pltpu.roll(jnp.where(span < 2, up, side), lanes - 2 * SPAN, 1)
    down1 = pltpu.roll(jnp.where(span == 3, down, side), SPAN, 1)
    down2 = pltpu.roll(jnp.where(span >= 2, down, side), 2 * SPAN, 1)
    out.append(8.0 * (up1 - down1) - (up2 - down2))
    return jnp.concatenate(out, axis=0)


def band(cr):
    def place(axis, none):
        i = lax.broadcasted_iota(jnp.int32, (2 * cr, 2 * cr), axis)
        j = i % SPAN
        beyond = jnp.where(j < REACH, cr + j, jnp.where(j >= SPAN - REACH, j - SPAN, none))
        return jnp.where(i < cr, i, beyond), jnp.where(i < cr, -1, i // SPAN)

    k, k_span = place(0, 4 * cr)
    n, n_span = place(1, -4 * cr)
    gap = k - n
    out = jnp.where(gap == 1, 8.0, 0.0) + jnp.where(gap == -1, -8.0, 0.0)
    out = out + jnp.where(gap == 2, -1.0, 0.0) + jnp.where(gap == -2, 1.0, 0.0)
    apart = (k_span >= 0) & (n_span >= 0) & (k_span != n_span)
    return jnp.where(apart, 0.0, out).astype(BF16)


def split_state(u):
    rho, m0, m1, m2, energy = u
    inv = 1.0 / rho
    vel = [m0 * inv, m1 * inv, m2 * inv]
    pres = GAMMA_M * (energy - 0.5 * (m0 * vel[0] + m1 * vel[1] + m2 * vel[2]))
    return [m0, m1, m2], vel, pres, energy


def flux(d, mom, vel, pres, energy):
    parts = [mom[d]]
    for j in range(3):
        parts.append(mom[d] * vel[j] + pres if j == d else mom[d] * vel[j])
    parts.append((energy + pres) * vel[d])
    return parts


def ax_only(u, fax, j):
    got = flux(0, *u)
    for f in range(5):
        fax[f, j, 0:ROWS] = got[f]


def both_sides(us, js, fax, part, banded):
    rows = []
    shape = (ROWS, banded.shape[0] // 2)
    span = lax.broadcasted_iota(jnp.int32, shape, 1) // SPAN
    mine = span == lax.broadcasted_iota(jnp.int32, shape, 0) // 8
    for u, j in zip(us, js):
        got = flux(0, *u)
        for f in range(5):
            fax[f, j] = got[f]
        got = flux(2, *u)
        for f in range(5):
            side = jnp.where(mine, jnp.concatenate([got[f][ROWS:]] * 4, axis=0), 0.0)
            rows.append(jnp.concatenate([got[f][0:ROWS], side], axis=1))
    rows = jnp.concatenate(rows, axis=0).astype(BF16)
    out = jnp.dot(rows, banded[...], preferred_element_type=F32)
    half = out.shape[1] // 2
    for i, (u, j) in enumerate(zip(us, js)):
        got = flux(1, *u)
        for f in range(5):
            at = (i * 5 + f) * ROWS
            side = out[at : at + 8, half:]
            for l in range(1, 4):
                side = jnp.where(span[0:8] == l, out[at + 8 * l : at + 8 * l + 8, half:], side)
            radial = jnp.concatenate([out[at : at + ROWS, 0:half], side], axis=0)
            part[f, j] = az_terms(got[f]) + radial


def change(fa, part, f, j, size):
    near = fa(j + 1)[0:size] - fa(j - 1)[0:size]
    far = fa(j + 2)[0:size] - fa(j - 2)[0:size]
    return SCALE * (8.0 * near - far + part[f, j, 0:size])


def window(fax, f):
    held = {}

    def get(j):
        if j not in held:
            held[j] = fax[f, j]
        return held[j]

    return get


def stages(n_ax, n_rad, ca, cz, slots, block, banded, cells_far, *refs):
    sides, refs = refs[: len(refs) - 12], refs[len(refs) - 12 :]
    sides, places = sides[: len(sides) // 2], sides[len(sides) // 2 :]
    q_out, u2_out, u0_out, ghost, first, second, fax, part, value, picked, cells, cells_sem = refs
    fetch = pltpu.make_async_copy(cells_far, cells, cells_sem)
    fetch.start()
    cr = block.shape[-1]
    low, high = REACH, REACH + ca
    ax = ax_index()
    rad = lax.axis_index("rad")

    lane = lax.broadcasted_iota(jnp.int32, (8, cr), 1)
    row = 4 * lax.broadcasted_iota(jnp.int32, (8, cr), 0) + lane // SPAN
    j = lane % SPAN
    steps_rad = jnp.where(
        (j < REACH) & (rad < n_rad - 1),
        1 + j // 2,
        jnp.where((j >= SPAN - REACH) & (rad > 0), 1 + (SPAN - 1 - j) // 2, 99),
    )
    beyond_row = jnp.maximum(OFF - row, row - (OFF + cz - 1))
    steps = steps_rad + jnp.where(beyond_row > 0, (beyond_row + 1) // 2, 0)
    base0 = jnp.where(steps_rad < 99, 0.0, 1.0)

    side = 0.0
    for got, place in zip(sides, places):
        side = side + jnp.dot(got[...], place[...], preferred_element_type=F32)
    group = side.shape[1] // cr
    count = (ca + 2 * MID) // group
    for f in range(5):
        for k in range(count):
            for i in range(group):
                at = (f * count + k) * 8
                tile = side[at : at + 8, i * cr : (i + 1) * cr]
                ghost[f, k * group + i] = tile + base0 if f == 0 else tile

    def start_state(j, both):
        u = []
        for f in range(5):
            x = block[f, j]
            u.append(jnp.concatenate([x, ghost[f, j - (REACH - MID)]], axis=0) if both else x)
        rho, vel, pres = u[0], u[1:4], u[4]
        mom = [rho * x for x in vel]
        energy = pres * (1.0 / GAMMA_M) + 0.5 * (mom[0] * vel[0] + mom[1] * vel[1] + mom[2] * vel[2])
        return rho, (mom, vel, pres, energy)

    def note(s, j, u):
        value[s, j] = (u[2] - P_REF + u[0][0])[0:ROWS]

    for j in (low - 6, low - 5, high + 4, high + 5):
        ax_only(start_state(j, False)[1], fax, j)

    step = (ca + 2 * MID) // STEPS

    @pl.loop(0, STEPS)
    def _(i):
        js = [low - 4 + step * i + k for k in range(step)]
        us = []
        for j in js:
            rho, u = start_state(j, True)
            for f, x in enumerate([rho] + u[0] + [u[3]]):
                first[f, j] = x
            note(0, j, u)
            us.append(u)
        both_sides(us, js, fax, part, banded)

    def update(f, j, fa, stage):
        a = max(low - j, j - (high - 1), 0)
        a = (a + 1) // 2
        lim = 2 - stage
        base = jnp.where(f == 0, 1.0, 0.0)
        size = ROWS if a == lim else TALL
        new = change(fa, part, f, j, size)
        u0 = first[f, j, 0:size]
        if stage == 0:
            new = u0 + new
        else:
            new = 0.75 * u0 + 0.25 * (second[f, j, 0:size] + new)
        beyond = (ax == 0) if j < low else (ax == n_ax - 1)
        home = new[0:ROWS]
        if a > 0:
            home = jnp.where(beyond, base, home)
        if size == ROWS:
            return home, None
        ok = steps <= lim - a
        if a > 0:
            ok = ok & jnp.logical_not(beyond)
        return home, jnp.where(ok, new[ROWS:], base)

    @pl.loop(0, 5)
    def _(f):
        fa = window(fax, f)
        for j in range(low - 4, high + 4):
            home, side = update(f, j, fa, 0)
            second[f, j, 0:ROWS] = home
            if side is not None:
                second[f, j, ROWS:] = side

    for j in (low - 4, low - 3, high + 2, high + 3):
        ax_only(split_state([second[f, j, 0:ROWS] for f in range(5)]), fax, j)

    step2 = (ca + MID) // STEPS

    @pl.loop(0, STEPS)
    def _(i):
        js = [low - 2 + step2 * i + k for k in range(step2)]
        us = []
        for j in js:
            u = split_state([second[f, j] for f in range(5)])
            note(1, j, u)
            us.append(u)
        both_sides(us, js, fax, part, banded)

    @pl.loop(0, 5)
    def _(f):
        fa = window(fax, f)
        for j in range(low - 2, high + 2):
            home, side = update(f, j, fa, 1)
            u2_out[f, j - (low - 2), 0:ROWS] = home
            if side is not None:
                u2_out[f, j - (low - 2), ROWS:] = side
        for j in range(low, high):
            u0_out[f, j - low] = first[f, j, 0:ROWS]

    @pl.loop(0, ca)
    def _(i):
        u = split_state([u2_out[f, i + 2, 0:ROWS] for f in range(5)])
        note(2, low + i, u)

    fetch.wait()
    picked[...] = jnp.zeros_like(picked)
    lanes = lax.broadcasted_iota(jnp.int32, (1, cr), 1)
    for p in range(slots):
        cell = cells[p]
        at = jnp.maximum(cell, 0)
        column = jnp.where(cell >= 0, lax.rem(at, cr), -1)
        at = lax.div(at, cr)
        plane = low + lax.div(at, cz)
        r = lax.rem(at, cz) + OFF
        r = 8 * lax.rem(r, 4) + lax.div(r, 4)
        hit = lanes == column
        for s in range(3):
            picked[pl.ds(s * slots + p, 1), :] = jnp.where(hit, value[s, plane, pl.ds(r, 1), :], 0.0)
    q = lax.dot_general(
        jnp.ones((8, cr), BF16),
        picked[...].astype(BF16),
        (((1,), (1,)), ((), ())),
        preferred_element_type=F32,
    )
    q_out[...] = jnp.broadcast_to(q[0:1][None], q_out.shape)


def last_stage(ca, cz, u2, u0, banded, state, fax, part):
    for j in (0, 1, ca + 2, ca + 3):
        ax_only(split_state([u2[f, j, 0:ROWS] for f in range(5)]), fax, j)

    step = ca // STEPS

    @pl.loop(0, STEPS)
    def _(i):
        js = [2 + step * i + k for k in range(step)]
        us = [split_state([u2[f, j] for f in range(5)]) for j in js]
        both_sides(us, js, fax, part, banded)

    first, quarter = OFF // 4, cz // 4

    @pl.loop(0, 5)
    def _(f):
        fa = window(fax, f)
        for k in range(ca):
            j = k + 2
            new = u2[f, j, 0:ROWS] + change(fa, part, f, j, ROWS)
            new = u0[f, k] * (1.0 / 3.0) + (2.0 / 3.0) * new
            for l in range(4):
                state[f, k, pl.ds(l, quarter, stride=4), :] = new[8 * l + first : 8 * l + first + quarter]


def signals(slots, rows, offsets, weight, out):
    ndev = rows.shape[0]
    group = 32
    cols = group * slots
    lanes = rows.shape[1]
    col = lax.broadcasted_iota(jnp.int32, (1, cols), 1)
    owner = lax.broadcasted_iota(jnp.int32, (group, cols), 0) == col // slots
    lane = lax.broadcasted_iota(jnp.int32, (lanes, cols), 0)
    time = lax.broadcasted_iota(jnp.int32, (NB, cols), 0).astype(F32)
    total = jnp.zeros(out.shape, F32)
    for g in range(ndev // group):
        q = rows[g * group : (g + 1) * group, :].astype(BF16)
        off = offsets[0:1, g * group : (g + 1) * group].astype(F32)
        off = jnp.broadcast_to(off, (8, group)).astype(BF16)
        bins = jnp.dot(off, owner.astype(BF16), preferred_element_type=F32)[0:1]
        table = jnp.zeros((NB, cols), F32)
        for s in range(3):
            pick = jnp.where(lane == s * slots + col % slots, 1.0, 0.0).astype(BF16)
            spread = jnp.dot(q, pick, preferred_element_type=F32)
            line = jnp.sum(jnp.where(owner, spread, 0.0), axis=0, keepdims=True)
            table = jnp.where(time == bins + s, line, table)
        total = total + lax.dot_general(
            weight[:, g * cols : (g + 1) * cols],
            table.astype(BF16),
            (((1,), (1,)), ((), ())),
            preferred_element_type=F32,
        )
    out[...] = total


def swap_pairs(count, periodic):
    one = [(i, i ^ 1) for i in range(count)]
    two = []
    for i in range(count):
        j = i - 1 if i % 2 == 0 else i + 1
        two.append((i, j % count if periodic or 0 <= j < count else i))
    return one, two


def swap(first, second, axis, periodic):
    count = 1
    for name in (axis,) if isinstance(axis, str) else axis:
        count = count * lax.axis_size(name)
    one, two = swap_pairs(count, periodic)
    if periodic:
        one, two = two, one
    return lax.ppermute(first, axis, one), lax.ppermute(second, axis, two)


def local(density, velocity, pressure, panel_cell, obs_weight, bin_offset):
    ca, cz, cr = density.shape
    slots = panel_cell.shape[0]
    ndev = bin_offset.shape[1]
    n_ax, n_rad = lax.axis_size("y") * lax.axis_size("core"), lax.axis_size("rad")
    planes = ca + 2 * REACH
    part = functools.partial
    given = (density.reshape(ca * cz, cr), velocity.reshape(3 * ca * cz, cr), pressure.reshape(ca * cz, cr))

    edge = struct((5 * REACH * cz, cr), BF16)
    strip = struct((5 * REACH * ca, cr), BF16)
    home, ax1, ax2, az1, az2 = call(
        part(load_and_pack, ca, cz),
        (struct((5 * ca * cz, cr)), edge, edge, strip, strip),
        [HBM] * 3,
        [pltpu.SemaphoreType.DMA((3,))],
    )(*[far(x) for x in given])
    ax1, ax2 = swap(ax1, ax2, ("y", "core"), False)
    az1, az2 = swap(az1, az2, "az", True)
    grid = struct((5 * planes * ROWS, cr))
    ends = ("either",) if n_rad == 2 else ("low", "high")
    tiles = cr // SLOT
    table = [struct((tiles * cr, cr), BF16)] * len(ends) + [struct((cr, tiles * cr // 4), BF16)] * len(ends)
    block, banded, *tables = call(
        part(prepare, ends, ca, cz, n_rad),
        (grid, struct((2 * cr, 2 * cr), BF16), *table),
        [VMEM],
    )(home)
    edges, places = tables[: len(ends)], tables[len(ends) :]

    corner = struct((5 * MID * 2 * MID, cr), BF16)
    near = pltpu.VMEM((5, 2 * MID * cz, cr), F32)
    corner1, corner2 = call(part(pack_corners, n_ax, cz), (corner, corner), [VMEM] * 2, [near])(ax1, ax2)
    corner1, corner2 = swap(corner1, corner2, "az", True)

    side = struct((5 * (ca + 2 * MID) * ROWS // tiles, cr), BF16)
    block = call(
        part(add_sides, n_ax, ca, cz),
        grid,
        [VMEM] * 5,
        [pltpu.VMEM((5, 2 * REACH * cz, cr), F32), pltpu.VMEM((2,) + strip.shape, F32)],
        mib=8,
        alias={0: 0},
        cost=pl.CostEstimate(flops=100_000_000, bytes_accessed=4_000_000, transcendentals=0),
    )(block, ax1, ax2, az1, az2)
    got = call(
        part(add_corners, len(ends), ca, cz),
        (grid,) + tuple(side for _ in ends),
        [VMEM] * (3 + len(ends)),
        [pltpu.VMEM((2,) + corner.shape, F32)],
        mib=8,
        alias={0: 0},
    )(block, corner1, corner2, *edges)
    block = got[0].reshape(5, planes, ROWS, cr)
    if n_rad == 2:
        sides = (lax.ppermute(got[1], "rad", [(0, 1), (1, 0)]),)
    else:
        up = [(i, i + 1) for i in range(n_rad - 1)]
        sides = (lax.ppermute(got[1], "rad", [(j, i) for i, j in up]), lax.ppermute(got[2], "rad", up))

    grid = (5, planes, TALL, cr)
    q, u2, u0 = call(
        part(stages, n_ax, n_rad, ca, cz, slots),
        (struct((ndev, 1, 128)), struct((5, ca + 4, TALL, cr)), struct((5, ca, ROWS, cr))),
        [VMEM, VMEM, HBM] + [VMEM] * (2 * len(sides)),
        [pltpu.VMEM((5, ca + 2 * MID, 8, cr), F32)]
        + [pltpu.VMEM(grid, F32) for _ in range(4)]
        + [pltpu.VMEM((3, planes, ROWS, cr), F32), pltpu.VMEM((128, cr), F32)]
        + [pltpu.SMEM((slots,), jnp.int32), pltpu.SemaphoreType.DMA],
        mib=28,
    )(block, banded, far(panel_cell), *sides, *places)

    rows = lax.all_to_all(q, ("y", "core", "az", "rad"), 0, 0, tiled=True).reshape(ndev, 128)

    grid = (5, ca + 4, TALL, cr)
    state = call(
        part(last_stage, ca, cz),
        struct((5, ca, cz, cr)),
        [VMEM] * 3,
        [pltpu.VMEM(grid, F32), pltpu.VMEM(grid, F32)],
        mib=12,
        cost=pl.CostEstimate(flops=400_000_000, bytes_accessed=8_000_000, transcendentals=0),
    )(u2, u0, banded)
    signal = call(
        part(signals, slots), struct((obs_weight.shape[0], NB)), [VMEM] * 3, mib=24
    )(rows, bin_offset, obs_weight)
    return (state, signal)


def solution(mesh):
    n_ax, n_az, n_rad = (mesh.shape[name] for name in ("ax", "az", "rad"))
    split = Mesh(mesh.devices.reshape(n_ax // 2, 2, n_az, n_rad), ("y", "core", "az", "rad"))
    ax = ("y", "core")
    every = ax + ("az", "rad")
    in_specs = (
        P(ax, "az", "rad"),
        P(None, ax, "az", "rad"),
        P(ax, "az", "rad"),
        P(every),
        P(every, None),
        P(every, None),
    )
    out_specs = (P(None, ax, "az", "rad"), P(every, None))
    return jax.shard_map(local, mesh=split, in_specs=in_specs, out_specs=out_specs, check_vma=False)
```

```python
import functools

import jax
import jax.numpy as jnp
from jax import lax
from jax.experimental import pallas as pl
from jax.experimental.pallas import tpu as pltpu
from jax.sharding import Mesh, PartitionSpec as P

NB = 128
GAMMA_M = 0.4
LAMBDA = 0.1
P_REF = 1.0
REACH = 6
MID = 4
SCALE = -LAMBDA / 12.0
ROWS = 32
OFF = 8
SPAN = 32
TALL = ROWS + 8
STEPS = 1
SLOT = 8
HBM = pltpu.MemorySpace.HBM
VMEM = pltpu.MemorySpace.VMEM
SMEM = pltpu.MemorySpace.SMEM
F32 = jnp.float32
BF16 = jnp.bfloat16


def call(kernel, outs, in_spaces, scratch=(), mib=8, cost=None, alias={}):
    return pl.pallas_call(
        kernel,
        out_shape=outs,
        in_specs=[pl.BlockSpec(memory_space=s) for s in in_spaces],
        out_specs=jax.tree.map(lambda _: pl.BlockSpec(memory_space=VMEM), outs),
        scratch_shapes=list(scratch),
        compiler_params=pltpu.CompilerParams(vmem_limit_bytes=mib * 1024 * 1024),
        cost_estimate=cost,
        input_output_aliases=alias,
    )


def far(x):
    return pltpu.with_memory_space_constraint(x, HBM)


def struct(shape, dtype=F32):
    return jax.ShapeDtypeStruct(shape, dtype)


def kept(row):
    return 8 * (row % 4) + row // 4


def ax_index():
    return lax.axis_index("y") * lax.axis_size("core") + lax.axis_index("core")


def first_is_up(axis):
    if axis == "ax":
        return lax.axis_index("core") == 0
    return lax.axis_index("az") % 2 == 1


def load_and_pack(ca, cz, den, vel, pre, home, ax1, ax2, az1, az2, sems):
    size = ca * cz
    copies = [
        pltpu.make_async_copy(den, home.at[pl.ds(0, size)], sems.at[0]),
        pltpu.make_async_copy(vel, home.at[pl.ds(size, 3 * size)], sems.at[1]),
        pltpu.make_async_copy(pre, home.at[pl.ds(4 * size, size)], sems.at[2]),
    ]
    for copy in copies:
        copy.start()
    for copy in copies:
        copy.wait()
    up = first_is_up("ax")
    edge = MID * cz
    for f in range(5):
        at = f * size
        low = home[at : at + edge, :]
        high = home[at + size - edge : at + size, :]
        rows = slice(f * edge, (f + 1) * edge)
        ax1[rows, :] = jnp.where(up, high, low).astype(BF16)
        ax2[rows, :] = jnp.where(up, low, high).astype(BF16)
    up = first_is_up("az")
    low, high = [], []
    for f in range(5):
        for d in range(REACH):
            low.append(home[pl.ds(f * size + d, ca, stride=cz), :])
            high.append(home[pl.ds(f * size + cz - 1 - d, ca, stride=cz), :])
    low, high = jnp.concatenate(low, axis=0), jnp.concatenate(high, axis=0)
    az1[...] = jnp.where(up, high, low).astype(BF16)
    az2[...] = jnp.where(up, low, high).astype(BF16)


def ax_sides(n_ax, got1, got2, rows):
    ax = ax_index()
    a, b = got1[rows, :].astype(F32), got2[rows, :].astype(F32)
    up = first_is_up("ax")
    lo = jnp.where(ax == 0, 0.0, jnp.where(up, b, a))
    hi = jnp.where(ax == n_ax - 1, 0.0, jnp.where(up, a, b))
    return lo, hi


def pack_corners(n_ax, cz, got1, got2, first_out, second_out, near):
    up = first_is_up("az")
    size = MID * cz
    for f in range(5):
        lo, hi = ax_sides(n_ax, got1, got2, slice(f * size, (f + 1) * size))
        near[f, 0:size, :] = lo
        near[f, size : 2 * size, :] = hi
    low, high = [], []
    for f in range(5):
        for d in range(MID):
            low.append(near[f, pl.ds(d, 2 * MID, stride=cz), :])
            high.append(near[f, pl.ds(cz - 1 - d, 2 * MID, stride=cz), :])
    low, high = jnp.concatenate(low, axis=0), jnp.concatenate(high, axis=0)
    first_out[...] = jnp.where(up, high, low).astype(BF16)
    second_out[...] = jnp.where(up, low, high).astype(BF16)


def spread_rows(planes, cz, f, plane, ref, at, block):
    quarter = cz // 4
    for l in range(4):
        row = (f * planes + plane) * ROWS + 8 * l + OFF // 4
        block[pl.ds(row, quarter), :] = ref[pl.ds(at + l, quarter, stride=4), :]


def prepare(ends, ca, cz, n_rad, home, block, banded, *tables):
    cr = home.shape[1]
    rad = lax.axis_index("rad")
    for f in range(5):
        for k in range(ca):
            spread_rows(ca + 2 * REACH, cz, f, REACH + k, home, (f * ca + k) * cz, block)
    banded[...] = band(cr)
    edges, places = tables[: len(ends)], tables[len(ends) :]
    tiles = cr // SLOT
    there = {"high": jnp.where(rad < n_rad - 1, 1.0, 0.0), "low": jnp.where(rad > 0, 1.0, 0.0)}
    high = place_matrix(0, tiles, cr) * there["high"]
    low = place_matrix(SPAN - REACH, tiles, cr) * there["low"]
    for end, edge, place in zip(ends, edges, places):
        start = {"low": 0, "high": cr - REACH, "either": jnp.where(rad == 0, cr - REACH, 0)}[end]
        edge[...] = edge_matrix(start, tiles, cr)
        place[...] = {"low": high, "high": low, "either": high + low}[end].astype(BF16)


def edge_matrix(start, tiles, cr):
    k = lax.broadcasted_iota(jnp.int32, (tiles * cr, tiles * SLOT), 0)
    n = lax.broadcasted_iota(jnp.int32, (tiles * cr, tiles * SLOT), 1)
    hit = (k // cr == n // SLOT) & (n % SLOT < REACH) & (k % cr == n % SLOT + start)
    return jnp.where(hit, 1.0, 0.0).astype(BF16)


def place_matrix(start, tiles, cr):
    k = lax.broadcasted_iota(jnp.int32, (tiles * SLOT, tiles * cr // 4), 0)
    n = lax.broadcasted_iota(jnp.int32, (tiles * SLOT, tiles * cr // 4), 1)
    hit = (k // SLOT == n // SPAN) & (k % SLOT < REACH) & (n % SPAN == k % SLOT + start)
    return jnp.where(hit, 1.0, 0.0)


def add_sides(n_ax, ca, cz, block_in, ax1, ax2, az1, az2, block, sides, strips):
    planes = ca + 2 * REACH
    size = MID * cz
    for f in range(5):
        lo, hi = ax_sides(n_ax, ax1, ax2, slice(f * size, (f + 1) * size))
        sides[f, 0:size, :] = lo
        sides[f, size : 2 * size, :] = hi
    for f in range(5):
        for k in range(MID):
            spread_rows(planes, cz, f, REACH - MID + k, sides.at[f], k * cz, block)
            spread_rows(planes, cz, f, REACH + ca + k, sides.at[f], size + k * cz, block)
    up = first_is_up("az")
    a, b = az1[...].astype(F32), az2[...].astype(F32)
    strips[0] = jnp.where(up, b, a)
    strips[1] = jnp.where(up, a, b)
    for f in range(5):
        for d in range(REACH):
            for side, row in ((0, OFF - 1 - d), (1, OFF + cz + d)):
                at = kept(row) + (f * planes + REACH) * ROWS
                block[pl.ds(at, ca, stride=ROWS), :] = strips[side, pl.ds((f * REACH + d) * ca, ca), :]


def add_corners(count, ca, cz, block_in, home, corner1, corner2, *rest):
    edges, block, outs, corners = rest[:count], rest[count], rest[count + 1 : -3], rest[-1]
    far1, far2 = rest[-3:-1]
    cr = corner1.shape[1]
    planes = ca + 2 * REACH
    up = first_is_up("az")
    a, b = corner1[...].astype(F32), corner2[...].astype(F32)
    corners[0] = jnp.where(up, b, a)
    corners[1] = jnp.where(up, a, b)
    for f in range(5):
        for d in range(MID):
            for side, row in ((0, OFF - 1 - d), (1, OFF + cz + d)):
                at = kept(row) + f * planes * ROWS
                start = (f * MID + d) * 2 * MID
                got = corners[side, pl.ds(start, MID), :]
                block[pl.ds(at + (REACH - MID) * ROWS, MID, stride=ROWS), :] = got
                got = corners[side, pl.ds(start + MID, MID), :]
                block[pl.ds(at + (REACH + ca) * ROWS, MID, stride=ROWS), :] = got

    up = first_is_up("ax")
    size = (REACH - MID) * cz
    for f in range(5):
        at = f * ca * cz
        low = home[at + MID * cz : at + REACH * cz, :]
        high = home[at + (ca - REACH) * cz : at + (ca - MID) * cz, :]
        rows = slice(f * size, (f + 1) * size)
        far1[rows, :] = jnp.where(up, high, low).astype(BF16)
        far2[rows, :] = jnp.where(up, low, high).astype(BF16)

    tiles = cr // SLOT
    step = tiles * 8
    rows = []
    for f in range(5):
        for k in range((ca + 2 * MID) * ROWS // step):
            at = (f * planes + REACH - MID) * ROWS + k * step
            rows.append(jnp.concatenate([block[at + 8 * t : at + 8 * t + 8, :] for t in range(tiles)], axis=1))
    rows = jnp.concatenate(rows, axis=0).astype(BF16)
    for edge, out in zip(edges, outs):
        out[...] = jnp.dot(rows, edge[...], preferred_element_type=F32).astype(BF16)


def az_terms(flux):
    v = [flux[8 * l : 8 * l + 8] for l in range(4)]
    v = [pltpu.roll(v[2], 1, 0), pltpu.roll(v[3], 1, 0)] + v + [pltpu.roll(v[0], 7, 0), pltpu.roll(v[1], 7, 0)]
    out = [8.0 * (v[l + 3] - v[l + 1]) - (v[l + 4] - v[l]) for l in range(4)]
    side = flux[ROWS:]
    lanes = side.shape[1]
    span = lax.broadcasted_iota(jnp.int32, side.shape, 1) // SPAN
    up, down = pltpu.roll(side, 7, 0), pltpu.roll(side, 1, 0)
    up1 = pltpu.roll(jnp.where(span == 0, up, side), lanes - SPAN, 1)
    up2 = pltpu.roll(jnp.where(span < 2, up, side), lanes - 2 * SPAN, 1)
    down1 = pltpu.roll(jnp.where(span == 3, down, side), SPAN, 1)
    down2 = pltpu.roll(jnp.where(span >= 2, down, side), 2 * SPAN, 1)
    out.append(8.0 * (up1 - down1) - (up2 - down2))
    return jnp.concatenate(out, axis=0)


def band(cr):
    def place(axis, none):
        i = lax.broadcasted_iota(jnp.int32, (2 * cr, 2 * cr), axis)
        j = i % SPAN
        beyond = jnp.where(j < REACH, cr + j, jnp.where(j >= SPAN - REACH, j - SPAN, none))
        return jnp.where(i < cr, i, beyond), jnp.where(i < cr, -1, i // SPAN)

    k, k_span = place(0, 4 * cr)
    n, n_span = place(1, -4 * cr)
    gap = k - n
    out = jnp.where(gap == 1, 8.0, 0.0) + jnp.where(gap == -1, -8.0, 0.0)
    out = out + jnp.where(gap == 2, -1.0, 0.0) + jnp.where(gap == -2, 1.0, 0.0)
    apart = (k_span >= 0) & (n_span >= 0) & (k_span != n_span)
    return jnp.where(apart, 0.0, out).astype(BF16)


def split_state(u):
    rho, m0, m1, m2, energy = u
    inv = 1.0 / rho
    vel = [m0 * inv, m1 * inv, m2 * inv]
    pres = GAMMA_M * (energy - 0.5 * (m0 * vel[0] + m1 * vel[1] + m2 * vel[2]))
    return [m0, m1, m2], vel, pres, energy


def flux(d, mom, vel, pres, energy):
    parts = [mom[d]]
    for j in range(3):
        parts.append(mom[d] * vel[j] + pres if j == d else mom[d] * vel[j])
    parts.append((energy + pres) * vel[d])
    return parts


def ax_only(u, fax, j):
    got = flux(0, *u)
    for f in range(5):
        fax[f, j, 0:ROWS] = got[f]


def both_sides(us, js, fax, part, banded):
    rows = []
    shape = (ROWS, banded.shape[0] // 2)
    span = lax.broadcasted_iota(jnp.int32, shape, 1) // SPAN
    mine = span == lax.broadcasted_iota(jnp.int32, shape, 0) // 8
    for u, j in zip(us, js):
        got = flux(0, *u)
        for f in range(5):
            fax[f, j] = got[f]
        got = flux(2, *u)
        for f in range(5):
            side = jnp.where(mine, jnp.concatenate([got[f][ROWS:]] * 4, axis=0), 0.0)
            rows.append(jnp.concatenate([got[f][0:ROWS], side], axis=1))
    rows = jnp.concatenate(rows, axis=0).astype(BF16)
    out = jnp.dot(rows, banded[...], preferred_element_type=F32)
    half = out.shape[1] // 2
    for i, (u, j) in enumerate(zip(us, js)):
        got = flux(1, *u)
        for f in range(5):
            at = (i * 5 + f) * ROWS
            side = out[at : at + 8, half:]
            for l in range(1, 4):
                side = jnp.where(span[0:8] == l, out[at + 8 * l : at + 8 * l + 8, half:], side)
            radial = jnp.concatenate([out[at : at + ROWS, 0:half], side], axis=0)
            part[f, j] = az_terms(got[f]) + radial


def change(fa, part, f, j, size):
    near = fa(j + 1)[0:size] - fa(j - 1)[0:size]
    far = fa(j + 2)[0:size] - fa(j - 2)[0:size]
    return SCALE * (8.0 * near - far + part[f, j, 0:size])


def window(fax, f):
    held = {}

    def get(j):
        if j not in held:
            held[j] = fax[f, j]
        return held[j]

    return get


def stages(n_ax, n_rad, ca, cz, slots, block, banded, cells_far, *refs):
    sides, refs = refs[: len(refs) - 14], refs[len(refs) - 14 :]
    sides, (far1, far2) = sides[:-2], sides[-2:]
    sides, places = sides[: len(sides) // 2], sides[len(sides) // 2 :]
    q_out, u2_out, u0_out, ghost, first, second, fax, part, value, picked, cells, cells_sem, outer, layers = refs
    fetch = pltpu.make_async_copy(cells_far, cells, cells_sem)
    fetch.start()
    cr = block.shape[-1]
    low, high = REACH, REACH + ca
    ax = ax_index()
    rad = lax.axis_index("rad")

    lane = lax.broadcasted_iota(jnp.int32, (8, cr), 1)
    row = 4 * lax.broadcasted_iota(jnp.int32, (8, cr), 0) + lane // SPAN
    j = lane % SPAN
    steps_rad = jnp.where(
        (j < REACH) & (rad < n_rad - 1),
        1 + j // 2,
        jnp.where((j >= SPAN - REACH) & (rad > 0), 1 + (SPAN - 1 - j) // 2, 99),
    )
    beyond_row = jnp.maximum(OFF - row, row - (OFF + cz - 1))
    steps = steps_rad + jnp.where(beyond_row > 0, (beyond_row + 1) // 2, 0)
    base0 = jnp.where(steps_rad < 99, 0.0, 1.0)

    side = 0.0
    for got, place in zip(sides, places):
        side = side + jnp.dot(got[...], place[...], preferred_element_type=F32)
    group = side.shape[1] // cr
    count = (ca + 2 * MID) // group
    for f in range(5):
        for k in range(count):
            for i in range(group):
                at = (f * count + k) * 8
                tile = side[at : at + 8, i * cr : (i + 1) * cr]
                ghost[f, k * group + i] = tile + base0 if f == 0 else tile

    def start_state(j, both):
        u = []
        for f in range(5):
            x = block[f, j]
            u.append(jnp.concatenate([x, ghost[f, j - (REACH - MID)]], axis=0) if both else x)
        return conserved(u)

    def conserved(u):
        rho, vel, pres = u[0], u[1:4], u[4]
        mom = [rho * x for x in vel]
        energy = pres * (1.0 / GAMMA_M) + 0.5 * (mom[0] * vel[0] + mom[1] * vel[1] + mom[2] * vel[2])
        return rho, (mom, vel, pres, energy)

    def note(s, j, u):
        value[s, j] = (u[2] - P_REF + u[0][0])[0:ROWS]

    layers[0], layers[1] = ax_sides(n_ax, far1, far2, slice(0, far1.shape[0]))
    for f in range(5):
        for k in range(4):
            spread_rows(4, cz, f, k, layers.at[k // 2], (f * 2 + k % 2) * cz, outer)
    for k, j in enumerate((low - 6, low - 5, high + 4, high + 5)):
        ax_only(conserved([outer[(f * 4 + k) * ROWS : (f * 4 + k + 1) * ROWS, :] for f in range(5)])[1], fax, j)

    step = (ca + 2 * MID) // STEPS

    @pl.loop(0, STEPS)
    def _(i):
        js = [low - 4 + step * i + k for k in range(step)]
        us = []
        for j in js:
            rho, u = start_state(j, True)
            for f, x in enumerate([rho] + u[0] + [u[3]]):
                first[f, j] = x
            note(0, j, u)
            us.append(u)
        both_sides(us, js, fax, part, banded)

    def update(f, j, fa, stage):
        a = max(low - j, j - (high - 1), 0)
        a = (a + 1) // 2
        lim = 2 - stage
        base = jnp.where(f == 0, 1.0, 0.0)
        size = ROWS if a == lim else TALL
        new = change(fa, part, f, j, size)
        u0 = first[f, j, 0:size]
        if stage == 0:
            new = u0 + new
        else:
            new = 0.75 * u0 + 0.25 * (second[f, j, 0:size] + new)
        beyond = (ax == 0) if j < low else (ax == n_ax - 1)
        home = new[0:ROWS]
        if a > 0:
            home = jnp.where(beyond, base, home)
        if size == ROWS:
            return home, None
        ok = steps <= lim - a
        if a > 0:
            ok = ok & jnp.logical_not(beyond)
        return home, jnp.where(ok, new[ROWS:], base)

    @pl.loop(0, 5)
    def _(f):
        fa = window(fax, f)
        for j in range(low - 4, high + 4):
            home, side = update(f, j, fa, 0)
            second[f, j, 0:ROWS] = home
            if side is not None:
                second[f, j, ROWS:] = side

    for j in (low - 4, low - 3, high + 2, high + 3):
        ax_only(split_state([second[f, j, 0:ROWS] for f in range(5)]), fax, j)

    step2 = (ca + MID) // STEPS

    @pl.loop(0, STEPS)
    def _(i):
        js = [low - 2 + step2 * i + k for k in range(step2)]
        us = []
        for j in js:
            u = split_state([second[f, j] for f in range(5)])
            note(1, j, u)
            us.append(u)
        both_sides(us, js, fax, part, banded)

    @pl.loop(0, 5)
    def _(f):
        fa = window(fax, f)
        for j in range(low - 2, high + 2):
            home, side = update(f, j, fa, 1)
            u2_out[f, j - (low - 2), 0:ROWS] = home
            if side is not None:
                u2_out[f, j - (low - 2), ROWS:] = side
        for j in range(low, high):
            u0_out[f, j - low] = first[f, j, 0:ROWS]

    @pl.loop(0, ca)
    def _(i):
        u = split_state([u2_out[f, i + 2, 0:ROWS] for f in range(5)])
        note(2, low + i, u)

    fetch.wait()
    picked[...] = jnp.zeros_like(picked)
    lanes = lax.broadcasted_iota(jnp.int32, (1, cr), 1)
    for p in range(slots):
        cell = cells[p]
        at = jnp.maximum(cell, 0)
        column = jnp.where(cell >= 0, lax.rem(at, cr), -1)
        at = lax.div(at, cr)
        plane = low + lax.div(at, cz)
        r = lax.rem(at, cz) + OFF
        r = 8 * lax.rem(r, 4) + lax.div(r, 4)
        hit = lanes == column
        for s in range(3):
            picked[pl.ds(s * slots + p, 1), :] = jnp.where(hit, value[s, plane, pl.ds(r, 1), :], 0.0)
    q = lax.dot_general(
        jnp.ones((8, cr), BF16),
        picked[...].astype(BF16),
        (((1,), (1,)), ((), ())),
        preferred_element_type=F32,
    )
    q_out[...] = jnp.broadcast_to(q[0:1][None], q_out.shape)


def last_stage(ca, cz, u2, u0, banded, state, fax, part):
    for j in (0, 1, ca + 2, ca + 3):
        ax_only(split_state([u2[f, j, 0:ROWS] for f in range(5)]), fax, j)

    step = ca // STEPS

    @pl.loop(0, STEPS)
    def _(i):
        js = [2 + step * i + k for k in range(step)]
        us = [split_state([u2[f, j] for f in range(5)]) for j in js]
        both_sides(us, js, fax, part, banded)

    first, quarter = OFF // 4, cz // 4

    @pl.loop(0, 5)
    def _(f):
        fa = window(fax, f)
        for k in range(ca):
            j = k + 2
            new = u2[f, j, 0:ROWS] + change(fa, part, f, j, ROWS)
            new = u0[f, k] * (1.0 / 3.0) + (2.0 / 3.0) * new
            for l in range(4):
                state[f, k, pl.ds(l, quarter, stride=4), :] = new[8 * l + first : 8 * l + first + quarter]


def signals(slots, rows, offsets, weight, out):
    ndev = rows.shape[0]
    group = 32
    cols = group * slots
    lanes = rows.shape[1]
    col = lax.broadcasted_iota(jnp.int32, (1, cols), 1)
    owner = lax.broadcasted_iota(jnp.int32, (group, cols), 0) == col // slots
    lane = lax.broadcasted_iota(jnp.int32, (lanes, cols), 0)
    time = lax.broadcasted_iota(jnp.int32, (NB, cols), 0).astype(F32)
    total = jnp.zeros(out.shape, F32)
    for g in range(ndev // group):
        q = rows[g * group : (g + 1) * group, :].astype(BF16)
        off = offsets[0:1, g * group : (g + 1) * group].astype(F32)
        off = jnp.broadcast_to(off, (8, group)).astype(BF16)
        bins = jnp.dot(off, owner.astype(BF16), preferred_element_type=F32)[0:1]
        table = jnp.zeros((NB, cols), F32)
        for s in range(3):
            pick = jnp.where(lane == s * slots + col % slots, 1.0, 0.0).astype(BF16)
            spread = jnp.dot(q, pick, preferred_element_type=F32)
            line = jnp.sum(jnp.where(owner, spread, 0.0), axis=0, keepdims=True)
            table = jnp.where(time == bins + s, line, table)
        total = total + lax.dot_general(
            weight[:, g * cols : (g + 1) * cols],
            table.astype(BF16),
            (((1,), (1,)), ((), ())),
            preferred_element_type=F32,
        )
    out[...] = total


def swap_pairs(count, periodic):
    one = [(i, i ^ 1) for i in range(count)]
    two = []
    for i in range(count):
        j = i - 1 if i % 2 == 0 else i + 1
        two.append((i, j % count if periodic or 0 <= j < count else i))
    return one, two


def swap(first, second, axis, periodic):
    count = 1
    for name in (axis,) if isinstance(axis, str) else axis:
        count = count * lax.axis_size(name)
    one, two = swap_pairs(count, periodic)
    if periodic:
        one, two = two, one
    return lax.ppermute(first, axis, one), lax.ppermute(second, axis, two)


def local(density, velocity, pressure, panel_cell, obs_weight, bin_offset):
    ca, cz, cr = density.shape
    slots = panel_cell.shape[0]
    ndev = bin_offset.shape[1]
    n_ax, n_rad = lax.axis_size("y") * lax.axis_size("core"), lax.axis_size("rad")
    planes = ca + 2 * REACH
    part = functools.partial
    given = (density.reshape(ca * cz, cr), velocity.reshape(3 * ca * cz, cr), pressure.reshape(ca * cz, cr))

    edge = struct((5 * MID * cz, cr), BF16)
    strip = struct((5 * REACH * ca, cr), BF16)
    home, ax1, ax2, az1, az2 = call(
        part(load_and_pack, ca, cz),
        (struct((5 * ca * cz, cr)), edge, edge, strip, strip),
        [HBM] * 3,
        [pltpu.SemaphoreType.DMA((3,))],
    )(*[far(x) for x in given])
    ax1, ax2 = swap(ax1, ax2, ("y", "core"), False)
    az1, az2 = swap(az1, az2, "az", True)
    grid = struct((5 * planes * ROWS, cr))
    ends = ("either",) if n_rad == 2 else ("low", "high")
    tiles = cr // SLOT
    table = [struct((tiles * cr, cr), BF16)] * len(ends) + [struct((cr, tiles * cr // 4), BF16)] * len(ends)
    block, banded, *tables = call(
        part(prepare, ends, ca, cz, n_rad),
        (grid, struct((2 * cr, 2 * cr), BF16), *table),
        [VMEM],
    )(home)
    edges, places = tables[: len(ends)], tables[len(ends) :]

    corner = struct((5 * MID * 2 * MID, cr), BF16)
    near = pltpu.VMEM((5, 2 * MID * cz, cr), F32)
    corner1, corner2 = call(part(pack_corners, n_ax, cz), (corner, corner), [VMEM] * 2, [near])(ax1, ax2)
    corner1, corner2 = swap(corner1, corner2, "az", True)

    side = struct((5 * (ca + 2 * MID) * ROWS // tiles, cr), BF16)
    block = call(
        part(add_sides, n_ax, ca, cz),
        grid,
        [VMEM] * 5,
        [pltpu.VMEM((5, 2 * MID * cz, cr), F32), pltpu.VMEM((2,) + strip.shape, F32)],
        mib=8,
        alias={0: 0},
        cost=pl.CostEstimate(flops=100_000_000, bytes_accessed=4_000_000, transcendentals=0),
    )(block, ax1, ax2, az1, az2)
    far_edge = struct((5 * (REACH - MID) * cz, cr), BF16)
    got = call(
        part(add_corners, len(ends), ca, cz),
        (grid,) + tuple(side for _ in ends) + (far_edge,) * 2,
        [VMEM] * (4 + len(ends)),
        [pltpu.VMEM((2,) + corner.shape, F32)],
        mib=8,
        alias={0: 0},
    )(block, home, corner1, corner2, *edges)
    block = got[0].reshape(5, planes, ROWS, cr)
    if n_rad == 2:
        sides = (lax.ppermute(got[1], "rad", [(0, 1), (1, 0)]),)
    else:
        up = [(i, i + 1) for i in range(n_rad - 1)]
        sides = (lax.ppermute(got[1], "rad", [(j, i) for i, j in up]), lax.ppermute(got[2], "rad", up))

    far1, far2 = swap(got[-2], got[-1], ("y", "core"), False)

    grid = (5, planes, TALL, cr)
    q, u2, u0 = call(
        part(stages, n_ax, n_rad, ca, cz, slots),
        (struct((ndev, 1, 128)), struct((5, ca + 4, TALL, cr)), struct((5, ca, ROWS, cr))),
        [VMEM, VMEM, HBM] + [VMEM] * (2 * len(sides) + 2),
        [pltpu.VMEM((5, ca + 2 * MID, 8, cr), F32)]
        + [pltpu.VMEM(grid, F32) for _ in range(4)]
        + [pltpu.VMEM((3, planes, ROWS, cr), F32), pltpu.VMEM((128, cr), F32)]
        + [pltpu.SMEM((slots,), jnp.int32), pltpu.SemaphoreType.DMA]
        + [pltpu.VMEM((5 * 4 * ROWS, cr), F32), pltpu.VMEM((2,) + far_edge.shape, F32)],
        mib=28,
    )(block, banded, far(panel_cell), *sides, *places, far1, far2)

    rows = lax.all_to_all(q, ("y", "core", "az", "rad"), 0, 0, tiled=True).reshape(ndev, 128)

    grid = (5, ca + 4, TALL, cr)
    state = call(
        part(last_stage, ca, cz),
        struct((5, ca, cz, cr)),
        [VMEM] * 3,
        [pltpu.VMEM(grid, F32), pltpu.VMEM(grid, F32)],
        mib=12,
        cost=pl.CostEstimate(flops=400_000_000, bytes_accessed=8_000_000, transcendentals=0),
    )(u2, u0, banded)
    signal = call(
        part(signals, slots), struct((obs_weight.shape[0], NB)), [VMEM] * 3, mib=24
    )(rows, bin_offset, obs_weight)
    return (state, signal)


def solution(mesh):
    n_ax, n_az, n_rad = (mesh.shape[name] for name in ("ax", "az", "rad"))
    split = Mesh(mesh.devices.reshape(n_ax // 2, 2, n_az, n_rad), ("y", "core", "az", "rad"))
    ax = ("y", "core")
    every = ax + ("az", "rad")
    in_specs = (
        P(ax, "az", "rad"),
        P(None, ax, "az", "rad"),
        P(ax, "az", "rad"),
        P(every),
        P(every, None),
        P(every, None),
    )
    out_specs = (P(None, ax, "az", "rad"), P(every, None))
    return jax.shard_map(local, mesh=split, in_specs=in_specs, out_specs=out_specs, check_vma=False)
```

```python
import functools

import jax
import jax.numpy as jnp
from jax import lax
from jax.experimental import pallas as pl
from jax.experimental.pallas import tpu as pltpu
from jax.sharding import Mesh, PartitionSpec as P

NB = 128
GAMMA_M = 0.4
LAMBDA = 0.1
P_REF = 1.0
REACH = 6
MID = 4
SCALE = -LAMBDA / 12.0
ROWS = 32
OFF = 8
SPAN = 32
TALL = ROWS + 8
STEPS = 1
SLOT = 8
HBM = pltpu.MemorySpace.HBM
VMEM = pltpu.MemorySpace.VMEM
SMEM = pltpu.MemorySpace.SMEM
F32 = jnp.float32
BF16 = jnp.bfloat16


def call(kernel, outs, in_spaces, scratch=(), mib=8, cost=None, alias={}):
    return pl.pallas_call(
        kernel,
        out_shape=outs,
        in_specs=[pl.BlockSpec(memory_space=s) for s in in_spaces],
        out_specs=jax.tree.map(lambda _: pl.BlockSpec(memory_space=VMEM), outs),
        scratch_shapes=list(scratch),
        compiler_params=pltpu.CompilerParams(vmem_limit_bytes=mib * 1024 * 1024),
        cost_estimate=cost,
        input_output_aliases=alias,
    )


def far(x):
    return pltpu.with_memory_space_constraint(x, HBM)


def struct(shape, dtype=F32):
    return jax.ShapeDtypeStruct(shape, dtype)


def kept(row):
    return 8 * (row % 4) + row // 4


def ax_index():
    return lax.axis_index("y") * lax.axis_size("core") + lax.axis_index("core")


def first_is_up(axis):
    if axis == "ax":
        return lax.axis_index("core") == 0
    return lax.axis_index("az") % 2 == 1


def load_and_pack(ca, cz, den, vel, pre, home, ax1, ax2, sems):
    size = ca * cz
    copies = [
        pltpu.make_async_copy(den, home.at[pl.ds(0, size)], sems.at[0]),
        pltpu.make_async_copy(vel, home.at[pl.ds(size, 3 * size)], sems.at[1]),
        pltpu.make_async_copy(pre, home.at[pl.ds(4 * size, size)], sems.at[2]),
    ]
    for copy in copies:
        copy.start()
    for copy in copies:
        copy.wait()
    up = first_is_up("ax")
    edge = REACH * cz
    for f in range(5):
        at = f * size
        low = home[at : at + edge, :]
        high = home[at + size - edge : at + size, :]
        rows = slice(f * edge, (f + 1) * edge)
        ax1[rows, :] = jnp.where(up, high, low).astype(BF16)
        ax2[rows, :] = jnp.where(up, low, high).astype(BF16)


def pack_az(ca, cz, home, az1, az2):
    size = ca * cz
    up = first_is_up("az")
    low, high = [], []
    for f in range(5):
        for d in range(REACH):
            low.append(home[pl.ds(f * size + d, ca, stride=cz), :])
            high.append(home[pl.ds(f * size + cz - 1 - d, ca, stride=cz), :])
    low, high = jnp.concatenate(low, axis=0), jnp.concatenate(high, axis=0)
    az1[...] = jnp.where(up, high, low).astype(BF16)
    az2[...] = jnp.where(up, low, high).astype(BF16)


def ax_sides(n_ax, got1, got2, rows):
    ax = ax_index()
    a, b = got1[rows, :].astype(F32), got2[rows, :].astype(F32)
    up = first_is_up("ax")
    lo = jnp.where(ax == 0, 0.0, jnp.where(up, b, a))
    hi = jnp.where(ax == n_ax - 1, 0.0, jnp.where(up, a, b))
    return lo, hi


def pack_corners(n_ax, cz, got1, got2, first_out, second_out, near):
    up = first_is_up("az")
    half = MID * cz
    size = REACH * cz
    for f in range(5):
        lo, hi = ax_sides(n_ax, got1, got2, slice(f * size, (f + 1) * size))
        near[f, 0:half, :] = lo[size - half :]
        near[f, half : 2 * half, :] = hi[0:half]
    low, high = [], []
    for f in range(5):
        for d in range(MID):
            low.append(near[f, pl.ds(d, 2 * MID, stride=cz), :])
            high.append(near[f, pl.ds(cz - 1 - d, 2 * MID, stride=cz), :])
    low, high = jnp.concatenate(low, axis=0), jnp.concatenate(high, axis=0)
    first_out[...] = jnp.where(up, high, low).astype(BF16)
    second_out[...] = jnp.where(up, low, high).astype(BF16)


def spread_rows(planes, cz, f, plane, ref, at, block):
    quarter = cz // 4
    for l in range(4):
        row = (f * planes + plane) * ROWS + 8 * l + OFF // 4
        block[pl.ds(row, quarter), :] = ref[pl.ds(at + l, quarter, stride=4), :]


def prepare(ends, ca, cz, n_rad, home, block, banded, *tables):
    cr = home.shape[1]
    rad = lax.axis_index("rad")
    for f in range(5):
        for k in range(ca):
            spread_rows(ca + 2 * REACH, cz, f, REACH + k, home, (f * ca + k) * cz, block)
    banded[...] = band(cr)
    edges, places = tables[: len(ends)], tables[len(ends) :]
    tiles = cr // SLOT
    there = {"high": jnp.where(rad < n_rad - 1, 1.0, 0.0), "low": jnp.where(rad > 0, 1.0, 0.0)}
    high = place_matrix(0, tiles, cr) * there["high"]
    low = place_matrix(SPAN - REACH, tiles, cr) * there["low"]
    for end, edge, place in zip(ends, edges, places):
        start = {"low": 0, "high": cr - REACH, "either": jnp.where(rad == 0, cr - REACH, 0)}[end]
        edge[...] = edge_matrix(start, tiles, cr)
        place[...] = {"low": high, "high": low, "either": high + low}[end].astype(BF16)


def edge_matrix(start, tiles, cr):
    k = lax.broadcasted_iota(jnp.int32, (tiles * cr, tiles * SLOT), 0)
    n = lax.broadcasted_iota(jnp.int32, (tiles * cr, tiles * SLOT), 1)
    hit = (k // cr == n // SLOT) & (n % SLOT < REACH) & (k % cr == n % SLOT + start)
    return jnp.where(hit, 1.0, 0.0).astype(BF16)


def place_matrix(start, tiles, cr):
    k = lax.broadcasted_iota(jnp.int32, (tiles * SLOT, tiles * cr // 4), 0)
    n = lax.broadcasted_iota(jnp.int32, (tiles * SLOT, tiles * cr // 4), 1)
    hit = (k // SLOT == n // SPAN) & (k % SLOT < REACH) & (n % SPAN == k % SLOT + start)
    return jnp.where(hit, 1.0, 0.0)


def add_sides(n_ax, ca, cz, block_in, ax1, ax2, az1, az2, block, sides, strips):
    planes = ca + 2 * REACH
    size = REACH * cz
    for f in range(5):
        lo, hi = ax_sides(n_ax, ax1, ax2, slice(f * size, (f + 1) * size))
        sides[f, 0:size, :] = lo
        sides[f, size : 2 * size, :] = hi
    for f in range(5):
        for k in range(REACH):
            spread_rows(planes, cz, f, k, sides.at[f], k * cz, block)
            spread_rows(planes, cz, f, REACH + ca + k, sides.at[f], size + k * cz, block)
    up = first_is_up("az")
    a, b = az1[...].astype(F32), az2[...].astype(F32)
    strips[0] = jnp.where(up, b, a)
    strips[1] = jnp.where(up, a, b)
    for f in range(5):
        for d in range(REACH):
            for side, row in ((0, OFF - 1 - d), (1, OFF + cz + d)):
                at = kept(row) + (f * planes + REACH) * ROWS
                block[pl.ds(at, ca, stride=ROWS), :] = strips[side, pl.ds((f * REACH + d) * ca, ca), :]


def add_corners(count, ca, cz, block_in, corner1, corner2, *rest):
    edges, block, outs, corners = rest[:count], rest[count], rest[count + 1 : -1], rest[-1]
    cr = corner1.shape[1]
    planes = ca + 2 * REACH
    up = first_is_up("az")
    a, b = corner1[...].astype(F32), corner2[...].astype(F32)
    corners[0] = jnp.where(up, b, a)
    corners[1] = jnp.where(up, a, b)
    for f in range(5):
        for d in range(MID):
            for side, row in ((0, OFF - 1 - d), (1, OFF + cz + d)):
                at = kept(row) + f * planes * ROWS
                start = (f * MID + d) * 2 * MID
                got = corners[side, pl.ds(start, MID), :]
                block[pl.ds(at + (REACH - MID) * ROWS, MID, stride=ROWS), :] = got
                got = corners[side, pl.ds(start + MID, MID), :]
                block[pl.ds(at + (REACH + ca) * ROWS, MID, stride=ROWS), :] = got

    tiles = cr // SLOT
    step = tiles * 8
    rows = []
    for f in range(5):
        for k in range((ca + 2 * MID) * ROWS // step):
            at = (f * planes + REACH - MID) * ROWS + k * step
            rows.append(jnp.concatenate([block[at + 8 * t : at + 8 * t + 8, :] for t in range(tiles)], axis=1))
    rows = jnp.concatenate(rows, axis=0).astype(BF16)
    for edge, out in zip(edges, outs):
        out[...] = jnp.dot(rows, edge[...], preferred_element_type=F32).astype(BF16)


def az_terms(flux):
    v = [flux[8 * l : 8 * l + 8] for l in range(4)]
    v = [pltpu.roll(v[2], 1, 0), pltpu.roll(v[3], 1, 0)] + v + [pltpu.roll(v[0], 7, 0), pltpu.roll(v[1], 7, 0)]
    out = [8.0 * (v[l + 3] - v[l + 1]) - (v[l + 4] - v[l]) for l in range(4)]
    side = flux[ROWS:]
    lanes = side.shape[1]
    span = lax.broadcasted_iota(jnp.int32, side.shape, 1) // SPAN
    up, down = pltpu.roll(side, 7, 0), pltpu.roll(side, 1, 0)
    up1 = pltpu.roll(jnp.where(span == 0, up, side), lanes - SPAN, 1)
    up2 = pltpu.roll(jnp.where(span < 2, up, side), lanes - 2 * SPAN, 1)
    down1 = pltpu.roll(jnp.where(span == 3, down, side), SPAN, 1)
    down2 = pltpu.roll(jnp.where(span >= 2, down, side), 2 * SPAN, 1)
    out.append(8.0 * (up1 - down1) - (up2 - down2))
    return jnp.concatenate(out, axis=0)


def band(cr):
    def place(axis, none):
        i = lax.broadcasted_iota(jnp.int32, (2 * cr, 2 * cr), axis)
        j = i % SPAN
        beyond = jnp.where(j < REACH, cr + j, jnp.where(j >= SPAN - REACH, j - SPAN, none))
        return jnp.where(i < cr, i, beyond), jnp.where(i < cr, -1, i // SPAN)

    k, k_span = place(0, 4 * cr)
    n, n_span = place(1, -4 * cr)
    gap = k - n
    out = jnp.where(gap == 1, 8.0, 0.0) + jnp.where(gap == -1, -8.0, 0.0)
    out = out + jnp.where(gap == 2, -1.0, 0.0) + jnp.where(gap == -2, 1.0, 0.0)
    apart = (k_span >= 0) & (n_span >= 0) & (k_span != n_span)
    return jnp.where(apart, 0.0, out).astype(BF16)


def split_state(u):
    rho, m0, m1, m2, energy = u
    inv = 1.0 / rho
    vel = [m0 * inv, m1 * inv, m2 * inv]
    pres = GAMMA_M * (energy - 0.5 * (m0 * vel[0] + m1 * vel[1] + m2 * vel[2]))
    return [m0, m1, m2], vel, pres, energy


def flux(d, mom, vel, pres, energy):
    parts = [mom[d]]
    for j in range(3):
        parts.append(mom[d] * vel[j] + pres if j == d else mom[d] * vel[j])
    parts.append((energy + pres) * vel[d])
    return parts


def ax_only(u, fax, j):
    got = flux(0, *u)
    for f in range(5):
        fax[f, j, 0:ROWS] = got[f]


def both_sides(us, js, fax, part, banded):
    rows = []
    shape = (ROWS, banded.shape[0] // 2)
    span = lax.broadcasted_iota(jnp.int32, shape, 1) // SPAN
    mine = span == lax.broadcasted_iota(jnp.int32, shape, 0) // 8
    for u, j in zip(us, js):
        got = flux(0, *u)
        for f in range(5):
            fax[f, j] = got[f]
        got = flux(2, *u)
        for f in range(5):
            side = jnp.where(mine, jnp.concatenate([got[f][ROWS:]] * 4, axis=0), 0.0)
            rows.append(jnp.concatenate([got[f][0:ROWS], side], axis=1))
    rows = jnp.concatenate(rows, axis=0).astype(BF16)
    out = jnp.dot(rows, banded[...], preferred_element_type=F32)
    half = out.shape[1] // 2
    for i, (u, j) in enumerate(zip(us, js)):
        got = flux(1, *u)
        for f in range(5):
            at = (i * 5 + f) * ROWS
            side = out[at : at + 8, half:]
            for l in range(1, 4):
                side = jnp.where(span[0:8] == l, out[at + 8 * l : at + 8 * l + 8, half:], side)
            radial = jnp.concatenate([out[at : at + ROWS, 0:half], side], axis=0)
            part[f, j] = az_terms(got[f]) + radial


def change(fa, part, f, j, size):
    near = fa(j + 1)[0:size] - fa(j - 1)[0:size]
    far = fa(j + 2)[0:size] - fa(j - 2)[0:size]
    return SCALE * (8.0 * near - far + part[f, j, 0:size])


def window(fax, f):
    held = {}

    def get(j):
        if j not in held:
            held[j] = fax[f, j]
        return held[j]

    return get


def stages(n_ax, n_rad, ca, cz, slots, block, banded, cells_far, *refs):
    sides, refs = refs[: len(refs) - 12], refs[len(refs) - 12 :]
    sides, places = sides[: len(sides) // 2], sides[len(sides) // 2 :]
    q_out, u2_out, u0_out, ghost, first, second, fax, part, value, picked, cells, cells_sem = refs
    fetch = pltpu.make_async_copy(cells_far, cells, cells_sem)
    fetch.start()
    cr = block.shape[-1]
    low, high = REACH, REACH + ca
    ax = ax_index()
    rad = lax.axis_index("rad")

    lane = lax.broadcasted_iota(jnp.int32, (8, cr), 1)
    row = 4 * lax.broadcasted_iota(jnp.int32, (8, cr), 0) + lane // SPAN
    j = lane % SPAN
    steps_rad = jnp.where(
        (j < REACH) & (rad < n_rad - 1),
        1 + j // 2,
        jnp.where((j >= SPAN - REACH) & (rad > 0), 1 + (SPAN - 1 - j) // 2, 99),
    )
    beyond_row = jnp.maximum(OFF - row, row - (OFF + cz - 1))
    steps = steps_rad + jnp.where(beyond_row > 0, (beyond_row + 1) // 2, 0)
    base0 = jnp.where(steps_rad < 99, 0.0, 1.0)

    side = 0.0
    for got, place in zip(sides, places):
        side = side + jnp.dot(got[...], place[...], preferred_element_type=F32)
    group = side.shape[1] // cr
    count = (ca + 2 * MID) // group
    for f in range(5):
        for k in range(count):
            for i in range(group):
                at = (f * count + k) * 8
                tile = side[at : at + 8, i * cr : (i + 1) * cr]
                ghost[f, k * group + i] = tile + base0 if f == 0 else tile

    def start_state(j, both):
        u = []
        for f in range(5):
            x = block[f, j]
            u.append(jnp.concatenate([x, ghost[f, j - (REACH - MID)]], axis=0) if both else x)
        rho, vel, pres = u[0], u[1:4], u[4]
        mom = [rho * x for x in vel]
        energy = pres * (1.0 / GAMMA_M) + 0.5 * (mom[0] * vel[0] + mom[1] * vel[1] + mom[2] * vel[2])
        return rho, (mom, vel, pres, energy)

    def note(s, j, u):
        value[s, j] = (u[2] - P_REF + u[0][0])[0:ROWS]

    for j in (low - 6, low - 5, high + 4, high + 5):
        ax_only(start_state(j, False)[1], fax, j)

    step = (ca + 2 * MID) // STEPS

    @pl.loop(0, STEPS)
    def _(i):
        js = [low - 4 + step * i + k for k in range(step)]
        us = []
        for j in js:
            rho, u = start_state(j, True)
            for f, x in enumerate([rho] + u[0] + [u[3]]):
                first[f, j] = x
            note(0, j, u)
            us.append(u)
        both_sides(us, js, fax, part, banded)

    def update(f, j, fa, stage):
        a = max(low - j, j - (high - 1), 0)
        a = (a + 1) // 2
        lim = 2 - stage
        base = 1.0 if f == 0 else 0.0
        size = ROWS if a == lim else TALL
        new = change(fa, part, f, j, size)
        u0 = first[f, j, 0:size]
        if stage == 0:
            new = u0 + new
        else:
            new = 0.75 * u0 + 0.25 * (second[f, j, 0:size] + new)
        beyond = (ax == 0) if j < low else (ax == n_ax - 1)
        home = new[0:ROWS]
        if a > 0:
            home = jnp.where(beyond, base, home)
        if size == ROWS:
            return home, None
        ok = steps <= lim - a
        if a > 0:
            ok = ok & jnp.logical_not(beyond)
        return home, jnp.where(ok, new[ROWS:], base)

    for f in range(5):
        fa = window(fax, f)
        for j in range(low - 4, high + 4):
            home, side = update(f, j, fa, 0)
            second[f, j, 0:ROWS] = home
            if side is not None:
                second[f, j, ROWS:] = side

    for j in (low - 4, low - 3, high + 2, high + 3):
        ax_only(split_state([second[f, j, 0:ROWS] for f in range(5)]), fax, j)

    step2 = (ca + MID) // STEPS

    @pl.loop(0, STEPS)
    def _(i):
        js = [low - 2 + step2 * i + k for k in range(step2)]
        us = []
        for j in js:
            u = split_state([second[f, j] for f in range(5)])
            note(1, j, u)
            us.append(u)
        both_sides(us, js, fax, part, banded)

    for f in range(5):
        fa = window(fax, f)
        for j in range(low - 2, high + 2):
            home, side = update(f, j, fa, 1)
            u2_out[f, j - (low - 2), 0:ROWS] = home
            if side is not None:
                u2_out[f, j - (low - 2), ROWS:] = side
        for j in range(low, high):
            u0_out[f, j - low] = first[f, j, 0:ROWS]

    @pl.loop(0, ca)
    def _(i):
        u = split_state([u2_out[f, i + 2, 0:ROWS] for f in range(5)])
        note(2, low + i, u)

    fetch.wait()
    picked[...] = jnp.zeros_like(picked)
    lanes = lax.broadcasted_iota(jnp.int32, (1, cr), 1)
    for p in range(slots):
        cell = cells[p]
        at = jnp.maximum(cell, 0)
        column = jnp.where(cell >= 0, lax.rem(at, cr), -1)
        at = lax.div(at, cr)
        plane = low + lax.div(at, cz)
        r = lax.rem(at, cz) + OFF
        r = 8 * lax.rem(r, 4) + lax.div(r, 4)
        hit = lanes == column
        for s in range(3):
            picked[pl.ds(s * slots + p, 1), :] = jnp.where(hit, value[s, plane, pl.ds(r, 1), :], 0.0)
    q = lax.dot_general(
        jnp.ones((8, cr), BF16),
        picked[...].astype(BF16),
        (((1,), (1,)), ((), ())),
        preferred_element_type=F32,
    )
    q_out[...] = jnp.broadcast_to(q[0:1][None], q_out.shape)


def last_stage(ca, cz, u2, u0, banded, state, fax, part):
    for j in (0, 1, ca + 2, ca + 3):
        ax_only(split_state([u2[f, j, 0:ROWS] for f in range(5)]), fax, j)

    step = ca // STEPS

    @pl.loop(0, STEPS)
    def _(i):
        js = [2 + step * i + k for k in range(step)]
        us = [split_state([u2[f, j] for f in range(5)]) for j in js]
        both_sides(us, js, fax, part, banded)

    first, quarter = OFF // 4, cz // 4

    @pl.loop(0, 5)
    def _(f):
        fa = window(fax, f)
        for k in range(ca):
            j = k + 2
            new = u2[f, j, 0:ROWS] + change(fa, part, f, j, ROWS)
            new = u0[f, k] * (1.0 / 3.0) + (2.0 / 3.0) * new
            for l in range(4):
                state[f, k, pl.ds(l, quarter, stride=4), :] = new[8 * l + first : 8 * l + first + quarter]


def signals(slots, rows, offsets, weight, out):
    ndev = rows.shape[0]
    group = 32
    cols = group * slots
    lanes = rows.shape[1]
    col = lax.broadcasted_iota(jnp.int32, (1, cols), 1)
    owner = lax.broadcasted_iota(jnp.int32, (group, cols), 0) == col // slots
    lane = lax.broadcasted_iota(jnp.int32, (lanes, cols), 0)
    time = lax.broadcasted_iota(jnp.int32, (NB, cols), 0).astype(F32)
    total = jnp.zeros(out.shape, F32)
    for g in range(ndev // group):
        q = rows[g * group : (g + 1) * group, :].astype(BF16)
        off = offsets[0:1, g * group : (g + 1) * group].astype(F32)
        off = jnp.broadcast_to(off, (8, group)).astype(BF16)
        bins = jnp.dot(off, owner.astype(BF16), preferred_element_type=F32)[0:1]
        table = jnp.zeros((NB, cols), F32)
        for s in range(3):
            pick = jnp.where(lane == s * slots + col % slots, 1.0, 0.0).astype(BF16)
            spread = jnp.dot(q, pick, preferred_element_type=F32)
            line = jnp.sum(jnp.where(owner, spread, 0.0), axis=0, keepdims=True)
            table = jnp.where(time == bins + s, line, table)
        total = total + lax.dot_general(
            weight[:, g * cols : (g + 1) * cols],
            table.astype(BF16),
            (((1,), (1,)), ((), ())),
            preferred_element_type=F32,
        )
    out[...] = total


def swap_pairs(count, periodic):
    one = [(i, i ^ 1) for i in range(count)]
    two = []
    for i in range(count):
        j = i - 1 if i % 2 == 0 else i + 1
        two.append((i, j % count if periodic or 0 <= j < count else i))
    return one, two


def swap(first, second, axis, periodic):
    count = 1
    for name in (axis,) if isinstance(axis, str) else axis:
        count = count * lax.axis_size(name)
    one, two = swap_pairs(count, periodic)
    if periodic:
        one, two = two, one
    return lax.ppermute(first, axis, one), lax.ppermute(second, axis, two)


def local(density, velocity, pressure, panel_cell, obs_weight, bin_offset):
    ca, cz, cr = density.shape
    slots = panel_cell.shape[0]
    ndev = bin_offset.shape[1]
    n_ax, n_rad = lax.axis_size("y") * lax.axis_size("core"), lax.axis_size("rad")
    planes = ca + 2 * REACH
    part = functools.partial
    given = (density.reshape(ca * cz, cr), velocity.reshape(3 * ca * cz, cr), pressure.reshape(ca * cz, cr))

    edge = struct((5 * REACH * cz, cr), BF16)
    strip = struct((5 * REACH * ca, cr), BF16)
    home, ax1, ax2 = call(
        part(load_and_pack, ca, cz),
        (struct((5 * ca * cz, cr)), edge, edge),
        [HBM] * 3,
        [pltpu.SemaphoreType.DMA((3,))],
    )(*[far(x) for x in given])
    az1, az2 = call(part(pack_az, ca, cz), (strip, strip), [VMEM])(home)
    ax1, ax2 = swap(ax1, ax2, ("y", "core"), False)
    az1, az2 = swap(az1, az2, "az", True)
    grid = struct((5 * planes * ROWS, cr))
    ends = ("either",) if n_rad == 2 else ("low", "high")
    tiles = cr // SLOT
    table = [struct((tiles * cr, cr), BF16)] * len(ends) + [struct((cr, tiles * cr // 4), BF16)] * len(ends)
    block, banded, *tables = call(
        part(prepare, ends, ca, cz, n_rad),
        (grid, struct((2 * cr, 2 * cr), BF16), *table),
        [VMEM],
    )(home)
    edges, places = tables[: len(ends)], tables[len(ends) :]

    corner = struct((5 * MID * 2 * MID, cr), BF16)
    near = pltpu.VMEM((5, 2 * MID * cz, cr), F32)
    corner1, corner2 = call(part(pack_corners, n_ax, cz), (corner, corner), [VMEM] * 2, [near])(ax1, ax2)
    corner1, corner2 = swap(corner1, corner2, "az", True)

    side = struct((5 * (ca + 2 * MID) * ROWS // tiles, cr), BF16)
    block = call(
        part(add_sides, n_ax, ca, cz),
        grid,
        [VMEM] * 5,
        [pltpu.VMEM((5, 2 * REACH * cz, cr), F32), pltpu.VMEM((2,) + strip.shape, F32)],
        mib=8,
        alias={0: 0},
        cost=pl.CostEstimate(flops=100_000_000, bytes_accessed=4_000_000, transcendentals=0),
    )(block, ax1, ax2, az1, az2)
    got = call(
        part(add_corners, len(ends), ca, cz),
        (grid,) + tuple(side for _ in ends),
        [VMEM] * (3 + len(ends)),
        [pltpu.VMEM((2,) + corner.shape, F32)],
        mib=8,
        alias={0: 0},
    )(block, corner1, corner2, *edges)
    block = got[0].reshape(5, planes, ROWS, cr)
    if n_rad == 2:
        sides = (lax.ppermute(got[1], "rad", [(0, 1), (1, 0)]),)
    else:
        up = [(i, i + 1) for i in range(n_rad - 1)]
        sides = (lax.ppermute(got[1], "rad", [(j, i) for i, j in up]), lax.ppermute(got[2], "rad", up))

    grid = (5, planes, TALL, cr)
    q, u2, u0 = call(
        part(stages, n_ax, n_rad, ca, cz, slots),
        (struct((ndev, 1, 128)), struct((5, ca + 4, TALL, cr)), struct((5, ca, ROWS, cr))),
        [VMEM, VMEM, HBM] + [VMEM] * (2 * len(sides)),
        [pltpu.VMEM((5, ca + 2 * MID, 8, cr), F32)]
        + [pltpu.VMEM(grid, F32) for _ in range(4)]
        + [pltpu.VMEM((3, planes, ROWS, cr), F32), pltpu.VMEM((128, cr), F32)]
        + [pltpu.SMEM((slots,), jnp.int32), pltpu.SemaphoreType.DMA],
        mib=28,
    )(block, banded, far(panel_cell), *sides, *places)

    rows = lax.all_to_all(q, ("y", "core", "az", "rad"), 0, 0, tiled=True).reshape(ndev, 128)

    grid = (5, ca + 4, TALL, cr)
    state = call(
        part(last_stage, ca, cz),
        struct((5, ca, cz, cr)),
        [VMEM] * 3,
        [pltpu.VMEM(grid, F32), pltpu.VMEM(grid, F32)],
        mib=12,
        cost=pl.CostEstimate(flops=400_000_000, bytes_accessed=8_000_000, transcendentals=0),
    )(u2, u0, banded)
    signal = call(
        part(signals, slots), struct((obs_weight.shape[0], NB)), [VMEM] * 3, mib=24
    )(rows, bin_offset, obs_weight)
    return (state, signal)


def solution(mesh):
    n_ax, n_az, n_rad = (mesh.shape[name] for name in ("ax", "az", "rad"))
    split = Mesh(mesh.devices.reshape(n_ax // 2, 2, n_az, n_rad), ("y", "core", "az", "rad"))
    ax = ("y", "core")
    every = ax + ("az", "rad")
    in_specs = (
        P(ax, "az", "rad"),
        P(None, ax, "az", "rad"),
        P(ax, "az", "rad"),
        P(every),
        P(every, None),
        P(every, None),
    )
    out_specs = (P(None, ax, "az", "rad"), P(every, None))
    return jax.shard_map(local, mesh=split, in_specs=in_specs, out_specs=out_specs, check_vma=False)
```

```python
import functools

import jax
import jax.numpy as jnp
from jax import lax
from jax.experimental import pallas as pl
from jax.experimental.pallas import tpu as pltpu
from jax.sharding import Mesh, PartitionSpec as P

NB = 128
GAMMA_M = 0.4
LAMBDA = 0.1
P_REF = 1.0
REACH = 6
MID = 4
SCALE = -LAMBDA / 12.0
ROWS = 32
OFF = 8
SPAN = 32
TALL = ROWS + 8
STEPS = 1
SLOT = 8
HBM = pltpu.MemorySpace.HBM
VMEM = pltpu.MemorySpace.VMEM
SMEM = pltpu.MemorySpace.SMEM
F32 = jnp.float32
BF16 = jnp.bfloat16


def call(kernel, outs, in_spaces, scratch=(), mib=8, cost=None, alias={}):
    return pl.pallas_call(
        kernel,
        out_shape=outs,
        in_specs=[pl.BlockSpec(memory_space=s) for s in in_spaces],
        out_specs=jax.tree.map(lambda _: pl.BlockSpec(memory_space=VMEM), outs),
        scratch_shapes=list(scratch),
        compiler_params=pltpu.CompilerParams(vmem_limit_bytes=mib * 1024 * 1024),
        cost_estimate=cost,
        input_output_aliases=alias,
    )


def far(x):
    return pltpu.with_memory_space_constraint(x, HBM)


def struct(shape, dtype=F32):
    return jax.ShapeDtypeStruct(shape, dtype)


def kept(row):
    return 8 * (row % 4) + row // 4


def ax_index():
    return lax.axis_index("y") * lax.axis_size("core") + lax.axis_index("core")


def first_is_up(axis):
    if axis == "ax":
        return lax.axis_index("core") == 0
    return lax.axis_index("az") % 2 == 1


def load_and_pack(ca, cz, den, vel, pre, home, ax1, ax2, sems):
    size = ca * cz
    copies = [
        pltpu.make_async_copy(den, home.at[pl.ds(0, size)], sems.at[0]),
        pltpu.make_async_copy(vel, home.at[pl.ds(size, 3 * size)], sems.at[1]),
        pltpu.make_async_copy(pre, home.at[pl.ds(4 * size, size)], sems.at[2]),
    ]
    for copy in copies:
        copy.start()
    for copy in copies:
        copy.wait()
    up = first_is_up("ax")
    edge = REACH * cz
    for f in range(5):
        at = f * size
        low = home[at : at + edge, :]
        high = home[at + size - edge : at + size, :]
        rows = slice(f * edge, (f + 1) * edge)
        ax1[rows, :] = jnp.where(up, high, low).astype(BF16)
        ax2[rows, :] = jnp.where(up, low, high).astype(BF16)


def pack_az(ca, cz, home, az1, az2):
    size = ca * cz
    up = first_is_up("az")
    low, high = [], []
    for f in range(5):
        for d in range(REACH):
            low.append(home[pl.ds(f * size + d, ca, stride=cz), :])
            high.append(home[pl.ds(f * size + cz - 1 - d, ca, stride=cz), :])
    low, high = jnp.concatenate(low, axis=0), jnp.concatenate(high, axis=0)
    az1[...] = jnp.where(up, high, low).astype(BF16)
    az2[...] = jnp.where(up, low, high).astype(BF16)


def ax_sides(n_ax, got1, got2, rows):
    ax = ax_index()
    a, b = got1[rows, :].astype(F32), got2[rows, :].astype(F32)
    up = first_is_up("ax")
    lo = jnp.where(ax == 0, 0.0, jnp.where(up, b, a))
    hi = jnp.where(ax == n_ax - 1, 0.0, jnp.where(up, a, b))
    return lo, hi


def pack_corners(n_ax, cz, got1, got2, first_out, second_out, near):
    up = first_is_up("az")
    half = MID * cz
    size = REACH * cz
    for f in range(5):
        lo, hi = ax_sides(n_ax, got1, got2, slice(f * size, (f + 1) * size))
        near[f, 0:half, :] = lo[size - half :]
        near[f, half : 2 * half, :] = hi[0:half]
    low, high = [], []
    for f in range(5):
        for d in range(MID):
            low.append(near[f, pl.ds(d, 2 * MID, stride=cz), :])
            high.append(near[f, pl.ds(cz - 1 - d, 2 * MID, stride=cz), :])
    low, high = jnp.concatenate(low, axis=0), jnp.concatenate(high, axis=0)
    first_out[...] = jnp.where(up, high, low).astype(BF16)
    second_out[...] = jnp.where(up, low, high).astype(BF16)


def spread_rows(planes, cz, f, plane, ref, at, block):
    quarter = cz // 4
    for l in range(4):
        row = (f * planes + plane) * ROWS + 8 * l + OFF // 4
        block[pl.ds(row, quarter), :] = ref[pl.ds(at + l, quarter, stride=4), :]


def prepare(ends, ca, cz, n_rad, home, block, banded, *tables):
    cr = home.shape[1]
    rad = lax.axis_index("rad")
    for f in range(5):
        for k in range(ca):
            spread_rows(ca + 2 * REACH, cz, f, REACH + k, home, (f * ca + k) * cz, block)
    banded[...] = band(cr)
    edges, places = tables[: len(ends)], tables[len(ends) :]
    tiles = cr // SLOT
    there = {"high": jnp.where(rad < n_rad - 1, 1.0, 0.0), "low": jnp.where(rad > 0, 1.0, 0.0)}
    high = place_matrix(0, tiles, cr) * there["high"]
    low = place_matrix(SPAN - REACH, tiles, cr) * there["low"]
    for end, edge, place in zip(ends, edges, places):
        start = {"low": 0, "high": cr - REACH, "either": jnp.where(rad == 0, cr - REACH, 0)}[end]
        edge[...] = edge_matrix(start, tiles, cr)
        place[...] = {"low": high, "high": low, "either": high + low}[end].astype(BF16)


def edge_matrix(start, tiles, cr):
    k = lax.broadcasted_iota(jnp.int32, (tiles * cr, tiles * SLOT), 0)
    n = lax.broadcasted_iota(jnp.int32, (tiles * cr, tiles * SLOT), 1)
    hit = (k // cr == n // SLOT) & (n % SLOT < REACH) & (k % cr == n % SLOT + start)
    return jnp.where(hit, 1.0, 0.0).astype(BF16)


def place_matrix(start, tiles, cr):
    k = lax.broadcasted_iota(jnp.int32, (tiles * SLOT, tiles * cr // 4), 0)
    n = lax.broadcasted_iota(jnp.int32, (tiles * SLOT, tiles * cr // 4), 1)
    hit = (k // SLOT == n // SPAN) & (k % SLOT < REACH) & (n % SPAN == k % SLOT + start)
    return jnp.where(hit, 1.0, 0.0)


def add_sides(n_ax, ca, cz, block_in, ax1, ax2, az1, az2, block, sides, strips):
    planes = ca + 2 * REACH
    size = REACH * cz
    for f in range(5):
        lo, hi = ax_sides(n_ax, ax1, ax2, slice(f * size, (f + 1) * size))
        sides[f, 0:size, :] = lo
        sides[f, size : 2 * size, :] = hi
    for f in range(5):
        for k in range(REACH):
            spread_rows(planes, cz, f, k, sides.at[f], k * cz, block)
            spread_rows(planes, cz, f, REACH + ca + k, sides.at[f], size + k * cz, block)
    up = first_is_up("az")
    a, b = az1[...].astype(F32), az2[...].astype(F32)
    strips[0] = jnp.where(up, b, a)
    strips[1] = jnp.where(up, a, b)
    for f in range(5):
        for d in range(REACH):
            for side, row in ((0, OFF - 1 - d), (1, OFF + cz + d)):
                at = kept(row) + (f * planes + REACH) * ROWS
                block[pl.ds(at, ca, stride=ROWS), :] = strips[side, pl.ds((f * REACH + d) * ca, ca), :]


def add_corners(count, ca, cz, block_in, corner1, corner2, *rest):
    edges, block, outs, corners = rest[:count], rest[count], rest[count + 1 : -1], rest[-1]
    cr = corner1.shape[1]
    planes = ca + 2 * REACH
    up = first_is_up("az")
    a, b = corner1[...].astype(F32), corner2[...].astype(F32)
    corners[0] = jnp.where(up, b, a)
    corners[1] = jnp.where(up, a, b)
    for f in range(5):
        for d in range(MID):
            for side, row in ((0, OFF - 1 - d), (1, OFF + cz + d)):
                at = kept(row) + f * planes * ROWS
                start = (f * MID + d) * 2 * MID
                got = corners[side, pl.ds(start, MID), :]
                block[pl.ds(at + (REACH - MID) * ROWS, MID, stride=ROWS), :] = got
                got = corners[side, pl.ds(start + MID, MID), :]
                block[pl.ds(at + (REACH + ca) * ROWS, MID, stride=ROWS), :] = got

    tiles = cr // SLOT
    step = tiles * 8
    rows = []
    for f in range(5):
        for k in range((ca + 2 * MID) * ROWS // step):
            at = (f * planes + REACH - MID) * ROWS + k * step
            rows.append(jnp.concatenate([block[at + 8 * t : at + 8 * t + 8, :] for t in range(tiles)], axis=1))
    rows = jnp.concatenate(rows, axis=0).astype(BF16)
    for edge, out in zip(edges, outs):
        out[...] = jnp.dot(rows, edge[...], preferred_element_type=F32).astype(BF16)


def az_terms(flux):
    v = [flux[8 * l : 8 * l + 8] for l in range(4)]
    v = [pltpu.roll(v[2], 1, 0), pltpu.roll(v[3], 1, 0)] + v + [pltpu.roll(v[0], 7, 0), pltpu.roll(v[1], 7, 0)]
    out = [8.0 * (v[l + 3] - v[l + 1]) - (v[l + 4] - v[l]) for l in range(4)]
    side = flux[ROWS:]
    lanes = side.shape[1]
    span = lax.broadcasted_iota(jnp.int32, side.shape, 1) // SPAN
    up, down = pltpu.roll(side, 7, 0), pltpu.roll(side, 1, 0)
    up1 = pltpu.roll(jnp.where(span == 0, up, side), lanes - SPAN, 1)
    up2 = pltpu.roll(jnp.where(span < 2, up, side), lanes - 2 * SPAN, 1)
    down1 = pltpu.roll(jnp.where(span == 3, down, side), SPAN, 1)
    down2 = pltpu.roll(jnp.where(span >= 2, down, side), 2 * SPAN, 1)
    out.append(8.0 * (up1 - down1) - (up2 - down2))
    return jnp.concatenate(out, axis=0)


def band(cr):
    def place(axis, none):
        i = lax.broadcasted_iota(jnp.int32, (2 * cr, 2 * cr), axis)
        j = i % SPAN
        beyond = jnp.where(j < REACH, cr + j, jnp.where(j >= SPAN - REACH, j - SPAN, none))
        return jnp.where(i < cr, i, beyond), jnp.where(i < cr, -1, i // SPAN)

    k, k_span = place(0, 4 * cr)
    n, n_span = place(1, -4 * cr)
    gap = k - n
    out = jnp.where(gap == 1, 8.0, 0.0) + jnp.where(gap == -1, -8.0, 0.0)
    out = out + jnp.where(gap == 2, -1.0, 0.0) + jnp.where(gap == -2, 1.0, 0.0)
    apart = (k_span >= 0) & (n_span >= 0) & (k_span != n_span)
    return jnp.where(apart, 0.0, out).astype(BF16)


def split_state(u):
    rho, m0, m1, m2, energy = u
    inv = 1.0 / rho
    vel = [m0 * inv, m1 * inv, m2 * inv]
    pres = GAMMA_M * (energy - 0.5 * (m0 * vel[0] + m1 * vel[1] + m2 * vel[2]))
    return [m0, m1, m2], vel, pres, energy


def flux(d, mom, vel, pres, energy):
    parts = [mom[d]]
    for j in range(3):
        parts.append(mom[d] * vel[j] + pres if j == d else mom[d] * vel[j])
    parts.append((energy + pres) * vel[d])
    return parts


def ax_only(u, fax, j):
    got = flux(0, *u)
    for f in range(5):
        fax[f, j, 0:ROWS] = got[f]


def both_sides(us, js, fax, part, banded):
    rows = []
    shape = (ROWS, banded.shape[0] // 2)
    span = lax.broadcasted_iota(jnp.int32, shape, 1) // SPAN
    mine = span == lax.broadcasted_iota(jnp.int32, shape, 0) // 8
    for u, j in zip(us, js):
        got = flux(0, *u)
        for f in range(5):
            fax[f, j] = got[f]
        got = flux(2, *u)
        for f in range(5):
            side = jnp.where(mine, jnp.concatenate([got[f][ROWS:]] * 4, axis=0), 0.0)
            rows.append(jnp.concatenate([got[f][0:ROWS], side], axis=1))
    rows = jnp.concatenate(rows, axis=0).astype(BF16)
    out = jnp.dot(rows, banded[...], preferred_element_type=F32)
    half = out.shape[1] // 2
    for i, (u, j) in enumerate(zip(us, js)):
        got = flux(1, *u)
        for f in range(5):
            at = (i * 5 + f) * ROWS
            side = out[at : at + 8, half:]
            for l in range(1, 4):
                side = jnp.where(span[0:8] == l, out[at + 8 * l : at + 8 * l + 8, half:], side)
            radial = jnp.concatenate([out[at : at + ROWS, 0:half], side], axis=0)
            part[f, j] = az_terms(got[f]) + radial


def change(fa, part, f, j, size):
    near = fa(j + 1)[0:size] - fa(j - 1)[0:size]
    far = fa(j + 2)[0:size] - fa(j - 2)[0:size]
    return SCALE * (8.0 * near - far + part[f, j, 0:size])


def window(fax, f):
    held = {}

    def get(j):
        if j not in held:
            held[j] = fax[f, j]
        return held[j]

    return get


def stages(n_ax, n_rad, ca, cz, slots, block, banded, cells_far, *refs):
    sides, refs = refs[: len(refs) - 12], refs[len(refs) - 12 :]
    sides, places = sides[: len(sides) // 2], sides[len(sides) // 2 :]
    q_out, u2_out, u0_out, ghost, first, second, fax, part, value, picked, cells, cells_sem = refs
    fetch = pltpu.make_async_copy(cells_far, cells, cells_sem)
    fetch.start()
    cr = block.shape[-1]
    low, high = REACH, REACH + ca
    ax = ax_index()
    rad = lax.axis_index("rad")

    lane = lax.broadcasted_iota(jnp.int32, (8, cr), 1)
    row = 4 * lax.broadcasted_iota(jnp.int32, (8, cr), 0) + lane // SPAN
    j = lane % SPAN
    steps_rad = jnp.where(
        (j < REACH) & (rad < n_rad - 1),
        1 + j // 2,
        jnp.where((j >= SPAN - REACH) & (rad > 0), 1 + (SPAN - 1 - j) // 2, 99),
    )
    beyond_row = jnp.maximum(OFF - row, row - (OFF + cz - 1))
    steps = steps_rad + jnp.where(beyond_row > 0, (beyond_row + 1) // 2, 0)
    base0 = jnp.where(steps_rad < 99, 0.0, 1.0)

    side = 0.0
    for got, place in zip(sides, places):
        side = side + jnp.dot(got[...], place[...], preferred_element_type=F32)
    group = side.shape[1] // cr
    count = (ca + 2 * MID) // group
    for f in range(5):
        for k in range(count):
            for i in range(group):
                at = (f * count + k) * 8
                tile = side[at : at + 8, i * cr : (i + 1) * cr]
                ghost[f, k * group + i] = tile + base0 if f == 0 else tile

    def start_state(j, both):
        u = []
        for f in range(5):
            x = block[f, j]
            u.append(jnp.concatenate([x, ghost[f, j - (REACH - MID)]], axis=0) if both else x)
        rho, vel, pres = u[0], u[1:4], u[4]
        mom = [rho * x for x in vel]
        energy = pres * (1.0 / GAMMA_M) + 0.5 * (mom[0] * vel[0] + mom[1] * vel[1] + mom[2] * vel[2])
        return rho, (mom, vel, pres, energy)

    def note(s, j, u):
        value[s, j] = (u[2] - P_REF + u[0][0])[0:ROWS]

    for j in (low - 6, low - 5, high + 4, high + 5):
        ax_only(start_state(j, False)[1], fax, j)

    step = (ca + 2 * MID) // STEPS

    for i in range(STEPS):
        js = [low - 4 + step * i + k for k in range(step)]
        us = []
        for j in js:
            rho, u = start_state(j, True)
            for f, x in enumerate([rho] + u[0] + [u[3]]):
                first[f, j] = x
            note(0, j, u)
            us.append(u)
        both_sides(us, js, fax, part, banded)

    def update(f, j, fa, stage):
        a = max(low - j, j - (high - 1), 0)
        a = (a + 1) // 2
        lim = 2 - stage
        base = 1.0 if f == 0 else 0.0
        size = ROWS if a == lim else TALL
        new = change(fa, part, f, j, size)
        u0 = first[f, j, 0:size]
        if stage == 0:
            new = u0 + new
        else:
            new = 0.75 * u0 + 0.25 * (second[f, j, 0:size] + new)
        beyond = (ax == 0) if j < low else (ax == n_ax - 1)
        home = new[0:ROWS]
        if a > 0:
            home = jnp.where(beyond, base, home)
        if size == ROWS:
            return home, None
        ok = steps <= lim - a
        if a > 0:
            ok = ok & jnp.logical_not(beyond)
        return home, jnp.where(ok, new[ROWS:], base)

    for f in range(5):
        fa = window(fax, f)
        for j in range(low - 4, high + 4):
            home, side = update(f, j, fa, 0)
            second[f, j, 0:ROWS] = home
            if side is not None:
                second[f, j, ROWS:] = side

    for j in (low - 4, low - 3, high + 2, high + 3):
        ax_only(split_state([second[f, j, 0:ROWS] for f in range(5)]), fax, j)

    step2 = (ca + MID) // STEPS

    for i in range(STEPS):
        js = [low - 2 + step2 * i + k for k in range(step2)]
        us = []
        for j in js:
            u = split_state([second[f, j] for f in range(5)])
            note(1, j, u)
            us.append(u)
        both_sides(us, js, fax, part, banded)

    for f in range(5):
        fa = window(fax, f)
        for j in range(low - 2, high + 2):
            home, side = update(f, j, fa, 1)
            u2_out[f, j - (low - 2), 0:ROWS] = home
            if side is not None:
                u2_out[f, j - (low - 2), ROWS:] = side
        for j in range(low, high):
            u0_out[f, j - low] = first[f, j, 0:ROWS]

    for i in range(ca):
        u = split_state([u2_out[f, i + 2, 0:ROWS] for f in range(5)])
        note(2, low + i, u)

    fetch.wait()
    picked[...] = jnp.zeros_like(picked)
    lanes = lax.broadcasted_iota(jnp.int32, (1, cr), 1)
    for p in range(slots):
        cell = cells[p]
        at = jnp.maximum(cell, 0)
        column = jnp.where(cell >= 0, lax.rem(at, cr), -1)
        at = lax.div(at, cr)
        plane = low + lax.div(at, cz)
        r = lax.rem(at, cz) + OFF
        r = 8 * lax.rem(r, 4) + lax.div(r, 4)
        hit = lanes == column
        for s in range(3):
            picked[pl.ds(s * slots + p, 1), :] = jnp.where(hit, value[s, plane, pl.ds(r, 1), :], 0.0)
    q = lax.dot_general(
        jnp.ones((8, cr), BF16),
        picked[...].astype(BF16),
        (((1,), (1,)), ((), ())),
        preferred_element_type=F32,
    )
    q_out[...] = jnp.broadcast_to(q[0:1][None], q_out.shape)


def last_stage(ca, cz, u2, u0, banded, state, fax, part):
    for j in (0, 1, ca + 2, ca + 3):
        ax_only(split_state([u2[f, j, 0:ROWS] for f in range(5)]), fax, j)

    step = ca // STEPS

    for i in range(STEPS):
        js = [2 + step * i + k for k in range(step)]
        us = [split_state([u2[f, j] for f in range(5)]) for j in js]
        both_sides(us, js, fax, part, banded)

    first, quarter = OFF // 4, cz // 4

    @pl.loop(0, 5)
    def _(f):
        fa = window(fax, f)
        for k in range(ca):
            j = k + 2
            new = u2[f, j, 0:ROWS] + change(fa, part, f, j, ROWS)
            new = u0[f, k] * (1.0 / 3.0) + (2.0 / 3.0) * new
            for l in range(4):
                state[f, k, pl.ds(l, quarter, stride=4), :] = new[8 * l + first : 8 * l + first + quarter]


def signals(slots, rows, offsets, weight, out):
    ndev = rows.shape[0]
    group = 32
    cols = group * slots
    lanes = rows.shape[1]
    col = lax.broadcasted_iota(jnp.int32, (1, cols), 1)
    owner = lax.broadcasted_iota(jnp.int32, (group, cols), 0) == col // slots
    lane = lax.broadcasted_iota(jnp.int32, (lanes, cols), 0)
    time = lax.broadcasted_iota(jnp.int32, (NB, cols), 0).astype(F32)
    total = jnp.zeros(out.shape, F32)
    for g in range(ndev // group):
        q = rows[g * group : (g + 1) * group, :].astype(BF16)
        off = offsets[0:1, g * group : (g + 1) * group].astype(F32)
        off = jnp.broadcast_to(off, (8, group)).astype(BF16)
        bins = jnp.dot(off, owner.astype(BF16), preferred_element_type=F32)[0:1]
        table = jnp.zeros((NB, cols), F32)
        for s in range(3):
            pick = jnp.where(lane == s * slots + col % slots, 1.0, 0.0).astype(BF16)
            spread = jnp.dot(q, pick, preferred_element_type=F32)
            line = jnp.sum(jnp.where(owner, spread, 0.0), axis=0, keepdims=True)
            table = jnp.where(time == bins + s, line, table)
        total = total + lax.dot_general(
            weight[:, g * cols : (g + 1) * cols],
            table.astype(BF16),
            (((1,), (1,)), ((), ())),
            preferred_element_type=F32,
        )
    out[...] = total


def swap_pairs(count, periodic):
    one = [(i, i ^ 1) for i in range(count)]
    two = []
    for i in range(count):
        j = i - 1 if i % 2 == 0 else i + 1
        two.append((i, j % count if periodic or 0 <= j < count else i))
    return one, two


def swap(first, second, axis, periodic):
    count = 1
    for name in (axis,) if isinstance(axis, str) else axis:
        count = count * lax.axis_size(name)
    one, two = swap_pairs(count, periodic)
    if periodic:
        one, two = two, one
    return lax.ppermute(first, axis, one), lax.ppermute(second, axis, two)


def local(density, velocity, pressure, panel_cell, obs_weight, bin_offset):
    ca, cz, cr = density.shape
    slots = panel_cell.shape[0]
    ndev = bin_offset.shape[1]
    n_ax, n_rad = lax.axis_size("y") * lax.axis_size("core"), lax.axis_size("rad")
    planes = ca + 2 * REACH
    part = functools.partial
    given = (density.reshape(ca * cz, cr), velocity.reshape(3 * ca * cz, cr), pressure.reshape(ca * cz, cr))

    edge = struct((5 * REACH * cz, cr), BF16)
    strip = struct((5 * REACH * ca, cr), BF16)
    home, ax1, ax2 = call(
        part(load_and_pack, ca, cz),
        (struct((5 * ca * cz, cr)), edge, edge),
        [HBM] * 3,
        [pltpu.SemaphoreType.DMA((3,))],
    )(*[far(x) for x in given])
    az1, az2 = call(part(pack_az, ca, cz), (strip, strip), [VMEM])(home)
    ax1, ax2 = swap(ax1, ax2, ("y", "core"), False)
    az1, az2 = swap(az1, az2, "az", True)
    grid = struct((5 * planes * ROWS, cr))
    ends = ("either",) if n_rad == 2 else ("low", "high")
    tiles = cr // SLOT
    table = [struct((tiles * cr, cr), BF16)] * len(ends) + [struct((cr, tiles * cr // 4), BF16)] * len(ends)
    block, banded, *tables = call(
        part(prepare, ends, ca, cz, n_rad),
        (grid, struct((2 * cr, 2 * cr), BF16), *table),
        [VMEM],
    )(home)
    edges, places = tables[: len(ends)], tables[len(ends) :]

    corner = struct((5 * MID * 2 * MID, cr), BF16)
    near = pltpu.VMEM((5, 2 * MID * cz, cr), F32)
    corner1, corner2 = call(part(pack_corners, n_ax, cz), (corner, corner), [VMEM] * 2, [near])(ax1, ax2)
    corner1, corner2 = swap(corner1, corner2, "az", True)

    side = struct((5 * (ca + 2 * MID) * ROWS // tiles, cr), BF16)
    block = call(
        part(add_sides, n_ax, ca, cz),
        grid,
        [VMEM] * 5,
        [pltpu.VMEM((5, 2 * REACH * cz, cr), F32), pltpu.VMEM((2,) + strip.shape, F32)],
        mib=8,
        alias={0: 0},
        cost=pl.CostEstimate(flops=100_000_000, bytes_accessed=4_000_000, transcendentals=0),
    )(block, ax1, ax2, az1, az2)
    got = call(
        part(add_corners, len(ends), ca, cz),
        (grid,) + tuple(side for _ in ends),
        [VMEM] * (3 + len(ends)),
        [pltpu.VMEM((2,) + corner.shape, F32)],
        mib=8,
        alias={0: 0},
    )(block, corner1, corner2, *edges)
    block = got[0].reshape(5, planes, ROWS, cr)
    if n_rad == 2:
        sides = (lax.ppermute(got[1], "rad", [(0, 1), (1, 0)]),)
    else:
        up = [(i, i + 1) for i in range(n_rad - 1)]
        sides = (lax.ppermute(got[1], "rad", [(j, i) for i, j in up]), lax.ppermute(got[2], "rad", up))

    grid = (5, planes, TALL, cr)
    q, u2, u0 = call(
        part(stages, n_ax, n_rad, ca, cz, slots),
        (struct((ndev, 1, 128)), struct((5, ca + 4, TALL, cr)), struct((5, ca, ROWS, cr))),
        [VMEM, VMEM, HBM] + [VMEM] * (2 * len(sides)),
        [pltpu.VMEM((5, ca + 2 * MID, 8, cr), F32)]
        + [pltpu.VMEM(grid, F32) for _ in range(4)]
        + [pltpu.VMEM((3, planes, ROWS, cr), F32), pltpu.VMEM((128, cr), F32)]
        + [pltpu.SMEM((slots,), jnp.int32), pltpu.SemaphoreType.DMA],
        mib=28,
    )(block, banded, far(panel_cell), *sides, *places)

    rows = lax.all_to_all(q, ("y", "core", "az", "rad"), 0, 0, tiled=True).reshape(ndev, 128)

    grid = (5, ca + 4, TALL, cr)
    state = call(
        part(last_stage, ca, cz),
        struct((5, ca, cz, cr)),
        [VMEM] * 3,
        [pltpu.VMEM(grid, F32), pltpu.VMEM(grid, F32)],
        mib=12,
        cost=pl.CostEstimate(flops=400_000_000, bytes_accessed=8_000_000, transcendentals=0),
    )(u2, u0, banded)
    signal = call(
        part(signals, slots), struct((obs_weight.shape[0], NB)), [VMEM] * 3, mib=24
    )(rows, bin_offset, obs_weight)
    return (state, signal)


def solution(mesh):
    n_ax, n_az, n_rad = (mesh.shape[name] for name in ("ax", "az", "rad"))
    split = Mesh(mesh.devices.reshape(n_ax // 2, 2, n_az, n_rad), ("y", "core", "az", "rad"))
    ax = ("y", "core")
    every = ax + ("az", "rad")
    in_specs = (
        P(ax, "az", "rad"),
        P(None, ax, "az", "rad"),
        P(ax, "az", "rad"),
        P(every),
        P(every, None),
        P(every, None),
    )
    out_specs = (P(None, ax, "az", "rad"), P(every, None))
    return jax.shard_map(local, mesh=split, in_specs=in_specs, out_specs=out_specs, check_vma=False)
```
